32 devices in a mesh: dp: 8 (over y, x, core), seq: 4 (over z).
Axes of the slice: x: 2, y: 2, z: 4, core: 2. Of those that a mesh axis runs over, the one named last changes fastest.
Arguments:
- noisy_latents: float32 [24576, 16], P(('dp', 'seq')), may hold values from -6 to 6
- target_latents: float32 [24576, 16], P(('dp', 'seq')), may hold values from -6 to 6
- noise_levels: int32 [96], P(('dp', 'seq')), may hold values from 0 to 999
- clip_start: int32 [96], P(('dp', 'seq')), may hold values from 0 to 11, as said below
- qkv_weight: float32 [3072, 1024], P(('dp', 'seq')), may hold values from -0.09375 to 0.09375
- qkv_moment: float32 [3072, 1024], P(('dp', 'seq')), may hold values from -3.0517578e-05 to 3.0517578e-05
- out_weight: float32 [1024, 1024], P(('dp', 'seq')), may hold values from -0.75 to 0.75
- out_moment: float32 [1024, 1024], P(('dp', 'seq')), may hold values from -3.0517578e-05 to 3.0517578e-05
- up_weight: float32 [4096, 1024], P(('dp', 'seq')), may hold values from -0.1875 to 0.1875
- up_moment: float32 [4096, 1024], P(('dp', 'seq')), may hold values from -3.0517578e-05 to 3.0517578e-05
- down_weight: float32 [4096, 1024], P(('dp', 'seq')), may hold values from -0.09375 to 0.09375
- down_moment: float32 [4096, 1024], P(('dp', 'seq')), may hold values from -3.0517578e-05 to 3.0517578e-05
- ada_weight: float32 [6144, 1024], P(('dp', 'seq')), may hold values from -0.1875 to 0.1875
- ada_first: float32 [6144, 1024], P(('dp', 'seq')), may hold values from -3.8146973e-06 to 3.8146973e-06
- ada_second: float32 [6144, 1024], P(('dp', 'seq')), may hold values from 2.6490954e-13 to 1.0596382e-12
- patch_weight: float32 [2, 16, 1024], replicated, may hold values from -1.5 to 1.5
- patch_first: float32 [2, 16, 1024], replicated, may hold values from -7.6293945e-06 to 7.6293945e-06
- patch_second: float32 [2, 16, 1024], replicated, may hold values from 1.0596382e-12 to 4.2385527e-12
- vectors: float32 [8, 1024], replicated, may hold values from 0.5 to 1.5
- vec_first: float32 [8, 1024], replicated, may hold values from -1.9073486e-05 to 1.9073486e-05
- vec_second: float32 [8, 1024], replicated, may hold values from 6.6227384e-12 to 2.6490954e-11
Outputs:
- loss_sum: float32 [], replicated
- grad_norm: float32 [], replicated
- qkv_new: float32 [3072, 1024], P(('dp', 'seq'))
- qkv_moment_new: float32 [3072, 1024], P(('dp', 'seq'))
- out_new: float32 [1024, 1024], P(('dp', 'seq'))
- out_moment_new: float32 [1024, 1024], P(('dp', 'seq'))
- up_new: float32 [4096, 1024], P(('dp', 'seq'))
- up_moment_new: float32 [4096, 1024], P(('dp', 'seq'))
- down_new: float32 [4096, 1024], P(('dp', 'seq'))
- down_moment_new: float32 [4096, 1024], P(('dp', 'seq'))
- ada_new: float32 [6144, 1024], P(('dp', 'seq'))
- ada_first_new: float32 [6144, 1024], P(('dp', 'seq'))
- ada_second_new: float32 [6144, 1024], P(('dp', 'seq'))
- patch_new: float32 [2, 16, 1024], replicated
- patch_first_new: float32 [2, 16, 1024], replicated
- patch_second_new: float32 [2, 16, 1024], replicated
- vectors_new: float32 [8, 1024], replicated
- vec_first_new: float32 [8, 1024], replicated
- vec_second_new: float32 [8, 1024], replicated
The draws below stay inside these ranges and needn't reach their ends.
Inputs may be any that keep to these rules, and one draw needn't show every extreme that they name: `clip_start`: clips are runs of whole frames inside one group of 12 frames; every frame of a clip holds the group-local index of the clip's first frame; in every group one clip starts at a frame of the first device of seq other than the group's first frame and covers frames on every device of seq; the group's last frame starts a clip of its own.
All inputs are finite; a program needn't handle non-finite values.
Results may differ from the reference program's by a relative error of at most 0.0065.
Values may be sent and summed in bfloat16 or wider, within the bound.
No kernel may reach another device: no remote copies, remote signals or barrier semaphores. Data moves between devices by JAX's collectives and lax.ppermute only.
A program may use at most 256 MiB of HBM per device.

```python
import math
import jax
import jax.numpy as jnp
from jax import lax

D = 1024
HEADS = 16
FF = 4096
PATCH = 16
GRID = 16
FR_DEV = 3
NS_ITERS = 2
STEP = 10
FRAME_TOK = 256
GROUP_FR = 12
FRAMES = 96
TOKENS = 24576
N_DP = 8
N_SEQ = 4


def draw_clip_start(key, part):
    key = jax.random.fold_in(key, 7)
    group_frames = FR_DEV * N_SEQ
    key_long, key_cut, key_open = jax.random.split(key, 3)
    opening = jax.random.randint(key_open, (N_DP,), 1, FR_DEV)
    longest = jax.random.randint(key_long, (N_DP,), (N_SEQ - 1) * FR_DEV + 1, group_frames)
    cuts = jax.random.randint(key_cut, (N_DP, group_frames), 0, 2)
    frame = jnp.arange(group_frames, dtype=jnp.int32)[None, :]
    opens = (frame == 0) | (frame == opening[:, None]) | (frame == longest[:, None]) | (frame == group_frames - 1)
    opens = opens | (frame > longest[:, None]) & (cuts == 1)
    marks = jnp.where(opens, frame, 0)
    return lax.cummax(marks, axis=1).reshape(-1).astype(jnp.int32)


def set_ends(values, rng, least, high):
    longest = values.shape.index(max(values.shape))
    spots = []
    for shift in (0, 1):
        where = [jax.random.randint(jax.random.fold_in(rng, axis), (), 0, length) for axis, length in enumerate(values.shape)]
        where[longest] = (where[longest] + shift) % values.shape[longest]
        spots.append(tuple(where))
    return values.at[spots[0]].set(least).at[spots[1]].set(high)


def block_scale(rng, shape, shards, smallest, top_value):
    level, own = 1.0, jax.random.fold_in(rng, 6)
    for dim, blocks in shards:
        draws = jnp.exp(jax.random.uniform(jax.random.fold_in(own, dim), (blocks,), jnp.float32, smallest / len(shards), top_value / len(shards)))
        level = level * jnp.repeat(draws, shape[dim] // blocks).reshape([-1 if axis == dim else 1 for axis in range(len(shape))])
    return level


def gaussian(rng, dims, scale, reach, shards=(), held_as=jnp.bfloat16):
    result = jax.random.normal(rng, dims, jnp.float32) * scale
    if len(shards) > 0:
        result = block_scale(rng, dims, shards, -0.22, 0.18) * result
    return jnp.clip(result, min=-reach, max=reach).astype(held_as)


def setup_inputs(seed: int = 0) -> dict:
    key_list = jax.random.split(jax.random.key(seed), 22)
    return {
        "noisy_latents": gaussian(key_list[0], (TOKENS, PATCH), 1.0, 6.0, ((0, 32),), jnp.float32),
        "target_latents": gaussian(key_list[1], (TOKENS, PATCH), 1.0, 6.0, ((0, 32),), jnp.float32),
        "noise_levels": set_ends(jax.random.randint(key_list[2], (FRAMES,), 0, 1000), jax.random.fold_in(key_list[2], 1), 0, 999).astype(jnp.int32),
        "clip_start": draw_clip_start(jax.random.fold_in(key_list[21], 71), 0),
        "qkv_weight": gaussian(key_list[4], (3 * D, D), (4 * D) ** -0.5, 0.09375, ((0, 32),), jnp.float32),
        "qkv_moment": gaussian(key_list[5], (3 * D, D), (0.01 * (10 * D * D + 2 * FF * D) ** -0.5), 3.0517578125e-05, ((0, 32),), jnp.float32),
        "out_weight": gaussian(key_list[6], (D, D), (D // 16) ** -0.5, 0.75, ((0, 32),), jnp.float32),
        "out_moment": gaussian(key_list[7], (D, D), (0.01 * (10 * D * D + 2 * FF * D) ** -0.5), 3.0517578125e-05, ((0, 32),), jnp.float32),
        "up_weight": gaussian(key_list[8], (FF, D), D ** -0.5, 0.1875, ((0, 32),), jnp.float32),
        "up_moment": gaussian(key_list[9], (FF, D), (0.01 * (10 * D * D + 2 * FF * D) ** -0.5), 3.0517578125e-05, ((0, 32),), jnp.float32),
        "down_weight": gaussian(key_list[10], (FF, D), FF ** -0.5, 0.09375, ((0, 32),), jnp.float32),
        "down_moment": gaussian(key_list[11], (FF, D), (0.01 * (10 * D * D + 2 * FF * D) ** -0.5), 3.0517578125e-05, ((0, 32),), jnp.float32),
        "ada_weight": gaussian(key_list[12], (6 * D, D), D ** -0.5, 0.1875, ((0, 32),), jnp.float32),
        "ada_first": gaussian(key_list[13], (6 * D, D), (0.0011 * (10 * D * D + 2 * FF * D) ** -0.5), 3.814697265625e-06, ((0, 32),), jnp.float32),
        "ada_second": jnp.clip(jnp.exp(math.log(1.059638162805021e-12) - 1.3862944 * jax.random.uniform(key_list[14], (6 * D, D), jnp.float32) ** block_scale(key_list[14], (6 * D, D), ((0, 32),), -0.2, 0.2)), 2.649095407012553e-13, 1.059638162805021e-12),
        "patch_weight": gaussian(key_list[15], (2, PATCH, D), PATCH ** -0.5, 1.5, (), jnp.float32),
        "patch_first": gaussian(key_list[16], (2, PATCH, D), (0.0022 * (10 * D * D + 2 * FF * D) ** -0.5), 7.62939453125e-06, (), jnp.float32),
        "patch_second": jnp.clip(jnp.exp(jax.random.uniform(key_list[17], (2, PATCH, D), jnp.float32, math.log(1.059638162805021e-12), math.log(4.238552651220084e-12))), 1.059638162805021e-12, 4.238552651220084e-12),
        "vectors": jnp.clip(1.0 + 0.1 * jax.random.normal(key_list[18], (8, D), jnp.float32), 0.5, 1.5),
        "vec_first": gaussian(key_list[19], (8, D), (0.0055 * (10 * D * D + 2 * FF * D) ** -0.5), 1.9073486328125e-05, (), jnp.float32),
        "vec_second": jnp.clip(jnp.exp(jax.random.uniform(key_list[20], (8, D), jnp.float32, math.log(6.62273838200611e-12), math.log(2.649095352802444e-11))), 6.62273838200611e-12, 2.649095352802444e-11),
    }


@jax.custom_vjp
def low(v):
    return lax.optimization_barrier(v.astype(jnp.bfloat16)).astype(jnp.float32)

@jax.custom_vjp
def low_back(v):
    return v

def low_keep(v):
    return (low(v), None)

def low_pass(kept, grad):
    return (grad,)

def back_keep(v):
    return (v, None)

def back_low(kept, grad):
    return (low(grad),)
low.defvjp(low_keep, low_pass)
low_back.defvjp(back_keep, back_low)
highest = lax.Precision.HIGHEST
coef_one = 3.4445
coef_two = -4.775
coef_three = 2.0315

def layer_norm(value):
    mean = lax.optimization_barrier(jnp.mean(value, axis=-1, keepdims=True))
    centred = value - mean
    return centred * lax.rsqrt(lax.optimization_barrier(jnp.mean(centred * centred, axis=-1, keepdims=True)) + 1e-06)

def level_features(levels, width):
    half = width // 2
    freqs = jnp.exp(-math.log(10000.0) * jnp.arange(half, dtype=jnp.float32) / half)
    angle = levels.astype(jnp.float32)[:, None] * freqs[None, :]
    return jnp.concatenate([jnp.sin(angle), jnp.cos(angle)], axis=-1)

def rope_angles(time_pos, row_pos, col_pos, head_dim):
    sec_time = head_dim // 4
    sec_space = (head_dim - sec_time) // 2
    angles = []
    for where_pos, size in ((time_pos, sec_time), (row_pos, sec_space), (col_pos, sec_space)):
        half = size // 2
        freqs = jnp.exp(-math.log(10000.0) * jnp.arange(half, dtype=jnp.float32) * 2.0 / size)
        angles.append(where_pos[:, None] * freqs[None, :])
    return angles

def rotate(value, angles):
    pieces = []
    offset = 0
    for angle in angles:
        half = angle.shape[1]
        first = value[..., offset:offset + half]
        second = value[..., offset + half:offset + 2 * half]
        cosine = jnp.cos(angle)[:, None, :]
        sine = jnp.sin(angle)[:, None, :]
        pieces.append(first * cosine - second * sine)
        pieces.append(second * cosine + first * sine)
        offset += 2 * half
    return jnp.concatenate(pieces, axis=-1)

def group_attention(queries, keys, values, starts):
    group_tokens = queries.shape[0]
    scale = 1.0 / math.sqrt(queries.shape[-1])
    frames = jnp.arange(group_tokens, dtype=jnp.int32) // FRAME_TOK
    allowed = (frames[None, :] >= starts[frames][:, None]) & (frames[None, :] <= frames[:, None])

    def one_head(parts):
        query_head, key_head, value_head = parts
        scores = low_back(jnp.dot(query_head, key_head.T, precision=highest) * scale)
        scores = jnp.where(allowed, scores, -1e+30)
        top = lax.optimization_barrier(jnp.max(scores, axis=-1, keepdims=True))
        expo = jnp.exp(scores - top)
        probs = expo / lax.optimization_barrier(jnp.sum(expo, axis=-1, keepdims=True))
        return low(low_back(jnp.dot(low(probs), value_head, precision=highest)))
    moved = (jnp.moveaxis(queries, 1, 0), jnp.moveaxis(keys, 1, 0), jnp.moveaxis(values, 1, 0))
    return jnp.moveaxis(lax.map(jax.checkpoint(one_head), moved), 0, 1)

def forward(weights, noisy, target, levels, starts, places):
    qkv_w, out_w, up_w, down_w, ada_w, patch_w, vecs = weights
    time_tok, row_tok, col_tok, valid = places
    width = qkv_w.shape[1]
    head_dim = width // HEADS
    frames = levels.shape[0]
    ftok = noisy.shape[0] // frames
    state = (jnp.dot(noisy, patch_w[0], precision=highest) + vecs[0]).reshape(frames, ftok, width)
    cond = jax.nn.silu(level_features(levels, width))
    modul = low_back(jnp.dot(low(cond), low(ada_w).T, precision=highest))
    modul = modul.reshape(frames, 6, width) + vecs[2:8][None]
    mods = [modul[:, j][:, None, :] for j in range(6)]
    h_one = (layer_norm(state) * (1.0 + mods[1]) + mods[0]).reshape(-1, width)
    qkv = low_back(jnp.dot(low(h_one), low(qkv_w).T, precision=highest)).reshape(-1, 3, HEADS, head_dim)
    angles = rope_angles(time_tok, row_tok, col_tok, head_dim)
    queries = low(low_back(rotate(qkv[:, 0], angles)))
    keys_rot = low(low_back(rotate(qkv[:, 1], angles)))
    values = low(low_back(qkv[:, 2]))
    group_tokens = GROUP_FR * ftok
    shaped = (queries.reshape(N_DP, group_tokens, HEADS, head_dim), keys_rot.reshape(N_DP, group_tokens, HEADS, head_dim), values.reshape(N_DP, group_tokens, HEADS, head_dim), starts.reshape(N_DP, GROUP_FR))
    attended = lax.map(lambda blk: group_attention(*blk), shaped).reshape(-1, width)
    branch = low_back(jnp.dot(attended, low(out_w).T, precision=highest))
    state = state + mods[2] * branch.reshape(frames, ftok, width)
    h_two = (layer_norm(state) * (1.0 + mods[4]) + mods[3]).reshape(-1, width)
    hidden = low_back(jnp.dot(low(h_two), low(up_w).T, precision=highest))
    mixed = low_back(jnp.dot(low(jax.nn.gelu(hidden, approximate=True)), low(down_w), precision=highest))
    state = state + mods[5] * mixed.reshape(frames, ftok, width)
    final = (layer_norm(state) * vecs[1]).reshape(-1, width)
    pred = jnp.dot(final, patch_w[1].T, precision=highest).reshape(frames, -1)
    goal = target.reshape(frames, -1)
    prev_pred = jnp.concatenate([jnp.zeros_like(pred[:1]), pred[:-1]], axis=0)
    prev_goal = jnp.concatenate([jnp.zeros_like(goal[:1]), goal[:-1]], axis=0)
    diff = pred - prev_pred - (goal - prev_goal)
    return jnp.sum(jnp.where(valid[:, None], diff * diff, 0.0))

def muon(weight, moment, grad):
    rows = weight.shape[0]
    width = weight.shape[1]
    moment_new = 0.95 * moment + grad
    steer = grad + 0.95 * moment_new
    gram = jnp.dot(steer.T, steer, precision=highest)
    scale = jnp.sqrt(jnp.trace(gram)) + 1e-07
    current = steer / scale
    gram = gram / (scale * scale)
    for sweep in range(NS_ITERS):
        if sweep > 0:
            gram = jnp.dot(current.T, current, precision=highest)
        product = jnp.dot(current, gram, precision=highest)
        current = coef_one * current + coef_two * product + coef_three * jnp.dot(product, gram, precision=highest)
    factor = 2.0 * math.sqrt(max(1.0, rows / width))
    return (weight * (1.0 - 2.0 * 0.01) - factor * current, moment_new)

def adamw(weight, first, second, grad, rate):
    first = 0.9 * first + 0.1 * grad
    second = 0.95 * second + 0.05 * grad * grad
    first_hat = first / (1.0 - 0.9 ** STEP)
    second_hat = second / (1.0 - 0.95 ** STEP)
    weight = weight - rate * (first_hat / (jnp.sqrt(second_hat) + 1e-08) + 0.01 * weight)
    return (weight, first, second)

def reference(noisy_latents, target_latents, noise_levels, clip_start, qkv_weight, qkv_moment, out_weight, out_moment, up_weight, up_moment, down_weight, down_moment, ada_weight, ada_first, ada_second, patch_weight, patch_first, patch_second, vectors, vec_first, vec_second):
    frames = noise_levels.shape[0]
    frame_group = jnp.arange(frames, dtype=jnp.int32) % GROUP_FR
    valid = frame_group > clip_start
    time_frame = (frame_group - clip_start).astype(jnp.float32)
    token_ids = jnp.arange(frames * FRAME_TOK, dtype=jnp.int32)
    spot = token_ids % FRAME_TOK
    places = (time_frame[token_ids // FRAME_TOK], (spot // GRID).astype(jnp.float32), (spot % GRID).astype(jnp.float32), valid)
    count = jnp.float32(frames * FRAME_TOK * PATCH)
    weights = (qkv_weight, out_weight, up_weight, down_weight, ada_weight, patch_weight, vectors)

    def loss_of(*params):
        return forward(params, noisy_latents, target_latents, noise_levels, clip_start, places)
    loss_total, pullback = jax.vjp(loss_of, *weights)
    grads = pullback(1.0 / count)
    norm = jnp.sqrt(sum((jnp.sum(g * g) for g in grads)))
    clip = jnp.minimum(1.0, 0.01 / norm)
    grads = [clip * g for g in grads]
    qkv_new, qkv_mom = muon(qkv_weight, qkv_moment, grads[0])
    out_new, out_mom = muon(out_weight, out_moment, grads[1])
    up_new, up_mom = muon(up_weight, up_moment, grads[2])
    down_new, down_mom = muon(down_weight, down_moment, grads[3])
    ada_new, ada_one, ada_two = adamw(ada_weight, ada_first, ada_second, grads[4], 0.08)
    patch_new, patch_one, patch_two = adamw(patch_weight, patch_first, patch_second, grads[5], 0.15)
    vec_new, vec_one, vec_two = adamw(vectors, vec_first, vec_second, grads[6], 0.5)
    return (loss_total, norm, qkv_new, qkv_mom, out_new, out_mom, up_new, up_mom, down_new, down_mom, ada_new, ada_one, ada_two, patch_new, patch_one, patch_two, vec_new, vec_one, vec_two)
```

```python
from functools import partial
import math

import jax
import jax.numpy as jnp
import numpy as np
from jax import lax
from jax.experimental import pallas as pl
from jax.experimental.pallas import tpu as pltpu
from jax.sharding import Mesh, PartitionSpec as P

HEADS = 16
NS_ITERS = 2
STEP = 10
ALL = ("a", "x", "c", "z")

highest = lax.Precision.HIGHEST
coef_one = 3.4445
coef_two = -4.775
coef_three = 2.0315
low_type = jnp.bfloat16
wide = jnp.float32
NT = (((1,), (1,)), ((), ()))
TN = (((0,), (0,)), ((), ()))
MIB = 1 << 20


def dot_nt(left, right):
    return lax.dot_general(left, right, NT, preferred_element_type=wide)


def dot_tn(left, right):
    return lax.dot_general(left, right, TN, preferred_element_type=wide)


def dot_nn(left, right):
    return jnp.dot(left, right, preferred_element_type=wide)


def layer_stats(value):
    mean = jnp.mean(value, axis=-1, keepdims=True)
    centred = value - mean
    rstd = lax.rsqrt(jnp.mean(centred * centred, axis=-1, keepdims=True) + 1e-06)
    return (centred * rstd, rstd)


def layer_back(normed, rstd, upstream):
    return rstd * (
        upstream
        - jnp.mean(upstream, axis=-1, keepdims=True)
        - normed * jnp.mean(upstream * normed, axis=-1, keepdims=True)
    )


def level_features(levels, width):
    half = width // 2
    freqs = jnp.exp(-math.log(10000.0) * jnp.arange(half, dtype=jnp.float32) / half)
    angle = levels.astype(jnp.float32)[:, None] * freqs[None, :]
    return jnp.concatenate([jnp.sin(angle), jnp.cos(angle)], axis=-1)


def adamw(weight, first, second, grad, rate):
    first = 0.9 * first + 0.1 * grad
    second = 0.95 * second + 0.05 * grad * grad
    first_hat = first / (1.0 - 0.9**STEP)
    second_hat = second / (1.0 - 0.95**STEP)
    weight = weight - rate * (first_hat / (jnp.sqrt(second_hat) + 1e-08) + 0.01 * weight)
    return (weight, first, second)


def rope_tables(head_dim, heads, frame_tok):
    sec_time = head_dim // 4
    sec_space = (head_dim - sec_time) // 2
    side = math.isqrt(frame_tok)
    spot = np.arange(frame_tok)
    firsts, seconds, time_freq, space = [], [], [], []
    offset = 0
    for kind, size in ((0, sec_time), (1, sec_space), (2, sec_space)):
        half = size // 2
        freqs = np.exp(-math.log(10000.0) * np.arange(half, dtype=np.float64) * 2.0 / size)
        firsts += list(range(offset, offset + half))
        seconds += list(range(offset + half, offset + size))
        offset += size
        where = {0: np.zeros(frame_tok), 1: spot // side, 2: spot % side}[kind]
        space.append(where[:, None] * freqs[None, :])
        time_freq.append(freqs if kind == 0 else np.zeros(half))
    is_time = np.concatenate([np.ones(sec_time // 2), np.zeros(sec_space)])
    space = np.concatenate(space, axis=1)
    space_cos = np.where(is_time[None] > 0, 0.0, np.cos(space))
    space_sin = np.where(is_time[None] > 0, 0.0, np.sin(space))
    time_freq = np.concatenate(time_freq)
    order = np.concatenate(
        [
            np.concatenate([np.asarray(part) + h * head_dim for h in range(heads)])
            for part in (firsts, seconds)
        ]
    )
    total = heads * head_dim
    select = np.zeros((total, total), np.float32)
    select[np.arange(total), order] = 1.0
    tile = lambda t: np.tile(t, (1, heads)).astype(np.float32)
    return (
        tile(space_cos),
        tile(space_sin),
        np.tile(time_freq, heads).astype(np.float32),
        np.tile(is_time, heads).astype(np.float32),
        select,
    )


def split_mask(shape, axis, heads, half_lanes, value):
    lane = lax.broadcasted_iota(jnp.int32, shape, axis)
    if half_lanes is not None:
        lane = lane % half_lanes
        return lane // (half_lanes // heads) == value
    return lane // (shape[axis] // heads) == value


def embed_qkv_kernel(
    noisy_ref, pw_ref, bias_ref, mod_ref, w_ref, sel_ref, cs_ref, sn_ref, tc_ref, ts_ref,
    h_ref, q_ref, k_ref, v_ref, wq_scr, *, width, local, scale,
):
    @pl.when(pl.program_id(0) == 0)
    def _():
        for part in range(2):
            rows = pl.ds(part * local, local)
            wq_scr[rows, :] = dot_nn(sel_ref[...], w_ref[rows, :]).astype(low_type)
        rows = pl.ds(2 * local, local)
        wq_scr[rows, :] = w_ref[rows, :]

    state = lax.dot_general(
        noisy_ref[0], pw_ref[...], TN, precision=highest, preferred_element_type=wide
    ) + bias_ref[...]
    normed, _ = layer_stats(state)
    shift = mod_ref[0, :, 0:width]
    scl = mod_ref[0, :, width : 2 * width]
    h_low = (normed * (1.0 + scl) + shift).astype(low_type)
    h_ref[...] = h_low
    out = dot_nt(h_low, wq_scr[...])
    cosine = cs_ref[...] + tc_ref[0]
    sine = sn_ref[...] + ts_ref[0]
    half = local // 2
    for part, ref, mult in ((0, q_ref, scale), (1, k_ref, 1.0)):
        first = out[:, part * local : part * local + half]
        second = out[:, part * local + half : (part + 1) * local]
        ref[:, 0:half] = ((first * cosine - second * sine).astype(low_type).astype(wide) * mult).astype(low_type)
        ref[:, half:local] = ((second * cosine + first * sine).astype(low_type).astype(wide) * mult).astype(low_type)
    v_ref[...] = out[:, 2 * local : 3 * local].astype(low_type)


def embed_qkv(noisy_t, pw, bias, mod, w_local, tables, tcos, tsin, scale):
    frames, patch, ftok = noisy_t.shape
    width = pw.shape[1]
    local = w_local.shape[0] // 3
    cs, sn, _, _, sel = tables
    tokens = frames * ftok
    full = lambda shape: pl.BlockSpec(shape, lambda i: (0,) * len(shape))
    row = lambda cols: pl.BlockSpec((ftok, cols), lambda i: (i, 0))
    return pl.pallas_call(
        partial(embed_qkv_kernel, width=width, local=local, scale=scale),
        grid=(frames,),
        in_specs=[
            pl.BlockSpec((1, patch, ftok), lambda i: (i, 0, 0)),
            full(pw.shape),
            full((1, width)),
            pl.BlockSpec((1, 1, 6 * width), lambda i: (i, 0, 0)),
            full(w_local.shape),
            full(sel.shape),
            full(cs.shape),
            full(sn.shape),
            pl.BlockSpec((1, 1, local // 2), lambda i: (i, 0, 0)),
            pl.BlockSpec((1, 1, local // 2), lambda i: (i, 0, 0)),
        ],
        out_specs=[row(width), row(local), row(local), row(local)],
        out_shape=[
            jax.ShapeDtypeStruct((tokens, width), low_type),
            jax.ShapeDtypeStruct((tokens, local), low_type),
            jax.ShapeDtypeStruct((tokens, local), low_type),
            jax.ShapeDtypeStruct((tokens, local), low_type),
        ],
        scratch_shapes=[pltpu.VMEM(w_local.shape, low_type)],
        compiler_params=pltpu.CompilerParams(
            dimension_semantics=("arbitrary",), vmem_limit_bytes=40 * MIB
        ),
        cost_estimate=pl.CostEstimate(
            flops=2 * tokens * width * 3 * local, bytes_accessed=12 * MIB, transcendentals=0
        ),
        name="embed_qkv",
    )(noisy_t, pw, bias, mod, w_local, sel, cs, sn, tcos, tsin)


def attend_kernel(st_ref, q_ref, k_ref, v_ref, o_ref, ol_ref, lse_ref, vt_scr, s_scr, *, heads, ftok):
    i = pl.program_id(0)
    frames = pl.num_programs(0)
    local = q_ref.shape[1]
    hd = local // heads

    @pl.when(i == 0)
    def _():
        for f in range(vt_scr.shape[0]):
            vt_scr[f] = v_ref[f * ftok : (f + 1) * ftok, :].T

    first = st_ref[i]
    query = q_ref[...]
    zero = jnp.zeros_like(query)
    masked = [
        jnp.where(split_mask(query.shape, 1, heads, local // 2, h), query, zero)
        for h in range(heads)
    ]

    def scores(j, tops):
        key = k_ref[pl.ds(pl.multiple_of(j * ftok, ftok), ftok), :]
        new = []
        for h in range(heads):
            s = dot_nt(key, masked[h])
            s_scr[h, j] = s
            new.append(jnp.maximum(tops[h], jnp.max(s.reshape(ftok // 8, 8, ftok), axis=0)))
        return tuple(new)

    tops = lax.fori_loop(
        first, i + 1, scores, tuple(jnp.full((8, ftok), -1e30, wide) for _ in range(heads))
    )
    tops = [jnp.max(t, axis=0, keepdims=True) for t in tops]

    def values(j, carry):
        sums, accs = carry
        new_sums, new_accs = [], []
        vt = vt_scr[j]
        for h in range(heads):
            p = jnp.exp(s_scr[h, j] - tops[h])
            new_sums.append(sums[h] + jnp.sum(p.reshape(ftok // 8, 8, ftok), axis=0))
            new_accs.append(accs[h] + dot_nn(vt[h * hd : (h + 1) * hd, :], p.astype(low_type)))
        return (tuple(new_sums), tuple(new_accs))

    sums, accs = lax.fori_loop(
        first,
        i + 1,
        values,
        (
            tuple(jnp.zeros((8, ftok), wide) for _ in range(heads)),
            tuple(jnp.zeros((hd, ftok), wide) for _ in range(heads)),
        ),
    )
    outs, logs = [], []
    for h in range(heads):
        total = jnp.sum(sums[h], axis=0, keepdims=True)
        outs.append(accs[h] * (1.0 / total))
        logs.append(tops[h] + jnp.log(total))
    out = jnp.concatenate(outs, axis=0).T
    o_ref[...] = out
    ol_ref[...] = out.astype(low_type)
    lse_ref[0] = jnp.concatenate(logs + [jnp.zeros((8 - heads, ftok), wide)], axis=0)


def attend(starts, q, k, v, frames, heads):
    tokens, local = q.shape
    ftok = tokens // frames
    full = lambda shape: pl.BlockSpec(shape, lambda i, s: (0,) * len(shape))
    row = lambda cols: pl.BlockSpec((ftok, cols), lambda i, s: (i, 0))
    return pl.pallas_call(
        partial(attend_kernel, heads=heads, ftok=ftok),
        grid_spec=pltpu.PrefetchScalarGridSpec(
            num_scalar_prefetch=1,
            grid=(frames,),
            in_specs=[row(local), full(k.shape), full(v.shape)],
            out_specs=[row(local), row(local), pl.BlockSpec((1, 8, ftok), lambda i, s: (i, 0, 0))],
            scratch_shapes=[
                pltpu.VMEM((frames, local, ftok), low_type),
                pltpu.VMEM((heads, frames, ftok, ftok), wide),
            ],
        ),
        out_shape=[
            jax.ShapeDtypeStruct((tokens, local), wide),
            jax.ShapeDtypeStruct((tokens, local), low_type),
            jax.ShapeDtypeStruct((frames, 8, ftok), wide),
        ],
        compiler_params=pltpu.CompilerParams(
            dimension_semantics=("arbitrary",), vmem_limit_bytes=48 * MIB
        ),
        cost_estimate=pl.CostEstimate(
            flops=2 * 2 * tokens * tokens * local // 2, bytes_accessed=12 * MIB, transcendentals=0
        ),
        name="attend",
    )(starts, q, k, v)


def attend_back_kernel(
    st_ref, q_ref, do_ref, o_ref, lse_ref, k_ref, v_ref, dq_ref, dk_ref, dv_ref,
    kt_scr, dk_scr, dv_scr, dqt_scr, *, heads, ftok, scale,
):
    i = pl.program_id(0)
    frames = pl.num_programs(0)
    local = q_ref.shape[1]
    hd = local // heads
    hh = hd // 2
    half = local // 2

    @pl.when(i == 0)
    def _():
        for f in range(kt_scr.shape[0]):
            kt_scr[f] = k_ref[f * ftok : (f + 1) * ftok, :].T
        dk_scr[...] = jnp.zeros_like(dk_scr)
        dv_scr[...] = jnp.zeros_like(dv_scr)

    first = st_ref[i]
    query = q_ref[...]
    grad = do_ref[...]
    zero = jnp.zeros_like(query)
    q_mask = [
        jnp.where(split_mask(query.shape, 1, heads, half, h), query, zero) for h in range(heads)
    ]
    g_mask = [
        jnp.where(split_mask(query.shape, 1, heads, None, h), grad, zero) for h in range(heads)
    ]
    q_all = jnp.concatenate(q_mask, axis=0)
    g_all = jnp.concatenate(g_mask, axis=0)
    prod = (grad.astype(wide) * o_ref[...]).T
    delta = [
        jnp.sum(prod[h * hd : (h + 1) * hd, :], axis=0, keepdims=True) for h in range(heads)
    ]
    lse = [lse_ref[0, h : h + 1, :] for h in range(heads)]
    dqt_scr[...] = jnp.zeros_like(dqt_scr)

    def step(j, carry):
        rows = pl.ds(pl.multiple_of(j * ftok, ftok), ftok)
        key = k_ref[rows, :]
        val = v_ref[rows, :]
        kt = kt_scr[j]
        probs, d_scores = [], []
        for h in range(heads):
            p = jnp.exp(dot_nt(key, q_mask[h]) - lse[h])
            dp = dot_nt(val, g_mask[h])
            ds = (p * (dp - delta[h])).astype(low_type)
            probs.append(p.astype(low_type))
            d_scores.append(ds)
            kt_h = jnp.concatenate(
                [kt[h * hh : (h + 1) * hh, :], kt[half + h * hh : half + (h + 1) * hh, :]], axis=0
            )
            dqt_scr[h] += dot_nn(kt_h, ds)
        dv_scr[rows, :] += dot_nn(jnp.concatenate(probs, axis=1), g_all)
        dk_scr[rows, :] += dot_nn(jnp.concatenate(d_scores, axis=1), q_all)
        return carry

    lax.fori_loop(first, i + 1, step, 0)
    dqt = jnp.concatenate(
        [dqt_scr[h, 0:hh, :] for h in range(heads)] + [dqt_scr[h, hh:hd, :] for h in range(heads)],
        axis=0,
    )
    dq_ref[...] = (dqt.T * scale).astype(low_type)

    @pl.when(i == frames - 1)
    def _():
        dk_ref[...] = dk_scr[...].astype(low_type)
        dv_ref[...] = dv_scr[...].astype(low_type)


def attend_back(starts, q, grad, out, lse, k, v, frames, heads, scale):
    tokens, local = q.shape
    ftok = tokens // frames
    full = lambda shape: pl.BlockSpec(shape, lambda i, s: (0,) * len(shape))
    row = lambda cols: pl.BlockSpec((ftok, cols), lambda i, s: (i, 0))
    return pl.pallas_call(
        partial(attend_back_kernel, heads=heads, ftok=ftok, scale=scale),
        grid_spec=pltpu.PrefetchScalarGridSpec(
            num_scalar_prefetch=1,
            grid=(frames,),
            in_specs=[
                row(local), row(local), row(local),
                pl.BlockSpec((1, 8, ftok), lambda i, s: (i, 0, 0)),
                full(k.shape), full(v.shape),
            ],
            out_specs=[row(local), full(k.shape), full(v.shape)],
            scratch_shapes=[
                pltpu.VMEM((frames, local, ftok), low_type),
                pltpu.VMEM((tokens, local), wide),
                pltpu.VMEM((tokens, local), wide),
                pltpu.VMEM((heads, local // heads, ftok), wide),
            ],
        ),
        out_shape=[jax.ShapeDtypeStruct((tokens, local), low_type)] * 3,
        compiler_params=pltpu.CompilerParams(
            dimension_semantics=("arbitrary",), vmem_limit_bytes=48 * MIB
        ),
        cost_estimate=pl.CostEstimate(
            flops=5 * 2 * tokens * tokens * local // 2, bytes_accessed=16 * MIB, transcendentals=0
        ),
        name="attend_back",
    )(starts, q, grad, out, lse, k, v)


def qkv_back_kernel(
    dq_ref, dk_ref, dv_ref, h_ref, noisy_ref, pw_ref, bias_ref, mod_ref, w_ref, sel_ref,
    cs_ref, sn_ref, tc_ref, ts_ref, dw_ref, dmod_ref, demb_ref, dbias_ref,
    acc_scr, emb_scr, bias_scr, *, width, local,
):
    i = pl.program_id(0)

    @pl.when(i == 0)
    def _():
        acc_scr[...] = jnp.zeros_like(acc_scr)
        emb_scr[...] = jnp.zeros_like(emb_scr)
        bias_scr[...] = jnp.zeros_like(bias_scr)

    cosine = cs_ref[...] + tc_ref[0]
    sine = sn_ref[...] + ts_ref[0]
    half = local // 2
    parts = []
    for ref in (dq_ref, dk_ref):
        first = ref[:, 0:half].astype(wide)
        second = ref[:, half:local].astype(wide)
        turned = jnp.concatenate(
            [first * cosine + second * sine, second * cosine - first * sine], axis=1
        ).astype(low_type)
        parts.append(dot_nn(turned, sel_ref[...]).astype(low_type))
    parts.append(dv_ref[...])
    d_qkv = jnp.concatenate(parts, axis=1)
    acc_scr[...] += dot_tn(d_qkv, h_ref[...])
    d_h = dot_nn(d_qkv, w_ref[...])
    noisy = noisy_ref[0]
    state = lax.dot_general(
        noisy, pw_ref[...], TN, precision=highest, preferred_element_type=wide
    ) + bias_ref[...]
    normed, rstd = layer_stats(state)
    scl = mod_ref[0, :, width : 2 * width]
    dmod_ref[0, :, 0:width] = jnp.sum(d_h, axis=0, keepdims=True)
    dmod_ref[0, :, width : 2 * width] = jnp.sum(d_h * normed, axis=0, keepdims=True)
    d_state = layer_back(normed, rstd, d_h * (1.0 + scl))
    emb_scr[...] += jnp.dot(noisy, d_state, precision=highest, preferred_element_type=wide)
    bias_scr[...] += jnp.sum(d_state.reshape(-1, 8, width), axis=0)

    @pl.when(i == pl.num_programs(0) - 1)
    def _():
        dw_ref[...] = acc_scr[...].astype(dw_ref.dtype)
        demb_ref[...] = emb_scr[...]
        dbias_ref[...] = jnp.sum(bias_scr[...], axis=0, keepdims=True)


def qkv_back(dq, dk, dv, h_one, noisy_t, pw, bias, mod, w_local, tables, tcos, tsin):
    frames, patch, ftok = noisy_t.shape
    tokens, width = h_one.shape
    local = dq.shape[1]
    cs, sn, _, _, sel = tables
    full = lambda shape: pl.BlockSpec(shape, lambda i: (0,) * len(shape))
    row = lambda cols: pl.BlockSpec((ftok, cols), lambda i: (i, 0))
    return pl.pallas_call(
        partial(qkv_back_kernel, width=width, local=local),
        grid=(frames,),
        in_specs=[
            row(local), row(local), row(local), row(width),
            pl.BlockSpec((1, patch, ftok), lambda i: (i, 0, 0)),
            full(pw.shape),
            full((1, width)),
            pl.BlockSpec((1, 1, 6 * width), lambda i: (i, 0, 0)),
            full(w_local.shape),
            full(sel.shape),
            full(cs.shape),
            full(sn.shape),
            pl.BlockSpec((1, 1, local // 2), lambda i: (i, 0, 0)),
            pl.BlockSpec((1, 1, local // 2), lambda i: (i, 0, 0)),
        ],
        out_specs=[
            full(w_local.shape),
            pl.BlockSpec((1, 1, 2 * width), lambda i: (i, 0, 0)),
            full(pw.shape),
            full((1, width)),
        ],
        out_shape=[
            jax.ShapeDtypeStruct(w_local.shape, low_type),
            jax.ShapeDtypeStruct((frames, 1, 2 * width), wide),
            jax.ShapeDtypeStruct(pw.shape, wide),
            jax.ShapeDtypeStruct((1, width), wide),
        ],
        scratch_shapes=[
            pltpu.VMEM(w_local.shape, wide),
            pltpu.VMEM(pw.shape, wide),
            pltpu.VMEM((8, width), wide),
        ],
        compiler_params=pltpu.CompilerParams(
            dimension_semantics=("arbitrary",), vmem_limit_bytes=48 * MIB
        ),
        cost_estimate=pl.CostEstimate(
            flops=2 * 2 * tokens * width * 3 * local, bytes_accessed=16 * MIB, transcendentals=0
        ),
        name="qkv_back",
    )(dq, dk, dv, h_one, noisy_t, pw, bias, mod, w_local, sel, cs, sn, tcos, tsin)


def tri_blocks(count):
    return [(r, c) for r in range(count) for c in range(r, count)]


def polish_kernel(u_ref, g_ref, o_ref, g_scr, *, count, blk):
    pairs = tri_blocks(count)
    trace = jnp.zeros((1, 1), wide)
    diag = lax.broadcasted_iota(jnp.int32, (blk, blk), 0) == lax.broadcasted_iota(
        jnp.int32, (blk, blk), 1
    )
    for n, (r, c) in enumerate(pairs):
        piece = g_ref[0, n]
        g_scr[r * blk : (r + 1) * blk, c * blk : (c + 1) * blk] = piece
        if r == c:
            trace += jnp.sum(jnp.where(diag, piece.astype(wide), 0.0), keepdims=True)
        else:
            g_scr[c * blk : (c + 1) * blk, r * blk : (r + 1) * blk] = piece.T
    scale = jnp.sqrt(trace) + 1e-07
    inverse = 1.0 / scale
    inverse_sq = inverse * inverse
    rows = u_ref.shape[1]

    def times(value):
        high = value.astype(low_type)
        rest = (value - high.astype(wide)).astype(low_type)
        both = dot_nn(jnp.concatenate([high, rest], axis=0), g_scr[...])
        return (both[:rows] + both[rows:]) * inverse_sq

    def cubic(value):
        once = times(value)
        return coef_one * value + coef_two * once + coef_three * times(once)

    current = cubic(u_ref[0] * inverse)
    for _ in range(NS_ITERS - 1):
        second = cubic(cubic(times(current)))
        third = cubic(cubic(times(second)))
        current = coef_one * current + coef_two * second + coef_three * third
    o_ref[0] = current


def polish(u, gram_blocks, blk):
    mats, rows, width = u.shape
    count = width // blk
    pairs = len(tri_blocks(count))
    return pl.pallas_call(
        partial(polish_kernel, count=count, blk=blk),
        grid=(mats,),
        in_specs=[
            pl.BlockSpec((1, rows, width), lambda i: (i, 0, 0)),
            pl.BlockSpec((1, pairs, blk, blk), lambda i: (i, 0, 0, 0)),
        ],
        out_specs=pl.BlockSpec((1, rows, width), lambda i: (i, 0, 0)),
        out_shape=jax.ShapeDtypeStruct(u.shape, wide),
        scratch_shapes=[pltpu.VMEM((width, width), low_type)],
        compiler_params=pltpu.CompilerParams(
            dimension_semantics=("arbitrary",), vmem_limit_bytes=40 * MIB
        ),
        cost_estimate=pl.CostEstimate(
            flops=2 * 24 * mats * rows * width * width, bytes_accessed=12 * MIB, transcendentals=0
        ),
        name="polish",
    )(u, gram_blocks)


def gram_kernel(u_ref, o_ref, *, count, blk):
    low = u_ref[0].astype(low_type)
    for n, (r, c) in enumerate(tri_blocks(count)):
        o_ref[0, n] = dot_tn(low[:, r * blk : (r + 1) * blk], low[:, c * blk : (c + 1) * blk])


def gram_parts(u, blk):
    mats, rows, width = u.shape
    count = width // blk
    pairs = len(tri_blocks(count))
    return pl.pallas_call(
        partial(gram_kernel, count=count, blk=blk),
        grid=(mats,),
        in_specs=[pl.BlockSpec((1, rows, width), lambda i: (i, 0, 0))],
        out_specs=pl.BlockSpec((1, pairs, blk, blk), lambda i: (i, 0, 0, 0)),
        out_shape=jax.ShapeDtypeStruct((mats, pairs, blk, blk), wide),
        compiler_params=pltpu.CompilerParams(
            dimension_semantics=("arbitrary",), vmem_limit_bytes=40 * MIB
        ),
        name="gram_parts",
    )(u)


def bit_stages(count_a):
    stages = {}
    bits_a = count_a.bit_length() - 1
    for b in range(bits_a):
        stages["a%d" % (bits_a - 1 - b)] = ("a", 1 << (bits_a - 1 - b), b)
    stages["x"] = ("x", 1, bits_a)
    stages["c"] = ("c", 1, bits_a + 1)
    stages["z1"] = ("z", 2, bits_a + 2)
    stages["z0"] = ("z", 1, bits_a + 3)
    return stages


def swap(value, axis, distance):
    size = lax.axis_size(axis)
    return lax.ppermute(value, axis, [(i, i ^ distance) for i in range(size)])


def bit_of(axis, distance):
    return (lax.axis_index(axis) // distance) % 2


def scatter_sum(blocks, order, stages, wire):
    for name in order:
        axis, distance, dim = stages[name]
        mine = bit_of(axis, distance)
        send = lax.dynamic_index_in_dim(blocks, 1 - mine, dim, keepdims=True)
        keep = lax.dynamic_index_in_dim(blocks, mine, dim, keepdims=True)
        got = swap(send.astype(wire), axis, distance)
        blocks = keep.astype(wide) + got.astype(wide)
    return blocks


def gather_back(block, order, stages):
    for name in order:
        axis, distance, dim = stages[name]
        mine = bit_of(axis, distance)
        got = swap(block, axis, distance)
        block = jnp.concatenate(
            [jnp.where(mine == 0, block, got), jnp.where(mine == 0, got, block)], axis=dim
        )
    return block


def three_orders(stages):
    names_a = [n for n in stages if n.startswith("a")]
    return (
        ["x"] + names_a + ["z0", "z1"],
        names_a + ["z0", "x", "z1"],
        ["z0", "x"] + names_a + ["z1"],
    )


def spread(payload):
    count = math.prod(lax.axis_size(n) for n in ALL)
    return lax.all_to_all(
        jnp.broadcast_to(payload[None], (count,) + payload.shape),
        ALL, split_axis=0, concat_axis=0, tiled=True,
    )


def unit_plan(devices):
    quarter = devices // 4
    edges = []
    for unit in range(3 * devices):
        section, place = unit // devices, unit % devices
        member, rest = place // quarter, place % quarter
        index = section * quarter + rest
        pos, slot = index // 3, index % 3
        a, z = pos // 4, pos % 4
        dest = ((a * 2 + member // 2) * 2 + member % 2) * 4 + z
        edges.append((unit // 3, unit % 3, dest, slot))
    left = list(edges)
    colors = []
    for _ in range(3):
        match = {}

        def augment(src, seen):
            for e in left:
                if e[0] != src or e[2] in seen:
                    continue
                seen.add(e[2])
                if e[2] not in match or augment(match[e[2]][0], seen):
                    match[e[2]] = e
                    return True
            return False

        for src in range(devices):
            assert augment(src, set())
        chosen = list(match.values())
        for e in chosen:
            left.remove(e)
        colors.append(chosen)
    return colors


def send_units(units, plan, back):
    devices = len(plan[0])
    here = lax.axis_index(ALL)
    src_key, dst_key = ((2, 3), (0, 1)) if back else ((0, 1), (2, 3))
    got = []
    for chosen in plan:
        table = np.zeros(devices, np.int32)
        for e in chosen:
            table[e[src_key[0]]] = e[src_key[1]]
        slot = jnp.asarray(table)[here]
        piece = lax.dynamic_index_in_dim(units, slot, 0, keepdims=False)
        got.append(lax.ppermute(piece, ALL, [(e[src_key[0]], e[dst_key[0]]) for e in chosen]))
    place = np.zeros((devices, 3), np.int32)
    for color, chosen in enumerate(plan):
        for e in chosen:
            place[e[dst_key[0]], e[dst_key[1]]] = color
    where_from = jnp.asarray(place)[here]
    out = []
    for slot in range(3):
        pick = where_from[slot]
        out.append(jnp.where(pick == 0, got[0], jnp.where(pick == 1, got[1], got[2])))
    return jnp.stack(out)


def body(
    noisy_latents,
    target_latents,
    noise_levels,
    clip_start,
    qkv_weight,
    qkv_moment,
    out_weight,
    out_moment,
    up_weight,
    up_moment,
    down_weight,
    down_moment,
    ada_weight,
    ada_first,
    ada_second,
    patch_weight,
    patch_first,
    patch_second,
    vectors,
    vec_first,
    vec_second,
):
    count_a = lax.axis_size("a")
    members = lax.axis_size("x") * lax.axis_size("c")
    devices = count_a * members * lax.axis_size("z")
    groups = count_a * lax.axis_size("z")
    frames_dev = noise_levels.shape[0]
    tokens_dev = noisy_latents.shape[0]
    frame_tok = tokens_dev // frames_dev
    width = patch_weight.shape[2]
    patch_size = patch_weight.shape[1]
    head_dim = width // HEADS
    local_heads = HEADS // members
    local = local_heads * head_dim
    group_frames = frames_dev * members
    frames_all = frames_dev * devices
    group_tokens = group_frames * frame_tok
    score_scale = 1.0 / math.sqrt(head_dim)
    hidden_units = up_weight.shape[0] * devices
    stages = bit_stages(count_a)
    my_a, my_z = lax.axis_index("a"), lax.axis_index("z")
    my_group = my_a * 4 + my_z
    my_member = lax.axis_index("x") * 2 + lax.axis_index("c")
    tables = rope_tables(head_dim, local_heads, frame_tok)
    tables = tables[:4] + (jnp.asarray(tables[4], low_type),)
    plan = unit_plan(devices)

    up_full = lax.all_gather(up_weight.astype(low_type), ALL, axis=0, tiled=True)
    down_full = lax.all_gather(down_weight.astype(low_type), ALL, axis=0, tiled=True)
    out_full = lax.all_gather(out_weight.astype(low_type), ALL, axis=0, tiled=True)

    meta = jnp.concatenate([noise_levels, clip_start]).astype(wide)
    meta = jnp.pad(meta, (0, 128 - meta.shape[0]))[None]
    meta_all = spread(meta)[:, 0]
    levels_all = meta_all[:, :frames_dev].reshape(frames_all)
    starts_all = meta_all[:, frames_dev : 2 * frames_dev].reshape(frames_all)
    starts_group = lax.dynamic_slice_in_dim(starts_all, my_group * group_frames, group_frames)
    starts_int = starts_group.astype(jnp.int32)

    swap_axes = ("x", "c", "z")
    moves = [(g * 4 + z, z * 4 + g) for g in range(4) for z in range(4)]
    noisy_t = noisy_latents.T.reshape(patch_size, frames_dev, frame_tok).transpose(1, 0, 2)
    target_t = target_latents.T.reshape(patch_size, frames_dev, frame_tok).transpose(1, 0, 2)
    mine = lax.ppermute(jnp.stack([noisy_t, target_t]), swap_axes, moves)
    noisy_mine, target_mine = mine[0], mine[1]
    noisy_group = gather_back(
        noisy_mine.reshape(1, 1, frames_dev, patch_size, frame_tok),
        ["c", "x"],
        {"x": ("x", 1, 0), "c": ("c", 1, 1)},
    ).reshape(group_frames, patch_size, frame_tok)

    rows_unit = qkv_weight.shape[0] // 3
    units = send_units(qkv_weight.astype(low_type).reshape(3, rows_unit, width), plan, False)
    names_a = [n for n in stages if n.startswith("a")]
    bits_a = len(names_a)
    az_stages = {n: ("a", 1 << (bits_a - 1 - k), k) for k, n in enumerate(names_a)}
    az_stages["z1"] = ("z", 2, bits_a)
    az_stages["z0"] = ("z", 1, bits_a + 1)
    qkv_local = gather_back(
        units.reshape((1,) * (bits_a + 2) + (3 * rows_unit, width)),
        ["z1", "z0"] + names_a[::-1],
        az_stages,
    ).reshape(3 * local, width)

    cond_low = jax.nn.silu(level_features(levels_all, width)).astype(low_type)
    ada_rows = ada_weight.shape[0]
    mod_rows = dot_nt(cond_low, ada_weight.astype(low_type))
    mod_out = jnp.broadcast_to(
        mod_rows.reshape(count_a, 1, 4, group_frames, ada_rows),
        (count_a, members, 4, group_frames, ada_rows),
    ).reshape(devices, group_frames, ada_rows)
    mod_in = lax.all_to_all(mod_out, ALL, split_axis=0, concat_axis=0, tiled=True)
    modul = mod_in.transpose(1, 0, 2).reshape(group_frames, 6 * width) + vectors[2:8].reshape(
        1, 6 * width
    )
    mod3 = modul.reshape(group_frames, 1, 6 * width)
    mod_mine = lax.dynamic_slice_in_dim(modul, my_member * frames_dev, frames_dev).reshape(
        frames_dev, 6, width
    )
    gate_one, shift_two, scale_two, gate_two = [mod_mine[:, j][:, None, :] for j in (2, 3, 4, 5)]

    frame_ids = jnp.arange(group_frames, dtype=jnp.int32)
    time_pos = (frame_ids - starts_int).astype(wide)
    t_angle = time_pos[:, None] * tables[2][None, :]
    tcos = (jnp.cos(t_angle) * tables[3][None, :])[:, None, :]
    tsin = (jnp.sin(t_angle) * tables[3][None, :])[:, None, :]

    pw_in = patch_weight[0]
    bias_in = vectors[0:1]
    h_one, q, k, v = embed_qkv(
        noisy_group, pw_in, bias_in, mod3, qkv_local, tables, tcos, tsin, score_scale
    )
    att, att_low, lse = attend(starts_int, q, k, v, group_frames, local_heads)
    framed = lax.all_to_all(
        att_low.reshape(members, tokens_dev, local), ("x", "c"), split_axis=0, concat_axis=0,
        tiled=True,
    ).transpose(1, 0, 2).reshape(tokens_dev, width)

    state_zero = (
        lax.dot_general(
            noisy_mine.transpose(0, 2, 1).reshape(tokens_dev, patch_size), pw_in,
            (((1,), (0,)), ((), ())), precision=highest,
        ) + bias_in
    ).reshape(frames_dev, frame_tok, width)
    branch = dot_nt(framed, out_full)
    branch3 = branch.reshape(frames_dev, frame_tok, width)
    state_one = state_zero + gate_one * branch3
    normed_two, rstd_two = layer_stats(state_one)
    h_two = (normed_two * (1.0 + scale_two) + shift_two).reshape(tokens_dev, width).astype(low_type)
    hidden = dot_nt(h_two, up_full)
    activated, gelu_pull = jax.vjp(partial(jax.nn.gelu, approximate=True), hidden)
    act_low = activated.astype(low_type)
    mixed = dot_nn(act_low, down_full)
    mixed3 = mixed.reshape(frames_dev, frame_tok, width)
    state_two = state_one + gate_two * mixed3
    normed_three, rstd_three = layer_stats(state_two)
    final_tok = (normed_three * vectors[1]).reshape(tokens_dev, width)
    prediction = jnp.einsum("nd,pd->np", final_tok, patch_weight[1], precision=highest)
    pred_rows = prediction.reshape(frames_dev, frame_tok, patch_size)
    goal_rows = target_mine.transpose(0, 2, 1)
    member_axes = ("x", "c")
    ahead = [(i, i + 1) for i in range(members - 1)]
    behind = [(i + 1, i) for i in range(members - 1)]
    edge = lax.ppermute(
        jnp.stack([pred_rows[-1].T, goal_rows[-1].T]).astype(low_type), member_axes, ahead
    ).astype(wide).transpose(0, 2, 1)
    prev_pred = jnp.concatenate([edge[0:1], pred_rows[:-1]], axis=0)
    prev_goal = jnp.concatenate([edge[1:2], goal_rows[:-1]], axis=0)
    diff = pred_rows - prev_pred - (goal_rows - prev_goal)
    my_frames = my_member * frames_dev + jnp.arange(frames_dev, dtype=jnp.int32)
    valid = my_frames > lax.dynamic_slice_in_dim(starts_int, my_member * frames_dev, frames_dev)
    loss_local = jnp.sum(jnp.where(valid[:, None, None], diff * diff, 0.0))
    entry_count = float(frames_all * frame_tok * patch_size)
    d_diff = jnp.where(valid[:, None, None], (2.0 / entry_count) * diff, 0.0)
    returned = lax.ppermute(d_diff[0].T, member_axes, behind).T
    d_pred = (d_diff - jnp.concatenate([d_diff[1:], returned[None]], axis=0)).reshape(
        tokens_dev, patch_size
    )
    d_head = jnp.einsum("np,nd->pd", d_pred, final_tok, precision=highest)
    d_final = jnp.dot(d_pred, patch_weight[1], precision=highest).reshape(
        frames_dev, frame_tok, width
    )
    d_gain = jnp.sum(d_final * normed_three, axis=(0, 1))
    d_state = layer_back(normed_three, rstd_three, d_final * vectors[1])
    d_mixed = (d_state * gate_two).reshape(tokens_dev, width).astype(low_type)
    d_gate_two = jnp.sum(d_state * mixed3, axis=1)
    d_down = dot_tn(act_low, d_mixed)
    d_act = dot_nt(d_mixed, down_full)
    d_hidden = gelu_pull(d_act)[0].astype(low_type)
    d_up = dot_tn(d_hidden, h_two)
    d_h_two = dot_nn(d_hidden, up_full).reshape(frames_dev, frame_tok, width)
    d_scale_two = jnp.sum(d_h_two * normed_two, axis=1)
    d_shift_two = jnp.sum(d_h_two, axis=1)
    d_state = d_state + layer_back(normed_two, rstd_two, d_h_two * (1.0 + scale_two))
    d_branch = (d_state * gate_one).reshape(tokens_dev, width).astype(low_type)
    d_gate_one = jnp.sum(d_state * branch3, axis=1)
    d_out = dot_tn(d_branch, framed)
    d_framed = dot_nn(d_branch, out_full).astype(low_type)
    d_att = lax.all_to_all(
        d_framed.reshape(tokens_dev, members, local).transpose(1, 0, 2), ("x", "c"),
        split_axis=0, concat_axis=0, tiled=True,
    ).reshape(group_tokens, local)
    d_tokens = d_state.reshape(tokens_dev, width)
    d_embed_top = jnp.einsum("fpt,ftd->pd", noisy_mine, d_state, precision=highest)
    d_bias_top = jnp.sum(d_tokens, axis=0)

    leading = (2,) * (len(stages))
    orders = three_orders(stages)

    def reduce_rows(grad, which):
        rows = grad.shape[0] // devices
        blocks = grad.reshape(leading + (rows, width))
        return scatter_sum(blocks, ["c"] + orders[which], stages, low_type).reshape(rows, width)

    g_down = reduce_rows(d_down, 0)
    g_up = reduce_rows(d_up, 1)
    g_out = reduce_rows(d_out, 2)

    dq, dk, dv = attend_back(
        starts_int, q, d_att, att, lse, k, v, group_frames, local_heads, score_scale
    )
    dw_local, d_mod_one, d_embed, d_bias = qkv_back(
        dq, dk, dv, h_one, noisy_group, pw_in, bias_in, mod3, qkv_local, tables, tcos, tsin
    )
    sent = lax.all_to_all(
        dw_local.reshape(groups, 3 * rows_unit, width), ("a", "z"), split_axis=0, concat_axis=0,
        tiled=True,
    )
    g_units = jnp.sum(sent.astype(wide), axis=0).reshape(3, rows_unit, width)
    g_qkv = send_units(g_units, plan, True).reshape(3 * rows_unit, width)

    d_rest = jnp.stack([d_gate_one, d_shift_two, d_scale_two, d_gate_two], axis=1).reshape(
        frames_dev, 4 * width
    )
    d_rest = lax.dynamic_update_slice_in_dim(
        jnp.zeros((group_frames, 4 * width), wide), d_rest, my_member * frames_dev, 0
    )
    d_mod = jnp.concatenate([d_mod_one[:, 0], d_rest], axis=1)
    d_mod = d_mod.reshape(group_frames, devices, ada_rows).transpose(1, 0, 2)
    smalls = jnp.concatenate(
        [d_embed + d_embed_top, d_head, d_bias + d_bias_top[None], d_gain[None]], axis=0
    )
    small_rows = smalls.shape[0]
    small_part = small_rows * width // devices
    mod_part = group_frames * ada_rows
    packed = jnp.concatenate(
        [d_mod.reshape(devices, mod_part), smalls.reshape(devices, small_part)], axis=1
    )
    pad = -packed.shape[1] % 128
    packed = jnp.pad(packed, ((0, 0), (0, pad))).reshape(devices, -1, 128)
    arrived = lax.all_to_all(packed, ALL, split_axis=0, concat_axis=0, tiled=True).reshape(
        devices, -1
    )
    small_mine = jnp.sum(arrived[:, mod_part : mod_part + small_part], axis=0)
    mod_grad = (
        arrived[:, :mod_part]
        .reshape(count_a, members, 4, group_frames, ada_rows)
        .sum(axis=1)
        .reshape(frames_all, ada_rows)
    )
    bias_mine = jnp.sum(mod_grad, axis=0)
    g_ada = dot_tn(mod_grad.astype(low_type), cond_low)

    shards = (g_qkv, g_out, g_up, g_down)
    local_sq = (
        sum((jnp.sum(piece * piece) for piece in shards))
        + jnp.sum(g_ada * g_ada)
        + jnp.sum(small_mine * small_mine)
        + jnp.sum(bias_mine * bias_mine)
    )
    report = jnp.concatenate([small_mine, bias_mine, local_sq[None], loss_local[None]])
    size = report.shape[0]
    report = jnp.pad(report, (0, -size % 128)).reshape(-1, 128)
    everyone = spread(report).reshape(devices, -1)
    small_all = everyone[:, :small_part].reshape(small_rows, width)
    bias_all = everyone[:, small_part : small_part + ada_rows].reshape(6, width)
    norm = jnp.sqrt(jnp.sum(everyone[:, size - 2]))
    loss_total = jnp.sum(everyone[:, size - 1])
    g_patch = small_all[: 2 * patch_size].reshape(2, patch_size, width)
    g_vec = jnp.concatenate([small_all[2 * patch_size :], bias_all], axis=0)
    clip = jnp.minimum(1.0, 0.01 / norm)

    olds = (qkv_weight, out_weight, up_weight, down_weight)
    moments = (qkv_moment, out_moment, up_moment, down_moment)
    moments_new = [0.95 * moments[j] + clip * shards[j] for j in range(4)]
    most = max(m.shape[0] for m in olds)
    steers = jnp.stack(
        [
            jnp.pad(
                clip * shards[j] + 0.95 * moments_new[j], ((0, most - olds[j].shape[0]), (0, 0))
            )
            for j in range(4)
        ]
    )
    blk = 256
    parts = gram_parts(steers, blk)
    flat = parts.reshape(-1, blk)
    total_rows = flat.shape[0]
    unit = total_rows // devices // 8
    cuts = [unit // 3 + (1 if r < unit % 3 else 0) for r in range(3)]
    pieces, offset = [], 0
    for which in range(3):
        rows = cuts[which] * 8 * devices
        piece = flat[offset : offset + rows].reshape(leading + (rows // devices, blk))
        offset += rows
        piece = scatter_sum(piece, ["c"] + orders[which], stages, low_type)
        piece = gather_back(piece.astype(low_type), orders[which][::-1] + ["c"], stages)
        pieces.append(piece.reshape(rows, blk))
    grams = jnp.concatenate(pieces, axis=0).reshape(parts.shape)
    current = polish(steers, grams, blk)
    updated = []
    for j in range(4):
        rows_dev = olds[j].shape[0]
        factor_rate = 2.0 * math.sqrt(max(1.0, rows_dev * devices / width))
        updated.append(olds[j] * (1.0 - 2.0 * 0.01) - factor_rate * current[j, :rows_dev])
    ada_new, ada_one, ada_two = adamw(ada_weight, ada_first, ada_second, clip * g_ada, 0.08)
    patch_new, patch_one, patch_two = adamw(
        patch_weight, patch_first, patch_second, clip * g_patch, 0.15
    )
    vec_new, vec_one, vec_two = adamw(vectors, vec_first, vec_second, clip * g_vec, 0.5)
    return (
        loss_total,
        norm,
        updated[0],
        moments_new[0],
        updated[1],
        moments_new[1],
        updated[2],
        moments_new[2],
        updated[3],
        moments_new[3],
        ada_new,
        ada_one,
        ada_two,
        patch_new,
        patch_one,
        patch_two,
        vec_new,
        vec_one,
        vec_two,
    )


def solution(mesh):
    groups, line = mesh.shape["dp"], mesh.shape["seq"]
    inner = Mesh(mesh.devices.reshape(groups // 4, 2, 2, line), ALL)
    split = P(ALL, None)
    copied = P()
    placed = (split, split, P(ALL), P(ALL)) + (split,) * 11 + (copied,) * 6
    return jax.shard_map(
        body,
        mesh=inner,
        in_specs=placed,
        out_specs=(copied, copied) + (split,) * 11 + (copied,) * 6,
        check_vma=False,
    )
```

```python
from functools import partial
import math

import jax
import jax.numpy as jnp
import numpy as np
from jax import lax
from jax.experimental import pallas as pl
from jax.experimental.pallas import tpu as pltpu
from jax.sharding import Mesh, PartitionSpec as P

HEADS = 16
NS_ITERS = 2
STEP = 10
ALL = ("a", "x", "c", "z")

highest = lax.Precision.HIGHEST
coef_one = 3.4445
coef_two = -4.775
coef_three = 2.0315
low_type = jnp.bfloat16
wide = jnp.float32
NT = (((1,), (1,)), ((), ()))
TN = (((0,), (0,)), ((), ()))
MIB = 1 << 20


def dot_nt(left, right):
    return lax.dot_general(left, right, NT, preferred_element_type=wide)


def dot_tn(left, right):
    return lax.dot_general(left, right, TN, preferred_element_type=wide)


def dot_nn(left, right):
    return jnp.dot(left, right, preferred_element_type=wide)


def layer_stats(value):
    mean = jnp.mean(value, axis=-1, keepdims=True)
    centred = value - mean
    rstd = lax.rsqrt(jnp.mean(centred * centred, axis=-1, keepdims=True) + 1e-06)
    return (centred * rstd, rstd)


def layer_back(normed, rstd, upstream):
    return rstd * (
        upstream
        - jnp.mean(upstream, axis=-1, keepdims=True)
        - normed * jnp.mean(upstream * normed, axis=-1, keepdims=True)
    )


def level_features(levels, width):
    half = width // 2
    freqs = jnp.exp(-math.log(10000.0) * jnp.arange(half, dtype=jnp.float32) / half)
    angle = levels.astype(jnp.float32)[:, None] * freqs[None, :]
    return jnp.concatenate([jnp.sin(angle), jnp.cos(angle)], axis=-1)


def adamw(weight, first, second, grad, rate):
    first = 0.9 * first + 0.1 * grad
    second = 0.95 * second + 0.05 * grad * grad
    first_hat = first / (1.0 - 0.9**STEP)
    second_hat = second / (1.0 - 0.95**STEP)
    weight = weight - rate * (first_hat / (jnp.sqrt(second_hat) + 1e-08) + 0.01 * weight)
    return (weight, first, second)


def rope_tables(head_dim, heads, frame_tok):
    sec_time = head_dim // 4
    sec_space = (head_dim - sec_time) // 2
    side = math.isqrt(frame_tok)
    spot = np.arange(frame_tok)
    firsts, seconds, time_freq, space = [], [], [], []
    offset = 0
    for kind, size in ((0, sec_time), (1, sec_space), (2, sec_space)):
        half = size // 2
        freqs = np.exp(-math.log(10000.0) * np.arange(half, dtype=np.float64) * 2.0 / size)
        firsts += list(range(offset, offset + half))
        seconds += list(range(offset + half, offset + size))
        offset += size
        where = {0: np.zeros(frame_tok), 1: spot // side, 2: spot % side}[kind]
        space.append(where[:, None] * freqs[None, :])
        time_freq.append(freqs if kind == 0 else np.zeros(half))
    is_time = np.concatenate([np.ones(sec_time // 2), np.zeros(sec_space)])
    space = np.concatenate(space, axis=1)
    space_cos = np.where(is_time[None] > 0, 0.0, np.cos(space))
    space_sin = np.where(is_time[None] > 0, 0.0, np.sin(space))
    time_freq = np.concatenate(time_freq)
    order = np.concatenate(
        [
            np.concatenate([np.asarray(part) + h * head_dim for h in range(heads)])
            for part in (firsts, seconds)
        ]
    )
    total = heads * head_dim
    select = np.zeros((total, total), np.float32)
    select[np.arange(total), order] = 1.0
    tile = lambda t: np.tile(t, (1, heads)).astype(np.float32)
    return (
        tile(space_cos),
        tile(space_sin),
        np.tile(time_freq, heads).astype(np.float32),
        np.tile(is_time, heads).astype(np.float32),
        select,
    )


def split_mask(shape, axis, heads, half_lanes, value):
    lane = lax.broadcasted_iota(jnp.int32, shape, axis)
    if half_lanes is not None:
        lane = lane % half_lanes
        return lane // (half_lanes // heads) == value
    return lane // (shape[axis] // heads) == value


def split_two(value):
    high = value.astype(low_type)
    return high, (value - high.astype(wide)).astype(low_type)


def split_three(value):
    high = value.astype(low_type)
    rest = value - high.astype(wide)
    middle = rest.astype(low_type)
    return high, middle, (rest - middle.astype(wide)).astype(low_type)


def pack_left(value):
    high, middle, least = split_three(value)
    return jnp.concatenate([high, high, middle, high, middle, least], axis=0)


def pack_right(value):
    high, middle, least = split_three(value)
    return jnp.concatenate([high, middle, high, least, middle, high], axis=0)


def thin_product(thin, tall):
    t_high, t_low = split_two(thin)
    high, low = split_two(tall)
    rows = thin.shape[0]
    both = dot_nn(jnp.concatenate([t_high, t_low], axis=0), high)
    return both[:rows] + both[rows:] + dot_nn(t_high, low)


def line_rows(scr, refs, me_ref, split, places):
    total = sum(split)
    other = jnp.bitwise_and(jnp.bitwise_xor(pl.program_id(0), me_ref[0]), 1)

    def fill(parts):
        for zz in range(4):
            apart = jnp.bitwise_xor(me_ref[1], zz)
            at = zz * total
            for ref, rows, (dim_one, dim_zero) in zip(parts, split, places):
                index = [0] * (len(ref.shape) - 2)
                index[dim_one] = lax.shift_right_logical(apart, 1)
                index[dim_zero] = jnp.bitwise_and(apart, 1)
                scr[at : at + rows, :] = ref[tuple(index) + (slice(0, rows),)]
                at += rows

    @pl.when(other == 0)
    def _():
        fill(refs[0::2])

    @pl.when(other == 1)
    def _():
        fill(refs[1::2])


def once(shape):
    return pl.BlockSpec(shape, lambda *_: (0,) * len(shape), pipeline_mode=pl.Buffered(1))


def embed_qkv_kernel(
    noisy_ref, pw_ref, bias_ref, mod_ref, w_ref, sel_ref, cs_ref, sn_ref, tc_ref, ts_ref,
    h_ref, q_ref, k_ref, v_ref, wq_scr, pw_scr, *, width, local, scale,
):
    @pl.when(pl.program_id(0) == 0)
    def _():
        pw_scr[...] = pack_right(pw_ref[...])
        for part in range(2):
            rows = pl.ds(part * local, local)
            wq_scr[rows, :] = dot_nn(sel_ref[...], w_ref[rows, :]).astype(low_type)
        rows = pl.ds(2 * local, local)
        wq_scr[rows, :] = w_ref[rows, :]

    state = dot_tn(pack_left(noisy_ref[0]), pw_scr[...]) + bias_ref[...]
    normed, _ = layer_stats(state)
    shift = mod_ref[0, :, 0:width]
    scl = mod_ref[0, :, width : 2 * width]
    h_low = (normed * (1.0 + scl) + shift).astype(low_type)
    h_ref[...] = h_low
    out = dot_nt(h_low, wq_scr[...])
    cosine = cs_ref[...] + tc_ref[0]
    sine = sn_ref[...] + ts_ref[0]
    half = local // 2
    for part, ref, mult in ((0, q_ref, scale), (1, k_ref, 1.0)):
        first = out[:, part * local : part * local + half]
        second = out[:, part * local + half : (part + 1) * local]
        ref[:, 0:half] = ((first * cosine - second * sine).astype(low_type).astype(wide) * mult).astype(low_type)
        ref[:, half:local] = ((second * cosine + first * sine).astype(low_type).astype(wide) * mult).astype(low_type)
    v_ref[...] = out[:, 2 * local : 3 * local].astype(low_type)


def embed_qkv(noisy_t, pw, bias, mod, w_local, tables, tcos, tsin, scale):
    frames, patch, ftok = noisy_t.shape
    width = pw.shape[1]
    local = w_local.shape[0] // 3
    cs, sn, _, _, sel = tables
    tokens = frames * ftok
    full = lambda shape: pl.BlockSpec(shape, lambda i: (0,) * len(shape))
    row = lambda cols: pl.BlockSpec((ftok, cols), lambda i: (i, 0))
    return pl.pallas_call(
        partial(embed_qkv_kernel, width=width, local=local, scale=scale),
        grid=(frames,),
        in_specs=[
            pl.BlockSpec((1, patch, ftok), lambda i: (i, 0, 0)),
            full(pw.shape),
            full((1, width)),
            pl.BlockSpec((1, 1, 6 * width), lambda i: (i, 0, 0)),
            full(w_local.shape),
            full(sel.shape),
            full(cs.shape),
            full(sn.shape),
            pl.BlockSpec((1, 1, local // 2), lambda i: (i, 0, 0)),
            pl.BlockSpec((1, 1, local // 2), lambda i: (i, 0, 0)),
        ],
        out_specs=[row(width), row(local), row(local), row(local)],
        out_shape=[
            jax.ShapeDtypeStruct((tokens, width), low_type),
            jax.ShapeDtypeStruct((tokens, local), low_type),
            jax.ShapeDtypeStruct((tokens, local), low_type),
            jax.ShapeDtypeStruct((tokens, local), low_type),
        ],
        scratch_shapes=[
            pltpu.VMEM(w_local.shape, low_type),
            pltpu.VMEM((6 * patch, width), low_type),
        ],
        compiler_params=pltpu.CompilerParams(
            dimension_semantics=("arbitrary",), vmem_limit_bytes=40 * MIB
        ),
        cost_estimate=pl.CostEstimate(
            flops=2 * tokens * width * 3 * local, bytes_accessed=12 * MIB, transcendentals=0
        ),
        name="embed_qkv",
    )(noisy_t, pw, bias, mod, w_local, sel, cs, sn, tcos, tsin)


def attend_kernel(
    st_ref, q_ref, k_ref, v_ref, *rest, heads, ftok, begin, last, skip
):
    o_ref, ol_ref, lse_ref, vt_scr, s_scr = rest[skip:]
    i = pl.program_id(0) + begin
    local = q_ref.shape[1]
    hd = local // heads

    @pl.when(i == begin)
    def _():
        for f in range(last):
            vt_scr[f] = v_ref[f * ftok : (f + 1) * ftok, :].T

    first = st_ref[i]
    query = q_ref[...]
    zero = jnp.zeros_like(query)
    masked = [
        jnp.where(split_mask(query.shape, 1, heads, local // 2, h), query, zero)
        for h in range(heads)
    ]

    def scores(j, tops):
        key = k_ref[pl.ds(pl.multiple_of(j * ftok, ftok), ftok), :]
        new = []
        for h in range(heads):
            s = dot_nt(key, masked[h])
            s_scr[h, j] = s
            new.append(jnp.maximum(tops[h], jnp.max(s.reshape(ftok // 8, 8, ftok), axis=0)))
        return tuple(new)

    tops = lax.fori_loop(
        first, i + 1, scores, tuple(jnp.full((8, ftok), -1e30, wide) for _ in range(heads))
    )
    tops = [jnp.max(t, axis=0, keepdims=True) for t in tops]

    def values(j, carry):
        sums, accs = carry
        new_sums, new_accs = [], []
        vt = vt_scr[j]
        for h in range(heads):
            p = jnp.exp(s_scr[h, j] - tops[h])
            new_sums.append(sums[h] + jnp.sum(p.reshape(ftok // 8, 8, ftok), axis=0))
            new_accs.append(accs[h] + dot_nn(vt[h * hd : (h + 1) * hd, :], p.astype(low_type)))
        return (tuple(new_sums), tuple(new_accs))

    sums, accs = lax.fori_loop(
        first,
        i + 1,
        values,
        (
            tuple(jnp.zeros((8, ftok), wide) for _ in range(heads)),
            tuple(jnp.zeros((hd, ftok), wide) for _ in range(heads)),
        ),
    )
    outs, logs = [], []
    for h in range(heads):
        total = jnp.sum(sums[h], axis=0, keepdims=True)
        outs.append(accs[h] * (1.0 / total))
        logs.append(tops[h] + jnp.log(total))
    out = jnp.concatenate(outs, axis=0).T
    o_ref[...] = out
    ol_ref[...] = out.astype(low_type)
    lse_ref[0] = jnp.concatenate(logs + [jnp.zeros((8 - heads, ftok), wide)], axis=0)


def attend(starts, q, k, v, before, begin, last, frames, heads):
    tokens, local = q.shape
    ftok = tokens // frames
    row = lambda: pl.BlockSpec((ftok, local), lambda i, s: (i + begin, 0))
    return pl.pallas_call(
        partial(
            attend_kernel, heads=heads, ftok=ftok, begin=begin, last=last, skip=len(before)
        ),
        grid_spec=pltpu.PrefetchScalarGridSpec(
            num_scalar_prefetch=1,
            grid=(last - begin,),
            in_specs=[row(), once(k.shape), once(v.shape)]
            + [pl.BlockSpec(memory_space=pl.ANY)] * len(before),
            out_specs=[
                row(), row(), pl.BlockSpec((1, 8, ftok), lambda i, s: (i + begin, 0, 0))
            ],
            scratch_shapes=[
                pltpu.VMEM((last, local, ftok), low_type),
                pltpu.VMEM((heads, last, ftok, ftok), wide),
            ],
        ),
        out_shape=[
            jax.ShapeDtypeStruct((tokens, local), wide),
            jax.ShapeDtypeStruct((tokens, local), low_type),
            jax.ShapeDtypeStruct((frames, 8, ftok), wide),
        ],
        input_output_aliases={4 + n: n for n in range(len(before))},
        compiler_params=pltpu.CompilerParams(
            dimension_semantics=("arbitrary",), vmem_limit_bytes=48 * MIB
        ),
        cost_estimate=pl.CostEstimate(
            flops=20_000_000_000, bytes_accessed=12 * MIB, transcendentals=0
        ),
        name="attend",
    )(starts, q, k, v, *before)


def attend_back_kernel(
    st_ref, q_ref, do_ref, o_ref, lse_ref, k_ref, v_ref, *rest, heads, ftok, scale, begin, last
):
    if begin:
        _, dk_in, dv_in, dq_ref, dk_ref, dv_ref, kt_scr, dk_scr, dv_scr, dqt_scr = rest
    else:
        dq_ref, dk_ref, dv_ref, kt_scr, dk_scr, dv_scr, dqt_scr = rest
    step_id = pl.program_id(0)
    steps = pl.num_programs(0)
    i = step_id + begin
    local = q_ref.shape[1]
    hd = local // heads
    hh = hd // 2
    half = local // 2

    @pl.when(step_id == 0)
    def _():
        for f in range(last):
            kt_scr[f] = k_ref[f * ftok : (f + 1) * ftok, :].T
        if begin:
            dk_scr[...] = dk_in[...]
            dv_scr[...] = dv_in[...]
        else:
            dk_scr[...] = jnp.zeros_like(dk_scr)
            dv_scr[...] = jnp.zeros_like(dv_scr)

    first = st_ref[i]
    query = q_ref[...]
    grad = do_ref[...]
    zero = jnp.zeros_like(query)
    q_mask = [
        jnp.where(split_mask(query.shape, 1, heads, half, h), query, zero) for h in range(heads)
    ]
    g_mask = [
        jnp.where(split_mask(query.shape, 1, heads, None, h), grad, zero) for h in range(heads)
    ]
    q_all = jnp.concatenate(q_mask, axis=0)
    g_all = jnp.concatenate(g_mask, axis=0)
    prod = (grad.astype(wide) * o_ref[...]).T
    delta = [
        jnp.sum(prod[h * hd : (h + 1) * hd, :], axis=0, keepdims=True) for h in range(heads)
    ]
    lse = [lse_ref[0, h : h + 1, :] for h in range(heads)]
    dqt_scr[...] = jnp.zeros_like(dqt_scr)

    def step(j, carry):
        rows = pl.ds(pl.multiple_of(j * ftok, ftok), ftok)
        key = k_ref[rows, :]
        val = v_ref[rows, :]
        kt = kt_scr[j]
        probs, d_scores = [], []
        for h in range(heads):
            p = jnp.exp(dot_nt(key, q_mask[h]) - lse[h])
            dp = dot_nt(val, g_mask[h])
            ds = (p * (dp - delta[h])).astype(low_type)
            probs.append(p.astype(low_type))
            d_scores.append(ds)
            kt_h = jnp.concatenate(
                [kt[h * hh : (h + 1) * hh, :], kt[half + h * hh : half + (h + 1) * hh, :]], axis=0
            )
            dqt_scr[h] += dot_nn(kt_h, ds)
        dv_scr[rows, :] += dot_nn(jnp.concatenate(probs, axis=1), g_all)
        dk_scr[rows, :] += dot_nn(jnp.concatenate(d_scores, axis=1), q_all)
        return carry

    lax.fori_loop(first, i + 1, step, 0)
    dqt = jnp.concatenate(
        [dqt_scr[h, 0:hh, :] for h in range(heads)] + [dqt_scr[h, hh:hd, :] for h in range(heads)],
        axis=0,
    )
    dq_ref[...] = (dqt.T * scale).astype(low_type)

    @pl.when(step_id == steps - 1)
    def _():
        dk_ref[...] = dk_scr[...].astype(dk_ref.dtype)
        dv_ref[...] = dv_scr[...].astype(dv_ref.dtype)


def attend_back(starts, q, grad, out, lse, k, v, sums, begin, last, frames, heads, scale):
    tokens, local = q.shape
    ftok = tokens // frames
    row = lambda cols: pl.BlockSpec((ftok, cols), lambda i, s: (i + begin, 0))
    kind = low_type if last == frames else wide
    return pl.pallas_call(
        partial(attend_back_kernel, heads=heads, ftok=ftok, scale=scale, begin=begin, last=last),
        grid_spec=pltpu.PrefetchScalarGridSpec(
            num_scalar_prefetch=1,
            grid=(last - begin,),
            in_specs=[
                row(local), row(local), row(local),
                pl.BlockSpec((1, 8, ftok), lambda i, s: (i + begin, 0, 0)),
                once(k.shape), once(v.shape),
            ] + ([pl.BlockSpec(memory_space=pl.ANY)] + [once(k.shape)] * 2)[: len(sums)],
            out_specs=[row(local), once(k.shape), once(v.shape)],
            scratch_shapes=[
                pltpu.VMEM((frames, local, ftok), low_type),
                pltpu.VMEM((tokens, local), wide),
                pltpu.VMEM((tokens, local), wide),
                pltpu.VMEM((heads, local // heads, ftok), wide),
            ],
        ),
        out_shape=[
            jax.ShapeDtypeStruct((tokens, local), low_type),
            jax.ShapeDtypeStruct((tokens, local), kind),
            jax.ShapeDtypeStruct((tokens, local), kind),
        ],
        input_output_aliases={7: 0} if sums else {},
        compiler_params=pltpu.CompilerParams(
            dimension_semantics=("arbitrary",), vmem_limit_bytes=48 * MIB
        ),
        cost_estimate=pl.CostEstimate(
            flops=30_000_000_000, bytes_accessed=16 * MIB, transcendentals=0
        ),
        name="attend_back",
    )(starts, q, grad, out, lse, k, v, *sums)


def post_attend_kernel(
    me_ref, fr_ref, noisy_ref, pw_ref, bias_ref, mod_ref, two_a, two_b, st_ref, br_ref, h_ref,
    full_ref, *, width, maps, skip,
):
    local = fr_ref.shape[2]

    @pl.when(pl.program_id(0) == 0)
    def _():
        rows_out = width // (2 * len(maps))
        for two_ref, other in ((two_a, 0), (two_b, 4)):
            for pos, apart in enumerate(maps):
                dev = jnp.bitwise_xor(me_ref[0], apart + other)
                full_ref[pl.ds(pl.multiple_of(dev * rows_out, rows_out), rows_out), :] = two_ref[
                    pos, skip:, :
                ]

    out_full = full_ref[...]
    state = dot_tn(pack_left(noisy_ref[0]), pack_right(pw_ref[...])) + bias_ref[...]
    branch = dot_nt(fr_ref[0], out_full[:, 0:local])
    for m in range(1, fr_ref.shape[0]):
        branch += dot_nt(fr_ref[m], out_full[:, m * local : (m + 1) * local])
    state = state + mod_ref[0, :, 2 * width : 3 * width] * branch
    normed, _ = layer_stats(state)
    st_ref[...] = state
    br_ref[...] = branch
    h_ref[...] = (
        normed * (1.0 + mod_ref[0, :, 4 * width : 5 * width])
        + mod_ref[0, :, 3 * width : 4 * width]
    ).astype(low_type)


def post_attend(me, framed, noisy_t, pw, bias, mod, part_two, order_two, skip):
    members, tokens, local = framed.shape
    frames, patch, ftok = noisy_t.shape
    width = pw.shape[1]
    part_two = [p.reshape((-1,) + p.shape[-2:]) for p in part_two]
    row = lambda: pl.BlockSpec((ftok, width), lambda i, me: (i, 0))
    return pl.pallas_call(
        partial(post_attend_kernel, width=width, maps=tile_places(order_two), skip=skip),
        grid_spec=pltpu.PrefetchScalarGridSpec(
            num_scalar_prefetch=1,
            grid=(frames,),
            in_specs=[
                pl.BlockSpec((members, ftok, local), lambda i, me: (0, i, 0)),
                pl.BlockSpec((1, patch, ftok), lambda i, me: (i, 0, 0)),
                once(pw.shape),
                once((1, width)),
                pl.BlockSpec((1, 1, 6 * width), lambda i, me: (i, 0, 0)),
            ] + [once(p.shape) for p in part_two],
            out_specs=[row(), row(), row(), once((width, width))],
        ),
        out_shape=[
            jax.ShapeDtypeStruct((tokens, width), wide),
            jax.ShapeDtypeStruct((tokens, width), wide),
            jax.ShapeDtypeStruct((tokens, width), low_type),
            jax.ShapeDtypeStruct((width, width), low_type),
        ],
        compiler_params=pltpu.CompilerParams(
            dimension_semantics=("arbitrary",), vmem_limit_bytes=40 * MIB
        ),
        cost_estimate=pl.CostEstimate(
            flops=2 * tokens * width * width, bytes_accessed=12 * MIB, transcendentals=0
        ),
        name="post_attend",
    )(me, framed, noisy_t, pw, bias, mod, *part_two)


def part_specs(me_block, orders, shapes):
    bits = sorted((n for n in orders[0] if n[0] == "a"), reverse=True) + ["x", "c"]
    specs = []
    for order, shape in zip(orders, shapes):

        def place(n, me, order=order):
            apart = me_block(n, me)
            index = []
            for name in order:
                if name[0] == "z":
                    index.append(0)
                else:
                    index.append(
                        jnp.bitwise_and(
                            lax.shift_right_logical(apart, len(bits) - 1 - bits.index(name)), 1
                        )
                    )
            return tuple(index) + (0, 0)

        block = tuple(2 if n[0] == "z" else 1 for n in order) + shape[-2:]
        specs += [pl.BlockSpec(block, place)] * 2
    return specs


def line_apart(n, me):
    return jnp.bitwise_xor(n, me[0])


def gelu_parts(value):
    k = math.sqrt(2.0 / math.pi)
    square = value * value
    t = jnp.tanh(k * value * (1.0 + 0.044715 * square))
    half = 0.5 * (1.0 + t)
    slope = half + (0.5 * k) * value * (1.0 - t * t) * (1.0 + (3 * 0.044715) * square)
    return value * half, slope


def ff_kernel(
    me_ref, h_ref, st_ref, mod_ref, one_a, one_b, two_a, two_b, down_ref, gain_ref, pw_ref, act_ref,
    slope_ref, mixed_ref, pred_ref, acc_scr, up_scr, *, width, frames, ftok, split, places,
):
    n = pl.program_id(0)
    four, rows, _ = down_ref.shape
    line_rows(up_scr, (one_a, one_b, two_a, two_b), me_ref, split, places)
    hidden = dot_nt(h_ref[...], up_scr[...])
    act, slope = gelu_parts(hidden)
    act = act.astype(low_type)
    act_ref[...] = act
    slope_ref[...] = slope.astype(low_type)
    part = dot_nn(act, down_ref[...].reshape(four * rows, width))

    @pl.when(n == 0)
    def _():
        acc_scr[...] = part

    @pl.when(n > 0)
    def _():
        acc_scr[...] += part

    @pl.when(n == pl.num_programs(0) - 1)
    def _():
        patch = pw_ref.shape[0]
        head, rest = split_two(pw_ref[...])
        both = jnp.concatenate([head, rest], axis=0)
        for f in range(frames):
            at = slice(f * ftok, (f + 1) * ftok)
            mixed = acc_scr[at, :]
            mixed_ref[at, :] = mixed
            normed, _ = layer_stats(st_ref[at, :] + mod_ref[f, :, 5 * width : 6 * width] * mixed)
            f_high, f_low = split_two(normed * gain_ref[...])
            two = dot_nt(f_high, both)
            one = dot_nt(f_low, head)
            pred_ref[f] = (two[:, :patch] + two[:, patch:] + one).T


def ff_forward(me, h_two, state_one, mod, parts, orders, split, down, gain, pw_out, ftok):
    tokens, width = h_two.shape
    devices, rows, _ = down.shape
    steps = devices // 4
    chunk = 4 * rows
    frames = tokens // ftok
    patch = pw_out.shape[0]
    columns = lambda: pl.BlockSpec((tokens, chunk), lambda n, me: (0, n))
    return pl.pallas_call(
        partial(
            ff_kernel, width=width, frames=frames, ftok=ftok, split=split,
            places=[(o.index("z1"), o.index("z0")) for o in orders],
        ),
        grid_spec=pltpu.PrefetchScalarGridSpec(
            num_scalar_prefetch=1,
            grid=(steps,),
            in_specs=[once(h_two.shape), once(state_one.shape), once(mod.shape)]
            + part_specs(line_apart, orders, [p[0].shape for p in parts])
            + [
                pl.BlockSpec((4, rows, width), lambda n, me: (n, 0, 0)),
                once(gain.shape),
                once(pw_out.shape),
            ],
            out_specs=[columns(), columns(), once((tokens, width)), once((frames, patch, ftok))],
            scratch_shapes=[
                pltpu.VMEM((tokens, width), wide),
                pltpu.VMEM((chunk, width), low_type),
            ],
        ),
        out_shape=[
            jax.ShapeDtypeStruct((tokens, chunk * steps), low_type),
            jax.ShapeDtypeStruct((tokens, chunk * steps), low_type),
            jax.ShapeDtypeStruct((tokens, width), wide),
            jax.ShapeDtypeStruct((frames, patch, ftok), wide),
        ],
        compiler_params=pltpu.CompilerParams(
            dimension_semantics=("arbitrary",), vmem_limit_bytes=56 * MIB
        ),
        cost_estimate=pl.CostEstimate(
            flops=4 * tokens * width * chunk * steps, bytes_accessed=40 * MIB, transcendentals=0
        ),
        name="ff_forward",
    )(me, h_two, state_one, mod, *parts[0], *parts[1], down, gain, pw_out)


def ff_back_kernel(
    me_ref, dp_ref, st_ref, mixed_ref, br_ref, mod_ref, noisy_ref, gain_ref, pw_ref, one_a,
    one_b, two_a, two_b, down_ref, out_ref, slope_ref, dh_ref, dm_ref, db_ref, df_ref, small_ref, sums_ref,
    dmod_ref, ds_scr, acc_scr, up_scr, *, width, frames, ftok, split, places,
):
    n = pl.program_id(0)
    four, rows, _ = down_ref.shape
    line_rows(up_scr, (one_a, one_b, two_a, two_b), me_ref, split, places)
    patch = pw_ref.shape[0]

    def fold(value):
        return jnp.sum(value.reshape(-1, 8, width), axis=0).sum(axis=0, keepdims=True)

    @pl.when(n == 0)
    def _():
        d_head = jnp.zeros((patch, width), wide)
        d_gain = jnp.zeros((1, width), wide)
        right = pack_right(pw_ref[...])
        for f in range(frames):
            at = slice(f * ftok, (f + 1) * ftok)
            gate = mod_ref[f, :, 5 * width : 6 * width]
            mixed = mixed_ref[at, :]
            normed, rstd = layer_stats(st_ref[at, :] + gate * mixed)
            d_pred = dp_ref[f]
            d_final = dot_tn(pack_left(d_pred), right)
            d_head += thin_product(d_pred, normed * gain_ref[...])
            d_gain += fold(d_final * normed)
            d_state = layer_back(normed, rstd, d_final * gain_ref[...])
            ds_scr[at, :] = d_state
            dmod_ref[f, 3:4, :] = fold(d_state * mixed)
            dm_ref[at, :] = (d_state * gate).astype(low_type)
        small_ref[0] = d_head
        sums_ref[0:1, :] = d_gain

    d_act = dot_nt(dm_ref[...], down_ref[...].reshape(four * rows, width))
    d_hidden = (d_act * slope_ref[...].astype(wide)).astype(low_type)
    dh_ref[...] = d_hidden
    part = dot_nn(d_hidden, up_scr[...])

    @pl.when(n == 0)
    def _():
        acc_scr[...] = part

    @pl.when(n > 0)
    def _():
        acc_scr[...] += part

    @pl.when(n == pl.num_programs(0) - 1)
    def _():
        out_full = out_ref[...]
        d_embed = jnp.zeros((patch, width), wide)
        d_bias = jnp.zeros((1, width), wide)
        local = df_ref.shape[2]
        for f in range(frames):
            at = slice(f * ftok, (f + 1) * ftok)
            normed, rstd = layer_stats(st_ref[at, :])
            d_h = acc_scr[at, :]
            dmod_ref[f, 1:2, :] = fold(d_h)
            dmod_ref[f, 2:3, :] = fold(d_h * normed)
            d_state = ds_scr[at, :] + layer_back(
                normed, rstd, d_h * (1.0 + mod_ref[f, :, 4 * width : 5 * width])
            )
            dmod_ref[f, 0:1, :] = fold(d_state * br_ref[at, :])
            d_branch = (d_state * mod_ref[f, :, 2 * width : 3 * width]).astype(low_type)
            db_ref[at, :] = d_branch
            d_framed = dot_nn(d_branch, out_full).astype(low_type)
            for m in range(df_ref.shape[0]):
                df_ref[m, at, :] = d_framed[:, m * local : (m + 1) * local]
            d_embed += thin_product(noisy_ref[f], d_state)
            d_bias += fold(d_state)
        small_ref[1] = d_embed
        sums_ref[1:2, :] = d_bias


def ff_backward(
    me, d_pred, state_one, mixed, branch, mod, noisy_t, gain, pw_out, parts, orders, split, down,
    out_full, slope, members,
):
    tokens, width = state_one.shape
    devices, rows, _ = down.shape
    steps = devices // 4
    chunk = 4 * rows
    frames, patch, ftok = noisy_t.shape
    local = width // members
    columns = lambda: pl.BlockSpec((tokens, chunk), lambda n, me: (0, n))
    return pl.pallas_call(
        partial(
            ff_back_kernel, width=width, frames=frames, ftok=ftok, split=split,
            places=[(o.index("z1"), o.index("z0")) for o in orders],
        ),
        grid_spec=pltpu.PrefetchScalarGridSpec(
            num_scalar_prefetch=1,
            grid=(steps,),
            in_specs=[
                once(d_pred.shape),
                once(state_one.shape),
                once(state_one.shape),
                once(state_one.shape),
                once(mod.shape),
                once(noisy_t.shape),
                once(gain.shape),
                once(pw_out.shape),
            ]
            + part_specs(line_apart, orders, [p[0].shape for p in parts])
            + [
                pl.BlockSpec((4, rows, width), lambda n, me: (n, 0, 0)),
                once(out_full.shape),
                columns(),
            ],
            out_specs=[
                columns(),
                once((tokens, width)),
                once((tokens, width)),
                once((members, tokens, local)),
                once((2, patch, width)),
                once((2, width)),
                once((frames, 4, width)),
            ],
            scratch_shapes=[
                pltpu.VMEM((tokens, width), wide),
                pltpu.VMEM((tokens, width), wide),
                pltpu.VMEM((chunk, width), low_type),
            ],
        ),
        out_shape=[
            jax.ShapeDtypeStruct((tokens, chunk * steps), low_type),
            jax.ShapeDtypeStruct((tokens, width), low_type),
            jax.ShapeDtypeStruct((tokens, width), low_type),
            jax.ShapeDtypeStruct((members, tokens, local), low_type),
            jax.ShapeDtypeStruct((2, patch, width), wide),
            jax.ShapeDtypeStruct((2, width), wide),
            jax.ShapeDtypeStruct((frames, 4, width), wide),
        ],
        compiler_params=pltpu.CompilerParams(
            dimension_semantics=("arbitrary",), vmem_limit_bytes=56 * MIB
        ),
        cost_estimate=pl.CostEstimate(
            flops=4 * tokens * width * chunk * steps, bytes_accessed=40 * MIB, transcendentals=0
        ),
        name="ff_backward",
    )(
        me, d_pred, state_one, mixed, branch, mod, noisy_t, gain, pw_out, *parts[0], *parts[1],
        down, out_full, slope,
    )


def wide_grads_kernel(
    me_ref, dh_ref, act_ref, db_ref, h_ref, dm_ref, fr_ref, *outs, spans, places, narrow, half
):
    *outs, scr = outs
    adds, outs = outs[: len(outs) - len(spans)], outs[len(outs) - len(spans) :]
    up = dot_tn(dh_ref[...], h_ref[...])
    down = dot_tn(act_ref[...], dm_ref[...])
    left = db_ref[...]
    out = jnp.concatenate([dot_tn(left, fr_ref[m]) for m in range(fr_ref.shape[0])], axis=1)
    if narrow < left.shape[1]:
        scr[...] = out
        block = jnp.bitwise_xor(me_ref[0], 2 * pl.program_id(0) + half)
        at = lax.rem(block, left.shape[1] // narrow) * narrow
        out = scr[pl.ds(pl.multiple_of(at, narrow), narrow), :]
    my_z = me_ref[1]
    for zz in range(4):
        pieces = [
            arr[zz * (arr.shape[0] // 4) : (zz + 1) * (arr.shape[0] // 4)] for arr in (up, down, out)
        ]
        whole = jnp.concatenate(pieces, axis=0)
        apart = jnp.bitwise_xor(my_z, zz)
        for k, (ref, (begin, end), (dim_one, dim_zero)) in enumerate(zip(outs, spans, places)):
            index = [0] * (len(ref.shape) - 2)
            index[dim_one] = lax.shift_right_logical(apart, 1)
            index[dim_zero] = jnp.bitwise_and(apart, 1)
            part = whole[begin:end]
            if adds:
                part = part + adds[k][tuple(index)].astype(wide)
            ref[tuple(index)] = part.astype(ref.dtype)


def wide_grads(me, half, d_hidden, act, d_branch, h_two, d_mixed, framed, orders, devices, adds=()):
    tokens, width = h_two.shape
    members, _, local = framed.shape
    chunk = act.shape[1] // (devices // 4)
    out_chunk = width // (devices // 4)
    out_wide = max(out_chunk, 128)
    bits = sorted((n for n in orders[0] if n[0] == "a"), reverse=True) + ["x"]
    rows_dev = (2 * chunk + out_chunk) // 4
    part_rows = rows_dev // 3
    spans = [(k * part_rows, (k + 1) * part_rows) for k in range(3)]

    def block(q, me):
        return jnp.bitwise_xor(me[0], 2 * q + half)

    def out_spec(order):
        def place(q, me):
            index = []
            for name in order:
                if name[0] in "ax":
                    index.append(
                        jnp.bitwise_and(
                            lax.shift_right_logical(q, len(bits) - 1 - bits.index(name)), 1
                        )
                    )
                else:
                    index.append(0)
            return tuple(index) + (0, 0)

        shape = tuple(1 if n[0] in "ax" else 2 for n in order) + (part_rows, width)
        return pl.BlockSpec(shape, place)

    return pl.pallas_call(
        partial(
            wide_grads_kernel,
            spans=spans,
            places=[(o.index("z1"), o.index("z0")) for o in orders],
            narrow=out_chunk,
            half=half,
        ),
        grid_spec=pltpu.PrefetchScalarGridSpec(
            num_scalar_prefetch=1,
            grid=(devices // 8,),
            in_specs=[
                pl.BlockSpec((tokens, chunk), lambda q, me: (0, block(q, me))),
                pl.BlockSpec((tokens, chunk), lambda q, me: (0, block(q, me))),
                pl.BlockSpec(
                    (tokens, out_wide),
                    lambda q, me: (0, lax.div(block(q, me), out_wide // out_chunk)),
                ),
                once(h_two.shape),
                once(d_mixed.shape),
                once(framed.shape),
            ] + [out_spec(o) for o in orders][: len(adds)],
            out_specs=[out_spec(o) for o in orders],
            scratch_shapes=[pltpu.VMEM((out_wide, width), wide)],
        ),
        out_shape=[
            jax.ShapeDtypeStruct((2,) * len(o) + (part_rows, width), low_type) for o in orders
        ],
        compiler_params=pltpu.CompilerParams(
            dimension_semantics=("arbitrary",), vmem_limit_bytes=48 * MIB
        ),
        cost_estimate=pl.CostEstimate(
            flops=2 * tokens * width * (2 * chunk + out_chunk) * (devices // 8),
            bytes_accessed=24 * MIB, transcendentals=0,
        ),
        name="wide_grads",
    )(me, d_hidden, act, d_branch, h_two, d_mixed, framed, *adds)


def qkv_back_kernel(
    me_ref, dq_ref, dk_ref, dv_ref, h_ref, noisy_ref, pw_ref, bias_ref, mod_ref, w_ref, sel_ref,
    cs_ref, sn_ref, tc_ref, ts_ref, dw_one, dw_two, dmod_ref, demb_ref, dbias_ref,
    acc_scr, emb_scr, bias_scr, pw_scr, *, width, local, maps,
):
    i = pl.program_id(0)

    @pl.when(i == 0)
    def _():
        pw_scr[...] = pack_right(pw_ref[...])
        acc_scr[...] = jnp.zeros_like(acc_scr)
        emb_scr[...] = jnp.zeros_like(emb_scr)
        bias_scr[...] = jnp.zeros_like(bias_scr)

    cosine = cs_ref[...] + tc_ref[0]
    sine = sn_ref[...] + ts_ref[0]
    half = local // 2
    parts = []
    for ref in (dq_ref, dk_ref):
        first = ref[:, 0:half].astype(wide)
        second = ref[:, half:local].astype(wide)
        turned = jnp.concatenate(
            [first * cosine + second * sine, second * cosine - first * sine], axis=1
        ).astype(low_type)
        parts.append(dot_nn(turned, sel_ref[...]).astype(low_type))
    parts.append(dv_ref[...])
    d_qkv = jnp.concatenate(parts, axis=1)
    acc_scr[...] += dot_tn(d_qkv, h_ref[...])
    d_h = dot_nn(d_qkv, w_ref[...])
    noisy = noisy_ref[0]
    state = dot_tn(pack_left(noisy), pw_scr[...]) + bias_ref[...]
    normed, rstd = layer_stats(state)
    scl = mod_ref[0, :, width : 2 * width]
    dmod_ref[0, :, 0:width] = jnp.sum(d_h, axis=0, keepdims=True)
    dmod_ref[0, :, width : 2 * width] = jnp.sum(d_h * normed, axis=0, keepdims=True)
    d_state = layer_back(normed, rstd, d_h * (1.0 + scl))
    emb_scr[...] += thin_product(noisy, d_state)
    bias_scr[...] += jnp.sum(d_state.reshape(-1, 8, width), axis=0)

    @pl.when(i == pl.num_programs(0) - 1)
    def _():
        rows = acc_scr.shape[0] // len(maps[0])
        at = 0
        for ref, places in ((dw_one, maps[0]), (dw_two, maps[1])):
            count = ref.shape[1]
            for pos, apart in enumerate(places):
                dev = jnp.bitwise_xor(me_ref[0], apart)
                begin = pl.multiple_of(dev * rows + at, 8)
                ref[pos] = acc_scr[pl.ds(begin, count), :].astype(ref.dtype)
            at += count
        demb_ref[...] = emb_scr[...]
        dbias_ref[...] = jnp.sum(bias_scr[...], axis=0, keepdims=True)


def near_places(order):
    natural = sorted((n for n in order if n[0] == "a"), reverse=True) + ["z1", "z0"]
    places = []
    for pos in range(1 << len(order)):
        value = 0
        for d, name in enumerate(order):
            if (pos >> (len(order) - 1 - d)) & 1:
                value |= 1 << (len(natural) - 1 - natural.index(name))
        places.append(value)
    return places


def qkv_back(me, orders, dq, dk, dv, h_one, noisy_t, pw, bias, mod, w_local, tables, tcos, tsin):
    frames, patch, ftok = noisy_t.shape
    tokens, width = h_one.shape
    local = dq.shape[1]
    cs, sn, _, _, sel = tables
    count = 1 << len(orders[0])
    rows = w_local.shape[0] // count
    first = -(-rows // 16) * 8
    block_one, block_two = (count, first, width), (count, rows - first, width)
    full = lambda shape: pl.BlockSpec(shape, lambda i, me: (0,) * len(shape))
    row = lambda cols: pl.BlockSpec((ftok, cols), lambda i, me: (i, 0))
    return pl.pallas_call(
        partial(
            qkv_back_kernel, width=width, local=local, maps=[near_places(o) for o in orders]
        ),
        grid_spec=pltpu.PrefetchScalarGridSpec(num_scalar_prefetch=1, grid=(frames,),
        in_specs=[
            row(local), row(local), row(local), row(width),
            pl.BlockSpec((1, patch, ftok), lambda i, me: (i, 0, 0)),
            full(pw.shape),
            full((1, width)),
            pl.BlockSpec((1, 1, 6 * width), lambda i, me: (i, 0, 0)),
            full(w_local.shape),
            full(sel.shape),
            full(cs.shape),
            full(sn.shape),
            pl.BlockSpec((1, 1, local // 2), lambda i, me: (i, 0, 0)),
            pl.BlockSpec((1, 1, local // 2), lambda i, me: (i, 0, 0)),
        ],
        out_specs=[
            full(block_one), full(block_two),
            pl.BlockSpec((1, 1, 2 * width), lambda i, me: (i, 0, 0)),
            full(pw.shape),
            full((1, width)),
        ],
        scratch_shapes=[
            pltpu.VMEM(w_local.shape, wide),
            pltpu.VMEM(pw.shape, wide),
            pltpu.VMEM((8, width), wide),
            pltpu.VMEM((6 * patch, width), low_type),
        ],
        ),
        out_shape=[
            jax.ShapeDtypeStruct(block_one, low_type),
            jax.ShapeDtypeStruct(block_two, low_type),
            jax.ShapeDtypeStruct((frames, 1, 2 * width), wide),
            jax.ShapeDtypeStruct(pw.shape, wide),
            jax.ShapeDtypeStruct((1, width), wide),
        ],
        compiler_params=pltpu.CompilerParams(
            dimension_semantics=("arbitrary",), vmem_limit_bytes=48 * MIB
        ),
        cost_estimate=pl.CostEstimate(
            flops=2 * 2 * tokens * width * 3 * local, bytes_accessed=16 * MIB, transcendentals=0
        ),
        name="qkv_back",
    )(me, dq, dk, dv, h_one, noisy_t, pw, bias, mod, w_local, sel, cs, sn, tcos, tsin)


def tri_blocks(count):
    return [(r, c) for r in range(count) for c in range(r, count)]


def tile_places(order):
    natural = sorted((n for n in order if n[0] == "a"), reverse=True) + ["x", "c", "z1", "z0"]
    places = []
    for pos in range(1 << len(order)):
        value = 0
        for d, name in enumerate(order):
            if (pos >> (len(order) - 1 - d)) & 1:
                value |= 1 << (len(natural) - 1 - natural.index(name))
        places.append(value)
    return places


def gram_kernel(me_ref, u_ref, *refs, blk, cuts, maps):
    outs, scr = refs[:-1], refs[-1]
    mats, _, width = u_ref.shape
    pairs = tri_blocks(width // blk)
    me = me_ref[0]
    clusters = len(maps[0]) // 32
    low = [u_ref[m].astype(low_type) for m in range(mats)]
    for n, (r, c) in enumerate(pairs):
        for m in range(mats):
            scr[m] = dot_tn(low[m][:, r * blk : (r + 1) * blk], low[m][:, c * blk : (c + 1) * blk])
        for m in range(mats // clusters):
            index = m * len(pairs) + n
            for part, ref in enumerate(outs):
                if cuts[part] <= index < cuts[part + 1]:
                    inner = index - cuts[part]
                    for pos, apart in enumerate(maps[part]):
                        which, top, left = tile_of(jnp.bitwise_xor(me, apart), mats // clusters, blk)
                        ref[pos, inner * 16 : (inner + 1) * 16, :] = scr[
                            which + m, pl.ds(pl.multiple_of(top, 16), 16),
                            pl.ds(pl.multiple_of(left, blk // 2), blk // 2),
                        ].astype(ref.dtype)


def tile_of(dev, mats_each, blk):
    return (
        lax.shift_right_logical(dev, 5) * mats_each,
        jnp.bitwise_and(lax.shift_right_logical(dev, 1), 15) * 16,
        jnp.bitwise_and(dev, 1) * (blk // 2),
    )


def gram_parts(me, u, blk, cuts, orders, devices):
    mats, rows, width = u.shape
    maps = [tile_places(o) for o in orders]
    shapes = [(devices, (cuts[k + 1] - cuts[k]) * 16, blk // 2) for k in range(len(orders))]
    return pl.pallas_call(
        partial(gram_kernel, blk=blk, cuts=cuts, maps=maps),
        grid_spec=pltpu.PrefetchScalarGridSpec(
            num_scalar_prefetch=1,
            grid=(1,),
            in_specs=[once(u.shape)],
            out_specs=[once(s) for s in shapes],
            scratch_shapes=[pltpu.VMEM((mats, blk, blk), wide)],
        ),
        out_shape=[jax.ShapeDtypeStruct(s, low_type) for s in shapes],
        compiler_params=pltpu.CompilerParams(
            dimension_semantics=("arbitrary",), vmem_limit_bytes=40 * MIB
        ),
        name="gram_parts",
    )(me, u)


def polish_kernel(me_ref, u_ref, *refs, blk, cuts, maps, factors):
    mats, rows, width = u_ref.shape
    parts, olds, outs, g_scr = refs[: 2 * len(maps)], refs[2 * len(maps) : -mats - 1], refs[-mats - 1 : -1], refs[-1]
    pairs = tri_blocks(width // blk)
    me = me_ref[0]
    clusters = len(maps[0]) // 16
    diag = lax.broadcasted_iota(jnp.int32, (blk, blk), 0) == lax.broadcasted_iota(
        jnp.int32, (blk, blk), 1
    )
    for m in range(mats // clusters):
        for n, (r, c) in enumerate(pairs):
            index = m * len(pairs) + n
            for part, places in enumerate(maps):
                if not cuts[part] <= index < cuts[part + 1]:
                    continue
                inner = index - cuts[part]
                for ref, other in ((parts[2 * part], 0), (parts[2 * part + 1], 4)):
                    for pos, apart in enumerate(places):
                        which, top, left = tile_of(
                            jnp.bitwise_xor(me, apart + other), mats // clusters, blk
                        )
                        g_scr[
                            which + m, pl.ds(pl.multiple_of(r * blk + top, 16), 16),
                            pl.ds(pl.multiple_of(c * blk + left, blk // 2), blk // 2),
                        ] = ref[pos, inner * 16 : (inner + 1) * 16, :]
    for m in range(mats):
        trace = jnp.zeros((1, 1), wide)
        for r, c in pairs:
            piece = g_scr[m, r * blk : (r + 1) * blk, c * blk : (c + 1) * blk]
            if r == c:
                trace += jnp.sum(jnp.where(diag, piece.astype(wide), 0.0), keepdims=True)
            else:
                g_scr[m, c * blk : (c + 1) * blk, r * blk : (r + 1) * blk] = piece.T
        scale = jnp.sqrt(trace) + 1e-07
        inverse = 1.0 / scale
        inverse_sq = inverse * inverse
        own = outs[m].shape[0]

        def times(value):
            both = dot_nn(jnp.concatenate(split_two(value), axis=0), g_scr[m])
            return (both[:own] + both[own:]) * inverse_sq

        def cubic(value):
            once_ = times(value)
            return coef_one * value + coef_two * once_ + coef_three * times(once_)

        current = cubic(u_ref[m, :own, :] * inverse)
        for _ in range(NS_ITERS - 1):
            second = cubic(cubic(times(current)))
            third = cubic(cubic(times(second)))
            current = coef_one * current + coef_two * second + coef_three * third
        outs[m][...] = olds[m][...] * (1.0 - 2.0 * 0.01) - factors[m] * current


def polish(me, u, parts, olds, blk, cuts, orders, factors):
    mats, rows, width = u.shape
    maps = [tile_places(o) for o in orders]
    return pl.pallas_call(
        partial(polish_kernel, blk=blk, cuts=cuts, maps=maps, factors=factors),
        grid_spec=pltpu.PrefetchScalarGridSpec(
            num_scalar_prefetch=1,
            grid=(1,),
            in_specs=[once(u.shape)] + [once(p.shape) for p in parts] + [once(o.shape) for o in olds],
            out_specs=[once(o.shape) for o in olds],
            scratch_shapes=[pltpu.VMEM((mats, width, width), low_type)],
        ),
        out_shape=[jax.ShapeDtypeStruct(o.shape, wide) for o in olds],
        compiler_params=pltpu.CompilerParams(
            dimension_semantics=("arbitrary",), vmem_limit_bytes=40 * MIB
        ),
        cost_estimate=pl.CostEstimate(
            flops=2 * 24 * mats * rows * width * width, bytes_accessed=12 * MIB, transcendentals=0
        ),
        name="polish",
    )(me, u, *parts, *olds)


def bit_stages(count_a):
    stages = {}
    bits_a = count_a.bit_length() - 1
    for b in range(bits_a):
        stages["a%d" % (bits_a - 1 - b)] = ("a", 1 << (bits_a - 1 - b), b)
    stages["x"] = ("x", 1, bits_a)
    stages["c"] = ("c", 1, bits_a + 1)
    stages["z1"] = ("z", 2, bits_a + 2)
    stages["z0"] = ("z", 1, bits_a + 3)
    return stages


def swap(value, axis, distance):
    size = lax.axis_size(axis)
    return lax.ppermute(value, axis, [(i, i ^ distance) for i in range(size)])


def bit_of(axis, distance):
    return (lax.axis_index(axis) // distance) % 2


def in_order(blocks, names):
    for dim, name in enumerate(names):
        axis = name[0]
        distance = {"z1": 2, "a1": 2, "a2": 4}.get(name, 1)
        mine = bit_of(axis, distance)
        flipped = jnp.flip(blocks, dim)
        blocks = jnp.where(mine == 0, blocks, flipped)
    natural = sorted(n for n in names if n[0] == "a")[::-1] + [
        n for n in ("x", "c", "z1", "z0") if n in names
    ]
    order = [names.index(n) for n in natural] + list(range(len(names), blocks.ndim))
    return blocks.transpose(order)


def three_orders(stages):
    names_a = [n for n in stages if n.startswith("a")]
    return (
        ["x"] + names_a + ["z0", "z1"],
        names_a + ["z0", "x", "z1"],
        ["z0", "x"] + names_a + ["z1"],
    )


def after(value, *others):
    return lax.optimization_barrier((value,) + others)[0]


def halve(blocks, order, stages):
    keep, send = blocks[0], blocks[1]
    for step, name in enumerate(order):
        axis, distance, _ = stages[name]
        got = swap(send.astype(low_type), axis, distance)
        if step == len(order) - 1:
            return keep.astype(wide) + got.astype(wide)
        send = (keep[1].astype(wide) + got[1].astype(wide)).astype(low_type)
        keep = keep[0].astype(wide) + got[0].astype(wide)


class Ladder:
    def __init__(self, blocks, orders, stages):
        self.orders, self.stages, self.rung = orders, stages, 0
        self.keep = [b[0] for b in blocks]
        self.send = [b[1] for b in blocks]

    def exchange(self):
        self.got = []
        for order, send in zip(self.orders, self.send):
            axis, distance, _ = self.stages[order[self.rung]]
            self.got.append(swap(send.astype(low_type), axis, distance))
        self.rung += 1

    def add(self, *first):
        got = lax.optimization_barrier(tuple(self.got) + first)[: len(self.got)]
        pairs = list(zip(self.keep, got))
        if self.rung == len(self.orders[0]):
            return [k.astype(wide) + g.astype(wide) for k, g in pairs]
        self.send = [(k[1].astype(wide) + g[1].astype(wide)).astype(low_type) for k, g in pairs]
        self.keep = [k[0].astype(wide) + g[0].astype(wide) for k, g in pairs]


def double(block, order, stages):
    for name in order:
        axis, distance, _ = stages[name]
        block = jnp.stack([block, swap(block, axis, distance)])
    return block


def spread(payload):
    count = math.prod(lax.axis_size(n) for n in ALL)
    return lax.all_to_all(
        jnp.broadcast_to(payload[None], (count,) + payload.shape),
        ALL, split_axis=0, concat_axis=0, tiled=True,
    )


def unit_plan(devices):
    quarter = devices // 4
    edges = []
    for unit in range(3 * devices):
        section, place = unit // devices, unit % devices
        member, rest = place // quarter, place % quarter
        index = section * quarter + rest
        pos, slot = index // 3, index % 3
        a, z = pos // 4, pos % 4
        dest = ((a * 2 + member // 2) * 2 + member % 2) * 4 + z
        edges.append((unit // 3, unit % 3, dest, slot))
    left = list(edges)
    colors = []
    for _ in range(3):
        match = {}

        def augment(src, seen):
            for e in left:
                if e[0] != src or e[2] in seen:
                    continue
                seen.add(e[2])
                if e[2] not in match or augment(match[e[2]][0], seen):
                    match[e[2]] = e
                    return True
            return False

        for src in range(devices):
            assert augment(src, set())
        chosen = list(match.values())
        for e in chosen:
            left.remove(e)
        colors.append(chosen)
    return colors


def send_units(units, plan, back):
    devices = len(plan[0])
    here = lax.axis_index(ALL)
    src_key, dst_key = ((2, 3), (0, 1)) if back else ((0, 1), (2, 3))
    got = []
    for chosen in plan:
        table = np.zeros(devices, np.int32)
        for e in chosen:
            table[e[src_key[0]]] = e[src_key[1]]
        slot = jnp.asarray(table)[here]
        piece = lax.dynamic_index_in_dim(units, slot, 0, keepdims=False)
        got.append(lax.ppermute(piece, ALL, [(e[src_key[0]], e[dst_key[0]]) for e in chosen]))
    place = np.zeros((devices, 3), np.int32)
    for color, chosen in enumerate(plan):
        for e in chosen:
            place[e[dst_key[0]], e[dst_key[1]]] = color
    where_from = jnp.asarray(place)[here]
    out = []
    for slot in range(3):
        pick = where_from[slot]
        out.append(jnp.where(pick == 0, got[0], jnp.where(pick == 1, got[1], got[2])))
    return jnp.stack(out)


def body(
    noisy_latents,
    target_latents,
    noise_levels,
    clip_start,
    qkv_weight,
    qkv_moment,
    out_weight,
    out_moment,
    up_weight,
    up_moment,
    down_weight,
    down_moment,
    ada_weight,
    ada_first,
    ada_second,
    patch_weight,
    patch_first,
    patch_second,
    vectors,
    vec_first,
    vec_second,
):
    count_a = lax.axis_size("a")
    members = lax.axis_size("x") * lax.axis_size("c")
    devices = count_a * members * lax.axis_size("z")
    groups = count_a * lax.axis_size("z")
    frames_dev = noise_levels.shape[0]
    tokens_dev = noisy_latents.shape[0]
    frame_tok = tokens_dev // frames_dev
    width = patch_weight.shape[2]
    patch_size = patch_weight.shape[1]
    head_dim = width // HEADS
    local_heads = HEADS // members
    local = local_heads * head_dim
    group_frames = frames_dev * members
    frames_all = frames_dev * devices
    group_tokens = group_frames * frame_tok
    score_scale = 1.0 / math.sqrt(head_dim)
    stages = bit_stages(count_a)
    my_a, my_z = lax.axis_index("a"), lax.axis_index("z")
    my_group = my_a * 4 + my_z
    my_member = lax.axis_index("x") * 2 + lax.axis_index("c")
    tables = rope_tables(head_dim, local_heads, frame_tok)
    tables = tables[:4] + (jnp.asarray(tables[4], low_type),)
    plan = unit_plan(devices)

    rows_unit = qkv_weight.shape[0] // 3
    units = send_units(qkv_weight.astype(low_type).reshape(3, rows_unit, width), plan, False)
    names_a = [n for n in stages if n.startswith("a")]

    swap_axes = ("x", "c", "z")
    moves = [(g * 4 + z, z * 4 + g) for g in range(4) for z in range(4)]
    noisy_t = noisy_latents.T.reshape(patch_size, frames_dev, frame_tok).transpose(1, 0, 2)
    target_t = target_latents.T.reshape(patch_size, frames_dev, frame_tok).transpose(1, 0, 2)
    mine = lax.ppermute(jnp.stack([noisy_t, target_t]), swap_axes, moves)

    meta = jnp.concatenate([noise_levels, clip_start]).astype(wide)
    meta = jnp.pad(meta, (0, 128 - meta.shape[0]))[None]
    meta_all = spread(meta)[:, 0]
    meta_all, units, mine = lax.optimization_barrier((meta_all, units, mine))
    levels_all = meta_all[:, :frames_dev].reshape(frames_all)
    starts_all = meta_all[:, frames_dev : 2 * frames_dev].reshape(frames_all)
    starts_group = lax.dynamic_slice_in_dim(starts_all, my_group * group_frames, group_frames)
    starts_int = starts_group.astype(jnp.int32)
    noisy_mine, target_mine = mine[0], mine[1]
    pair = double(noisy_mine, ["c"], stages)

    far = double(units, ["z1"], stages)
    rows_up, rows_out = up_weight.shape[0], out_weight.shape[0]
    split = ((rows_up + rows_out) // 2, rows_up - (rows_up + rows_out) // 2)
    rising = [["z1", "z0"] + names_a[::-1] + ["x"], ["z1", "x", "z0"] + names_a[::-1]]
    gather_orders = [o[::-1] for o in rising]
    shares = [
        after(up_weight[: split[0]].astype(low_type), meta_all),
        jnp.concatenate([up_weight[split[0] :], out_weight], axis=0).astype(low_type),
    ]
    climb = lambda shares, rung: [
        double(share, [order[rung]], stages) for share, order in zip(shares, rising)
    ]
    shares = climb(shares, 0)
    cond_low = jax.nn.silu(level_features(levels_all, width)).astype(low_type)
    ada_rows = ada_weight.shape[0]
    mod_rows = dot_nt(cond_low, ada_weight.astype(low_type))
    mod_rows, far, pair = lax.optimization_barrier((mod_rows, far, pair))
    mod_out = jnp.broadcast_to(
        mod_rows.reshape(count_a, 1, 4, group_frames, ada_rows),
        (count_a, members, 4, group_frames, ada_rows),
    ).reshape(devices, group_frames, ada_rows)
    mod_in = lax.all_to_all(mod_out, ALL, split_axis=0, concat_axis=0, tiled=True)
    noisy_group = in_order(double(pair, ["x"], stages), ["x", "c"]).reshape(
        group_frames, patch_size, frame_tok
    )
    half_one = double(far[:, :, : rows_unit // 2], ["z0"], stages)
    half_two = double(far[:, :, rows_unit // 2 :], names_a[::-1], stages)
    down_full = lax.all_gather(
        after(down_weight.astype(low_type), mod_out), ALL, axis=0, tiled=True
    ).reshape(devices, -1, width)
    mod_in, half_one, half_two = lax.optimization_barrier((mod_in, half_one, half_two))
    half_one = in_order(double(half_one, names_a[::-1], stages), names_a + ["z0", "z1"])
    half_two = in_order(double(half_two, ["z0"], stages), ["z0"] + names_a + ["z1"])
    qkv_local = jnp.concatenate(
        [half_one.reshape(3 * groups, -1, width), half_two.reshape(3 * groups, -1, width)], axis=1
    ).reshape(3 * local, width)
    modul = mod_in.transpose(1, 0, 2).reshape(group_frames, 6 * width) + vectors[2:8].reshape(
        1, 6 * width
    )
    mod3 = modul.reshape(group_frames, 1, 6 * width)
    *shares, mod3 = lax.optimization_barrier((*shares, mod3))
    shares = climb(shares, 1)
    mod_mine = lax.dynamic_slice_in_dim(mod3, my_member * frames_dev, frames_dev)

    frame_ids = jnp.arange(group_frames, dtype=jnp.int32)
    time_pos = (frame_ids - starts_int).astype(wide)
    t_angle = time_pos[:, None] * tables[2][None, :]
    tcos = (jnp.cos(t_angle) * tables[3][None, :])[:, None, :]
    tsin = (jnp.sin(t_angle) * tables[3][None, :])[:, None, :]

    pw_in = patch_weight[0]
    bias_in = vectors[0:1]
    h_one, q, k, v = embed_qkv(
        noisy_group, pw_in, bias_in, mod3, qkv_local, tables, tcos, tsin, score_scale
    )
    me = lax.axis_index(ALL).astype(jnp.int32)
    place = jnp.stack([me // 4, me % 4])
    middle = group_frames * 7 // 12
    *shares, q = lax.optimization_barrier((*shares, q))
    shares = climb(shares, 2)
    att, att_low, lse = attend(starts_int, q, k, v, (), 0, middle, group_frames, local_heads)
    *shares, q_late = lax.optimization_barrier((*shares, q, att))[:-1]
    for rung in range(3, len(rising[0])):
        shares = climb(shares, rung)
    att, att_low, lse = attend(
        starts_int, q_late, k, v, (att, att_low, lse), middle, group_frames, group_frames,
        local_heads,
    )
    *shares, att_low = lax.optimization_barrier((*shares, att_low))
    shares = [(share, swap(share, "c", 1)) for share in shares]
    framed = lax.all_to_all(
        att_low.reshape(members, tokens_dev, local), ("x", "c"), split_axis=0, concat_axis=0,
        tiled=True,
    )

    gain = vectors[1:2]
    pw_out = patch_weight[1]
    state_one, branch, h_two, out_full = post_attend(
        me[None], framed, noisy_mine, pw_in, bias_in, mod_mine, shares[1], gather_orders[1], split[1]
    )
    act, slope, mixed, pred = ff_forward(
        place, h_two, state_one, mod_mine, shares, gather_orders, split, down_full, gain, pw_out,
        frame_tok,
    )
    member_axes = ("x", "c")
    ahead = [(i, i + 1) for i in range(members - 1)]
    behind = [(i + 1, i) for i in range(members - 1)]
    edge = lax.ppermute(
        jnp.stack([pred[-1], target_mine[-1]]).astype(low_type), member_axes, ahead
    ).astype(wide)
    prev_pred = jnp.concatenate([edge[0:1], pred[:-1]], axis=0)
    prev_goal = jnp.concatenate([edge[1:2], target_mine[:-1]], axis=0)
    diff = pred - prev_pred - (target_mine - prev_goal)
    my_frames = my_member * frames_dev + jnp.arange(frames_dev, dtype=jnp.int32)
    valid = my_frames > lax.dynamic_slice_in_dim(starts_int, my_member * frames_dev, frames_dev)
    loss_local = jnp.sum(jnp.where(valid[:, None, None], diff * diff, 0.0))
    entry_count = float(frames_all * frame_tok * patch_size)
    d_diff = jnp.where(valid[:, None, None], (2.0 / entry_count) * diff, 0.0)
    returned = lax.ppermute(d_diff[0], member_axes, behind)
    d_pred = d_diff - jnp.concatenate([d_diff[1:], returned[None]], axis=0)
    d_hidden, d_mixed, d_branch, d_framed, d_small, d_sums, d_mod_rest = ff_backward(
        place, d_pred, state_one, mixed, branch, mod_mine, noisy_mine, gain, pw_out, shares,
        gather_orders, split, down_full, out_full, slope, members,
    )
    d_att = lax.all_to_all(d_framed, ("x", "c"), split_axis=0, concat_axis=0, tiled=True).reshape(
        group_tokens, local
    )

    orders = three_orders(stages)
    grads_of = lambda half, adds=(): wide_grads(
        place, half, d_hidden, act, d_branch, h_two, d_mixed, framed, orders, devices, adds
    )
    others = grads_of(1)
    core_axis, core_distance, _ = stages["c"]
    passed = [swap(o, core_axis, core_distance) for o in others]

    cuts = [group_frames * n // 12 for n in (0, 5, 8, 10, 12)]

    def part_back(n, q, sums):
        return attend_back(
            starts_int, q, d_att, att, lse, k, v, sums, cuts[n], cuts[n + 1], group_frames,
            local_heads, score_scale,
        )

    dq, dk, dv = part_back(0, after(q, *others), ())
    adds = lax.optimization_barrier(tuple(passed) + (dk,))[:3]
    ladder = Ladder(grads_of(0, adds), orders, stages)
    ladder.exchange()
    dq, dk, dv = part_back(1, after(q, *ladder.send), (dq, dk, dv))
    ladder.add(dk)
    ladder.exchange()
    dq, dk, dv = part_back(2, after(q, *ladder.send), (dq, dk, dv))
    ladder.add(dk)
    ladder.exchange()
    dq, dk, dv = part_back(3, after(q, *ladder.send), (dq, dk, dv))
    ladder.add(dk)
    ladder.exchange()
    near_orders = [names_a + ["z0", "z1"], ["z0"] + names_a + ["z1"]]
    dw_one, dw_two, d_mod_one, d_embed, d_bias = qkv_back(
        (my_a * 4 + my_z).astype(jnp.int32)[None], near_orders, dq, after(dk, *ladder.send), dv, h_one, noisy_group, pw_in, bias_in, mod3, qkv_local,
        tables, tcos, tsin,
    )
    while ladder.rung < len(orders[0]):
        ladder.add()
        ladder.exchange()
    near_dims = (2,) * len(near_orders[0])
    near = Ladder(
        [d.reshape(near_dims + d.shape[1:]) for d in (dw_one, dw_two)], near_orders, stages
    )
    near.exchange()
    ladder.got = list(lax.optimization_barrier(tuple(ladder.got) + (d_bias,)))[:3]
    g_wide = jnp.concatenate(ladder.add(), axis=0)
    g_up, g_down, g_out = (
        g_wide[:rows_up], g_wide[rows_up : 2 * rows_up], g_wide[2 * rows_up :]
    )
    d_rest = lax.dynamic_update_slice_in_dim(
        jnp.zeros((group_frames, 4 * width), wide),
        d_mod_rest.reshape(frames_dev, 4 * width), my_member * frames_dev, 0,
    )
    d_mod = jnp.concatenate([d_mod_one[:, 0], d_rest], axis=1)
    d_mod = d_mod.reshape(group_frames, devices, ada_rows).transpose(1, 0, 2)
    smalls = jnp.concatenate(
        [d_embed + d_small[1], d_small[0], d_bias + d_sums[1:2], d_sums[0:1]], axis=0
    )
    small_rows = smalls.shape[0]
    small_part = small_rows * width // devices
    mod_part = group_frames * ada_rows
    packed = jnp.concatenate(
        [d_mod.reshape(devices, mod_part), smalls.reshape(devices, small_part)], axis=1
    )
    pad = -packed.shape[1] % 128
    packed = jnp.pad(packed, ((0, 0), (0, pad))).reshape(devices, -1, 128)
    packed = after(packed, *ladder.got)
    arrived = lax.all_to_all(packed, ALL, split_axis=0, concat_axis=0, tiled=True).reshape(
        devices, -1
    )
    while near.rung < len(near_orders[0]):
        near.add()
        near.exchange()
    g_one, g_two = near.add()
    g_units = jnp.concatenate([g_one, g_two], axis=0).reshape(3, rows_unit, width)
    g_qkv = send_units(g_units, plan, True).reshape(3 * rows_unit, width)
    small_mine = jnp.sum(arrived[:, mod_part : mod_part + small_part], axis=0)
    mod_grad = (
        arrived[:, :mod_part]
        .reshape(count_a, members, 4, group_frames, ada_rows)
        .sum(axis=1)
        .reshape(frames_all, ada_rows)
    )
    bias_mine = jnp.sum(mod_grad, axis=0)
    g_ada = dot_tn(mod_grad.astype(low_type), cond_low)

    shards = (g_qkv, g_out, g_up, g_down)
    local_sq = (
        sum((jnp.sum(piece * piece) for piece in shards))
        + jnp.sum(g_ada * g_ada)
        + jnp.sum(small_mine * small_mine)
        + jnp.sum(bias_mine * bias_mine)
    )
    report = jnp.concatenate([small_mine, bias_mine, local_sq[None], loss_local[None]])
    size = report.shape[0]
    report = jnp.pad(report, (0, -size % 128)).reshape(-1, 128)
    everyone = spread(report).reshape(devices, -1)
    small_all = everyone[:, :small_part].reshape(small_rows, width)
    bias_all = everyone[:, small_part : small_part + ada_rows].reshape(6, width)
    norm = jnp.sqrt(jnp.sum(everyone[:, size - 2]))
    loss_total = jnp.sum(everyone[:, size - 1])
    g_patch = small_all[: 2 * patch_size].reshape(2, patch_size, width)
    g_vec = jnp.concatenate([small_all[2 * patch_size :], bias_all], axis=0)
    clip = jnp.minimum(1.0, 0.01 / norm)

    olds = (qkv_weight, out_weight, up_weight, down_weight)
    moments = (qkv_moment, out_moment, up_moment, down_moment)
    moments_new = [0.95 * moments[j] + clip * shards[j] for j in range(4)]
    most = max(m.shape[0] for m in olds)
    steers = jnp.stack(
        [
            jnp.pad(
                clip * shards[j] + 0.95 * moments_new[j], ((0, most - olds[j].shape[0]), (0, 0))
            )
            for j in range(4)
        ]
    )
    blk = 256
    gram_orders = [["c"] + o for o in orders[:2]]
    pairs = len(tri_blocks(width // blk)) * 4 // (devices // 32)
    cuts = (0, pairs // 2, pairs)
    parts = []
    for k, part in enumerate(gram_parts(me[None], steers, blk, cuts, gram_orders, devices)):
        shape = (2,) * len(stages) + part.shape[1:]
        total = halve(part.reshape(shape), gram_orders[k], stages).astype(low_type)
        line = double(total, gram_orders[k][:0:-1], stages).reshape((-1,) + part.shape[1:])
        parts += [line, swap(line, "c", 1)]
    factors = [2.0 * math.sqrt(max(1.0, o.shape[0] * devices / width)) for o in olds]
    updated = polish(
        me[None], steers, parts, olds, blk, cuts, [o[1:] for o in gram_orders], factors
    )
    ada_new, ada_one, ada_two = adamw(ada_weight, ada_first, ada_second, clip * g_ada, 0.08)
    patch_new, patch_one, patch_two = adamw(
        patch_weight, patch_first, patch_second, clip * g_patch, 0.15
    )
    vec_new, vec_one, vec_two = adamw(vectors, vec_first, vec_second, clip * g_vec, 0.5)
    return (
        loss_total,
        norm,
        updated[0],
        moments_new[0],
        updated[1],
        moments_new[1],
        updated[2],
        moments_new[2],
        updated[3],
        moments_new[3],
        ada_new,
        ada_one,
        ada_two,
        patch_new,
        patch_one,
        patch_two,
        vec_new,
        vec_one,
        vec_two,
    )


def solution(mesh):
    groups, line = mesh.shape["dp"], mesh.shape["seq"]
    inner = Mesh(mesh.devices.reshape(groups // 4, 2, 2, line), ALL)
    split = P(ALL, None)
    copied = P()
    placed = (split, split, P(ALL), P(ALL)) + (split,) * 11 + (copied,) * 6
    return jax.shard_map(
        body,
        mesh=inner,
        in_specs=placed,
        out_specs=(copied, copied) + (split,) * 11 + (copied,) * 6,
        check_vma=False,
    )
```

```python
from functools import partial
import math

import jax
import jax.numpy as jnp
import numpy as np
from jax import lax
from jax.experimental import pallas as pl
from jax.experimental.pallas import tpu as pltpu
from jax.sharding import Mesh, PartitionSpec as P

HEADS = 16
NS_ITERS = 2
STEP = 10
ALL = ("a", "x", "c", "z")

highest = lax.Precision.HIGHEST
coef_one = 3.4445
coef_two = -4.775
coef_three = 2.0315
low_type = jnp.bfloat16
wide = jnp.float32
NT = (((1,), (1,)), ((), ()))
TN = (((0,), (0,)), ((), ()))
MIB = 1 << 20


def dot_nt(left, right):
    return lax.dot_general(left, right, NT, preferred_element_type=wide)


def dot_tn(left, right):
    return lax.dot_general(left, right, TN, preferred_element_type=wide)


def dot_nn(left, right):
    return jnp.dot(left, right, preferred_element_type=wide)


def layer_stats(value):
    mean = jnp.mean(value, axis=-1, keepdims=True)
    centred = value - mean
    rstd = lax.rsqrt(jnp.mean(centred * centred, axis=-1, keepdims=True) + 1e-06)
    return (centred * rstd, rstd)


def layer_back(normed, rstd, upstream):
    return rstd * (
        upstream
        - jnp.mean(upstream, axis=-1, keepdims=True)
        - normed * jnp.mean(upstream * normed, axis=-1, keepdims=True)
    )


def level_features(levels, width):
    half = width // 2
    freqs = jnp.exp(-math.log(10000.0) * jnp.arange(half, dtype=jnp.float32) / half)
    angle = levels.astype(jnp.float32)[:, None] * freqs[None, :]
    return jnp.concatenate([jnp.sin(angle), jnp.cos(angle)], axis=-1)


def adamw(weight, first, second, grad, rate):
    first = 0.9 * first + 0.1 * grad
    second = 0.95 * second + 0.05 * grad * grad
    first_hat = first / (1.0 - 0.9**STEP)
    second_hat = second / (1.0 - 0.95**STEP)
    weight = weight - rate * (first_hat / (jnp.sqrt(second_hat) + 1e-08) + 0.01 * weight)
    return (weight, first, second)


def rope_tables(head_dim, heads, frame_tok):
    sec_time = head_dim // 4
    sec_space = (head_dim - sec_time) // 2
    side = math.isqrt(frame_tok)
    spot = np.arange(frame_tok)
    firsts, seconds, time_freq, space = [], [], [], []
    offset = 0
    for kind, size in ((0, sec_time), (1, sec_space), (2, sec_space)):
        half = size // 2
        freqs = np.exp(-math.log(10000.0) * np.arange(half, dtype=np.float64) * 2.0 / size)
        firsts += list(range(offset, offset + half))
        seconds += list(range(offset + half, offset + size))
        offset += size
        where = {0: np.zeros(frame_tok), 1: spot // side, 2: spot % side}[kind]
        space.append(where[:, None] * freqs[None, :])
        time_freq.append(freqs if kind == 0 else np.zeros(half))
    is_time = np.concatenate([np.ones(sec_time // 2), np.zeros(sec_space)])
    space = np.concatenate(space, axis=1)
    space_cos = np.where(is_time[None] > 0, 0.0, np.cos(space))
    space_sin = np.where(is_time[None] > 0, 0.0, np.sin(space))
    time_freq = np.concatenate(time_freq)
    order = np.concatenate(
        [
            np.concatenate([np.asarray(part) + h * head_dim for h in range(heads)])
            for part in (firsts, seconds)
        ]
    )
    total = heads * head_dim
    select = np.zeros((total, total), np.float32)
    select[np.arange(total), order] = 1.0
    tile = lambda t: np.tile(t, (1, heads)).astype(np.float32)
    return (
        tile(space_cos),
        tile(space_sin),
        np.tile(time_freq, heads).astype(np.float32),
        np.tile(is_time, heads).astype(np.float32),
        select,
    )


def split_mask(shape, axis, heads, half_lanes, value):
    lane = lax.broadcasted_iota(jnp.int32, shape, axis)
    if half_lanes is not None:
        lane = lane % half_lanes
        return lane // (half_lanes // heads) == value
    return lane // (shape[axis] // heads) == value


def split_two(value):
    high = value.astype(low_type)
    return high, (value - high.astype(wide)).astype(low_type)


def split_three(value):
    high = value.astype(low_type)
    rest = value - high.astype(wide)
    middle = rest.astype(low_type)
    return high, middle, (rest - middle.astype(wide)).astype(low_type)


def pack_left(value):
    high, middle, least = split_three(value)
    return jnp.concatenate([high, high, middle, high, middle, least], axis=0)


def pack_right(value):
    high, middle, least = split_three(value)
    return jnp.concatenate([high, middle, high, least, middle, high], axis=0)


def thin_product(thin, tall):
    t_high, t_low = split_two(thin)
    high, low = split_two(tall)
    rows = thin.shape[0]
    both = dot_nn(jnp.concatenate([t_high, t_low], axis=0), high)
    return both[:rows] + both[rows:] + dot_nn(t_high, low)


def line_rows(scrs, refs, me_ref, layout, places):
    other = jnp.bitwise_and(jnp.bitwise_xor(pl.program_id(0), me_ref[0]), 1)

    def fill(parts):
        for zz in range(4):
            apart = jnp.bitwise_xor(me_ref[1], zz)
            for scr, pieces in zip(scrs, layout):
                at = zz * (scr.shape[0] // 4)
                for part, begin, rows in pieces:
                    ref, (dim_one, dim_zero) = parts[part], places[part]
                    index = [0] * (len(ref.shape) - 2)
                    index[dim_one] = lax.shift_right_logical(apart, 1)
                    index[dim_zero] = jnp.bitwise_and(apart, 1)
                    scr[at : at + rows, :] = ref[tuple(index) + (slice(begin, begin + rows),)]
                    at += rows

    @pl.when(other == 0)
    def _():
        fill(refs[0::2])

    @pl.when(other == 1)
    def _():
        fill(refs[1::2])


def part_layout(rows_up, rows_out):
    size = (2 * rows_up + rows_out) // 3
    layout, at = [], 0
    for rows in (rows_up, rows_up, rows_out):
        pieces = []
        while rows:
            count = min(rows, size - at % size)
            pieces.append((at // size, at % size, count))
            at, rows = at + count, rows - count
        layout.append(pieces)
    return layout


def once(shape):
    return pl.BlockSpec(shape, lambda *_: (0,) * len(shape), pipeline_mode=pl.Buffered(1))


def embed_qkv_kernel(
    noisy_ref, pw_ref, bias_ref, mod_ref, w_ref, sel_ref, cs_ref, sn_ref, tc_ref, ts_ref,
    q_ref, k_ref, v_ref, wq_scr, pw_scr, *, width, local, scale,
):
    @pl.when(pl.program_id(0) == 0)
    def _():
        pw_scr[...] = pack_right(pw_ref[...])
        for part in range(2):
            rows = pl.ds(part * local, local)
            wq_scr[rows, :] = dot_nn(sel_ref[...], w_ref[rows, :]).astype(low_type)
        rows = pl.ds(2 * local, local)
        wq_scr[rows, :] = w_ref[rows, :]

    state = dot_tn(pack_left(noisy_ref[0]), pw_scr[...]) + bias_ref[...]
    normed, _ = layer_stats(state)
    shift = mod_ref[0, :, 0:width]
    scl = mod_ref[0, :, width : 2 * width]
    h_low = (normed * (1.0 + scl) + shift).astype(low_type)
    out = dot_nt(h_low, wq_scr[...])
    cosine = cs_ref[...] + tc_ref[0]
    sine = sn_ref[...] + ts_ref[0]
    half = local // 2
    for part, ref, mult in ((0, q_ref, scale), (1, k_ref, 1.0)):
        first = out[:, part * local : part * local + half]
        second = out[:, part * local + half : (part + 1) * local]
        ref[:, 0:half] = ((first * cosine - second * sine).astype(low_type).astype(wide) * mult).astype(low_type)
        ref[:, half:local] = ((second * cosine + first * sine).astype(low_type).astype(wide) * mult).astype(low_type)
    v_ref[...] = out[:, 2 * local : 3 * local].astype(low_type)


def embed_qkv(noisy_t, pw, bias, mod, w_local, tables, tcos, tsin, scale):
    frames, patch, ftok = noisy_t.shape
    width = pw.shape[1]
    local = w_local.shape[0] // 3
    cs, sn, _, _, sel = tables
    tokens = frames * ftok
    full = lambda shape: pl.BlockSpec(shape, lambda i: (0,) * len(shape))
    row = lambda cols: pl.BlockSpec((ftok, cols), lambda i: (i, 0))
    return pl.pallas_call(
        partial(embed_qkv_kernel, width=width, local=local, scale=scale),
        grid=(frames,),
        in_specs=[
            pl.BlockSpec((1, patch, ftok), lambda i: (i, 0, 0)),
            full(pw.shape),
            full((1, width)),
            pl.BlockSpec((1, 1, 6 * width), lambda i: (i, 0, 0)),
            full(w_local.shape),
            full(sel.shape),
            full(cs.shape),
            full(sn.shape),
            pl.BlockSpec((1, 1, local // 2), lambda i: (i, 0, 0)),
            pl.BlockSpec((1, 1, local // 2), lambda i: (i, 0, 0)),
        ],
        out_specs=[row(local), row(local), row(local)],
        out_shape=[
            jax.ShapeDtypeStruct((tokens, local), low_type),
            jax.ShapeDtypeStruct((tokens, local), low_type),
            jax.ShapeDtypeStruct((tokens, local), low_type),
        ],
        scratch_shapes=[
            pltpu.VMEM(w_local.shape, low_type),
            pltpu.VMEM((6 * patch, width), low_type),
        ],
        compiler_params=pltpu.CompilerParams(
            dimension_semantics=("arbitrary",), vmem_limit_bytes=24 * MIB
        ),
        cost_estimate=pl.CostEstimate(
            flops=2 * tokens * width * 3 * local, bytes_accessed=12 * MIB, transcendentals=0
        ),
        name="embed_qkv",
    )(noisy_t, pw, bias, mod, w_local, sel, cs, sn, tcos, tsin)


def attend_kernel(
    st_ref, q_ref, k_ref, v_ref, o_ref, ol_ref, lse_ref, vt_scr, even, odd, *, heads, ftok
):
    i = pl.program_id(0)
    local = q_ref.shape[1]
    hd = local // heads

    @pl.when(i == 0)
    def _():
        for f in range(vt_scr.shape[0]):
            vt_scr[f] = v_ref[f * ftok : (f + 1) * ftok, :].T

    first = st_ref[i]
    query = q_ref[...]
    zero = jnp.zeros_like(query)
    masked = [
        jnp.where(split_mask(query.shape, 1, heads, local // 2, h), query, zero)
        for h in range(heads)
    ]

    def key_rows(j):
        return k_ref[pl.ds(pl.multiple_of(j * ftok, ftok), ftok), :]

    def step(j, here, following, there, carry):
        vt = vt_scr[j]
        key = None if following is None else key_rows(following)
        new, probs, stats = [], [], []

        def attended(g):
            top, total, shrink = stats[g]
            acc = carry[g][2] * shrink + dot_nn(vt[g * hd : (g + 1) * hd, :], probs[g])
            new.append((top, total, acc))

        for h in range(heads):
            if key is not None:
                there[h] = dot_nt(key, masked[h])
            top, total, _ = carry[h]
            s = here[h]
            peak = jnp.max(jnp.max(s.reshape(ftok // 8, 8, ftok), axis=0), axis=0, keepdims=True)
            higher = jnp.maximum(top, peak)
            p = jnp.exp(s - higher)
            shrink = jnp.exp(top - higher)
            total = total * shrink + jnp.sum(p.reshape(ftok // 8, 8, ftok), axis=0)
            probs.append(p.astype(low_type))
            stats.append((higher, total, shrink))
            if h > 0:
                attended(h - 1)
        attended(heads - 1)
        return tuple(new)

    count = i + 1 - first
    key = key_rows(first)
    for h in range(heads):
        even[h] = dot_nt(key, masked[h])

    def pair(t, carry):
        j = first + 2 * t
        carry = step(j, even, j + 1, odd, carry)
        return step(j + 1, odd, jnp.minimum(j + 2, i), even, carry)

    start = tuple(
        (
            jnp.full((1, ftok), -1e30, wide),
            jnp.zeros((8, ftok), wide),
            jnp.zeros((hd, ftok), wide),
        )
        for _ in range(heads)
    )
    carry = lax.fori_loop(0, lax.div(count, 2), pair, start)
    carry = lax.cond(
        lax.rem(count, 2) == 1, lambda c: step(i, even, None, None, c), lambda c: c, carry
    )
    outs, logs = [], []
    for top, total, acc in carry:
        total = jnp.sum(total, axis=0, keepdims=True)
        outs.append(acc * (1.0 / total))
        logs.append(top + jnp.log(total))
    out = jnp.concatenate(outs, axis=0)
    o_ref[0] = out
    ol_ref[...] = out.astype(low_type).T
    lse_ref[0] = jnp.concatenate(logs + [jnp.zeros((8 - heads, ftok), wide)], axis=0)


def attend(starts, q, k, v, frames, heads):
    tokens, local = q.shape
    ftok = tokens // frames
    row = lambda: pl.BlockSpec((ftok, local), lambda i, s: (i, 0))
    return pl.pallas_call(
        partial(attend_kernel, heads=heads, ftok=ftok),
        grid_spec=pltpu.PrefetchScalarGridSpec(
            num_scalar_prefetch=1,
            grid=(frames,),
            in_specs=[row(), once(k.shape), once(v.shape)],
            out_specs=[
                pl.BlockSpec((1, local, ftok), lambda i, s: (i, 0, 0)),
                row(),
                pl.BlockSpec((1, 8, ftok), lambda i, s: (i, 0, 0)),
            ],
            scratch_shapes=[
                pltpu.VMEM((frames, local, ftok), low_type),
                pltpu.VMEM((heads, ftok, ftok), wide),
                pltpu.VMEM((heads, ftok, ftok), wide),
            ],
        ),
        out_shape=[
            jax.ShapeDtypeStruct((frames, local, ftok), wide),
            jax.ShapeDtypeStruct((tokens, local), low_type),
            jax.ShapeDtypeStruct((frames, 8, ftok), wide),
        ],
        compiler_params=pltpu.CompilerParams(
            dimension_semantics=("arbitrary",), vmem_limit_bytes=24 * MIB
        ),
        cost_estimate=pl.CostEstimate(
            flops=40_000_000_000, bytes_accessed=12 * MIB, transcendentals=0
        ),
        name="attend",
    )(starts, q, k, v)


def attend_back_kernel(
    st_ref, q_ref, do_ref, o_ref, lse_ref, k_ref, v_ref, *rest, heads, ftok, scale, begin, last
):
    if begin:
        _, dk_in, dv_in, *rest = rest
    dq_ref, dk_ref, dv_ref, kt_scr, dk_scr, dv_scr, dqt_scr, *slots = rest
    step_id = pl.program_id(0)
    steps = pl.num_programs(0)
    i = step_id + begin
    local = q_ref.shape[1]
    hd = local // heads
    hh = hd // 2
    half = local // 2

    @pl.when(step_id == 0)
    def _():
        for f in range(last):
            kt_scr[f] = k_ref[f * ftok : (f + 1) * ftok, :].T
        if begin:
            dk_scr[...] = dk_in[...]
            dv_scr[...] = dv_in[...]
        else:
            dk_scr[...] = jnp.zeros_like(dk_scr)
            dv_scr[...] = jnp.zeros_like(dv_scr)

    first = st_ref[i]
    query = q_ref[...]
    grad = do_ref[...]
    zero = jnp.zeros_like(query)
    q_mask = [
        jnp.where(split_mask(query.shape, 1, heads, half, h), query, zero) for h in range(heads)
    ]
    g_mask = [
        jnp.where(split_mask(query.shape, 1, heads, None, h), grad, zero) for h in range(heads)
    ]
    prod = grad.T.astype(wide) * o_ref[0]
    delta = [
        jnp.sum(prod[h * hd : (h + 1) * hd, :], axis=0, keepdims=True) for h in range(heads)
    ]
    lse = [lse_ref[0, h : h + 1, :] for h in range(heads)]
    dqt_scr[...] = jnp.zeros_like(dqt_scr)

    def rows(j):
        return pl.ds(pl.multiple_of(j * ftok, ftok), ftok)

    def front(h, key, val, slot):
        s_ref, p_ref = slot
        s_ref[h] = dot_nt(key, q_mask[h])
        p_ref[h] = dot_nt(val, g_mask[h])

    def step(j, here, following, there):
        kt = kt_scr[j]
        if following is not None:
            key, val = k_ref[rows(following), :], v_ref[rows(following), :]
        s_ref, p_ref = here
        probs, d_scores = [], []

        def sums(g):
            kt_g = jnp.concatenate(
                [kt[g * hh : (g + 1) * hh, :], kt[half + g * hh : half + (g + 1) * hh, :]], axis=0
            )
            dqt_scr[g] += dot_nn(kt_g, d_scores[g])
            dv_scr[rows(j), :] += dot_nn(probs[g], g_mask[g])
            dk_scr[rows(j), :] += dot_nn(d_scores[g], q_mask[g])

        for h in range(heads):
            if following is not None:
                front(h, key, val, there)
            p = jnp.exp(s_ref[h] - lse[h])
            d_scores.append((p * (p_ref[h] - delta[h])).astype(low_type))
            probs.append(p.astype(low_type))
            if h > 0:
                sums(h - 1)
        sums(heads - 1)

    even, odd = slots[:2], slots[2:]
    count = i + 1 - first
    key, val = k_ref[rows(first), :], v_ref[rows(first), :]
    for h in range(heads):
        front(h, key, val, even)

    def pair(t, carry):
        j = first + 2 * t
        step(j, even, j + 1, odd)
        step(j + 1, odd, jnp.minimum(j + 2, i), even)
        return carry

    lax.fori_loop(0, lax.div(count, 2), pair, 0)

    @pl.when(lax.rem(count, 2) == 1)
    def _():
        step(i, even, None, None)

    dqt = jnp.concatenate(
        [dqt_scr[h, 0:hh, :] for h in range(heads)] + [dqt_scr[h, hh:hd, :] for h in range(heads)],
        axis=0,
    )
    dq_ref[...] = (dqt * scale).astype(low_type).T

    @pl.when(step_id == steps - 1)
    def _():
        dk_ref[...] = dk_scr[...].astype(dk_ref.dtype)
        dv_ref[...] = dv_scr[...].astype(dv_ref.dtype)


def attend_back(starts, q, grad, out, lse, k, v, sums, begin, last, frames, heads, scale):
    tokens, local = q.shape
    ftok = tokens // frames
    row = lambda cols: pl.BlockSpec((ftok, cols), lambda i, s: (i + begin, 0))
    kind = low_type if last == frames else wide
    return pl.pallas_call(
        partial(attend_back_kernel, heads=heads, ftok=ftok, scale=scale, begin=begin, last=last),
        grid_spec=pltpu.PrefetchScalarGridSpec(
            num_scalar_prefetch=1,
            grid=(last - begin,),
            in_specs=[
                row(local), row(local),
                pl.BlockSpec((1, local, ftok), lambda i, s: (i + begin, 0, 0)),
                pl.BlockSpec((1, 8, ftok), lambda i, s: (i + begin, 0, 0)),
                once(k.shape), once(v.shape),
            ] + ([pl.BlockSpec(memory_space=pl.ANY)] + [once(k.shape)] * 2)[: len(sums)],
            out_specs=[row(local), once(k.shape), once(v.shape)],
            scratch_shapes=[
                pltpu.VMEM((frames, local, ftok), low_type),
                pltpu.VMEM((tokens, local), wide),
                pltpu.VMEM((tokens, local), wide),
                pltpu.VMEM((heads, local // heads, ftok), wide),
            ] + [pltpu.VMEM((heads, ftok, ftok), wide)] * 4,
        ),
        out_shape=[
            jax.ShapeDtypeStruct((tokens, local), low_type),
            jax.ShapeDtypeStruct((tokens, local), kind),
            jax.ShapeDtypeStruct((tokens, local), kind),
        ],
        input_output_aliases={7: 0} if sums else {},
        compiler_params=pltpu.CompilerParams(
            dimension_semantics=("arbitrary",), vmem_limit_bytes=36 * MIB
        ),
        cost_estimate=pl.CostEstimate(
            flops=30_000_000_000, bytes_accessed=16 * MIB, transcendentals=0
        ),
        name="attend_back",
    )(starts, q, grad, out, lse, k, v, *sums)


def post_attend_kernel(
    me_ref, fr_ref, noisy_ref, pw_ref, bias_ref, mod_ref, two_a, two_b, st_ref, br_ref, h_ref,
    full_ref, *, width, maps, skip,
):
    local = fr_ref.shape[2]

    @pl.when(pl.program_id(0) == 0)
    def _():
        rows_out = width // (2 * len(maps))
        for two_ref, other in ((two_a, 0), (two_b, 4)):
            for pos, apart in enumerate(maps):
                dev = jnp.bitwise_xor(me_ref[0], apart + other)
                full_ref[pl.ds(pl.multiple_of(dev * rows_out, rows_out), rows_out), :] = two_ref[
                    pos, skip:, :
                ]

    out_full = full_ref[...]
    state = dot_tn(pack_left(noisy_ref[0]), pack_right(pw_ref[...])) + bias_ref[...]
    branch = dot_nt(fr_ref[0], out_full[:, 0:local])
    for m in range(1, fr_ref.shape[0]):
        branch += dot_nt(fr_ref[m], out_full[:, m * local : (m + 1) * local])
    state = state + mod_ref[0, :, 2 * width : 3 * width] * branch
    normed, _ = layer_stats(state)
    st_ref[...] = state
    br_ref[...] = branch
    h_ref[...] = (
        normed * (1.0 + mod_ref[0, :, 4 * width : 5 * width])
        + mod_ref[0, :, 3 * width : 4 * width]
    ).astype(low_type)


def post_attend(me, framed, noisy_t, pw, bias, mod, part_two, order_two, skip):
    members, tokens, local = framed.shape
    frames, patch, ftok = noisy_t.shape
    width = pw.shape[1]
    part_two = [p.reshape((-1,) + p.shape[-2:]) for p in part_two]
    row = lambda: pl.BlockSpec((ftok, width), lambda i, me: (i, 0))
    return pl.pallas_call(
        partial(post_attend_kernel, width=width, maps=tile_places(order_two), skip=skip),
        grid_spec=pltpu.PrefetchScalarGridSpec(
            num_scalar_prefetch=1,
            grid=(frames,),
            in_specs=[
                pl.BlockSpec((members, ftok, local), lambda i, me: (0, i, 0)),
                pl.BlockSpec((1, patch, ftok), lambda i, me: (i, 0, 0)),
                once(pw.shape),
                once((1, width)),
                pl.BlockSpec((1, 1, 6 * width), lambda i, me: (i, 0, 0)),
            ] + [once(p.shape) for p in part_two],
            out_specs=[row(), row(), row(), once((width, width))],
        ),
        out_shape=[
            jax.ShapeDtypeStruct((tokens, width), wide),
            jax.ShapeDtypeStruct((tokens, width), wide),
            jax.ShapeDtypeStruct((tokens, width), low_type),
            jax.ShapeDtypeStruct((width, width), low_type),
        ],
        compiler_params=pltpu.CompilerParams(
            dimension_semantics=("arbitrary",), vmem_limit_bytes=24 * MIB
        ),
        cost_estimate=pl.CostEstimate(
            flops=2 * tokens * width * width, bytes_accessed=12 * MIB, transcendentals=0
        ),
        name="post_attend",
    )(me, framed, noisy_t, pw, bias, mod, *part_two)


def part_specs(me_block, orders, shapes):
    bits = sorted((n for n in orders[0] if n[0] == "a"), reverse=True) + ["x", "c"]
    specs = []
    for order, shape in zip(orders, shapes):

        def place(n, me, order=order):
            apart = me_block(n, me)
            index = []
            for name in order:
                if name[0] == "z":
                    index.append(0)
                else:
                    index.append(
                        jnp.bitwise_and(
                            lax.shift_right_logical(apart, len(bits) - 1 - bits.index(name)), 1
                        )
                    )
            return tuple(index) + (0, 0)

        block = tuple(2 if n[0] == "z" else 1 for n in order) + shape[-2:]
        specs += [pl.BlockSpec(block, place)] * 2
    return specs


def line_apart(n, me):
    return jnp.bitwise_xor(n, me[0])


def gelu_parts(value):
    k = math.sqrt(2.0 / math.pi)
    square = value * value
    t = jnp.tanh(k * value * (1.0 + 0.044715 * square))
    half = 0.5 * (1.0 + t)
    slope = half + (0.5 * k) * value * (1.0 - t * t) * (1.0 + (3 * 0.044715) * square)
    return value * half, slope


def ff_kernel(
    me_ref, h_ref, st_ref, mod_ref, one_a, one_b, two_a, two_b, three_a, three_b, gain_ref, pw_ref,
    act_ref, slope_ref, mixed_ref, pred_ref, acc_scr, up_scr, down_scr,
    *, width, frames, ftok, layout, places,
):
    n = pl.program_id(0)
    line_rows(
        (up_scr, down_scr), (one_a, one_b, two_a, two_b, three_a, three_b), me_ref, layout, places
    )
    @pl.when(n == 0)
    def _():
        acc_scr[...] = jnp.zeros_like(acc_scr)

    spots = [slice(f * ftok, (f + 1) * ftok) for f in range(frames)]
    hidden = [None] * frames
    acts = [None] * frames

    def activate(f):
        act, slope = gelu_parts(hidden[f])
        acts[f] = act.astype(low_type)
        act_ref[spots[f], :] = acts[f]
        slope_ref[spots[f], :] = slope.astype(low_type)

    for f in range(frames + 2):
        if f < frames:
            hidden[f] = dot_nt(h_ref[spots[f], :], up_scr[...])
        if 0 < f <= frames:
            activate(f - 1)
        if f > 1:
            acc_scr[spots[f - 2], :] += dot_nn(acts[f - 2], down_scr[...])

    @pl.when(n == pl.num_programs(0) - 1)
    def _():
        patch = pw_ref.shape[0]
        head, rest = split_two(pw_ref[...])
        both = jnp.concatenate([head, rest], axis=0)
        for f in range(frames):
            at = slice(f * ftok, (f + 1) * ftok)
            mixed = acc_scr[at, :]
            mixed_ref[at, :] = mixed
            normed, _ = layer_stats(st_ref[at, :] + mod_ref[f, :, 5 * width : 6 * width] * mixed)
            f_high, f_low = split_two(normed * gain_ref[...])
            two = dot_nt(f_high, both)
            one = dot_nt(f_low, head)
            pred_ref[f] = (two[:, :patch] + two[:, patch:] + one).T


def ff_forward(me, h_two, state_one, mod, parts, orders, layout, gain, pw_out, ftok):
    tokens, width = h_two.shape
    steps = 1 << (len(orders[0]) - 1)
    chunk = 4 * sum(rows for _, _, rows in layout[0])
    frames = tokens // ftok
    patch = pw_out.shape[0]
    columns = lambda: pl.BlockSpec((tokens, chunk), lambda n, me: (0, n))
    return pl.pallas_call(
        partial(
            ff_kernel, width=width, frames=frames, ftok=ftok, layout=layout[:2],
            places=[(o.index("z1"), o.index("z0")) for o in orders],
        ),
        grid_spec=pltpu.PrefetchScalarGridSpec(
            num_scalar_prefetch=1,
            grid=(steps,),
            in_specs=[once(h_two.shape), once(state_one.shape), once(mod.shape)]
            + part_specs(line_apart, orders, [p[0].shape for p in parts])
            + [once(gain.shape), once(pw_out.shape)],
            out_specs=[columns(), columns(), once((tokens, width)), once((frames, patch, ftok))],
            scratch_shapes=[
                pltpu.VMEM((tokens, width), wide),
                pltpu.VMEM((chunk, width), low_type),
                pltpu.VMEM((chunk, width), low_type),
            ],
        ),
        out_shape=[
            jax.ShapeDtypeStruct((tokens, chunk * steps), low_type),
            jax.ShapeDtypeStruct((tokens, chunk * steps), low_type),
            jax.ShapeDtypeStruct((tokens, width), wide),
            jax.ShapeDtypeStruct((frames, patch, ftok), wide),
        ],
        compiler_params=pltpu.CompilerParams(
            dimension_semantics=("arbitrary",), vmem_limit_bytes=40 * MIB
        ),
        cost_estimate=pl.CostEstimate(
            flops=4 * tokens * width * chunk * steps, bytes_accessed=40 * MIB, transcendentals=0
        ),
        name="ff_forward",
    )(me, h_two, state_one, mod, *parts[0], *parts[1], *parts[2], gain, pw_out)


def ff_back_kernel(
    me_ref, dp_ref, st_ref, mixed_ref, br_ref, mod_ref, noisy_ref, gain_ref, pw_ref, one_a,
    one_b, two_a, two_b, three_a, three_b, out_ref, slope_ref, dh_ref, dm_ref, db_ref, df_ref,
    small_ref, sums_ref, dmod_ref, ds_scr, acc_scr, up_scr, down_scr,
    *, width, frames, ftok, layout, places,
):
    n = pl.program_id(0)
    line_rows(
        (up_scr, down_scr), (one_a, one_b, two_a, two_b, three_a, three_b), me_ref, layout, places
    )
    patch = pw_ref.shape[0]

    def fold(value):
        return jnp.sum(value.reshape(-1, 8, width), axis=0).sum(axis=0, keepdims=True)

    @pl.when(n == 0)
    def _():
        d_head = jnp.zeros((patch, width), wide)
        d_gain = jnp.zeros((1, width), wide)
        right = pack_right(pw_ref[...])
        for f in range(frames):
            at = slice(f * ftok, (f + 1) * ftok)
            gate = mod_ref[f, :, 5 * width : 6 * width]
            mixed = mixed_ref[at, :]
            normed, rstd = layer_stats(st_ref[at, :] + gate * mixed)
            d_pred = dp_ref[f]
            d_final = dot_tn(pack_left(d_pred), right)
            d_head += thin_product(d_pred, normed * gain_ref[...])
            d_gain += fold(d_final * normed)
            d_state = layer_back(normed, rstd, d_final * gain_ref[...])
            ds_scr[at, :] = d_state
            dmod_ref[f, 3:4, :] = fold(d_state * mixed)
            dm_ref[at, :] = (d_state * gate).astype(low_type)
        small_ref[0] = d_head
        sums_ref[0:1, :] = d_gain

    d_act = dot_nt(dm_ref[...], down_scr[...])
    d_hidden = (d_act * slope_ref[...].astype(wide)).astype(low_type)
    dh_ref[...] = d_hidden
    part = dot_nn(d_hidden, up_scr[...])

    @pl.when(n == 0)
    def _():
        acc_scr[...] = part

    @pl.when(n > 0)
    def _():
        acc_scr[...] += part

    @pl.when(n == pl.num_programs(0) - 1)
    def _():
        out_full = out_ref[...]
        d_embed = jnp.zeros((patch, width), wide)
        d_bias = jnp.zeros((1, width), wide)
        local = df_ref.shape[2]
        for f in range(frames):
            at = slice(f * ftok, (f + 1) * ftok)
            normed, rstd = layer_stats(st_ref[at, :])
            d_h = acc_scr[at, :]
            dmod_ref[f, 1:2, :] = fold(d_h)
            dmod_ref[f, 2:3, :] = fold(d_h * normed)
            d_state = ds_scr[at, :] + layer_back(
                normed, rstd, d_h * (1.0 + mod_ref[f, :, 4 * width : 5 * width])
            )
            dmod_ref[f, 0:1, :] = fold(d_state * br_ref[at, :])
            d_branch = (d_state * mod_ref[f, :, 2 * width : 3 * width]).astype(low_type)
            db_ref[at, :] = d_branch
            d_framed = dot_nn(d_branch, out_full).astype(low_type)
            for m in range(df_ref.shape[0]):
                df_ref[m, at, :] = d_framed[:, m * local : (m + 1) * local]
            d_embed += thin_product(noisy_ref[f], d_state)
            d_bias += fold(d_state)
        small_ref[1] = d_embed
        sums_ref[1:2, :] = d_bias


def ff_backward(
    me, d_pred, state_one, mixed, branch, mod, noisy_t, gain, pw_out, parts, orders, layout,
    out_full, slope, members,
):
    tokens, width = state_one.shape
    steps = 1 << (len(orders[0]) - 1)
    chunk = 4 * sum(rows for _, _, rows in layout[0])
    frames, patch, ftok = noisy_t.shape
    local = width // members
    columns = lambda: pl.BlockSpec((tokens, chunk), lambda n, me: (0, n))
    return pl.pallas_call(
        partial(
            ff_back_kernel, width=width, frames=frames, ftok=ftok, layout=layout[:2],
            places=[(o.index("z1"), o.index("z0")) for o in orders],
        ),
        grid_spec=pltpu.PrefetchScalarGridSpec(
            num_scalar_prefetch=1,
            grid=(steps,),
            in_specs=[
                once(d_pred.shape),
                once(state_one.shape),
                once(state_one.shape),
                once(state_one.shape),
                once(mod.shape),
                once(noisy_t.shape),
                once(gain.shape),
                once(pw_out.shape),
            ]
            + part_specs(line_apart, orders, [p[0].shape for p in parts])
            + [once(out_full.shape), columns()],
            out_specs=[
                columns(),
                once((tokens, width)),
                once((tokens, width)),
                once((members, tokens, local)),
                once((2, patch, width)),
                once((2, width)),
                once((frames, 4, width)),
            ],
            scratch_shapes=[
                pltpu.VMEM((tokens, width), wide),
                pltpu.VMEM((tokens, width), wide),
                pltpu.VMEM((chunk, width), low_type),
                pltpu.VMEM((chunk, width), low_type),
            ],
        ),
        out_shape=[
            jax.ShapeDtypeStruct((tokens, chunk * steps), low_type),
            jax.ShapeDtypeStruct((tokens, width), low_type),
            jax.ShapeDtypeStruct((tokens, width), low_type),
            jax.ShapeDtypeStruct((members, tokens, local), low_type),
            jax.ShapeDtypeStruct((2, patch, width), wide),
            jax.ShapeDtypeStruct((2, width), wide),
            jax.ShapeDtypeStruct((frames, 4, width), wide),
        ],
        compiler_params=pltpu.CompilerParams(
            dimension_semantics=("arbitrary",), vmem_limit_bytes=50 * MIB
        ),
        cost_estimate=pl.CostEstimate(
            flops=4 * tokens * width * chunk * steps, bytes_accessed=40 * MIB, transcendentals=0
        ),
        name="ff_backward",
    )(
        me, d_pred, state_one, mixed, branch, mod, noisy_t, gain, pw_out, *parts[0], *parts[1],
        *parts[2], out_full, slope,
    )


def wide_grads_kernel(
    me_ref, dh_ref, act_ref, db_ref, h_ref, dm_ref, fr_ref, *outs, spans, places, narrow, half
):
    *outs, scr = outs
    adds, outs = outs[: len(outs) - len(spans)], outs[len(outs) - len(spans) :]
    up = dot_tn(dh_ref[...], h_ref[...])
    down = dot_tn(act_ref[...], dm_ref[...])
    left = db_ref[...]
    out = jnp.concatenate([dot_tn(left, fr_ref[m]) for m in range(fr_ref.shape[0])], axis=1)
    if narrow < left.shape[1]:
        scr[...] = out
        block = jnp.bitwise_xor(me_ref[0], 2 * pl.program_id(0) + half)
        at = lax.rem(block, left.shape[1] // narrow) * narrow
        out = scr[pl.ds(pl.multiple_of(at, narrow), narrow), :]
    my_z = me_ref[1]
    for zz in range(4):
        pieces = [
            arr[zz * (arr.shape[0] // 4) : (zz + 1) * (arr.shape[0] // 4)] for arr in (up, down, out)
        ]
        whole = jnp.concatenate(pieces, axis=0)
        apart = jnp.bitwise_xor(my_z, zz)
        for k, (ref, (begin, end), (dim_one, dim_zero)) in enumerate(zip(outs, spans, places)):
            index = [0] * (len(ref.shape) - 2)
            index[dim_one] = lax.shift_right_logical(apart, 1)
            index[dim_zero] = jnp.bitwise_and(apart, 1)
            part = whole[begin:end]
            if adds:
                part = part + adds[k][tuple(index)].astype(wide)
            ref[tuple(index)] = part.astype(ref.dtype)


def wide_grads(me, half, d_hidden, act, d_branch, h_two, d_mixed, framed, orders, devices, adds=()):
    tokens, width = h_two.shape
    members, _, local = framed.shape
    chunk = act.shape[1] // (devices // 4)
    out_chunk = width // (devices // 4)
    out_wide = max(out_chunk, 128)
    bits = sorted((n for n in orders[0] if n[0] == "a"), reverse=True) + ["x"]
    rows_dev = (2 * chunk + out_chunk) // 4
    part_rows = rows_dev // 3
    spans = [(k * part_rows, (k + 1) * part_rows) for k in range(3)]

    def block(q, me):
        return jnp.bitwise_xor(me[0], 2 * q + half)

    def out_spec(order):
        def place(q, me):
            index = []
            for name in order:
                if name[0] in "ax":
                    index.append(
                        jnp.bitwise_and(
                            lax.shift_right_logical(q, len(bits) - 1 - bits.index(name)), 1
                        )
                    )
                else:
                    index.append(0)
            return tuple(index) + (0, 0)

        shape = tuple(1 if n[0] in "ax" else 2 for n in order) + (part_rows, width)
        return pl.BlockSpec(shape, place)

    return pl.pallas_call(
        partial(
            wide_grads_kernel,
            spans=spans,
            places=[(o.index("z1"), o.index("z0")) for o in orders],
            narrow=out_chunk,
            half=half,
        ),
        grid_spec=pltpu.PrefetchScalarGridSpec(
            num_scalar_prefetch=1,
            grid=(devices // 8,),
            in_specs=[
                pl.BlockSpec((tokens, chunk), lambda q, me: (0, block(q, me))),
                pl.BlockSpec((tokens, chunk), lambda q, me: (0, block(q, me))),
                pl.BlockSpec(
                    (tokens, out_wide),
                    lambda q, me: (0, lax.div(block(q, me), out_wide // out_chunk)),
                ),
                once(h_two.shape),
                once(d_mixed.shape),
                once(framed.shape),
            ] + [out_spec(o) for o in orders][: len(adds)],
            out_specs=[out_spec(o) for o in orders],
            scratch_shapes=[pltpu.VMEM((out_wide, width), wide)],
        ),
        out_shape=[
            jax.ShapeDtypeStruct((2,) * len(o) + (part_rows, width), low_type) for o in orders
        ],
        compiler_params=pltpu.CompilerParams(
            dimension_semantics=("arbitrary",), vmem_limit_bytes=36 * MIB
        ),
        cost_estimate=pl.CostEstimate(
            flops=2 * tokens * width * (2 * chunk + out_chunk) * (devices // 8),
            bytes_accessed=24 * MIB, transcendentals=0,
        ),
        name="wide_grads",
    )(me, d_hidden, act, d_branch, h_two, d_mixed, framed, *adds)


def qkv_back_kernel(
    me_ref, dq_ref, dk_ref, dv_ref, noisy_ref, pw_ref, bias_ref, mod_ref, w_ref, sel_ref,
    cs_ref, sn_ref, tc_ref, ts_ref, dw_one, dw_two, dmod_ref, demb_ref, dbias_ref,
    acc_scr, emb_scr, bias_scr, pw_scr, *, width, local, maps,
):
    i = pl.program_id(0)

    @pl.when(i == 0)
    def _():
        pw_scr[...] = pack_right(pw_ref[...])
        acc_scr[...] = jnp.zeros_like(acc_scr)
        emb_scr[...] = jnp.zeros_like(emb_scr)
        bias_scr[...] = jnp.zeros_like(bias_scr)

    cosine = cs_ref[...] + tc_ref[0]
    sine = sn_ref[...] + ts_ref[0]
    half = local // 2
    parts = []
    for ref in (dq_ref, dk_ref):
        first = ref[:, 0:half].astype(wide)
        second = ref[:, half:local].astype(wide)
        turned = jnp.concatenate(
            [first * cosine + second * sine, second * cosine - first * sine], axis=1
        ).astype(low_type)
        parts.append(dot_nn(turned, sel_ref[...]).astype(low_type))
    parts.append(dv_ref[...])
    d_qkv = jnp.concatenate(parts, axis=1)
    d_h = dot_nn(d_qkv, w_ref[...])
    noisy = noisy_ref[0]
    state = dot_tn(pack_left(noisy), pw_scr[...]) + bias_ref[...]
    normed, rstd = layer_stats(state)
    scl = mod_ref[0, :, width : 2 * width]
    h_low = (normed * (1.0 + scl) + mod_ref[0, :, 0:width]).astype(low_type)
    acc_scr[...] += dot_tn(d_qkv, h_low)
    dmod_ref[0, :, 0:width] = jnp.sum(d_h, axis=0, keepdims=True)
    dmod_ref[0, :, width : 2 * width] = jnp.sum(d_h * normed, axis=0, keepdims=True)
    d_state = layer_back(normed, rstd, d_h * (1.0 + scl))
    emb_scr[...] += thin_product(noisy, d_state)
    bias_scr[...] += jnp.sum(d_state.reshape(-1, 8, width), axis=0)

    @pl.when(i == pl.num_programs(0) - 1)
    def _():
        rows = acc_scr.shape[0] // len(maps[0])
        at = 0
        for ref, places in ((dw_one, maps[0]), (dw_two, maps[1])):
            count = ref.shape[1]
            for pos, apart in enumerate(places):
                dev = jnp.bitwise_xor(me_ref[0], apart)
                begin = pl.multiple_of(dev * rows + at, 8)
                ref[pos] = acc_scr[pl.ds(begin, count), :].astype(ref.dtype)
            at += count
        demb_ref[...] = emb_scr[...]
        dbias_ref[...] = jnp.sum(bias_scr[...], axis=0, keepdims=True)


def near_places(order):
    natural = sorted((n for n in order if n[0] == "a"), reverse=True) + ["z1", "z0"]
    places = []
    for pos in range(1 << len(order)):
        value = 0
        for d, name in enumerate(order):
            if (pos >> (len(order) - 1 - d)) & 1:
                value |= 1 << (len(natural) - 1 - natural.index(name))
        places.append(value)
    return places


def qkv_back(me, orders, dq, dk, dv, noisy_t, pw, bias, mod, w_local, tables, tcos, tsin):
    frames, patch, ftok = noisy_t.shape
    tokens, local = dq.shape
    width = pw.shape[1]
    cs, sn, _, _, sel = tables
    count = 1 << len(orders[0])
    rows = w_local.shape[0] // count
    first = -(-rows // 16) * 8
    block_one, block_two = (count, first, width), (count, rows - first, width)
    full = lambda shape: pl.BlockSpec(shape, lambda i, me: (0,) * len(shape))
    row = lambda cols: pl.BlockSpec((ftok, cols), lambda i, me: (i, 0))
    return pl.pallas_call(
        partial(
            qkv_back_kernel, width=width, local=local, maps=[near_places(o) for o in orders]
        ),
        grid_spec=pltpu.PrefetchScalarGridSpec(num_scalar_prefetch=1, grid=(frames,),
        in_specs=[
            row(local), row(local), row(local),
            pl.BlockSpec((1, patch, ftok), lambda i, me: (i, 0, 0)),
            full(pw.shape),
            full((1, width)),
            pl.BlockSpec((1, 1, 6 * width), lambda i, me: (i, 0, 0)),
            full(w_local.shape),
            full(sel.shape),
            full(cs.shape),
            full(sn.shape),
            pl.BlockSpec((1, 1, local // 2), lambda i, me: (i, 0, 0)),
            pl.BlockSpec((1, 1, local // 2), lambda i, me: (i, 0, 0)),
        ],
        out_specs=[
            full(block_one), full(block_two),
            pl.BlockSpec((1, 1, 2 * width), lambda i, me: (i, 0, 0)),
            full(pw.shape),
            full((1, width)),
        ],
        scratch_shapes=[
            pltpu.VMEM(w_local.shape, wide),
            pltpu.VMEM(pw.shape, wide),
            pltpu.VMEM((8, width), wide),
            pltpu.VMEM((6 * patch, width), low_type),
        ],
        ),
        out_shape=[
            jax.ShapeDtypeStruct(block_one, low_type),
            jax.ShapeDtypeStruct(block_two, low_type),
            jax.ShapeDtypeStruct((frames, 1, 2 * width), wide),
            jax.ShapeDtypeStruct(pw.shape, wide),
            jax.ShapeDtypeStruct((1, width), wide),
        ],
        compiler_params=pltpu.CompilerParams(
            dimension_semantics=("arbitrary",), vmem_limit_bytes=28 * MIB
        ),
        cost_estimate=pl.CostEstimate(
            flops=2 * 2 * tokens * width * 3 * local, bytes_accessed=16 * MIB, transcendentals=0
        ),
        name="qkv_back",
    )(me, dq, dk, dv, noisy_t, pw, bias, mod, w_local, sel, cs, sn, tcos, tsin)


def tri_blocks(count):
    return [(r, c) for r in range(count) for c in range(r, count)]


def tile_places(order):
    natural = sorted((n for n in order if n[0] == "a"), reverse=True) + ["x", "c", "z1", "z0"]
    places = []
    for pos in range(1 << len(order)):
        value = 0
        for d, name in enumerate(order):
            if (pos >> (len(order) - 1 - d)) & 1:
                value |= 1 << (len(natural) - 1 - natural.index(name))
        places.append(value)
    return places


def gram_kernel(me_ref, u_ref, *refs, blk, cuts, maps):
    outs, scr = refs[:-1], refs[-1]
    mats, _, width = u_ref.shape
    pairs = tri_blocks(width // blk)
    me = me_ref[0]
    clusters = len(maps[0]) // 32
    low = [u_ref[m].astype(low_type) for m in range(mats)]
    for n, (r, c) in enumerate(pairs):
        for m in range(mats):
            scr[m] = dot_tn(low[m][:, r * blk : (r + 1) * blk], low[m][:, c * blk : (c + 1) * blk])
        for m in range(mats // clusters):
            index = m * len(pairs) + n
            for part, ref in enumerate(outs):
                if cuts[part] <= index < cuts[part + 1]:
                    inner = index - cuts[part]
                    for pos, apart in enumerate(maps[part]):
                        which, top, left = tile_of(jnp.bitwise_xor(me, apart), mats // clusters, blk)
                        ref[pos, inner * 16 : (inner + 1) * 16, :] = scr[
                            which + m, pl.ds(pl.multiple_of(top, 16), 16),
                            pl.ds(pl.multiple_of(left, blk // 2), blk // 2),
                        ].astype(ref.dtype)


def tile_of(dev, mats_each, blk):
    return (
        lax.shift_right_logical(dev, 5) * mats_each,
        jnp.bitwise_and(lax.shift_right_logical(dev, 1), 15) * 16,
        jnp.bitwise_and(dev, 1) * (blk // 2),
    )


def gram_parts(me, u, blk, cuts, orders, devices):
    mats, rows, width = u.shape
    maps = [tile_places(o) for o in orders]
    shapes = [(devices, (cuts[k + 1] - cuts[k]) * 16, blk // 2) for k in range(len(orders))]
    return pl.pallas_call(
        partial(gram_kernel, blk=blk, cuts=cuts, maps=maps),
        grid_spec=pltpu.PrefetchScalarGridSpec(
            num_scalar_prefetch=1,
            grid=(1,),
            in_specs=[once(u.shape)],
            out_specs=[once(s) for s in shapes],
            scratch_shapes=[pltpu.VMEM((mats, blk, blk), wide)],
        ),
        out_shape=[jax.ShapeDtypeStruct(s, low_type) for s in shapes],
        compiler_params=pltpu.CompilerParams(
            dimension_semantics=("arbitrary",), vmem_limit_bytes=24 * MIB
        ),
        name="gram_parts",
    )(me, u)


def polish_kernel(me_ref, u_ref, *refs, blk, cuts, maps, factors):
    mats, rows, width = u_ref.shape
    parts, olds, outs, g_scr = refs[: 2 * len(maps)], refs[2 * len(maps) : -mats - 1], refs[-mats - 1 : -1], refs[-1]
    pairs = tri_blocks(width // blk)
    me = me_ref[0]
    clusters = len(maps[0]) // 16
    diag = lax.broadcasted_iota(jnp.int32, (blk, blk), 0) == lax.broadcasted_iota(
        jnp.int32, (blk, blk), 1
    )
    for m in range(mats // clusters):
        for n, (r, c) in enumerate(pairs):
            index = m * len(pairs) + n
            for part, places in enumerate(maps):
                if not cuts[part] <= index < cuts[part + 1]:
                    continue
                inner = index - cuts[part]
                for ref, other in ((parts[2 * part], 0), (parts[2 * part + 1], 4)):
                    for pos, apart in enumerate(places):
                        which, top, left = tile_of(
                            jnp.bitwise_xor(me, apart + other), mats // clusters, blk
                        )
                        g_scr[
                            which + m, pl.ds(pl.multiple_of(r * blk + top, 16), 16),
                            pl.ds(pl.multiple_of(c * blk + left, blk // 2), blk // 2),
                        ] = ref[pos, inner * 16 : (inner + 1) * 16, :]
    for m in range(mats):
        trace = jnp.zeros((1, 1), wide)
        for r, c in pairs:
            piece = g_scr[m, r * blk : (r + 1) * blk, c * blk : (c + 1) * blk]
            if r == c:
                trace += jnp.sum(jnp.where(diag, piece.astype(wide), 0.0), keepdims=True)
            else:
                g_scr[m, c * blk : (c + 1) * blk, r * blk : (r + 1) * blk] = piece.T
        scale = jnp.sqrt(trace) + 1e-07
        inverse = 1.0 / scale
        inverse_sq = inverse * inverse
        own = outs[m].shape[0]

        def times(value):
            return dot_nn(value.astype(low_type), g_scr[m]) * inverse_sq

        def cubic(value):
            once_ = times(value)
            return coef_one * value + coef_two * once_ + coef_three * times(once_)

        current = cubic(u_ref[m, :own, :] * inverse)
        for _ in range(NS_ITERS - 1):
            second = cubic(cubic(times(current)))
            third = cubic(cubic(times(second)))
            current = coef_one * current + coef_two * second + coef_three * third
        outs[m][...] = olds[m][...] * (1.0 - 2.0 * 0.01) - factors[m] * current


def polish(me, u, parts, olds, blk, cuts, orders, factors):
    mats, rows, width = u.shape
    maps = [tile_places(o) for o in orders]
    return pl.pallas_call(
        partial(polish_kernel, blk=blk, cuts=cuts, maps=maps, factors=factors),
        grid_spec=pltpu.PrefetchScalarGridSpec(
            num_scalar_prefetch=1,
            grid=(1,),
            in_specs=[once(u.shape)] + [once(p.shape) for p in parts] + [once(o.shape) for o in olds],
            out_specs=[once(o.shape) for o in olds],
            scratch_shapes=[pltpu.VMEM((mats, width, width), low_type)],
        ),
        out_shape=[jax.ShapeDtypeStruct(o.shape, wide) for o in olds],
        compiler_params=pltpu.CompilerParams(
            dimension_semantics=("arbitrary",), vmem_limit_bytes=32 * MIB
        ),
        cost_estimate=pl.CostEstimate(
            flops=2 * 24 * mats * rows * width * width, bytes_accessed=12 * MIB, transcendentals=0
        ),
        name="polish",
    )(me, u, *parts, *olds)


def bit_stages(count_a):
    stages = {}
    bits_a = count_a.bit_length() - 1
    for b in range(bits_a):
        stages["a%d" % (bits_a - 1 - b)] = ("a", 1 << (bits_a - 1 - b), b)
    stages["x"] = ("x", 1, bits_a)
    stages["c"] = ("c", 1, bits_a + 1)
    stages["z1"] = ("z", 2, bits_a + 2)
    stages["z0"] = ("z", 1, bits_a + 3)
    return stages


def swap(value, axis, distance):
    size = lax.axis_size(axis)
    return lax.ppermute(value, axis, [(i, i ^ distance) for i in range(size)])


def bit_of(axis, distance):
    return (lax.axis_index(axis) // distance) % 2


def in_order(blocks, names):
    for dim, name in enumerate(names):
        axis = name[0]
        distance = {"z1": 2, "a1": 2, "a2": 4}.get(name, 1)
        mine = bit_of(axis, distance)
        flipped = jnp.flip(blocks, dim)
        blocks = jnp.where(mine == 0, blocks, flipped)
    natural = sorted(n for n in names if n[0] == "a")[::-1] + [
        n for n in ("x", "c", "z1", "z0") if n in names
    ]
    order = [names.index(n) for n in natural] + list(range(len(names), blocks.ndim))
    return blocks.transpose(order)


def three_orders(stages):
    names_a = [n for n in stages if n.startswith("a")]
    return (
        ["x"] + names_a + ["z0", "z1"],
        names_a + ["z0", "x", "z1"],
        ["z0", "x"] + names_a + ["z1"],
    )


def after(value, *others):
    return lax.optimization_barrier((value,) + others)[0]


def halve(blocks, order, stages):
    keep, send = blocks[0], blocks[1]
    for step, name in enumerate(order):
        axis, distance, _ = stages[name]
        got = swap(send.astype(low_type), axis, distance)
        if step == len(order) - 1:
            return keep.astype(wide) + got.astype(wide)
        send = (keep[1].astype(wide) + got[1].astype(wide)).astype(low_type)
        keep = keep[0].astype(wide) + got[0].astype(wide)


class Ladder:
    def __init__(self, blocks, orders, stages):
        self.orders, self.stages, self.rung = orders, stages, 0
        self.keep = [b[0] for b in blocks]
        self.send = [b[1] for b in blocks]

    def exchange(self):
        self.got = []
        for order, send in zip(self.orders, self.send):
            axis, distance, _ = self.stages[order[self.rung]]
            self.got.append(swap(send.astype(low_type), axis, distance))
        self.rung += 1

    def add(self, *first):
        got = lax.optimization_barrier(tuple(self.got) + first)[: len(self.got)]
        pairs = list(zip(self.keep, got))
        if self.rung == len(self.orders[0]):
            return [k.astype(wide) + g.astype(wide) for k, g in pairs]
        self.send = [(k[1].astype(wide) + g[1].astype(wide)).astype(low_type) for k, g in pairs]
        self.keep = [k[0].astype(wide) + g[0].astype(wide) for k, g in pairs]


def double(block, order, stages):
    for name in order:
        axis, distance, _ = stages[name]
        block = jnp.stack([block, swap(block, axis, distance)])
    return block


def spread(payload):
    count = math.prod(lax.axis_size(n) for n in ALL)
    return lax.all_to_all(
        jnp.broadcast_to(payload[None], (count,) + payload.shape),
        ALL, split_axis=0, concat_axis=0, tiled=True,
    )


def unit_plan(devices):
    quarter = devices // 4
    edges = []
    for unit in range(3 * devices):
        section, place = unit // devices, unit % devices
        member, rest = place // quarter, place % quarter
        index = section * quarter + rest
        pos, slot = index // 3, index % 3
        a, z = pos // 4, pos % 4
        dest = ((a * 2 + member // 2) * 2 + member % 2) * 4 + z
        edges.append((unit // 3, unit % 3, dest, slot))
    left = list(edges)
    colors = []
    for _ in range(3):
        match = {}

        def augment(src, seen):
            for e in left:
                if e[0] != src or e[2] in seen:
                    continue
                seen.add(e[2])
                if e[2] not in match or augment(match[e[2]][0], seen):
                    match[e[2]] = e
                    return True
            return False

        for src in range(devices):
            assert augment(src, set())
        chosen = list(match.values())
        for e in chosen:
            left.remove(e)
        colors.append(chosen)
    return colors


def send_units(units, plan, back):
    devices = len(plan[0])
    here = lax.axis_index(ALL)
    src_key, dst_key = ((2, 3), (0, 1)) if back else ((0, 1), (2, 3))
    got = []
    for chosen in plan:
        table = np.zeros(devices, np.int32)
        for e in chosen:
            table[e[src_key[0]]] = e[src_key[1]]
        slot = jnp.asarray(table)[here]
        piece = lax.dynamic_index_in_dim(units, slot, 0, keepdims=False)
        got.append(lax.ppermute(piece, ALL, [(e[src_key[0]], e[dst_key[0]]) for e in chosen]))
    place = np.zeros((devices, 3), np.int32)
    for color, chosen in enumerate(plan):
        for e in chosen:
            place[e[dst_key[0]], e[dst_key[1]]] = color
    where_from = jnp.asarray(place)[here]
    out = []
    for slot in range(3):
        pick = where_from[slot]
        out.append(jnp.where(pick == 0, got[0], jnp.where(pick == 1, got[1], got[2])))
    return jnp.stack(out)


def body(
    noisy_latents,
    target_latents,
    noise_levels,
    clip_start,
    qkv_weight,
    qkv_moment,
    out_weight,
    out_moment,
    up_weight,
    up_moment,
    down_weight,
    down_moment,
    ada_weight,
    ada_first,
    ada_second,
    patch_weight,
    patch_first,
    patch_second,
    vectors,
    vec_first,
    vec_second,
):
    count_a = lax.axis_size("a")
    members = lax.axis_size("x") * lax.axis_size("c")
    devices = count_a * members * lax.axis_size("z")
    groups = count_a * lax.axis_size("z")
    frames_dev = noise_levels.shape[0]
    tokens_dev = noisy_latents.shape[0]
    frame_tok = tokens_dev // frames_dev
    width = patch_weight.shape[2]
    patch_size = patch_weight.shape[1]
    head_dim = width // HEADS
    local_heads = HEADS // members
    local = local_heads * head_dim
    group_frames = frames_dev * members
    frames_all = frames_dev * devices
    group_tokens = group_frames * frame_tok
    score_scale = 1.0 / math.sqrt(head_dim)
    stages = bit_stages(count_a)
    my_a, my_z = lax.axis_index("a"), lax.axis_index("z")
    my_group = my_a * 4 + my_z
    my_member = lax.axis_index("x") * 2 + lax.axis_index("c")
    tables = rope_tables(head_dim, local_heads, frame_tok)
    tables = tables[:4] + (jnp.asarray(tables[4], low_type),)
    plan = unit_plan(devices)

    rows_unit = qkv_weight.shape[0] // 3
    units = send_units(qkv_weight.astype(low_type).reshape(3, rows_unit, width), plan, False)
    names_a = [n for n in stages if n.startswith("a")]

    swap_axes = ("x", "c", "z")
    moves = [(g * 4 + z, z * 4 + g) for g in range(4) for z in range(4)]
    noisy_t = noisy_latents.T.reshape(patch_size, frames_dev, frame_tok).transpose(1, 0, 2)
    target_t = target_latents.T.reshape(patch_size, frames_dev, frame_tok).transpose(1, 0, 2)
    mine = lax.ppermute(jnp.stack([noisy_t, target_t]), swap_axes, moves)

    meta = jnp.concatenate([noise_levels, clip_start]).astype(wide)
    meta = jnp.pad(meta, (0, 128 - meta.shape[0]))[None]
    meta_all = spread(after(meta, units))[:, 0]
    rows_up, rows_out = up_weight.shape[0], out_weight.shape[0]
    layout = part_layout(rows_up, rows_out)
    rising = [
        ["z1", "z0"] + names_a[::-1] + ["x"],
        ["z1", "x", "z0"] + names_a[::-1],
        ["z1"] + names_a[::-1] + ["x", "z0"],
    ]
    gather_orders = [o[::-1] for o in rising]
    rows_part = (2 * rows_up + rows_out) // 3
    bulk = jnp.concatenate([up_weight, down_weight, out_weight], axis=0).astype(low_type)
    shares = [bulk[n * rows_part : (n + 1) * rows_part] for n in range(3)]
    climb = lambda shares, rung: [
        double(share, [order[rung]], stages) for share, order in zip(shares, rising)
    ]
    far = double(units, ["z1"], stages)
    meta_all, far, mine = lax.optimization_barrier((meta_all, far, mine))
    shares = climb([after(share, far) for share in shares], 0)
    levels_all = meta_all[:, :frames_dev].reshape(frames_all)
    starts_all = meta_all[:, frames_dev : 2 * frames_dev].reshape(frames_all)
    starts_group = lax.dynamic_slice_in_dim(starts_all, my_group * group_frames, group_frames)
    starts_int = starts_group.astype(jnp.int32)
    noisy_mine, target_mine = mine[0], mine[1]
    pair = double(noisy_mine, ["c"], stages)

    half_one = double(far[:, :, : rows_unit // 2], ["z0"], stages)
    half_two = double(far[:, :, rows_unit // 2 :], names_a[::-1], stages)
    cond_low = jax.nn.silu(level_features(levels_all, width)).astype(low_type)
    ada_rows = ada_weight.shape[0]
    mod_rows = dot_nt(cond_low, ada_weight.astype(low_type))
    mod_rows, half_one, half_two, pair = lax.optimization_barrier(
        (mod_rows, half_one, half_two, pair)
    )
    mod_out = jnp.broadcast_to(
        mod_rows.reshape(count_a, 1, 4, group_frames, ada_rows),
        (count_a, members, 4, group_frames, ada_rows),
    ).reshape(devices, group_frames, ada_rows)
    mod_in = lax.all_to_all(
        mod_out.astype(low_type), ALL, split_axis=0, concat_axis=0, tiled=True
    ).astype(wide)
    noisy_group = in_order(double(pair, ["x"], stages), ["x", "c"]).reshape(
        group_frames, patch_size, frame_tok
    )
    half_one = double(half_one, names_a[::-1], stages)
    half_two = double(half_two, ["z0"], stages)
    mod_in, half_one, half_two, noisy_group, *shares = lax.optimization_barrier(
        (mod_in, half_one, half_two, noisy_group, *shares)
    )
    shares = climb(shares, 1)
    half_one = in_order(half_one, names_a + ["z0", "z1"])
    half_two = in_order(half_two, ["z0"] + names_a + ["z1"])
    qkv_local = jnp.concatenate(
        [half_one.reshape(3 * groups, -1, width), half_two.reshape(3 * groups, -1, width)], axis=1
    ).reshape(3 * local, width)
    modul = mod_in.transpose(1, 0, 2).reshape(group_frames, 6 * width) + vectors[2:8].reshape(
        1, 6 * width
    )
    mod3 = modul.reshape(group_frames, 1, 6 * width)
    *shares, mod3 = lax.optimization_barrier((*shares, mod3))
    shares = climb(shares, 2)
    mod_mine = lax.dynamic_slice_in_dim(mod3, my_member * frames_dev, frames_dev)

    frame_ids = jnp.arange(group_frames, dtype=jnp.int32)
    time_pos = (frame_ids - starts_int).astype(wide)
    t_angle = time_pos[:, None] * tables[2][None, :]
    tcos = (jnp.cos(t_angle) * tables[3][None, :])[:, None, :]
    tsin = (jnp.sin(t_angle) * tables[3][None, :])[:, None, :]

    pw_in = patch_weight[0]
    bias_in = vectors[0:1]
    q, k, v = embed_qkv(
        noisy_group, pw_in, bias_in, mod3, qkv_local, tables, tcos, tsin, score_scale
    )
    me = lax.axis_index(ALL).astype(jnp.int32)
    place = jnp.stack([me // 4, me % 4])
    *shares, q = lax.optimization_barrier((*shares, q))
    for rung in range(3, len(rising[0])):
        shares = climb(shares, rung)
    att, att_low, lse = attend(starts_int, q, k, v, group_frames, local_heads)
    *shares, att_low = lax.optimization_barrier((*shares, att_low))
    shares = [(share, swap(share, "c", 1)) for share in shares]
    framed = lax.all_to_all(
        att_low.reshape(members, tokens_dev, local), ("x", "c"), split_axis=0, concat_axis=0,
        tiled=True,
    )

    gain = vectors[1:2]
    pw_out = patch_weight[1]
    state_one, branch, h_two, out_full = post_attend(
        me[None], framed, noisy_mine, pw_in, bias_in, mod_mine, shares[2], gather_orders[2],
        layout[2][0][1],
    )
    act, slope, mixed, pred = ff_forward(
        place, h_two, state_one, mod_mine, shares, gather_orders, layout, gain, pw_out, frame_tok,
    )
    member_axes = ("x", "c")
    ahead = [(i, i + 1) for i in range(members - 1)]
    behind = [(i + 1, i) for i in range(members - 1)]
    edge = lax.ppermute(
        jnp.stack([pred[-1], target_mine[-1]]).astype(low_type), member_axes, ahead
    ).astype(wide)
    prev_pred = jnp.concatenate([edge[0:1], pred[:-1]], axis=0)
    prev_goal = jnp.concatenate([edge[1:2], target_mine[:-1]], axis=0)
    diff = pred - prev_pred - (target_mine - prev_goal)
    my_frames = my_member * frames_dev + jnp.arange(frames_dev, dtype=jnp.int32)
    valid = my_frames > lax.dynamic_slice_in_dim(starts_int, my_member * frames_dev, frames_dev)
    loss_local = jnp.sum(jnp.where(valid[:, None, None], diff * diff, 0.0))
    entry_count = float(frames_all * frame_tok * patch_size)
    d_diff = jnp.where(valid[:, None, None], (2.0 / entry_count) * diff, 0.0)
    returned = lax.ppermute(d_diff[0], member_axes, behind)
    d_pred = d_diff - jnp.concatenate([d_diff[1:], returned[None]], axis=0)
    d_hidden, d_mixed, d_branch, d_framed, d_small, d_sums, d_mod_rest = ff_backward(
        place, d_pred, state_one, mixed, branch, mod_mine, noisy_mine, gain, pw_out, shares,
        gather_orders, layout, out_full, slope, members,
    )
    d_att = lax.all_to_all(d_framed, ("x", "c"), split_axis=0, concat_axis=0, tiled=True).reshape(
        group_tokens, local
    )

    orders = three_orders(stages)
    grads_of = lambda half, adds=(): wide_grads(
        place, half, d_hidden, act, d_branch, h_two, d_mixed, framed, orders, devices, adds
    )
    others = grads_of(1)
    core_axis, core_distance, _ = stages["c"]
    passed = [swap(o, core_axis, core_distance) for o in others]

    cuts = [group_frames * n // 12 for n in (0, 5, 9, 11, 12)]

    def part_back(n, q, sums):
        return attend_back(
            starts_int, q, d_att, att, lse, k, v, sums, cuts[n], cuts[n + 1], group_frames,
            local_heads, score_scale,
        )

    dq, dk, dv = part_back(0, after(q, *others), ())
    adds = lax.optimization_barrier(tuple(passed) + (dk,))[:3]
    ladder = Ladder(grads_of(0, adds), orders, stages)
    ladder.exchange()
    dq, dk, dv = part_back(1, after(q, *ladder.send), (dq, dk, dv))
    ladder.add(dk)
    ladder.exchange()
    dq, dk, dv = part_back(2, after(q, *ladder.send), (dq, dk, dv))
    ladder.add(dk)
    ladder.exchange()
    dq, dk, dv = part_back(3, after(q, *ladder.send), (dq, dk, dv))
    ladder.add(dk)
    ladder.exchange()
    near_orders = [names_a + ["z0", "z1"], ["z0"] + names_a + ["z1"]]
    dw_one, dw_two, d_mod_one, d_embed, d_bias = qkv_back(
        (my_a * 4 + my_z).astype(jnp.int32)[None], near_orders, dq, after(dk, *ladder.send), dv, noisy_group, pw_in, bias_in, mod3, qkv_local,
        tables, tcos, tsin,
    )
    while ladder.rung < len(orders[0]):
        ladder.add()
        ladder.exchange()
    near_dims = (2,) * len(near_orders[0])
    near = Ladder(
        [d.reshape(near_dims + d.shape[1:]) for d in (dw_one, dw_two)], near_orders, stages
    )
    near.exchange()
    ladder.got = list(lax.optimization_barrier(tuple(ladder.got) + (d_bias,)))[:3]
    g_wide = jnp.concatenate(ladder.add(), axis=0)
    g_up, g_down, g_out = (
        g_wide[:rows_up], g_wide[rows_up : 2 * rows_up], g_wide[2 * rows_up :]
    )
    d_rest = lax.dynamic_update_slice_in_dim(
        jnp.zeros((group_frames, 4 * width), wide),
        d_mod_rest.reshape(frames_dev, 4 * width), my_member * frames_dev, 0,
    )
    d_mod = jnp.concatenate([d_mod_one[:, 0], d_rest], axis=1)
    d_mod = d_mod.reshape(group_frames, devices, ada_rows).transpose(1, 0, 2)
    smalls = jnp.concatenate(
        [d_embed + d_small[1], d_small[0], d_bias + d_sums[1:2], d_sums[0:1]], axis=0
    )
    small_rows = smalls.shape[0]
    small_part = small_rows * width // devices
    mod_part = group_frames * ada_rows
    packed = jnp.concatenate(
        [d_mod.reshape(devices, mod_part), smalls.reshape(devices, small_part)], axis=1
    )
    pad = -packed.shape[1] % 128
    packed = jnp.pad(packed, ((0, 0), (0, pad))).reshape(devices, -1, 128)
    packed = after(packed, *ladder.got)
    arrived = lax.all_to_all(packed, ALL, split_axis=0, concat_axis=0, tiled=True).reshape(
        devices, -1
    )
    while near.rung < len(near_orders[0]):
        near.add()
        near.exchange()
    g_one, g_two = near.add()
    g_units = jnp.concatenate([g_one, g_two], axis=0).reshape(3, rows_unit, width)
    g_qkv = send_units(g_units, plan, True).reshape(3 * rows_unit, width)
    small_mine = jnp.sum(arrived[:, mod_part : mod_part + small_part], axis=0)
    mod_grad = (
        arrived[:, :mod_part]
        .reshape(count_a, members, 4, group_frames, ada_rows)
        .sum(axis=1)
        .reshape(frames_all, ada_rows)
    )
    bias_mine = jnp.sum(mod_grad, axis=0)
    g_ada = dot_tn(mod_grad.astype(low_type), cond_low)

    shards = (g_qkv, g_out, g_up, g_down)
    local_sq = (
        sum((jnp.sum(piece * piece) for piece in (g_units,) + shards[1:]))
        + jnp.sum(g_ada * g_ada)
        + jnp.sum(small_mine * small_mine)
        + jnp.sum(bias_mine * bias_mine)
    )
    totals = jnp.where(lax.broadcasted_iota(jnp.int32, (1, 128), 1) == 0, local_sq, loss_local)
    for name in ["c", "x"] + names_a + ["z0", "z1"]:
        axis, distance, _ = stages[name]
        totals = totals + swap(totals, axis, distance)
    norm = jnp.sqrt(totals[0, 0])
    loss_total = totals[0, 1]
    report = jnp.concatenate([small_mine, bias_mine])
    report = jnp.pad(report, (0, -report.shape[0] % 128)).reshape(-1, 128)
    report = after(report, norm)
    clip = jnp.minimum(1.0, 0.01 / norm)

    olds = (qkv_weight, out_weight, up_weight, down_weight)
    moments = (qkv_moment, out_moment, up_moment, down_moment)
    moments_new = [0.95 * moments[j] + clip * shards[j] for j in range(4)]
    most = max(m.shape[0] for m in olds)
    steers = jnp.stack(
        [
            jnp.pad(
                clip * shards[j] + 0.95 * moments_new[j], ((0, most - olds[j].shape[0]), (0, 0))
            )
            for j in range(4)
        ]
    )
    ada_new, ada_one, ada_two = adamw(ada_weight, ada_first, ada_second, clip * g_ada, 0.08)
    blk = 256
    gram_orders = [["c"] + o for o in orders[:2]]
    pairs = len(tri_blocks(width // blk)) * 4 // (devices // 32)
    cuts = (0, pairs // 2, pairs)
    parts = []
    report_order = ["z1", "z0"] + names_a[::-1] + ["x", "c"]
    ladders = []
    for k, part in enumerate(gram_parts(me[None], steers, blk, cuts, gram_orders, devices)):
        ladders.append(Ladder([part.reshape((2,) * len(stages) + part.shape[1:])], [gram_orders[k]], stages))
    for rung in range(len(stages)):
        for ladder in ladders:
            ladder.exchange()
        report = double(after(report, ladders[0].got[0]), [report_order[rung]], stages)
        ties = []
        if rung == 2:
            ties = [ada_new, ada_one, ada_two]
        results = []
        for ladder in ladders:
            got, *ties = lax.optimization_barrier((ladder.got[0], *ties))
            ladder.got = [got]
            results.append(ladder.add())
        if rung == 2:
            ada_new, ada_one, ada_two = ties
    everyone = in_order(report, report_order[::-1]).reshape(devices, -1)
    small_all = everyone[:, :small_part].reshape(small_rows, width)
    bias_all = everyone[:, small_part : small_part + ada_rows].reshape(6, width)
    g_patch = small_all[: 2 * patch_size].reshape(2, patch_size, width)
    g_vec = jnp.concatenate([small_all[2 * patch_size :], bias_all], axis=0)
    patch_new, patch_one, patch_two = adamw(
        patch_weight, patch_first, patch_second, clip * g_patch, 0.15
    )
    vec_new, vec_one, vec_two = adamw(vectors, vec_first, vec_second, clip * g_vec, 0.5)
    lines = [result[0].astype(low_type) for result in results]
    late = [patch_new, patch_one, patch_two, vec_new, vec_one, vec_two]
    for rung in range(1, len(stages)):
        lines = [
            double(line, [gram_orders[n][:0:-1][rung - 1]], stages) for n, line in enumerate(lines)
        ]
        if rung == len(stages) - 2:
            lines[0], *late = lax.optimization_barrier((lines[0], *late))
    patch_new, patch_one, patch_two, vec_new, vec_one, vec_two = late
    parts = []
    for line in lines:
        line = line.reshape((-1,) + line.shape[-2:])
        parts += [line, swap(line, "c", 1)]
    factors = [2.0 * math.sqrt(max(1.0, o.shape[0] * devices / width)) for o in olds]
    updated = polish(
        me[None], steers, parts, olds, blk, cuts, [o[1:] for o in gram_orders], factors
    )
    return (
        loss_total,
        norm,
        updated[0],
        moments_new[0],
        updated[1],
        moments_new[1],
        updated[2],
        moments_new[2],
        updated[3],
        moments_new[3],
        ada_new,
        ada_one,
        ada_two,
        patch_new,
        patch_one,
        patch_two,
        vec_new,
        vec_one,
        vec_two,
    )


def solution(mesh):
    groups, line = mesh.shape["dp"], mesh.shape["seq"]
    inner = Mesh(mesh.devices.reshape(groups // 4, 2, 2, line), ALL)
    split = P(ALL, None)
    copied = P()
    placed = (split, split, P(ALL), P(ALL)) + (split,) * 11 + (copied,) * 6
    return jax.shard_map(
        body,
        mesh=inner,
        in_specs=placed,
        out_specs=(copied, copied) + (split,) * 11 + (copied,) * 6,
        check_vma=False,
    )
```

```python
from functools import partial
import math

import jax
import jax.numpy as jnp
import numpy as np
from jax import lax
from jax.experimental import pallas as pl
from jax.experimental.pallas import tpu as pltpu
from jax.sharding import Mesh, PartitionSpec as P

HEADS = 16
NS_ITERS = 2
STEP = 10
ALL = ("a", "x", "c", "z")

highest = lax.Precision.HIGHEST
coef_one = 3.4445
coef_two = -4.775
coef_three = 2.0315
low_type = jnp.bfloat16
wide = jnp.float32
NT = (((1,), (1,)), ((), ()))
TN = (((0,), (0,)), ((), ()))
MIB = 1 << 20


def dot_nt(left, right):
    return lax.dot_general(left, right, NT, preferred_element_type=wide)


def dot_tn(left, right):
    return lax.dot_general(left, right, TN, preferred_element_type=wide)


def dot_nn(left, right):
    return jnp.dot(left, right, preferred_element_type=wide)


def layer_stats(value):
    mean = jnp.mean(value, axis=-1, keepdims=True)
    centred = value - mean
    rstd = lax.rsqrt(jnp.mean(centred * centred, axis=-1, keepdims=True) + 1e-06)
    return (centred * rstd, rstd)


def layer_back(normed, rstd, upstream):
    return rstd * (
        upstream
        - jnp.mean(upstream, axis=-1, keepdims=True)
        - normed * jnp.mean(upstream * normed, axis=-1, keepdims=True)
    )


def level_features(levels, width):
    half = width // 2
    freqs = jnp.exp(-math.log(10000.0) * jnp.arange(half, dtype=jnp.float32) / half)
    angle = levels.astype(jnp.float32)[:, None] * freqs[None, :]
    return jnp.concatenate([jnp.sin(angle), jnp.cos(angle)], axis=-1)


def adamw(weight, first, second, grad, rate):
    first = 0.9 * first + 0.1 * grad
    second = 0.95 * second + 0.05 * grad * grad
    first_hat = first / (1.0 - 0.9**STEP)
    second_hat = second / (1.0 - 0.95**STEP)
    weight = weight - rate * (first_hat / (jnp.sqrt(second_hat) + 1e-08) + 0.01 * weight)
    return (weight, first, second)


def rope_tables(head_dim, heads, frame_tok):
    sec_time = head_dim // 4
    sec_space = (head_dim - sec_time) // 2
    side = math.isqrt(frame_tok)
    spot = np.arange(frame_tok)
    firsts, seconds, time_freq, space = [], [], [], []
    offset = 0
    for kind, size in ((0, sec_time), (1, sec_space), (2, sec_space)):
        half = size // 2
        freqs = np.exp(-math.log(10000.0) * np.arange(half, dtype=np.float64) * 2.0 / size)
        firsts += list(range(offset, offset + half))
        seconds += list(range(offset + half, offset + size))
        offset += size
        where = {0: np.zeros(frame_tok), 1: spot // side, 2: spot % side}[kind]
        space.append(where[:, None] * freqs[None, :])
        time_freq.append(freqs if kind == 0 else np.zeros(half))
    is_time = np.concatenate([np.ones(sec_time // 2), np.zeros(sec_space)])
    space = np.concatenate(space, axis=1)
    space_cos = np.where(is_time[None] > 0, 0.0, np.cos(space))
    space_sin = np.where(is_time[None] > 0, 0.0, np.sin(space))
    time_freq = np.concatenate(time_freq)
    order = np.concatenate(
        [
            np.concatenate([np.asarray(part) + h * head_dim for h in range(heads)])
            for part in (firsts, seconds)
        ]
    )
    total = heads * head_dim
    select = np.zeros((total, total), np.float32)
    select[np.arange(total), order] = 1.0
    tile = lambda t: np.tile(t, (1, heads)).astype(np.float32)
    return (
        tile(space_cos),
        tile(space_sin),
        np.tile(time_freq, heads).astype(np.float32),
        np.tile(is_time, heads).astype(np.float32),
        select,
    )


def split_mask(shape, axis, heads, half_lanes, value):
    lane = lax.broadcasted_iota(jnp.int32, shape, axis)
    if half_lanes is not None:
        lane = lane % half_lanes
        return lane // (half_lanes // heads) == value
    return lane // (shape[axis] // heads) == value


def split_two(value):
    high = value.astype(low_type)
    return high, (value - high.astype(wide)).astype(low_type)


def split_three(value):
    high = value.astype(low_type)
    rest = value - high.astype(wide)
    middle = rest.astype(low_type)
    return high, middle, (rest - middle.astype(wide)).astype(low_type)


def pack_left(value):
    high, middle, least = split_three(value)
    return jnp.concatenate([high, high, middle, high, middle, least], axis=0)


def pack_right(value):
    high, middle, least = split_three(value)
    return jnp.concatenate([high, middle, high, least, middle, high], axis=0)


def thin_product(thin, tall):
    t_high, t_low = split_two(thin)
    high, low = split_two(tall)
    rows = thin.shape[0]
    both = dot_nn(jnp.concatenate([t_high, t_low], axis=0), high)
    return both[:rows] + both[rows:] + dot_nn(t_high, low)


def line_rows(scrs, refs, me_ref, layout, places):
    other = jnp.bitwise_and(jnp.bitwise_xor(pl.program_id(0), me_ref[0]), 1)

    def fill(parts):
        for zz in range(4):
            apart = jnp.bitwise_xor(me_ref[1], zz)
            for scr, pieces in zip(scrs, layout):
                at = zz * (scr.shape[0] // 4)
                for part, begin, rows in pieces:
                    ref, (dim_one, dim_zero) = parts[part], places[part]
                    index = [0] * (len(ref.shape) - 2)
                    index[dim_one] = lax.shift_right_logical(apart, 1)
                    index[dim_zero] = jnp.bitwise_and(apart, 1)
                    scr[at : at + rows, :] = ref[tuple(index) + (slice(begin, begin + rows),)]
                    at += rows

    @pl.when(other == 0)
    def _():
        fill(refs[0::2])

    @pl.when(other == 1)
    def _():
        fill(refs[1::2])


def part_layout(rows_up, rows_out):
    size = (2 * rows_up + rows_out) // 3
    layout, at = [], 0
    for rows in (rows_up, rows_up, rows_out):
        pieces = []
        while rows:
            count = min(rows, size - at % size)
            pieces.append((at // size, at % size, count))
            at, rows = at + count, rows - count
        layout.append(pieces)
    return layout


def once(shape):
    return pl.BlockSpec(shape, lambda *_: (0,) * len(shape), pipeline_mode=pl.Buffered(1))


def embed_qkv_kernel(
    noisy_ref, pw_ref, bias_ref, mod_ref, w_ref, sel_ref, cs_ref, sn_ref, tc_ref, ts_ref,
    q_ref, k_ref, v_ref, wq_scr, pw_scr, *, width, local, scale,
):
    @pl.when(pl.program_id(0) == 0)
    def _():
        pw_scr[...] = pack_right(pw_ref[...])
        for part in range(2):
            rows = pl.ds(part * local, local)
            wq_scr[rows, :] = dot_nn(sel_ref[...], w_ref[rows, :]).astype(low_type)
        rows = pl.ds(2 * local, local)
        wq_scr[rows, :] = w_ref[rows, :]

    state = dot_tn(pack_left(noisy_ref[0]), pw_scr[...]) + bias_ref[...]
    normed, _ = layer_stats(state)
    shift = mod_ref[0, :, 0:width]
    scl = mod_ref[0, :, width : 2 * width]
    h_low = (normed * (1.0 + scl) + shift).astype(low_type)
    out = dot_nt(h_low, wq_scr[...])
    cosine = cs_ref[...] + tc_ref[0]
    sine = sn_ref[...] + ts_ref[0]
    half = local // 2
    for part, ref, mult in ((0, q_ref, scale), (1, k_ref, 1.0)):
        first = out[:, part * local : part * local + half]
        second = out[:, part * local + half : (part + 1) * local]
        ref[:, 0:half] = ((first * cosine - second * sine).astype(low_type).astype(wide) * mult).astype(low_type)
        ref[:, half:local] = ((second * cosine + first * sine).astype(low_type).astype(wide) * mult).astype(low_type)
    v_ref[...] = out[:, 2 * local : 3 * local].astype(low_type)


def embed_qkv(noisy_t, pw, bias, mod, w_local, tables, tcos, tsin, scale):
    frames, patch, ftok = noisy_t.shape
    width = pw.shape[1]
    local = w_local.shape[0] // 3
    cs, sn, _, _, sel = tables
    tokens = frames * ftok
    full = lambda shape: pl.BlockSpec(shape, lambda i: (0,) * len(shape))
    row = lambda cols: pl.BlockSpec((ftok, cols), lambda i: (i, 0))
    return pl.pallas_call(
        partial(embed_qkv_kernel, width=width, local=local, scale=scale),
        grid=(frames,),
        in_specs=[
            pl.BlockSpec((1, patch, ftok), lambda i: (i, 0, 0)),
            full(pw.shape),
            full((1, width)),
            pl.BlockSpec((1, 1, 6 * width), lambda i: (i, 0, 0)),
            full(w_local.shape),
            full(sel.shape),
            full(cs.shape),
            full(sn.shape),
            pl.BlockSpec((1, 1, local // 2), lambda i: (i, 0, 0)),
            pl.BlockSpec((1, 1, local // 2), lambda i: (i, 0, 0)),
        ],
        out_specs=[row(local), row(local), row(local)],
        out_shape=[
            jax.ShapeDtypeStruct((tokens, local), low_type),
            jax.ShapeDtypeStruct((tokens, local), low_type),
            jax.ShapeDtypeStruct((tokens, local), low_type),
        ],
        scratch_shapes=[
            pltpu.VMEM(w_local.shape, low_type),
            pltpu.VMEM((6 * patch, width), low_type),
        ],
        compiler_params=pltpu.CompilerParams(
            dimension_semantics=("arbitrary",), vmem_limit_bytes=16 * MIB
        ),
        cost_estimate=pl.CostEstimate(
            flops=2 * tokens * width * 3 * local, bytes_accessed=12 * MIB, transcendentals=0
        ),
        name="embed_qkv",
    )(noisy_t, pw, bias, mod, w_local, sel, cs, sn, tcos, tsin)


def attend_kernel(
    st_ref, q_ref, k_ref, v_ref, o_ref, ol_ref, lse_ref, vt_scr, even, odd, *, heads, ftok
):
    i = pl.program_id(0)
    local = q_ref.shape[1]
    hd = local // heads

    @pl.when(i == 0)
    def _():
        for f in range(vt_scr.shape[0]):
            vt_scr[f] = v_ref[f * ftok : (f + 1) * ftok, :].T

    first = st_ref[i]
    query = q_ref[...]
    zero = jnp.zeros_like(query)
    masked = [
        jnp.where(split_mask(query.shape, 1, heads, local // 2, h), query, zero)
        for h in range(heads)
    ]

    def key_rows(j):
        return k_ref[pl.ds(pl.multiple_of(j * ftok, ftok), ftok), :]

    def step(j, here, following, there, carry):
        vt = vt_scr[j]
        key = None if following is None else key_rows(following)
        new, probs, stats = [], [], []

        def attended(g):
            top, total, shrink = stats[g]
            acc = carry[g][2] * shrink + dot_nn(vt[g * hd : (g + 1) * hd, :], probs[g])
            new.append((top, total, acc))

        for h in range(heads):
            if key is not None:
                there[h] = dot_nt(key, masked[h])
            top, total, _ = carry[h]
            s = here[h]
            peak = jnp.max(jnp.max(s.reshape(ftok // 8, 8, ftok), axis=0), axis=0, keepdims=True)
            higher = jnp.maximum(top, peak)
            p = jnp.exp(s - higher)
            shrink = jnp.exp(top - higher)
            total = total * shrink + jnp.sum(p.reshape(ftok // 8, 8, ftok), axis=0)
            probs.append(p.astype(low_type))
            stats.append((higher, total, shrink))
            if h > 0:
                attended(h - 1)
        attended(heads - 1)
        return tuple(new)

    count = i + 1 - first
    key = key_rows(first)
    for h in range(heads):
        even[h] = dot_nt(key, masked[h])

    def pair(t, carry):
        j = first + 2 * t
        carry = step(j, even, j + 1, odd, carry)
        return step(j + 1, odd, jnp.minimum(j + 2, i), even, carry)

    start = tuple(
        (
            jnp.full((1, ftok), -1e30, wide),
            jnp.zeros((8, ftok), wide),
            jnp.zeros((hd, ftok), wide),
        )
        for _ in range(heads)
    )
    carry = lax.fori_loop(0, lax.div(count, 2), pair, start)
    carry = lax.cond(
        lax.rem(count, 2) == 1, lambda c: step(i, even, None, None, c), lambda c: c, carry
    )
    outs, logs = [], []
    for top, total, acc in carry:
        total = jnp.sum(total, axis=0, keepdims=True)
        outs.append(acc * (1.0 / total))
        logs.append(top + jnp.log(total))
    out = jnp.concatenate(outs, axis=0)
    o_ref[0] = out
    ol_ref[...] = out.astype(low_type).T
    lse_ref[0] = jnp.concatenate(logs + [jnp.zeros((8 - heads, ftok), wide)], axis=0)


def attend(starts, q, k, v, frames, heads):
    tokens, local = q.shape
    ftok = tokens // frames
    row = lambda: pl.BlockSpec((ftok, local), lambda i, s: (i, 0))
    return pl.pallas_call(
        partial(attend_kernel, heads=heads, ftok=ftok),
        grid_spec=pltpu.PrefetchScalarGridSpec(
            num_scalar_prefetch=1,
            grid=(frames,),
            in_specs=[row(), once(k.shape), once(v.shape)],
            out_specs=[
                pl.BlockSpec((1, local, ftok), lambda i, s: (i, 0, 0)),
                row(),
                pl.BlockSpec((1, 8, ftok), lambda i, s: (i, 0, 0)),
            ],
            scratch_shapes=[
                pltpu.VMEM((frames, local, ftok), low_type),
                pltpu.VMEM((heads, ftok, ftok), wide),
                pltpu.VMEM((heads, ftok, ftok), wide),
            ],
        ),
        out_shape=[
            jax.ShapeDtypeStruct((frames, local, ftok), wide),
            jax.ShapeDtypeStruct((tokens, local), low_type),
            jax.ShapeDtypeStruct((frames, 8, ftok), wide),
        ],
        compiler_params=pltpu.CompilerParams(
            dimension_semantics=("arbitrary",), vmem_limit_bytes=16 * MIB
        ),
        cost_estimate=pl.CostEstimate(
            flops=40_000_000_000, bytes_accessed=12 * MIB, transcendentals=0
        ),
        name="attend",
    )(starts, q, k, v)


def attend_back_kernel(
    st_ref, q_ref, do_ref, o_ref, lse_ref, k_ref, v_ref, *rest, heads, ftok, scale, begin, last
):
    if begin:
        _, dk_in, dv_in, *rest = rest
    dq_ref, dk_ref, dv_ref, kt_scr, dk_scr, dv_scr, dqt_scr, *slots = rest
    step_id = pl.program_id(0)
    steps = pl.num_programs(0)
    i = step_id + begin
    local = q_ref.shape[1]
    hd = local // heads
    hh = hd // 2
    half = local // 2

    @pl.when(step_id == 0)
    def _():
        for f in range(last):
            kt_scr[f] = k_ref[f * ftok : (f + 1) * ftok, :].T
        if begin:
            dk_scr[...] = dk_in[...]
            dv_scr[...] = dv_in[...]
        else:
            dk_scr[...] = jnp.zeros_like(dk_scr)
            dv_scr[...] = jnp.zeros_like(dv_scr)

    first = st_ref[i]
    query = q_ref[...]
    grad = do_ref[...]
    zero = jnp.zeros_like(query)
    q_mask = [
        jnp.where(split_mask(query.shape, 1, heads, half, h), query, zero) for h in range(heads)
    ]
    g_mask = [
        jnp.where(split_mask(query.shape, 1, heads, None, h), grad, zero) for h in range(heads)
    ]
    prod = grad.T.astype(wide) * o_ref[0]
    delta = [
        jnp.sum(prod[h * hd : (h + 1) * hd, :], axis=0, keepdims=True) for h in range(heads)
    ]
    lse = [lse_ref[0, h : h + 1, :] for h in range(heads)]
    dqt_scr[...] = jnp.zeros_like(dqt_scr)

    def rows(j):
        return pl.ds(pl.multiple_of(j * ftok, ftok), ftok)

    def front(h, key, val, slot):
        s_ref, p_ref = slot
        s_ref[h] = dot_nt(key, q_mask[h])
        p_ref[h] = dot_nt(val, g_mask[h])

    def step(j, here, following, there):
        kt = kt_scr[j]
        if following is not None:
            key, val = k_ref[rows(following), :], v_ref[rows(following), :]
        s_ref, p_ref = here
        probs, d_scores = [], []

        def sums(g):
            kt_g = jnp.concatenate(
                [kt[g * hh : (g + 1) * hh, :], kt[half + g * hh : half + (g + 1) * hh, :]], axis=0
            )
            dqt_scr[g] += dot_nn(kt_g, d_scores[g])
            dv_scr[rows(j), :] += dot_nn(probs[g], g_mask[g])
            dk_scr[rows(j), :] += dot_nn(d_scores[g], q_mask[g])

        for h in range(heads):
            if following is not None:
                front(h, key, val, there)
            p = jnp.exp(s_ref[h] - lse[h])
            d_scores.append((p * (p_ref[h] - delta[h])).astype(low_type))
            probs.append(p.astype(low_type))
            if h > 0:
                sums(h - 1)
        sums(heads - 1)

    even, odd = slots[:2], slots[2:]
    count = i + 1 - first
    key, val = k_ref[rows(first), :], v_ref[rows(first), :]
    for h in range(heads):
        front(h, key, val, even)

    def pair(t, carry):
        j = first + 2 * t
        step(j, even, j + 1, odd)
        step(j + 1, odd, jnp.minimum(j + 2, i), even)
        return carry

    lax.fori_loop(0, lax.div(count, 2), pair, 0)

    @pl.when(lax.rem(count, 2) == 1)
    def _():
        step(i, even, None, None)

    dqt = jnp.concatenate(
        [dqt_scr[h, 0:hh, :] for h in range(heads)] + [dqt_scr[h, hh:hd, :] for h in range(heads)],
        axis=0,
    )
    dq_ref[...] = (dqt * scale).astype(low_type).T

    @pl.when(step_id == steps - 1)
    def _():
        dk_ref[...] = dk_scr[...].astype(dk_ref.dtype)
        dv_ref[...] = dv_scr[...].astype(dv_ref.dtype)


def attend_back(starts, q, grad, out, lse, k, v, sums, begin, last, frames, heads, scale):
    tokens, local = q.shape
    ftok = tokens // frames
    row = lambda cols: pl.BlockSpec((ftok, cols), lambda i, s: (i + begin, 0))
    kind = low_type if last == frames else wide
    return pl.pallas_call(
        partial(attend_back_kernel, heads=heads, ftok=ftok, scale=scale, begin=begin, last=last),
        grid_spec=pltpu.PrefetchScalarGridSpec(
            num_scalar_prefetch=1,
            grid=(last - begin,),
            in_specs=[
                row(local), row(local),
                pl.BlockSpec((1, local, ftok), lambda i, s: (i + begin, 0, 0)),
                pl.BlockSpec((1, 8, ftok), lambda i, s: (i + begin, 0, 0)),
                once(k.shape), once(v.shape),
            ] + ([pl.BlockSpec(memory_space=pl.ANY)] + [once(k.shape)] * 2)[: len(sums)],
            out_specs=[row(local), once(k.shape), once(v.shape)],
            scratch_shapes=[
                pltpu.VMEM((frames, local, ftok), low_type),
                pltpu.VMEM((tokens, local), wide),
                pltpu.VMEM((tokens, local), wide),
                pltpu.VMEM((heads, local // heads, ftok), wide),
            ] + [pltpu.VMEM((heads, ftok, ftok), wide)] * 4,
        ),
        out_shape=[
            jax.ShapeDtypeStruct((tokens, local), low_type),
            jax.ShapeDtypeStruct((tokens, local), kind),
            jax.ShapeDtypeStruct((tokens, local), kind),
        ],
        input_output_aliases={7: 0} if sums else {},
        compiler_params=pltpu.CompilerParams(
            dimension_semantics=("arbitrary",), vmem_limit_bytes=44 * MIB
        ),
        cost_estimate=pl.CostEstimate(
            flops=30_000_000_000, bytes_accessed=16 * MIB, transcendentals=0
        ),
        name="attend_back",
    )(starts, q, grad, out, lse, k, v, *sums)


def post_attend_kernel(
    me_ref, fr_ref, noisy_ref, pw_ref, bias_ref, mod_ref, two_a, two_b, st_ref, br_ref, h_ref,
    full_ref, *, width, maps, skip,
):
    local = fr_ref.shape[2]

    @pl.when(pl.program_id(0) == 0)
    def _():
        rows_out = width // (2 * len(maps))
        for two_ref, other in ((two_a, 0), (two_b, 4)):
            for pos, apart in enumerate(maps):
                dev = jnp.bitwise_xor(me_ref[0], apart + other)
                full_ref[pl.ds(pl.multiple_of(dev * rows_out, rows_out), rows_out), :] = two_ref[
                    pos, skip:, :
                ]

    out_full = full_ref[...]
    state = dot_tn(pack_left(noisy_ref[0]), pack_right(pw_ref[...])) + bias_ref[...]
    branch = dot_nt(fr_ref[0], out_full[:, 0:local])
    for m in range(1, fr_ref.shape[0]):
        branch += dot_nt(fr_ref[m], out_full[:, m * local : (m + 1) * local])
    state = state + mod_ref[0, :, 2 * width : 3 * width] * branch
    normed, _ = layer_stats(state)
    st_ref[...] = state
    br_ref[...] = branch
    h_ref[...] = (
        normed * (1.0 + mod_ref[0, :, 4 * width : 5 * width])
        + mod_ref[0, :, 3 * width : 4 * width]
    ).astype(low_type)


def post_attend(me, framed, noisy_t, pw, bias, mod, part_two, order_two, skip):
    members, tokens, local = framed.shape
    frames, patch, ftok = noisy_t.shape
    width = pw.shape[1]
    part_two = [p.reshape((-1,) + p.shape[-2:]) for p in part_two]
    row = lambda: pl.BlockSpec((ftok, width), lambda i, me: (i, 0))
    return pl.pallas_call(
        partial(post_attend_kernel, width=width, maps=tile_places(order_two), skip=skip),
        grid_spec=pltpu.PrefetchScalarGridSpec(
            num_scalar_prefetch=1,
            grid=(frames,),
            in_specs=[
                pl.BlockSpec((members, ftok, local), lambda i, me: (0, i, 0)),
                pl.BlockSpec((1, patch, ftok), lambda i, me: (i, 0, 0)),
                once(pw.shape),
                once((1, width)),
                pl.BlockSpec((1, 1, 6 * width), lambda i, me: (i, 0, 0)),
            ] + [once(p.shape) for p in part_two],
            out_specs=[row(), row(), row(), once((width, width))],
        ),
        out_shape=[
            jax.ShapeDtypeStruct((tokens, width), wide),
            jax.ShapeDtypeStruct((tokens, width), wide),
            jax.ShapeDtypeStruct((tokens, width), low_type),
            jax.ShapeDtypeStruct((width, width), low_type),
        ],
        compiler_params=pltpu.CompilerParams(
            dimension_semantics=("arbitrary",), vmem_limit_bytes=18 * MIB
        ),
        cost_estimate=pl.CostEstimate(
            flops=2 * tokens * width * width, bytes_accessed=12 * MIB, transcendentals=0
        ),
        name="post_attend",
    )(me, framed, noisy_t, pw, bias, mod, *part_two)


def part_specs(me_block, orders, shapes):
    bits = sorted((n for n in orders[0] if n[0] == "a"), reverse=True) + ["x", "c"]
    specs = []
    for order, shape in zip(orders, shapes):

        def place(n, me, order=order):
            apart = me_block(n, me)
            index = []
            for name in order:
                if name[0] == "z":
                    index.append(0)
                else:
                    index.append(
                        jnp.bitwise_and(
                            lax.shift_right_logical(apart, len(bits) - 1 - bits.index(name)), 1
                        )
                    )
            return tuple(index) + (0, 0)

        block = tuple(2 if n[0] == "z" else 1 for n in order) + shape[-2:]
        specs += [pl.BlockSpec(block, place)] * 2
    return specs


def line_apart(n, me):
    return jnp.bitwise_xor(n, me[0])


def gelu_parts(value):
    k = math.sqrt(2.0 / math.pi)
    square = value * value
    t = jnp.tanh(k * value * (1.0 + 0.044715 * square))
    half = 0.5 * (1.0 + t)
    slope = half + (0.5 * k) * value * (1.0 - t * t) * (1.0 + (3 * 0.044715) * square)
    return value * half, slope


def ff_kernel(
    me_ref, h_ref, st_ref, mod_ref, one_a, one_b, two_a, two_b, three_a, three_b, gain_ref, pw_ref,
    act_ref, slope_ref, mixed_ref, pred_ref, acc_scr, up_scr, down_scr,
    *, width, frames, ftok, layout, places,
):
    n = pl.program_id(0)
    line_rows(
        (up_scr, down_scr), (one_a, one_b, two_a, two_b, three_a, three_b), me_ref, layout, places
    )
    @pl.when(n == 0)
    def _():
        acc_scr[...] = jnp.zeros_like(acc_scr)

    spots = [slice(f * ftok, (f + 1) * ftok) for f in range(frames)]
    hidden = [None] * frames
    acts = [None] * frames

    def activate(f):
        act, slope = gelu_parts(hidden[f])
        acts[f] = act.astype(low_type)
        act_ref[spots[f], :] = acts[f]
        slope_ref[spots[f], :] = slope.astype(low_type)

    for f in range(frames + 2):
        if f < frames:
            hidden[f] = dot_nt(h_ref[spots[f], :], up_scr[...])
        if 0 < f <= frames:
            activate(f - 1)
        if f > 1:
            acc_scr[spots[f - 2], :] += dot_nn(acts[f - 2], down_scr[...])

    @pl.when(n == pl.num_programs(0) - 1)
    def _():
        patch = pw_ref.shape[0]
        head, rest = split_two(pw_ref[...])
        both = jnp.concatenate([head, rest], axis=0)
        for f in range(frames):
            at = slice(f * ftok, (f + 1) * ftok)
            mixed = acc_scr[at, :]
            mixed_ref[at, :] = mixed
            normed, _ = layer_stats(st_ref[at, :] + mod_ref[f, :, 5 * width : 6 * width] * mixed)
            f_high, f_low = split_two(normed * gain_ref[...])
            two = dot_nt(f_high, both)
            one = dot_nt(f_low, head)
            pred_ref[f] = (two[:, :patch] + two[:, patch:] + one).T


def ff_forward(me, h_two, state_one, mod, parts, orders, layout, gain, pw_out, ftok):
    tokens, width = h_two.shape
    steps = 1 << (len(orders[0]) - 1)
    chunk = 4 * sum(rows for _, _, rows in layout[0])
    frames = tokens // ftok
    patch = pw_out.shape[0]
    columns = lambda: pl.BlockSpec((tokens, chunk), lambda n, me: (0, n))
    return pl.pallas_call(
        partial(
            ff_kernel, width=width, frames=frames, ftok=ftok, layout=layout[:2],
            places=[(o.index("z1"), o.index("z0")) for o in orders],
        ),
        grid_spec=pltpu.PrefetchScalarGridSpec(
            num_scalar_prefetch=1,
            grid=(steps,),
            in_specs=[once(h_two.shape), once(state_one.shape), once(mod.shape)]
            + part_specs(line_apart, orders, [p[0].shape for p in parts])
            + [once(gain.shape), once(pw_out.shape)],
            out_specs=[columns(), columns(), once((tokens, width)), once((frames, patch, ftok))],
            scratch_shapes=[
                pltpu.VMEM((tokens, width), wide),
                pltpu.VMEM((chunk, width), low_type),
                pltpu.VMEM((chunk, width), low_type),
            ],
        ),
        out_shape=[
            jax.ShapeDtypeStruct((tokens, chunk * steps), low_type),
            jax.ShapeDtypeStruct((tokens, chunk * steps), low_type),
            jax.ShapeDtypeStruct((tokens, width), wide),
            jax.ShapeDtypeStruct((frames, patch, ftok), wide),
        ],
        compiler_params=pltpu.CompilerParams(
            dimension_semantics=("arbitrary",), vmem_limit_bytes=32 * MIB
        ),
        cost_estimate=pl.CostEstimate(
            flops=4 * tokens * width * chunk * steps, bytes_accessed=40 * MIB, transcendentals=0
        ),
        name="ff_forward",
    )(me, h_two, state_one, mod, *parts[0], *parts[1], *parts[2], gain, pw_out)


def ff_back_kernel(
    me_ref, dp_ref, st_ref, mixed_ref, br_ref, mod_ref, noisy_ref, gain_ref, pw_ref, one_a,
    one_b, two_a, two_b, three_a, three_b, out_ref, slope_ref, dh_ref, dm_ref, db_ref, df_ref,
    small_ref, sums_ref, dmod_ref, ds_scr, acc_scr, up_scr, down_scr,
    *, width, frames, ftok, layout, places,
):
    n = pl.program_id(0)
    line_rows(
        (up_scr, down_scr), (one_a, one_b, two_a, two_b, three_a, three_b), me_ref, layout, places
    )
    patch = pw_ref.shape[0]

    def fold(value):
        return jnp.sum(value.reshape(-1, 8, width), axis=0).sum(axis=0, keepdims=True)

    @pl.when(n == 0)
    def _():
        d_head = jnp.zeros((patch, width), wide)
        d_gain = jnp.zeros((1, width), wide)
        right = pack_right(pw_ref[...])
        for f in range(frames):
            at = slice(f * ftok, (f + 1) * ftok)
            gate = mod_ref[f, :, 5 * width : 6 * width]
            mixed = mixed_ref[at, :]
            normed, rstd = layer_stats(st_ref[at, :] + gate * mixed)
            d_pred = dp_ref[f]
            d_final = dot_tn(pack_left(d_pred), right)
            d_head += thin_product(d_pred, normed * gain_ref[...])
            d_gain += fold(d_final * normed)
            d_state = layer_back(normed, rstd, d_final * gain_ref[...])
            ds_scr[at, :] = d_state
            dmod_ref[f, 3:4, :] = fold(d_state * mixed)
            dm_ref[at, :] = (d_state * gate).astype(low_type)
        small_ref[0] = d_head
        sums_ref[0:1, :] = d_gain

    d_act = dot_nt(dm_ref[...], down_scr[...])
    d_hidden = (d_act * slope_ref[...].astype(wide)).astype(low_type)
    dh_ref[...] = d_hidden
    part = dot_nn(d_hidden, up_scr[...])

    @pl.when(n == 0)
    def _():
        acc_scr[...] = part

    @pl.when(n > 0)
    def _():
        acc_scr[...] += part

    @pl.when(n == pl.num_programs(0) - 1)
    def _():
        out_full = out_ref[...]
        d_embed = jnp.zeros((patch, width), wide)
        d_bias = jnp.zeros((1, width), wide)
        local = df_ref.shape[2]
        for f in range(frames):
            at = slice(f * ftok, (f + 1) * ftok)
            normed, rstd = layer_stats(st_ref[at, :])
            d_h = acc_scr[at, :]
            dmod_ref[f, 1:2, :] = fold(d_h)
            dmod_ref[f, 2:3, :] = fold(d_h * normed)
            d_state = ds_scr[at, :] + layer_back(
                normed, rstd, d_h * (1.0 + mod_ref[f, :, 4 * width : 5 * width])
            )
            dmod_ref[f, 0:1, :] = fold(d_state * br_ref[at, :])
            d_branch = (d_state * mod_ref[f, :, 2 * width : 3 * width]).astype(low_type)
            db_ref[at, :] = d_branch
            d_framed = dot_nn(d_branch, out_full).astype(low_type)
            for m in range(df_ref.shape[0]):
                df_ref[m, at, :] = d_framed[:, m * local : (m + 1) * local]
            d_embed += thin_product(noisy_ref[f], d_state)
            d_bias += fold(d_state)
        small_ref[1] = d_embed
        sums_ref[1:2, :] = d_bias


def ff_backward(
    me, d_pred, state_one, mixed, branch, mod, noisy_t, gain, pw_out, parts, orders, layout,
    out_full, slope, members,
):
    tokens, width = state_one.shape
    steps = 1 << (len(orders[0]) - 1)
    chunk = 4 * sum(rows for _, _, rows in layout[0])
    frames, patch, ftok = noisy_t.shape
    local = width // members
    columns = lambda: pl.BlockSpec((tokens, chunk), lambda n, me: (0, n))
    return pl.pallas_call(
        partial(
            ff_back_kernel, width=width, frames=frames, ftok=ftok, layout=layout[:2],
            places=[(o.index("z1"), o.index("z0")) for o in orders],
        ),
        grid_spec=pltpu.PrefetchScalarGridSpec(
            num_scalar_prefetch=1,
            grid=(steps,),
            in_specs=[
                once(d_pred.shape),
                once(state_one.shape),
                once(state_one.shape),
                once(state_one.shape),
                once(mod.shape),
                once(noisy_t.shape),
                once(gain.shape),
                once(pw_out.shape),
            ]
            + part_specs(line_apart, orders, [p[0].shape for p in parts])
            + [once(out_full.shape), columns()],
            out_specs=[
                columns(),
                once((tokens, width)),
                once((tokens, width)),
                once((members, tokens, local)),
                once((2, patch, width)),
                once((2, width)),
                once((frames, 4, width)),
            ],
            scratch_shapes=[
                pltpu.VMEM((tokens, width), wide),
                pltpu.VMEM((tokens, width), wide),
                pltpu.VMEM((chunk, width), low_type),
                pltpu.VMEM((chunk, width), low_type),
            ],
        ),
        out_shape=[
            jax.ShapeDtypeStruct((tokens, chunk * steps), low_type),
            jax.ShapeDtypeStruct((tokens, width), low_type),
            jax.ShapeDtypeStruct((tokens, width), low_type),
            jax.ShapeDtypeStruct((members, tokens, local), low_type),
            jax.ShapeDtypeStruct((2, patch, width), wide),
            jax.ShapeDtypeStruct((2, width), wide),
            jax.ShapeDtypeStruct((frames, 4, width), wide),
        ],
        compiler_params=pltpu.CompilerParams(
            dimension_semantics=("arbitrary",), vmem_limit_bytes=42 * MIB
        ),
        cost_estimate=pl.CostEstimate(
            flops=4 * tokens * width * chunk * steps, bytes_accessed=40 * MIB, transcendentals=0
        ),
        name="ff_backward",
    )(
        me, d_pred, state_one, mixed, branch, mod, noisy_t, gain, pw_out, *parts[0], *parts[1],
        *parts[2], out_full, slope,
    )


def wide_grads_kernel(
    me_ref, dh_ref, act_ref, db_ref, h_ref, dm_ref, fr_ref, *outs, spans, places, narrow, half
):
    *outs, scr = outs
    adds, outs = outs[: len(outs) - len(spans)], outs[len(outs) - len(spans) :]
    up = dot_tn(dh_ref[...], h_ref[...])
    down = dot_tn(act_ref[...], dm_ref[...])
    left = db_ref[...]
    out = jnp.concatenate([dot_tn(left, fr_ref[m]) for m in range(fr_ref.shape[0])], axis=1)
    if narrow < left.shape[1]:
        scr[...] = out
        block = jnp.bitwise_xor(me_ref[0], 2 * pl.program_id(0) + half)
        at = lax.rem(block, left.shape[1] // narrow) * narrow
        out = scr[pl.ds(pl.multiple_of(at, narrow), narrow), :]
    my_z = me_ref[1]
    for zz in range(4):
        pieces = [
            arr[zz * (arr.shape[0] // 4) : (zz + 1) * (arr.shape[0] // 4)] for arr in (up, down, out)
        ]
        whole = jnp.concatenate(pieces, axis=0)
        apart = jnp.bitwise_xor(my_z, zz)
        for k, (ref, (begin, end), (dim_one, dim_zero)) in enumerate(zip(outs, spans, places)):
            index = [0] * (len(ref.shape) - 2)
            index[dim_one] = lax.shift_right_logical(apart, 1)
            index[dim_zero] = jnp.bitwise_and(apart, 1)
            part = whole[begin:end]
            if adds:
                part = part + adds[k][tuple(index)].astype(wide)
            ref[tuple(index)] = part.astype(ref.dtype)


def wide_grads(me, half, d_hidden, act, d_branch, h_two, d_mixed, framed, orders, devices, adds=()):
    tokens, width = h_two.shape
    members, _, local = framed.shape
    chunk = act.shape[1] // (devices // 4)
    out_chunk = width // (devices // 4)
    out_wide = max(out_chunk, 128)
    bits = sorted((n for n in orders[0] if n[0] == "a"), reverse=True) + ["x"]
    rows_dev = (2 * chunk + out_chunk) // 4
    part_rows = rows_dev // 3
    spans = [(k * part_rows, (k + 1) * part_rows) for k in range(3)]

    def block(q, me):
        return jnp.bitwise_xor(me[0], 2 * q + half)

    def out_spec(order):
        def place(q, me):
            index = []
            for name in order:
                if name[0] in "ax":
                    index.append(
                        jnp.bitwise_and(
                            lax.shift_right_logical(q, len(bits) - 1 - bits.index(name)), 1
                        )
                    )
                else:
                    index.append(0)
            return tuple(index) + (0, 0)

        shape = tuple(1 if n[0] in "ax" else 2 for n in order) + (part_rows, width)
        return pl.BlockSpec(shape, place)

    return pl.pallas_call(
        partial(
            wide_grads_kernel,
            spans=spans,
            places=[(o.index("z1"), o.index("z0")) for o in orders],
            narrow=out_chunk,
            half=half,
        ),
        grid_spec=pltpu.PrefetchScalarGridSpec(
            num_scalar_prefetch=1,
            grid=(devices // 8,),
            in_specs=[
                pl.BlockSpec((tokens, chunk), lambda q, me: (0, block(q, me))),
                pl.BlockSpec((tokens, chunk), lambda q, me: (0, block(q, me))),
                pl.BlockSpec(
                    (tokens, out_wide),
                    lambda q, me: (0, lax.div(block(q, me), out_wide // out_chunk)),
                ),
                once(h_two.shape),
                once(d_mixed.shape),
                once(framed.shape),
            ] + [out_spec(o) for o in orders][: len(adds)],
            out_specs=[out_spec(o) for o in orders],
            scratch_shapes=[pltpu.VMEM((out_wide, width), wide)],
        ),
        out_shape=[
            jax.ShapeDtypeStruct((2,) * len(o) + (part_rows, width), low_type) for o in orders
        ],
        compiler_params=pltpu.CompilerParams(
            dimension_semantics=("arbitrary",), vmem_limit_bytes=36 * MIB
        ),
        cost_estimate=pl.CostEstimate(
            flops=2 * tokens * width * (2 * chunk + out_chunk) * (devices // 8),
            bytes_accessed=24 * MIB, transcendentals=0,
        ),
        name="wide_grads",
    )(me, d_hidden, act, d_branch, h_two, d_mixed, framed, *adds)


def qkv_back_kernel(
    me_ref, dq_ref, dk_ref, dv_ref, noisy_ref, pw_ref, bias_ref, mod_ref, w_ref, sel_ref,
    cs_ref, sn_ref, tc_ref, ts_ref, *refs, width, local, maps, begin, last,
):
    i = pl.program_id(0)
    if begin:
        dw_in, demb_in, dbias_in, *refs = refs
    *dw_refs, dmod_ref, demb_ref, dbias_ref, acc_scr, emb_scr, bias_scr, pw_scr = refs

    @pl.when(i == 0)
    def _():
        pw_scr[...] = pack_right(pw_ref[...])
        bias_scr[...] = jnp.zeros_like(bias_scr)
        if begin:
            acc_scr[...] = dw_in[...]
            emb_scr[...] = demb_in[...]
            bias_scr[0:1, :] = dbias_in[...]
        else:
            acc_scr[...] = jnp.zeros_like(acc_scr)
            emb_scr[...] = jnp.zeros_like(emb_scr)

    cosine = cs_ref[...] + tc_ref[0]
    sine = sn_ref[...] + ts_ref[0]
    half = local // 2
    parts = []
    for ref in (dq_ref, dk_ref):
        first = ref[:, 0:half].astype(wide)
        second = ref[:, half:local].astype(wide)
        turned = jnp.concatenate(
            [first * cosine + second * sine, second * cosine - first * sine], axis=1
        ).astype(low_type)
        parts.append(dot_nn(turned, sel_ref[...]).astype(low_type))
    parts.append(dv_ref[...])
    d_qkv = jnp.concatenate(parts, axis=1)
    d_h = dot_nn(d_qkv, w_ref[...])
    noisy = noisy_ref[0]
    state = dot_tn(pack_left(noisy), pw_scr[...]) + bias_ref[...]
    normed, rstd = layer_stats(state)
    scl = mod_ref[0, :, width : 2 * width]
    h_low = (normed * (1.0 + scl) + mod_ref[0, :, 0:width]).astype(low_type)
    acc_scr[...] += dot_tn(d_qkv, h_low)
    dmod_ref[0, :, 0:width] = jnp.sum(d_h, axis=0, keepdims=True)
    dmod_ref[0, :, width : 2 * width] = jnp.sum(d_h * normed, axis=0, keepdims=True)
    d_state = layer_back(normed, rstd, d_h * (1.0 + scl))
    emb_scr[...] += thin_product(noisy, d_state)
    bias_scr[...] += jnp.sum(d_state.reshape(-1, 8, width), axis=0)

    @pl.when(i == pl.num_programs(0) - 1)
    def _():
        demb_ref[...] = emb_scr[...]
        dbias_ref[...] = jnp.sum(bias_scr[...], axis=0, keepdims=True)
        if not last:
            dw_refs[0][...] = acc_scr[...]
            return
        rows = acc_scr.shape[0] // len(maps[0])
        at = 0
        for ref, places in zip(dw_refs, maps):
            count = ref.shape[1]
            for pos, apart in enumerate(places):
                dev = jnp.bitwise_xor(me_ref[0], apart)
                begin = pl.multiple_of(dev * rows + at, 8)
                ref[pos] = acc_scr[pl.ds(begin, count), :].astype(ref.dtype)
            at += count


def near_places(order):
    natural = sorted((n for n in order if n[0] == "a"), reverse=True) + ["z1", "z0"]
    places = []
    for pos in range(1 << len(order)):
        value = 0
        for d, name in enumerate(order):
            if (pos >> (len(order) - 1 - d)) & 1:
                value |= 1 << (len(natural) - 1 - natural.index(name))
        places.append(value)
    return places


def qkv_back(me, orders, dq, dk, dv, noisy_t, pw, bias, mod, w_local, tables, tcos, tsin, sums, begin, last):
    frames, patch, ftok = noisy_t.shape
    tokens, local = dq.shape
    width = pw.shape[1]
    cs, sn, _, _, sel = tables
    count = 1 << len(orders[0])
    rows = w_local.shape[0] // count
    first = -(-rows // 16) * 8
    blocks = [(count, first, width), (count, rows - first, width)]
    if last < frames:
        blocks = [w_local.shape]
    full = lambda shape: pl.BlockSpec(shape, lambda i, me: (0,) * len(shape))
    row = lambda cols: pl.BlockSpec((ftok, cols), lambda i, me: (i + begin, 0))
    return pl.pallas_call(
        partial(
            qkv_back_kernel, width=width, local=local, maps=[near_places(o) for o in orders],
            begin=begin, last=last == frames,
        ),
        grid_spec=pltpu.PrefetchScalarGridSpec(num_scalar_prefetch=1, grid=(last - begin,),
        in_specs=[
            row(local), row(local), row(local),
            pl.BlockSpec((1, patch, ftok), lambda i, me: (i + begin, 0, 0)),
            full(pw.shape),
            full((1, width)),
            pl.BlockSpec((1, 1, 6 * width), lambda i, me: (i + begin, 0, 0)),
            full(w_local.shape),
            full(sel.shape),
            full(cs.shape),
            full(sn.shape),
            pl.BlockSpec((1, 1, local // 2), lambda i, me: (i + begin, 0, 0)),
            pl.BlockSpec((1, 1, local // 2), lambda i, me: (i + begin, 0, 0)),
        ] + [full(a.shape) for a in sums],
        out_specs=[
            *(full(b) for b in blocks),
            pl.BlockSpec((1, 1, 2 * width), lambda i, me: (i, 0, 0)),
            full(pw.shape),
            full((1, width)),
        ],
        scratch_shapes=[
            pltpu.VMEM(w_local.shape, wide),
            pltpu.VMEM(pw.shape, wide),
            pltpu.VMEM((8, width), wide),
            pltpu.VMEM((6 * patch, width), low_type),
        ],
        ),
        out_shape=[
            *(jax.ShapeDtypeStruct(b, low_type if last == frames else wide) for b in blocks),
            jax.ShapeDtypeStruct((last - begin, 1, 2 * width), wide),
            jax.ShapeDtypeStruct(pw.shape, wide),
            jax.ShapeDtypeStruct((1, width), wide),
        ],
        compiler_params=pltpu.CompilerParams(
            dimension_semantics=("arbitrary",), vmem_limit_bytes=28 * MIB
        ),
        cost_estimate=pl.CostEstimate(
            flops=2 * 2 * tokens * width * 3 * local, bytes_accessed=16 * MIB, transcendentals=0
        ),
        name="qkv_back",
    )(me, dq, dk, dv, noisy_t, pw, bias, mod, w_local, sel, cs, sn, tcos, tsin, *sums)


def tri_blocks(count):
    return [(r, c) for r in range(count) for c in range(r, count)]


def tile_places(order):
    natural = sorted((n for n in order if n[0] == "a"), reverse=True) + ["x", "c", "z1", "z0"]
    places = []
    for pos in range(1 << len(order)):
        value = 0
        for d, name in enumerate(order):
            if (pos >> (len(order) - 1 - d)) & 1:
                value |= 1 << (len(natural) - 1 - natural.index(name))
        places.append(value)
    return places


def steer_kernel(
    tab_ref, clip_ref, *refs, blk, cuts, maps, rows
):
    mats = len(rows)
    arrived, sums = refs[:3], refs[3:6]
    olds, refs = refs[6 : 6 + mats], refs[6 + mats :]
    news, u_ref = refs[:mats], refs[mats]
    outs, scr = refs[mats + 1 : -1], refs[-1]
    clip = clip_ref[0]
    me = tab_ref[12]
    width = u_ref.shape[2]
    units = []
    for slot in range(3):
        source = tab_ref[9 + slot]
        units.append(
            jnp.where(
                source == 0, arrived[0][...], jnp.where(source == 1, arrived[1][...], arrived[2][...])
            )
        )
    whole = jnp.concatenate([ref[...] for ref in sums], axis=0)
    up, down, out = rows[2], rows[3], rows[1]
    grads = (
        jnp.concatenate(units, axis=0), whole[up + down :], whole[:up], whole[up : up + down]
    )
    low = []
    for m in range(mats):
        grad = clip * grads[m]
        moment = 0.95 * olds[m][...] + grad
        news[m][...] = moment
        steer = grad + 0.95 * moment
        u_ref[m, : rows[m], :] = steer
        if rows[m] < u_ref.shape[1]:
            u_ref[m, rows[m] :, :] = jnp.zeros((u_ref.shape[1] - rows[m], width), wide)
        low.append(steer.astype(low_type))
    pairs = tri_blocks(width // blk)
    clusters = len(maps[0]) // 32
    for n, (r, c) in enumerate(pairs):
        for m in range(mats):
            scr[m] = dot_tn(low[m][:, r * blk : (r + 1) * blk], low[m][:, c * blk : (c + 1) * blk])
        for m in range(mats // clusters):
            index = m * len(pairs) + n
            for part, ref in enumerate(outs):
                if cuts[part] <= index < cuts[part + 1]:
                    inner = index - cuts[part]
                    for pos, apart in enumerate(maps[part]):
                        which, top, left = tile_of(jnp.bitwise_xor(me, apart), mats // clusters, blk)
                        ref[pos, inner * 16 : (inner + 1) * 16, :] = scr[
                            which + m, pl.ds(pl.multiple_of(top, 16), 16),
                            pl.ds(pl.multiple_of(left, blk // 2), blk // 2),
                        ].astype(ref.dtype)


def tile_of(dev, mats_each, blk):
    return (
        lax.shift_right_logical(dev, 5) * mats_each,
        jnp.bitwise_and(lax.shift_right_logical(dev, 1), 15) * 16,
        jnp.bitwise_and(dev, 1) * (blk // 2),
    )


def steer_grams(table, clip, arrived, sums, moments, blk, cuts, orders, devices):
    width = moments[0].shape[1]
    rows = [m.shape[0] for m in moments]
    maps = [tile_places(o) for o in orders]
    shapes = [(devices, (cuts[k + 1] - cuts[k]) * 16, blk // 2) for k in range(len(orders))]
    steer_shape = (len(rows), max(rows), width)
    results = pl.pallas_call(
        partial(steer_kernel, blk=blk, cuts=cuts, maps=maps, rows=rows),
        grid_spec=pltpu.PrefetchScalarGridSpec(
            num_scalar_prefetch=2,
            grid=(1,),
            in_specs=[once(a.shape) for a in (*arrived, *sums, *moments)],
            out_specs=[once(m.shape) for m in moments]
            + [once(steer_shape)]
            + [once(s) for s in shapes],
            scratch_shapes=[pltpu.VMEM((len(rows), blk, blk), wide)],
        ),
        out_shape=[jax.ShapeDtypeStruct(m.shape, wide) for m in moments]
        + [jax.ShapeDtypeStruct(steer_shape, wide)]
        + [jax.ShapeDtypeStruct(s, low_type) for s in shapes],
        compiler_params=pltpu.CompilerParams(
            dimension_semantics=("arbitrary",), vmem_limit_bytes=24 * MIB
        ),
        name="steer_grams",
    )(table, clip, *arrived, *sums, *moments)
    return results[:4], results[4], results[5:]


def home_kernel(tab_ref, one_ref, two_ref, *refs):
    outs, sq_ref = refs[:3], refs[3]
    rows = outs[0].shape[0]
    whole = jnp.concatenate([one_ref[...], two_ref[...]], axis=0)
    pieces = [whole[n * rows : (n + 1) * rows] for n in range(3)]
    for color in range(3):
        slot = tab_ref[6 + color]
        outs[color][...] = jnp.where(
            slot == 0, pieces[0], jnp.where(slot == 1, pieces[1], pieces[2])
        )
    sq_ref[...] = jnp.sum(whole * whole, keepdims=True)


def home_units(table, one, two):
    rows = (one.shape[0] + two.shape[0]) // 3
    width = one.shape[1]
    piece = (rows, width)
    *pieces, squares = pl.pallas_call(
        home_kernel,
        grid_spec=pltpu.PrefetchScalarGridSpec(
            num_scalar_prefetch=1,
            grid=(1,),
            in_specs=[once(one.shape), once(two.shape)],
            out_specs=[once(piece)] * 3 + [once((1, 1))],
        ),
        out_shape=[jax.ShapeDtypeStruct(piece, wide)] * 3 + [jax.ShapeDtypeStruct((1, 1), wide)],
        compiler_params=pltpu.CompilerParams(
            dimension_semantics=("arbitrary",), vmem_limit_bytes=16 * MIB
        ),
        name="home_units",
    )(table, one, two)
    return pieces, squares[0, 0]


def polish_kernel(me_ref, u_ref, *refs, blk, cuts, maps, factors):
    mats, rows, width = u_ref.shape
    parts, olds, outs, g_scr = refs[: 2 * len(maps)], refs[2 * len(maps) : -mats - 1], refs[-mats - 1 : -1], refs[-1]
    pairs = tri_blocks(width // blk)
    me = me_ref[0]
    clusters = len(maps[0]) // 16
    diag = lax.broadcasted_iota(jnp.int32, (blk, blk), 0) == lax.broadcasted_iota(
        jnp.int32, (blk, blk), 1
    )
    for m in range(mats // clusters):
        for n, (r, c) in enumerate(pairs):
            index = m * len(pairs) + n
            for part, places in enumerate(maps):
                if not cuts[part] <= index < cuts[part + 1]:
                    continue
                inner = index - cuts[part]
                for ref, other in ((parts[2 * part], 0), (parts[2 * part + 1], 4)):
                    for pos, apart in enumerate(places):
                        which, top, left = tile_of(
                            jnp.bitwise_xor(me, apart + other), mats // clusters, blk
                        )
                        g_scr[
                            which + m, pl.ds(pl.multiple_of(r * blk + top, 16), 16),
                            pl.ds(pl.multiple_of(c * blk + left, blk // 2), blk // 2),
                        ] = ref[pos, inner * 16 : (inner + 1) * 16, :]
    for m in range(mats):
        trace = jnp.zeros((1, 1), wide)
        for r, c in pairs:
            piece = g_scr[m, r * blk : (r + 1) * blk, c * blk : (c + 1) * blk]
            if r == c:
                trace += jnp.sum(jnp.where(diag, piece.astype(wide), 0.0), keepdims=True)
            else:
                g_scr[m, c * blk : (c + 1) * blk, r * blk : (r + 1) * blk] = piece.T
        scale = jnp.sqrt(trace) + 1e-07
        inverse = 1.0 / scale
        inverse_sq = inverse * inverse
        own = outs[m].shape[0]

        def times(value):
            return dot_nn(value.astype(low_type), g_scr[m]) * inverse_sq

        def cubic(value):
            once_ = times(value)
            return coef_one * value + coef_two * once_ + coef_three * times(once_)

        current = cubic(u_ref[m, :own, :] * inverse)
        for _ in range(NS_ITERS - 1):
            second = cubic(cubic(times(current)))
            third = cubic(cubic(times(second)))
            current = coef_one * current + coef_two * second + coef_three * third
        outs[m][...] = olds[m][...] * (1.0 - 2.0 * 0.01) - factors[m] * current


def polish(me, u, parts, olds, blk, cuts, orders, factors):
    mats, rows, width = u.shape
    maps = [tile_places(o) for o in orders]
    return pl.pallas_call(
        partial(polish_kernel, blk=blk, cuts=cuts, maps=maps, factors=factors),
        grid_spec=pltpu.PrefetchScalarGridSpec(
            num_scalar_prefetch=1,
            grid=(1,),
            in_specs=[once(u.shape)] + [once(p.shape) for p in parts] + [once(o.shape) for o in olds],
            out_specs=[once(o.shape) for o in olds],
            scratch_shapes=[pltpu.VMEM((mats, width, width), low_type)],
        ),
        out_shape=[jax.ShapeDtypeStruct(o.shape, wide) for o in olds],
        compiler_params=pltpu.CompilerParams(
            dimension_semantics=("arbitrary",), vmem_limit_bytes=32 * MIB
        ),
        cost_estimate=pl.CostEstimate(
            flops=2 * 24 * mats * rows * width * width, bytes_accessed=12 * MIB, transcendentals=0
        ),
        name="polish",
    )(me, u, *parts, *olds)


def bit_stages(count_a):
    stages = {}
    bits_a = count_a.bit_length() - 1
    for b in range(bits_a):
        stages["a%d" % (bits_a - 1 - b)] = ("a", 1 << (bits_a - 1 - b), b)
    stages["x"] = ("x", 1, bits_a)
    stages["c"] = ("c", 1, bits_a + 1)
    stages["z1"] = ("z", 2, bits_a + 2)
    stages["z0"] = ("z", 1, bits_a + 3)
    return stages


def swap(value, axis, distance):
    size = lax.axis_size(axis)
    return lax.ppermute(value, axis, [(i, i ^ distance) for i in range(size)])


def bit_of(axis, distance):
    return (lax.axis_index(axis) // distance) % 2


def in_order(blocks, names):
    for dim, name in enumerate(names):
        axis = name[0]
        distance = {"z1": 2, "a1": 2, "a2": 4}.get(name, 1)
        mine = bit_of(axis, distance)
        flipped = jnp.flip(blocks, dim)
        blocks = jnp.where(mine == 0, blocks, flipped)
    natural = sorted(n for n in names if n[0] == "a")[::-1] + [
        n for n in ("x", "c", "z1", "z0") if n in names
    ]
    order = [names.index(n) for n in natural] + list(range(len(names), blocks.ndim))
    return blocks.transpose(order)


def three_orders(stages):
    names_a = [n for n in stages if n.startswith("a")]
    return (
        ["x"] + names_a + ["z0", "z1"],
        names_a + ["z0", "x", "z1"],
        ["z0", "x"] + names_a + ["z1"],
    )


def after(value, *others):
    return lax.optimization_barrier((value,) + others)[0]


def halve(blocks, order, stages):
    keep, send = blocks[0], blocks[1]
    for step, name in enumerate(order):
        axis, distance, _ = stages[name]
        got = swap(send.astype(low_type), axis, distance)
        if step == len(order) - 1:
            return keep.astype(wide) + got.astype(wide)
        send = (keep[1].astype(wide) + got[1].astype(wide)).astype(low_type)
        keep = keep[0].astype(wide) + got[0].astype(wide)


class Ladder:
    def __init__(self, blocks, orders, stages):
        self.orders, self.stages, self.rung = orders, stages, 0
        self.keep = [b[0] for b in blocks]
        self.send = [b[1] for b in blocks]

    def exchange(self):
        self.got = []
        for order, send in zip(self.orders, self.send):
            axis, distance, _ = self.stages[order[self.rung]]
            self.got.append(swap(send.astype(low_type), axis, distance))
        self.rung += 1

    def add(self, *first):
        got = lax.optimization_barrier(tuple(self.got) + first)[: len(self.got)]
        pairs = list(zip(self.keep, got))
        if self.rung == len(self.orders[0]):
            return [k.astype(wide) + g.astype(wide) for k, g in pairs]
        self.send = [(k[1].astype(wide) + g[1].astype(wide)).astype(low_type) for k, g in pairs]
        self.keep = [k[0].astype(wide) + g[0].astype(wide) for k, g in pairs]


def double(block, order, stages):
    for name in order:
        axis, distance, _ = stages[name]
        block = jnp.stack([block, swap(block, axis, distance)])
    return block


def spread(payload):
    count = math.prod(lax.axis_size(n) for n in ALL)
    return lax.all_to_all(
        jnp.broadcast_to(payload[None], (count,) + payload.shape),
        ALL, split_axis=0, concat_axis=0, tiled=True,
    )


def unit_plan(devices):
    quarter = devices // 4
    edges = []
    for unit in range(3 * devices):
        section, place = unit // devices, unit % devices
        member, rest = place // quarter, place % quarter
        index = section * quarter + rest
        pos, slot = index // 3, index % 3
        a, z = pos // 4, pos % 4
        dest = ((a * 2 + member // 2) * 2 + member % 2) * 4 + z
        edges.append((unit // 3, unit % 3, dest, slot))
    left = list(edges)
    colors = []
    for _ in range(3):
        match = {}

        def augment(src, seen):
            for e in left:
                if e[0] != src or e[2] in seen:
                    continue
                seen.add(e[2])
                if e[2] not in match or augment(match[e[2]][0], seen):
                    match[e[2]] = e
                    return True
            return False

        for src in range(devices):
            assert augment(src, set())
        chosen = list(match.values())
        for e in chosen:
            left.remove(e)
        colors.append(chosen)
    return colors


def unit_tables(plan):
    devices = len(plan[0])
    tables = np.zeros((devices, 2, 2, 3), np.int32)
    for color, chosen in enumerate(plan):
        for src, src_slot, dst, dst_slot in chosen:
            tables[src, 0, 0, color], tables[dst, 0, 1, dst_slot] = src_slot, color
            tables[dst, 1, 0, color], tables[src, 1, 1, src_slot] = dst_slot, color
    return tables.reshape(devices, 12)


def away_kernel(tab_ref, w_ref, *outs):
    rows = outs[0].shape[0]
    whole = w_ref[...].astype(low_type)
    pieces = [whole[n * rows : (n + 1) * rows] for n in range(3)]
    for color in range(3):
        slot = tab_ref[color]
        outs[color][...] = jnp.where(
            slot == 0, pieces[0], jnp.where(slot == 1, pieces[1], pieces[2])
        )


def away_units(table, weight):
    piece = (weight.shape[0] // 3, weight.shape[1])
    return pl.pallas_call(
        away_kernel,
        grid_spec=pltpu.PrefetchScalarGridSpec(
            num_scalar_prefetch=1,
            grid=(1,),
            in_specs=[once(weight.shape)],
            out_specs=[once(piece)] * 3,
        ),
        out_shape=[jax.ShapeDtypeStruct(piece, low_type)] * 3,
        compiler_params=pltpu.CompilerParams(
            dimension_semantics=("arbitrary",), vmem_limit_bytes=16 * MIB
        ),
        name="away_units",
    )(table, weight)


def place_kernel(tab_ref, *refs):
    pieces, out_ref = refs[:3], refs[3]
    rows = pieces[0].shape[0]
    for slot in range(3):
        source = tab_ref[3 + slot]
        out_ref[slot * rows : (slot + 1) * rows, :] = jnp.where(
            source == 0, pieces[0][...], jnp.where(source == 1, pieces[1][...], pieces[2][...])
        )


def place_units(table, pieces):
    rows, width = pieces[0].shape
    return pl.pallas_call(
        place_kernel,
        grid_spec=pltpu.PrefetchScalarGridSpec(
            num_scalar_prefetch=1,
            grid=(1,),
            in_specs=[once((rows, width))] * 3,
            out_specs=once((3 * rows, width)),
        ),
        out_shape=jax.ShapeDtypeStruct((3 * rows, width), low_type),
        compiler_params=pltpu.CompilerParams(
            dimension_semantics=("arbitrary",), vmem_limit_bytes=16 * MIB
        ),
        name="place_units",
    )(table, *pieces)


def send_units(pieces, plan, back):
    src, dst = (2, 0) if back else (0, 2)
    return [
        lax.ppermute(piece, ALL, [(e[src], e[dst]) for e in chosen])
        for piece, chosen in zip(pieces, plan)
    ]


def body(
    noisy_latents,
    target_latents,
    noise_levels,
    clip_start,
    qkv_weight,
    qkv_moment,
    out_weight,
    out_moment,
    up_weight,
    up_moment,
    down_weight,
    down_moment,
    ada_weight,
    ada_first,
    ada_second,
    patch_weight,
    patch_first,
    patch_second,
    vectors,
    vec_first,
    vec_second,
):
    count_a = lax.axis_size("a")
    members = lax.axis_size("x") * lax.axis_size("c")
    devices = count_a * members * lax.axis_size("z")
    groups = count_a * lax.axis_size("z")
    frames_dev = noise_levels.shape[0]
    tokens_dev = noisy_latents.shape[0]
    frame_tok = tokens_dev // frames_dev
    width = patch_weight.shape[2]
    patch_size = patch_weight.shape[1]
    head_dim = width // HEADS
    local_heads = HEADS // members
    local = local_heads * head_dim
    group_frames = frames_dev * members
    frames_all = frames_dev * devices
    group_tokens = group_frames * frame_tok
    score_scale = 1.0 / math.sqrt(head_dim)
    stages = bit_stages(count_a)
    my_a, my_z = lax.axis_index("a"), lax.axis_index("z")
    my_group = my_a * 4 + my_z
    my_member = lax.axis_index("x") * 2 + lax.axis_index("c")
    tables = rope_tables(head_dim, local_heads, frame_tok)
    tables = tables[:4] + (jnp.asarray(tables[4], low_type),)
    plan = unit_plan(devices)

    rows_unit = qkv_weight.shape[0] // 3
    me = lax.axis_index(ALL).astype(jnp.int32)
    table = jnp.concatenate([jnp.asarray(unit_tables(plan))[me], me[None]])
    units = place_units(table, send_units(away_units(table, qkv_weight), plan, False))
    units = units.reshape(3, rows_unit, width)
    names_a = [n for n in stages if n.startswith("a")]

    swap_axes = ("x", "c", "z")
    moves = [(g * 4 + z, z * 4 + g) for g in range(4) for z in range(4)]
    noisy_t = noisy_latents.T.reshape(patch_size, frames_dev, frame_tok).transpose(1, 0, 2)
    target_t = target_latents.T.reshape(patch_size, frames_dev, frame_tok).transpose(1, 0, 2)
    mine = lax.ppermute(jnp.stack([noisy_t, target_t]), swap_axes, moves)

    meta = jnp.concatenate([noise_levels, clip_start]).astype(wide)
    meta = jnp.pad(meta, (0, 128 - meta.shape[0]))[None]
    meta_all = spread(after(meta, units))[:, 0]
    rows_up, rows_out = up_weight.shape[0], out_weight.shape[0]
    layout = part_layout(rows_up, rows_out)
    rising = [
        ["z1", "z0"] + names_a[::-1] + ["x"],
        ["z1", "x", "z0"] + names_a[::-1],
        ["z1"] + names_a[::-1] + ["x", "z0"],
    ]
    gather_orders = [o[::-1] for o in rising]
    rows_part = (2 * rows_up + rows_out) // 3
    bulk = jnp.concatenate([up_weight, down_weight, out_weight], axis=0).astype(low_type)
    shares = [bulk[n * rows_part : (n + 1) * rows_part] for n in range(3)]
    climb = lambda shares, rung: [
        double(share, [order[rung]], stages) for share, order in zip(shares, rising)
    ]
    far = double(units, ["z1"], stages)
    meta_all, far, mine = lax.optimization_barrier((meta_all, far, mine))
    shares = climb([after(share, far) for share in shares], 0)
    levels_all = meta_all[:, :frames_dev].reshape(frames_all)
    starts_all = meta_all[:, frames_dev : 2 * frames_dev].reshape(frames_all)
    starts_group = lax.dynamic_slice_in_dim(starts_all, my_group * group_frames, group_frames)
    starts_int = starts_group.astype(jnp.int32)
    noisy_mine, target_mine = mine[0], mine[1]
    pair = double(noisy_mine, ["c"], stages)

    half_one = double(far[:, :, : rows_unit // 2], ["z0"], stages)
    half_two = double(far[:, :, rows_unit // 2 :], names_a[::-1], stages)
    cond_low = jax.nn.silu(level_features(levels_all, width)).astype(low_type)
    ada_rows = ada_weight.shape[0]
    mod_rows = dot_nt(cond_low, ada_weight.astype(low_type))
    mod_rows, half_one, half_two, pair = lax.optimization_barrier(
        (mod_rows, half_one, half_two, pair)
    )
    mod_out = jnp.broadcast_to(
        mod_rows.reshape(count_a, 1, 4, group_frames, ada_rows),
        (count_a, members, 4, group_frames, ada_rows),
    ).reshape(devices, group_frames, ada_rows)
    mod_in = lax.all_to_all(
        mod_out.astype(low_type), ALL, split_axis=0, concat_axis=0, tiled=True
    ).astype(wide)
    noisy_group = in_order(double(pair, ["x"], stages), ["x", "c"]).reshape(
        group_frames, patch_size, frame_tok
    )
    half_one = double(half_one, names_a[::-1], stages)
    half_two = double(half_two, ["z0"], stages)
    *shares, mod_in = lax.optimization_barrier((*shares, mod_in))
    shares = climb(shares, 1)
    mod_in, half_one, half_two, noisy_group = lax.optimization_barrier(
        (mod_in, half_one, half_two, noisy_group)
    )
    half_one = in_order(half_one, names_a + ["z0", "z1"])
    half_two = in_order(half_two, ["z0"] + names_a + ["z1"])
    qkv_local = jnp.concatenate(
        [half_one.reshape(3 * groups, -1, width), half_two.reshape(3 * groups, -1, width)], axis=1
    ).reshape(3 * local, width)
    modul = mod_in.transpose(1, 0, 2).reshape(group_frames, 6 * width) + vectors[2:8].reshape(
        1, 6 * width
    )
    mod3 = modul.reshape(group_frames, 1, 6 * width)
    *shares, mod3 = lax.optimization_barrier((*shares, mod3))
    shares = climb(shares, 2)
    mod_mine = lax.dynamic_slice_in_dim(mod3, my_member * frames_dev, frames_dev)

    frame_ids = jnp.arange(group_frames, dtype=jnp.int32)
    time_pos = (frame_ids - starts_int).astype(wide)
    t_angle = time_pos[:, None] * tables[2][None, :]
    tcos = (jnp.cos(t_angle) * tables[3][None, :])[:, None, :]
    tsin = (jnp.sin(t_angle) * tables[3][None, :])[:, None, :]

    pw_in = patch_weight[0]
    bias_in = vectors[0:1]
    q, k, v = embed_qkv(
        noisy_group, pw_in, bias_in, mod3, qkv_local, tables, tcos, tsin, score_scale
    )
    place = jnp.stack([me // 4, me % 4])
    *shares, q = lax.optimization_barrier((*shares, q))
    for rung in range(3, len(rising[0]) - 1):
        shares = climb(shares, rung)
    final = []
    for share, order in zip(shares, rising):
        axis, distance, _ = stages[order[-1]]
        final.append(swap(share, axis, distance))
    att, att_low, lse = attend(starts_int, q, k, v, group_frames, local_heads)
    final = lax.optimization_barrier((*final, lse))[:3]
    shares = [jnp.stack(pair) for pair in zip(shares, final)]
    shares = [(share, swap(share, "c", 1)) for share in shares]
    framed = lax.all_to_all(
        att_low.reshape(members, tokens_dev, local), ("x", "c"), split_axis=0, concat_axis=0,
        tiled=True,
    )

    gain = vectors[1:2]
    pw_out = patch_weight[1]
    state_one, branch, h_two, out_full = post_attend(
        me[None], framed, noisy_mine, pw_in, bias_in, mod_mine, shares[2], gather_orders[2],
        layout[2][0][1],
    )
    act, slope, mixed, pred = ff_forward(
        place, h_two, state_one, mod_mine, shares, gather_orders, layout, gain, pw_out, frame_tok,
    )
    member_axes = ("x", "c")
    ahead = [(i, i + 1) for i in range(members - 1)]
    behind = [(i + 1, i) for i in range(members - 1)]
    edge = lax.ppermute(
        jnp.stack([pred[-1], target_mine[-1]]).astype(low_type), member_axes, ahead
    ).astype(wide)
    prev_pred = jnp.concatenate([edge[0:1], pred[:-1]], axis=0)
    prev_goal = jnp.concatenate([edge[1:2], target_mine[:-1]], axis=0)
    diff = pred - prev_pred - (target_mine - prev_goal)
    my_frames = my_member * frames_dev + jnp.arange(frames_dev, dtype=jnp.int32)
    valid = my_frames > lax.dynamic_slice_in_dim(starts_int, my_member * frames_dev, frames_dev)
    loss_local = jnp.sum(jnp.where(valid[:, None, None], diff * diff, 0.0))
    entry_count = float(frames_all * frame_tok * patch_size)
    d_diff = jnp.where(valid[:, None, None], (2.0 / entry_count) * diff, 0.0)
    returned = lax.ppermute(d_diff[0], member_axes, behind)
    d_pred = d_diff - jnp.concatenate([d_diff[1:], returned[None]], axis=0)
    d_hidden, d_mixed, d_branch, d_framed, d_small, d_sums, d_mod_rest = ff_backward(
        place, d_pred, state_one, mixed, branch, mod_mine, noisy_mine, gain, pw_out, shares,
        gather_orders, layout, out_full, slope, members,
    )
    d_att = lax.all_to_all(d_framed, ("x", "c"), split_axis=0, concat_axis=0, tiled=True).reshape(
        group_tokens, local
    )

    orders = three_orders(stages)
    grads_of = lambda half, adds=(): wide_grads(
        place, half, d_hidden, act, d_branch, h_two, d_mixed, framed, orders, devices, adds
    )
    others = grads_of(1)
    core_axis, core_distance, _ = stages["c"]
    passed = [swap(o, core_axis, core_distance) for o in others]

    cuts = [group_frames * n // 12 for n in (0, 10, 12)]

    def part_back(n, q, sums):
        return attend_back(
            starts_int, q, d_att, att, lse, k, v, sums, cuts[n], cuts[n + 1], group_frames,
            local_heads, score_scale,
        )

    ladder = Ladder(grads_of(0, passed), orders, stages)
    ladder.exchange()
    dq, dk, dv = part_back(0, after(q, *ladder.send), ())
    ladder.add(dk)
    ladder.exchange()
    dq, dk, dv = part_back(1, after(q, *ladder.send), (dq, dk, dv))
    ladder.add(dk)
    ladder.exchange()
    dv = after(dv, *ladder.send)
    near_orders = [names_a + ["z0", "z1"], ["z0"] + names_a + ["z1"]]

    def tail_back(dv, sums, begin, last):
        return qkv_back(
            (my_a * 4 + my_z).astype(jnp.int32)[None], near_orders, dq, dk, dv, noisy_group, pw_in,
            bias_in, mod3, qkv_local, tables, tcos, tsin, sums, begin, last,
        )

    middle = group_frames // 2
    dw, d_mod_early, d_embed, d_bias = tail_back(dv, (), 0, middle)
    while ladder.rung < len(orders[0]):
        ladder.add(d_bias)
        ladder.exchange()
    dw_one, dw_two, d_mod_late, d_embed, d_bias = tail_back(
        after(dv, *ladder.send), (dw, d_embed, d_bias), middle, group_frames
    )
    d_mod_one = jnp.concatenate([d_mod_early, d_mod_late], axis=0)
    near_dims = (2,) * len(near_orders[0])
    near = Ladder(
        [d.reshape(near_dims + d.shape[1:]) for d in (dw_one, dw_two)], near_orders, stages
    )
    near.exchange()
    near.got = list(lax.optimization_barrier((*near.got, *ladder.got)))[: len(near.got)]
    d_rest = lax.dynamic_update_slice_in_dim(
        jnp.zeros((group_frames, 4 * width), wide),
        d_mod_rest.reshape(frames_dev, 4 * width), my_member * frames_dev, 0,
    )
    d_mod = jnp.concatenate([d_mod_one[:, 0], d_rest], axis=1)
    d_mod = d_mod.reshape(group_frames, devices, ada_rows).transpose(1, 0, 2)
    smalls = jnp.concatenate(
        [d_embed + d_small[1], d_small[0], d_bias + d_sums[1:2], d_sums[0:1]], axis=0
    )
    small_rows = smalls.shape[0]
    small_part = small_rows * width // devices
    mod_part = group_frames * ada_rows
    packed = jnp.concatenate(
        [d_mod.reshape(devices, mod_part), smalls.reshape(devices, small_part)], axis=1
    )
    pad = -packed.shape[1] % 128
    packed = jnp.pad(packed, ((0, 0), (0, pad))).reshape(devices, -1, 128)
    arrived = lax.all_to_all(packed, ALL, split_axis=0, concat_axis=0, tiled=True).reshape(
        devices, -1
    )
    small_mine = jnp.sum(arrived[:, mod_part : mod_part + small_part], axis=0)
    mod_grad = (
        arrived[:, :mod_part]
        .reshape(count_a, members, 4, group_frames, ada_rows)
        .sum(axis=1)
        .reshape(frames_all, ada_rows)
    )
    bias_mine = jnp.sum(mod_grad, axis=0)
    g_ada = dot_tn(mod_grad.astype(low_type), cond_low)

    g_wide = ladder.add()
    rest_sq = (
        sum((jnp.sum(piece * piece) for piece in g_wide))
        + jnp.sum(g_ada * g_ada)
        + jnp.sum(small_mine * small_mine)
        + jnp.sum(bias_mine * bias_mine)
    )
    while near.rung < len(near_orders[0]):
        near.add()
        near.exchange()
    *near.got, rest_sq, g_ada = lax.optimization_barrier((*near.got, rest_sq, g_ada))
    g_one, g_two = near.add()
    units_out, units_sq = home_units(table, g_one, g_two)
    units_home = send_units(units_out, plan, True)
    local_sq = rest_sq + units_sq
    totals = jnp.where(lax.broadcasted_iota(jnp.int32, (1, 128), 1) == 0, local_sq, loss_local)
    totals = jnp.sum(spread(totals)[:, 0, :2], axis=0)
    norm = jnp.sqrt(totals[0])
    loss_total = totals[1]
    report = jnp.concatenate([small_mine, bias_mine])
    report = jnp.pad(report, (0, -report.shape[0] % 128)).reshape(-1, 128)
    report = after(report, norm)
    clip = jnp.minimum(1.0, 0.01 / norm)

    olds = (qkv_weight, out_weight, up_weight, down_weight)
    moments = (qkv_moment, out_moment, up_moment, down_moment)
    ada_new, ada_one, ada_two = adamw(ada_weight, ada_first, ada_second, clip * g_ada, 0.08)
    blk = 256
    gram_orders = [["c"] + o for o in orders[:2]]
    pairs = len(tri_blocks(width // blk)) * 4 // (devices // 32)
    cuts = (0, pairs // 2, pairs)
    parts = []
    report_order = ["z1", "z0"] + names_a[::-1] + ["x", "c"]
    ladders = []
    moments_new, steers, tiles = steer_grams(
        table, clip[None], units_home, g_wide, moments, blk, cuts, gram_orders, devices
    )
    for k, part in enumerate(tiles):
        ladders.append(Ladder([part.reshape((2,) * len(stages) + part.shape[1:])], [gram_orders[k]], stages))
    for rung in range(len(stages)):
        for ladder in ladders:
            ladder.exchange()
        report = double(after(report, ladders[0].got[0]), [report_order[rung]], stages)
        ties = []
        if rung == 2:
            ties = [ada_new, ada_one, ada_two]
        results = []
        for ladder in ladders:
            got, *ties = lax.optimization_barrier((ladder.got[0], *ties))
            ladder.got = [got]
            results.append(ladder.add())
        if rung == 2:
            ada_new, ada_one, ada_two = ties
    everyone = in_order(report, report_order[::-1]).reshape(devices, -1)
    small_all = everyone[:, :small_part].reshape(small_rows, width)
    bias_all = everyone[:, small_part : small_part + ada_rows].reshape(6, width)
    g_patch = small_all[: 2 * patch_size].reshape(2, patch_size, width)
    g_vec = jnp.concatenate([small_all[2 * patch_size :], bias_all], axis=0)
    patch_new, patch_one, patch_two = adamw(
        patch_weight, patch_first, patch_second, clip * g_patch, 0.15
    )
    vec_new, vec_one, vec_two = adamw(vectors, vec_first, vec_second, clip * g_vec, 0.5)
    lines = [result[0].astype(low_type) for result in results]
    late = [patch_new, patch_one, patch_two, vec_new, vec_one, vec_two]
    for rung in range(1, len(stages)):
        lines = [
            double(line, [gram_orders[n][:0:-1][rung - 1]], stages) for n, line in enumerate(lines)
        ]
        if rung == len(stages) - 2:
            lines[0], *late = lax.optimization_barrier((lines[0], *late))
    patch_new, patch_one, patch_two, vec_new, vec_one, vec_two = late
    parts = []
    for line in lines:
        line = line.reshape((-1,) + line.shape[-2:])
        parts += [line, swap(line, "c", 1)]
    factors = [2.0 * math.sqrt(max(1.0, o.shape[0] * devices / width)) for o in olds]
    updated = polish(
        me[None], steers, parts, olds, blk, cuts, [o[1:] for o in gram_orders], factors
    )
    return (
        loss_total,
        norm,
        updated[0],
        moments_new[0],
        updated[1],
        moments_new[1],
        updated[2],
        moments_new[2],
        updated[3],
        moments_new[3],
        ada_new,
        ada_one,
        ada_two,
        patch_new,
        patch_one,
        patch_two,
        vec_new,
        vec_one,
        vec_two,
    )


def solution(mesh):
    groups, line = mesh.shape["dp"], mesh.shape["seq"]
    inner = Mesh(mesh.devices.reshape(groups // 4, 2, 2, line), ALL)
    split = P(ALL, None)
    copied = P()
    placed = (split, split, P(ALL), P(ALL)) + (split,) * 11 + (copied,) * 6
    return jax.shard_map(
        body,
        mesh=inner,
        in_specs=placed,
        out_specs=(copied, copied) + (split,) * 11 + (copied,) * 6,
        check_vma=False,
    )
```

```python
from functools import partial
import math

import jax
import jax.numpy as jnp
import numpy as np
from jax import lax
from jax.experimental import pallas as pl
from jax.experimental.pallas import tpu as pltpu
from jax.sharding import Mesh, PartitionSpec as P

HEADS = 16
NS_ITERS = 2
STEP = 10
ALL = ("a", "x", "c", "z")

highest = lax.Precision.HIGHEST
coef_one = 3.4445
coef_two = -4.775
coef_three = 2.0315
low_type = jnp.bfloat16
wide = jnp.float32
NT = (((1,), (1,)), ((), ()))
TN = (((0,), (0,)), ((), ()))
MIB = 1 << 20


def dot_nt(left, right):
    return lax.dot_general(left, right, NT, preferred_element_type=wide)


def dot_tn(left, right):
    return lax.dot_general(left, right, TN, preferred_element_type=wide)


def dot_nn(left, right):
    return jnp.dot(left, right, preferred_element_type=wide)


def layer_stats(value):
    mean = jnp.mean(value, axis=-1, keepdims=True)
    centred = value - mean
    rstd = lax.rsqrt(jnp.mean(centred * centred, axis=-1, keepdims=True) + 1e-06)
    return (centred * rstd, rstd)


def layer_back(normed, rstd, upstream):
    return rstd * (
        upstream
        - jnp.mean(upstream, axis=-1, keepdims=True)
        - normed * jnp.mean(upstream * normed, axis=-1, keepdims=True)
    )


def level_features(levels, width):
    half = width // 2
    freqs = jnp.exp(-math.log(10000.0) * jnp.arange(half, dtype=jnp.float32) / half)
    angle = levels.astype(jnp.float32)[:, None] * freqs[None, :]
    return jnp.concatenate([jnp.sin(angle), jnp.cos(angle)], axis=-1)


def adamw(weight, first, second, grad, rate):
    first = 0.9 * first + 0.1 * grad
    second = 0.95 * second + 0.05 * grad * grad
    first_hat = first / (1.0 - 0.9**STEP)
    second_hat = second / (1.0 - 0.95**STEP)
    weight = weight - rate * (first_hat / (jnp.sqrt(second_hat) + 1e-08) + 0.01 * weight)
    return (weight, first, second)


def rope_tables(head_dim, heads, frame_tok):
    sec_time = head_dim // 4
    sec_space = (head_dim - sec_time) // 2
    side = math.isqrt(frame_tok)
    spot = np.arange(frame_tok)
    firsts, seconds, time_freq, space = [], [], [], []
    offset = 0
    for kind, size in ((0, sec_time), (1, sec_space), (2, sec_space)):
        half = size // 2
        freqs = np.exp(-math.log(10000.0) * np.arange(half, dtype=np.float64) * 2.0 / size)
        firsts += list(range(offset, offset + half))
        seconds += list(range(offset + half, offset + size))
        offset += size
        where = {0: np.zeros(frame_tok), 1: spot // side, 2: spot % side}[kind]
        space.append(where[:, None] * freqs[None, :])
        time_freq.append(freqs if kind == 0 else np.zeros(half))
    is_time = np.concatenate([np.ones(sec_time // 2), np.zeros(sec_space)])
    space = np.concatenate(space, axis=1)
    space_cos = np.where(is_time[None] > 0, 0.0, np.cos(space))
    space_sin = np.where(is_time[None] > 0, 0.0, np.sin(space))
    time_freq = np.concatenate(time_freq)
    order = np.concatenate(
        [
            np.concatenate([np.asarray(part) + h * head_dim for h in range(heads)])
            for part in (firsts, seconds)
        ]
    )
    total = heads * head_dim
    select = np.zeros((total, total), np.float32)
    select[np.arange(total), order] = 1.0
    tile = lambda t: np.tile(t, (1, heads)).astype(np.float32)
    return (
        tile(space_cos),
        tile(space_sin),
        np.tile(time_freq, heads).astype(np.float32),
        np.tile(is_time, heads).astype(np.float32),
        select,
    )


def split_mask(shape, axis, heads, half_lanes, value):
    lane = lax.broadcasted_iota(jnp.int32, shape, axis)
    if half_lanes is not None:
        lane = lane % half_lanes
        return lane // (half_lanes // heads) == value
    return lane // (shape[axis] // heads) == value


def split_two(value):
    high = value.astype(low_type)
    return high, (value - high.astype(wide)).astype(low_type)


def split_three(value):
    high = value.astype(low_type)
    rest = value - high.astype(wide)
    middle = rest.astype(low_type)
    return high, middle, (rest - middle.astype(wide)).astype(low_type)


def pack_left(value):
    high, middle, least = split_three(value)
    return jnp.concatenate([high, high, middle, high, middle, least], axis=0)


def pack_right(value):
    high, middle, least = split_three(value)
    return jnp.concatenate([high, middle, high, least, middle, high], axis=0)


def thin_product(thin, tall):
    t_high, t_low = split_two(thin)
    high, low = split_two(tall)
    rows = thin.shape[0]
    both = dot_nn(jnp.concatenate([t_high, t_low], axis=0), high)
    return both[:rows] + both[rows:] + dot_nn(t_high, low)


def line_rows(scrs, refs, me_ref, layout, places):
    other = jnp.bitwise_and(jnp.bitwise_xor(pl.program_id(0), me_ref[0]), 1)

    def fill(parts):
        for zz in range(4):
            apart = jnp.bitwise_xor(me_ref[1], zz)
            for scr, pieces in zip(scrs, layout):
                at = zz * (scr.shape[0] // 4)
                for part, begin, rows in pieces:
                    ref, (dim_one, dim_zero) = parts[part], places[part]
                    index = [0] * (len(ref.shape) - 2)
                    index[dim_one] = lax.shift_right_logical(apart, 1)
                    index[dim_zero] = jnp.bitwise_and(apart, 1)
                    scr[at : at + rows, :] = ref[tuple(index) + (slice(begin, begin + rows),)]
                    at += rows

    @pl.when(other == 0)
    def _():
        fill(refs[0::2])

    @pl.when(other == 1)
    def _():
        fill(refs[1::2])


def part_layout(rows_up, rows_out):
    size = (2 * rows_up + rows_out) // 3
    layout, at = [], 0
    for rows in (rows_up, rows_up, rows_out):
        pieces = []
        while rows:
            count = min(rows, size - at % size)
            pieces.append((at // size, at % size, count))
            at, rows = at + count, rows - count
        layout.append(pieces)
    return layout


def once(shape):
    return pl.BlockSpec(shape, lambda *_: (0,) * len(shape), pipeline_mode=pl.Buffered(1))


def embed_qkv_kernel(
    noisy_ref, pw_ref, bias_ref, mod_ref, w_ref, sel_ref, cs_ref, sn_ref, tc_ref, ts_ref,
    q_ref, k_ref, v_ref, wq_scr, pw_scr, *, width, local, scale,
):
    @pl.when(pl.program_id(0) == 0)
    def _():
        pw_scr[...] = pack_right(pw_ref[...])
        for part in range(2):
            rows = pl.ds(part * local, local)
            wq_scr[rows, :] = dot_nn(sel_ref[...], w_ref[rows, :]).astype(low_type)
        rows = pl.ds(2 * local, local)
        wq_scr[rows, :] = w_ref[rows, :]

    ftok = cs_ref.shape[0]
    half = local // 2
    count = noisy_ref.shape[0]
    lows, outs = [None] * count, [None] * count

    def prepare(f):
        state = dot_tn(pack_left(noisy_ref[f]), pw_scr[...]) + bias_ref[...]
        normed, _ = layer_stats(state)
        shift = mod_ref[f, :, 0:width]
        scl = mod_ref[f, :, width : 2 * width]
        lows[f] = (normed * (1.0 + scl) + shift).astype(low_type)

    def turn(f):
        out = outs[f]
        at = slice(f * ftok, (f + 1) * ftok)
        cosine = cs_ref[...] + tc_ref[f]
        sine = sn_ref[...] + ts_ref[f]
        for part, ref, mult in ((0, q_ref, scale), (1, k_ref, 1.0)):
            first = out[:, part * local : part * local + half]
            second = out[:, part * local + half : (part + 1) * local]
            for lanes, value in (
                (slice(0, half), first * cosine - second * sine),
                (slice(half, local), second * cosine + first * sine),
            ):
                ref[at, lanes] = (value.astype(low_type).astype(wide) * mult).astype(low_type)
        v_ref[at, :] = out[:, 2 * local : 3 * local].astype(low_type)

    prepare(0)
    for f in range(count):
        outs[f] = dot_nt(lows[f], wq_scr[...])
        if f + 1 < count:
            prepare(f + 1)
        if f > 0:
            turn(f - 1)
    turn(count - 1)


def embed_qkv(noisy_t, pw, bias, mod, w_local, tables, tcos, tsin, scale):
    frames, patch, ftok = noisy_t.shape
    width = pw.shape[1]
    local = w_local.shape[0] // 3
    cs, sn, _, _, sel = tables
    tokens = frames * ftok
    step = math.gcd(frames, 3)
    full = lambda shape: pl.BlockSpec(shape, lambda i: (0,) * len(shape))
    row = lambda cols: pl.BlockSpec((step * ftok, cols), lambda i: (i, 0))
    return pl.pallas_call(
        partial(embed_qkv_kernel, width=width, local=local, scale=scale),
        grid=(frames // step,),
        in_specs=[
            pl.BlockSpec((step, patch, ftok), lambda i: (i, 0, 0)),
            full(pw.shape),
            full((1, width)),
            pl.BlockSpec((step, 1, 6 * width), lambda i: (i, 0, 0)),
            full(w_local.shape),
            full(sel.shape),
            full(cs.shape),
            full(sn.shape),
            pl.BlockSpec((step, 1, local // 2), lambda i: (i, 0, 0)),
            pl.BlockSpec((step, 1, local // 2), lambda i: (i, 0, 0)),
        ],
        out_specs=[row(local), row(local), row(local)],
        out_shape=[
            jax.ShapeDtypeStruct((tokens, local), low_type),
            jax.ShapeDtypeStruct((tokens, local), low_type),
            jax.ShapeDtypeStruct((tokens, local), low_type),
        ],
        scratch_shapes=[
            pltpu.VMEM(w_local.shape, low_type),
            pltpu.VMEM((6 * patch, width), low_type),
        ],
        compiler_params=pltpu.CompilerParams(
            dimension_semantics=("arbitrary",), vmem_limit_bytes=24 * MIB
        ),
        cost_estimate=pl.CostEstimate(
            flops=2 * tokens * width * 3 * local, bytes_accessed=12 * MIB, transcendentals=0
        ),
        name="embed_qkv",
    )(noisy_t, pw, bias, mod, w_local, sel, cs, sn, tcos, tsin)


def attend_kernel(
    st_ref, q_ref, k_ref, v_ref, o_ref, ol_ref, lse_ref, vt_scr, even, odd, *, heads, ftok
):
    i = pl.program_id(0)
    local = q_ref.shape[1]
    hd = local // heads

    @pl.when(i == 0)
    def _():
        for f in range(vt_scr.shape[0]):
            vt_scr[f] = v_ref[f * ftok : (f + 1) * ftok, :].T

    first = st_ref[i]
    query = q_ref[...]
    zero = jnp.zeros_like(query)
    masked = [
        jnp.where(split_mask(query.shape, 1, heads, local // 2, h), query, zero)
        for h in range(heads)
    ]

    def key_rows(j):
        return k_ref[pl.ds(pl.multiple_of(j * ftok, ftok), ftok), :]

    def step(j, here, following, there, carry):
        vt = vt_scr[j]
        key = None if following is None else key_rows(following)
        new, probs, stats = [], [], []

        def attended(g):
            top, total, shrink = stats[g]
            acc = carry[g][2] * shrink + dot_nn(vt[g * hd : (g + 1) * hd, :], probs[g])
            new.append((top, total, acc))

        for h in range(heads):
            if key is not None:
                there[h] = dot_nt(key, masked[h])
            top, total, _ = carry[h]
            s = here[h]
            peak = jnp.max(jnp.max(s.reshape(ftok // 8, 8, ftok), axis=0), axis=0, keepdims=True)
            higher = jnp.maximum(top, peak)
            p = jnp.exp(s - higher)
            shrink = jnp.exp(top - higher)
            total = total * shrink + jnp.sum(p.reshape(ftok // 8, 8, ftok), axis=0)
            probs.append(p.astype(low_type))
            stats.append((higher, total, shrink))
            if h > 0:
                attended(h - 1)
        attended(heads - 1)
        return tuple(new)

    count = i + 1 - first
    key = key_rows(first)
    for h in range(heads):
        even[h] = dot_nt(key, masked[h])

    def pair(t, carry):
        j = first + 2 * t
        carry = step(j, even, j + 1, odd, carry)
        return step(j + 1, odd, jnp.minimum(j + 2, i), even, carry)

    start = tuple(
        (
            jnp.full((1, ftok), -1e30, wide),
            jnp.zeros((8, ftok), wide),
            jnp.zeros((hd, ftok), wide),
        )
        for _ in range(heads)
    )
    carry = lax.fori_loop(0, lax.div(count, 2), pair, start)
    carry = lax.cond(
        lax.rem(count, 2) == 1, lambda c: step(i, even, None, None, c), lambda c: c, carry
    )
    outs, logs = [], []
    for top, total, acc in carry:
        total = jnp.sum(total, axis=0, keepdims=True)
        outs.append(acc * (1.0 / total))
        logs.append(top + jnp.log(total))
    out = jnp.concatenate(outs, axis=0)
    o_ref[0] = out
    ol_ref[...] = out.astype(low_type).T
    lse_ref[0] = jnp.concatenate(logs + [jnp.zeros((8 - heads, ftok), wide)], axis=0)


def attend(starts, q, k, v, frames, heads):
    tokens, local = q.shape
    ftok = tokens // frames
    row = lambda: pl.BlockSpec((ftok, local), lambda i, s: (i, 0))
    return pl.pallas_call(
        partial(attend_kernel, heads=heads, ftok=ftok),
        grid_spec=pltpu.PrefetchScalarGridSpec(
            num_scalar_prefetch=1,
            grid=(frames,),
            in_specs=[row(), once(k.shape), once(v.shape)],
            out_specs=[
                pl.BlockSpec((1, local, ftok), lambda i, s: (i, 0, 0)),
                row(),
                pl.BlockSpec((1, 8, ftok), lambda i, s: (i, 0, 0)),
            ],
            scratch_shapes=[
                pltpu.VMEM((frames, local, ftok), low_type),
                pltpu.VMEM((heads, ftok, ftok), wide),
                pltpu.VMEM((heads, ftok, ftok), wide),
            ],
        ),
        out_shape=[
            jax.ShapeDtypeStruct((frames, local, ftok), wide),
            jax.ShapeDtypeStruct((tokens, local), low_type),
            jax.ShapeDtypeStruct((frames, 8, ftok), wide),
        ],
        compiler_params=pltpu.CompilerParams(
            dimension_semantics=("arbitrary",), vmem_limit_bytes=16 * MIB
        ),
        cost_estimate=pl.CostEstimate(
            flops=40_000_000_000, bytes_accessed=12 * MIB, transcendentals=0
        ),
        name="attend",
    )(starts, q, k, v)


def attend_back_kernel(
    st_ref, q_ref, do_ref, o_ref, lse_ref, k_ref, v_ref, *rest, heads, ftok, scale, begin, last
):
    if begin:
        _, dk_in, dv_in, *rest = rest
    dq_ref, dk_ref, dv_ref, kt_scr, dk_scr, dv_scr, dqt_scr, *slots = rest
    step_id = pl.program_id(0)
    steps = pl.num_programs(0)
    i = step_id + begin
    local = q_ref.shape[1]
    hd = local // heads
    hh = hd // 2
    half = local // 2

    @pl.when(step_id == 0)
    def _():
        for f in range(last):
            kt_scr[f] = k_ref[f * ftok : (f + 1) * ftok, :].T
        if begin:
            dk_scr[...] = dk_in[...]
            dv_scr[...] = dv_in[...]
        else:
            dk_scr[...] = jnp.zeros_like(dk_scr)
            dv_scr[...] = jnp.zeros_like(dv_scr)

    first = st_ref[i]
    query = q_ref[...]
    grad = do_ref[...]
    zero = jnp.zeros_like(query)
    q_mask = [
        jnp.where(split_mask(query.shape, 1, heads, half, h), query, zero) for h in range(heads)
    ]
    g_mask = [
        jnp.where(split_mask(query.shape, 1, heads, None, h), grad, zero) for h in range(heads)
    ]
    prod = grad.T.astype(wide) * o_ref[0]
    delta = [
        jnp.sum(prod[h * hd : (h + 1) * hd, :], axis=0, keepdims=True) for h in range(heads)
    ]
    lse = [lse_ref[0, h : h + 1, :] for h in range(heads)]
    dqt_scr[...] = jnp.zeros_like(dqt_scr)

    def rows(j):
        return pl.ds(pl.multiple_of(j * ftok, ftok), ftok)

    def front(h, key, val, slot):
        s_ref, p_ref = slot
        s_ref[h] = dot_nt(key, q_mask[h])
        p_ref[h] = dot_nt(val, g_mask[h])

    def step(j, here, following, there):
        kt = kt_scr[j]
        if following is not None:
            key, val = k_ref[rows(following), :], v_ref[rows(following), :]
        s_ref, p_ref = here
        probs, d_scores = [], []

        def sums(g):
            kt_g = jnp.concatenate(
                [kt[g * hh : (g + 1) * hh, :], kt[half + g * hh : half + (g + 1) * hh, :]], axis=0
            )
            dqt_scr[g] += dot_nn(kt_g, d_scores[g])
            dv_scr[rows(j), :] += dot_nn(probs[g], g_mask[g])
            dk_scr[rows(j), :] += dot_nn(d_scores[g], q_mask[g])

        for h in range(heads):
            if following is not None:
                front(h, key, val, there)
            p = jnp.exp(s_ref[h] - lse[h])
            d_scores.append((p * (p_ref[h] - delta[h])).astype(low_type))
            probs.append(p.astype(low_type))
            if h > 0:
                sums(h - 1)
        sums(heads - 1)

    even, odd = slots[:2], slots[2:]
    count = i + 1 - first
    key, val = k_ref[rows(first), :], v_ref[rows(first), :]
    for h in range(heads):
        front(h, key, val, even)

    def pair(t, carry):
        j = first + 2 * t
        step(j, even, j + 1, odd)
        step(j + 1, odd, jnp.minimum(j + 2, i), even)
        return carry

    lax.fori_loop(0, lax.div(count, 2), pair, 0)

    @pl.when(lax.rem(count, 2) == 1)
    def _():
        step(i, even, None, None)

    dqt = jnp.concatenate(
        [dqt_scr[h, 0:hh, :] for h in range(heads)] + [dqt_scr[h, hh:hd, :] for h in range(heads)],
        axis=0,
    )
    dq_ref[...] = (dqt * scale).astype(low_type).T

    @pl.when(step_id == steps - 1)
    def _():
        dk_ref[...] = dk_scr[...].astype(dk_ref.dtype)
        dv_ref[...] = dv_scr[...].astype(dv_ref.dtype)


def attend_back(starts, q, grad, out, lse, k, v, sums, begin, last, frames, heads, scale):
    tokens, local = q.shape
    ftok = tokens // frames
    row = lambda cols: pl.BlockSpec((ftok, cols), lambda i, s: (i + begin, 0))
    kind = low_type if last == frames else wide
    return pl.pallas_call(
        partial(attend_back_kernel, heads=heads, ftok=ftok, scale=scale, begin=begin, last=last),
        grid_spec=pltpu.PrefetchScalarGridSpec(
            num_scalar_prefetch=1,
            grid=(last - begin,),
            in_specs=[
                row(local), row(local),
                pl.BlockSpec((1, local, ftok), lambda i, s: (i + begin, 0, 0)),
                pl.BlockSpec((1, 8, ftok), lambda i, s: (i + begin, 0, 0)),
                once(k.shape), once(v.shape),
            ] + ([pl.BlockSpec(memory_space=pl.ANY)] + [once(k.shape)] * 2)[: len(sums)],
            out_specs=[row(local), once(k.shape), once(v.shape)],
            scratch_shapes=[
                pltpu.VMEM((frames, local, ftok), low_type),
                pltpu.VMEM((tokens, local), wide),
                pltpu.VMEM((tokens, local), wide),
                pltpu.VMEM((heads, local // heads, ftok), wide),
            ] + [pltpu.VMEM((heads, ftok, ftok), wide)] * 4,
        ),
        out_shape=[
            jax.ShapeDtypeStruct((tokens, local), low_type),
            jax.ShapeDtypeStruct((tokens, local), kind),
            jax.ShapeDtypeStruct((tokens, local), kind),
        ],
        input_output_aliases={7: 0} if sums else {},
        compiler_params=pltpu.CompilerParams(
            dimension_semantics=("arbitrary",), vmem_limit_bytes=44 * MIB
        ),
        cost_estimate=pl.CostEstimate(
            flops=30_000_000_000, bytes_accessed=16 * MIB, transcendentals=0
        ),
        name="attend_back",
    )(starts, q, grad, out, lse, k, v, *sums)


def post_attend_kernel(
    me_ref, fr_ref, noisy_ref, pw_ref, bias_ref, mod_ref, two_a, two_b, st_ref, br_ref, h_ref,
    full_ref, *, width, maps, skip,
):
    local = fr_ref.shape[2]

    @pl.when(pl.program_id(0) == 0)
    def _():
        rows_out = width // (2 * len(maps))
        for two_ref, other in ((two_a, 0), (two_b, 4)):
            for pos, apart in enumerate(maps):
                dev = jnp.bitwise_xor(me_ref[0], apart + other)
                full_ref[pl.ds(pl.multiple_of(dev * rows_out, rows_out), rows_out), :] = two_ref[
                    pos, skip:, :
                ]

    out_full = full_ref[...]
    state = dot_tn(pack_left(noisy_ref[0]), pack_right(pw_ref[...])) + bias_ref[...]
    branch = dot_nt(fr_ref[0], out_full[:, 0:local])
    for m in range(1, fr_ref.shape[0]):
        branch += dot_nt(fr_ref[m], out_full[:, m * local : (m + 1) * local])
    state = state + mod_ref[0, :, 2 * width : 3 * width] * branch
    normed, _ = layer_stats(state)
    st_ref[...] = state
    br_ref[...] = branch
    h_ref[...] = (
        normed * (1.0 + mod_ref[0, :, 4 * width : 5 * width])
        + mod_ref[0, :, 3 * width : 4 * width]
    ).astype(low_type)


def post_attend(me, framed, noisy_t, pw, bias, mod, part_two, order_two, skip):
    members, tokens, local = framed.shape
    frames, patch, ftok = noisy_t.shape
    width = pw.shape[1]
    part_two = [p.reshape((-1,) + p.shape[-2:]) for p in part_two]
    row = lambda: pl.BlockSpec((ftok, width), lambda i, me: (i, 0))
    return pl.pallas_call(
        partial(post_attend_kernel, width=width, maps=tile_places(order_two), skip=skip),
        grid_spec=pltpu.PrefetchScalarGridSpec(
            num_scalar_prefetch=1,
            grid=(frames,),
            in_specs=[
                pl.BlockSpec((members, ftok, local), lambda i, me: (0, i, 0)),
                pl.BlockSpec((1, patch, ftok), lambda i, me: (i, 0, 0)),
                once(pw.shape),
                once((1, width)),
                pl.BlockSpec((1, 1, 6 * width), lambda i, me: (i, 0, 0)),
            ] + [once(p.shape) for p in part_two],
            out_specs=[row(), row(), row(), once((width, width))],
        ),
        out_shape=[
            jax.ShapeDtypeStruct((tokens, width), wide),
            jax.ShapeDtypeStruct((tokens, width), wide),
            jax.ShapeDtypeStruct((tokens, width), low_type),
            jax.ShapeDtypeStruct((width, width), low_type),
        ],
        compiler_params=pltpu.CompilerParams(
            dimension_semantics=("arbitrary",), vmem_limit_bytes=18 * MIB
        ),
        cost_estimate=pl.CostEstimate(
            flops=2 * tokens * width * width, bytes_accessed=12 * MIB, transcendentals=0
        ),
        name="post_attend",
    )(me, framed, noisy_t, pw, bias, mod, *part_two)


def part_specs(me_block, orders, shapes):
    bits = sorted((n for n in orders[0] if n[0] == "a"), reverse=True) + ["x", "c"]
    specs = []
    for order, shape in zip(orders, shapes):

        def place(n, me, order=order):
            apart = me_block(n, me)
            index = []
            for name in order:
                if name[0] == "z":
                    index.append(0)
                else:
                    index.append(
                        jnp.bitwise_and(
                            lax.shift_right_logical(apart, len(bits) - 1 - bits.index(name)), 1
                        )
                    )
            return tuple(index) + (0, 0)

        block = tuple(2 if n[0] == "z" else 1 for n in order) + shape[-2:]
        specs += [pl.BlockSpec(block, place)] * 2
    return specs


def line_apart(n, me):
    return jnp.bitwise_xor(n, me[0])


def gelu_parts(value):
    k = math.sqrt(2.0 / math.pi)
    square = value * value
    t = jnp.tanh(k * value * (1.0 + 0.044715 * square))
    half = 0.5 * (1.0 + t)
    slope = half + (0.5 * k) * value * (1.0 - t * t) * (1.0 + (3 * 0.044715) * square)
    return value * half, slope


def ff_kernel(
    me_ref, h_ref, st_ref, mod_ref, one_a, one_b, two_a, two_b, three_a, three_b, gain_ref, pw_ref,
    act_ref, slope_ref, mixed_ref, pred_ref, acc_scr, up_scr, down_scr,
    *, width, frames, ftok, layout, places,
):
    n = pl.program_id(0)
    line_rows(
        (up_scr, down_scr), (one_a, one_b, two_a, two_b, three_a, three_b), me_ref, layout, places
    )
    @pl.when(n == 0)
    def _():
        acc_scr[...] = jnp.zeros_like(acc_scr)

    spots = [slice(f * ftok, (f + 1) * ftok) for f in range(frames)]
    hidden = [None] * frames
    acts = [None] * frames

    def activate(f):
        act, slope = gelu_parts(hidden[f])
        acts[f] = act.astype(low_type)
        act_ref[spots[f], :] = acts[f]
        slope_ref[spots[f], :] = slope.astype(low_type)

    for f in range(frames + 2):
        if f < frames:
            hidden[f] = dot_nt(h_ref[spots[f], :], up_scr[...])
        if 0 < f <= frames:
            activate(f - 1)
        if f > 1:
            acc_scr[spots[f - 2], :] += dot_nn(acts[f - 2], down_scr[...])

    @pl.when(n == pl.num_programs(0) - 1)
    def _():
        patch = pw_ref.shape[0]
        head, rest = split_two(pw_ref[...])
        both = jnp.concatenate([head, rest], axis=0)
        for f in range(frames):
            at = slice(f * ftok, (f + 1) * ftok)
            mixed = acc_scr[at, :]
            mixed_ref[at, :] = mixed
            normed, _ = layer_stats(st_ref[at, :] + mod_ref[f, :, 5 * width : 6 * width] * mixed)
            f_high, f_low = split_two(normed * gain_ref[...])
            two = dot_nt(f_high, both)
            one = dot_nt(f_low, head)
            pred_ref[f] = (two[:, :patch] + two[:, patch:] + one).T


def ff_forward(me, h_two, state_one, mod, parts, orders, layout, gain, pw_out, ftok):
    tokens, width = h_two.shape
    steps = 1 << (len(orders[0]) - 1)
    chunk = 4 * sum(rows for _, _, rows in layout[0])
    frames = tokens // ftok
    patch = pw_out.shape[0]
    columns = lambda: pl.BlockSpec((tokens, chunk), lambda n, me: (0, n))
    return pl.pallas_call(
        partial(
            ff_kernel, width=width, frames=frames, ftok=ftok, layout=layout[:2],
            places=[(o.index("z1"), o.index("z0")) for o in orders],
        ),
        grid_spec=pltpu.PrefetchScalarGridSpec(
            num_scalar_prefetch=1,
            grid=(steps,),
            in_specs=[once(h_two.shape), once(state_one.shape), once(mod.shape)]
            + part_specs(line_apart, orders, [p[0].shape for p in parts])
            + [once(gain.shape), once(pw_out.shape)],
            out_specs=[columns(), columns(), once((tokens, width)), once((frames, patch, ftok))],
            scratch_shapes=[
                pltpu.VMEM((tokens, width), wide),
                pltpu.VMEM((chunk, width), low_type),
                pltpu.VMEM((chunk, width), low_type),
            ],
        ),
        out_shape=[
            jax.ShapeDtypeStruct((tokens, chunk * steps), low_type),
            jax.ShapeDtypeStruct((tokens, chunk * steps), low_type),
            jax.ShapeDtypeStruct((tokens, width), wide),
            jax.ShapeDtypeStruct((frames, patch, ftok), wide),
        ],
        compiler_params=pltpu.CompilerParams(
            dimension_semantics=("arbitrary",), vmem_limit_bytes=32 * MIB
        ),
        cost_estimate=pl.CostEstimate(
            flops=4 * tokens * width * chunk * steps, bytes_accessed=40 * MIB, transcendentals=0
        ),
        name="ff_forward",
    )(me, h_two, state_one, mod, *parts[0], *parts[1], *parts[2], gain, pw_out)


def ff_back_kernel(
    me_ref, dp_ref, st_ref, mixed_ref, br_ref, mod_ref, noisy_ref, gain_ref, pw_ref, one_a,
    one_b, two_a, two_b, three_a, three_b, out_ref, slope_ref, dh_ref, dm_ref, db_ref, df_ref,
    small_ref, sums_ref, dmod_ref, ds_scr, acc_scr, up_scr, down_scr,
    *, width, frames, ftok, layout, places,
):
    n = pl.program_id(0)
    line_rows(
        (up_scr, down_scr), (one_a, one_b, two_a, two_b, three_a, three_b), me_ref, layout, places
    )
    patch = pw_ref.shape[0]

    def fold(value):
        return jnp.sum(value.reshape(-1, 8, width), axis=0).sum(axis=0, keepdims=True)

    @pl.when(n == 0)
    def _():
        d_head = jnp.zeros((patch, width), wide)
        d_gain = jnp.zeros((1, width), wide)
        right = pack_right(pw_ref[...])
        for f in range(frames):
            at = slice(f * ftok, (f + 1) * ftok)
            gate = mod_ref[f, :, 5 * width : 6 * width]
            mixed = mixed_ref[at, :]
            normed, rstd = layer_stats(st_ref[at, :] + gate * mixed)
            d_pred = dp_ref[f]
            d_final = dot_tn(pack_left(d_pred), right)
            d_head += thin_product(d_pred, normed * gain_ref[...])
            d_gain += fold(d_final * normed)
            d_state = layer_back(normed, rstd, d_final * gain_ref[...])
            ds_scr[at, :] = d_state
            dmod_ref[f, 3:4, :] = fold(d_state * mixed)
            dm_ref[at, :] = (d_state * gate).astype(low_type)
        small_ref[0] = d_head
        sums_ref[0:1, :] = d_gain

    @pl.when(n == 0)
    def _():
        acc_scr[...] = jnp.zeros_like(acc_scr)

    spots = [slice(f * ftok, (f + 1) * ftok) for f in range(frames)]
    d_acts = [None] * frames
    for f in range(frames + 1):
        if f < frames:
            d_acts[f] = dot_nt(dm_ref[spots[f], :], down_scr[...])
        if f > 0:
            at = spots[f - 1]
            d_hidden = (d_acts[f - 1] * slope_ref[at, :].astype(wide)).astype(low_type)
            dh_ref[at, :] = d_hidden
            acc_scr[at, :] += dot_nn(d_hidden, up_scr[...])

    @pl.when(n == pl.num_programs(0) - 1)
    def _():
        out_full = out_ref[...]
        d_embed = jnp.zeros((patch, width), wide)
        d_bias = jnp.zeros((1, width), wide)
        local = df_ref.shape[2]
        for f in range(frames):
            at = slice(f * ftok, (f + 1) * ftok)
            normed, rstd = layer_stats(st_ref[at, :])
            d_h = acc_scr[at, :]
            dmod_ref[f, 1:2, :] = fold(d_h)
            dmod_ref[f, 2:3, :] = fold(d_h * normed)
            d_state = ds_scr[at, :] + layer_back(
                normed, rstd, d_h * (1.0 + mod_ref[f, :, 4 * width : 5 * width])
            )
            dmod_ref[f, 0:1, :] = fold(d_state * br_ref[at, :])
            d_branch = (d_state * mod_ref[f, :, 2 * width : 3 * width]).astype(low_type)
            db_ref[at, :] = d_branch
            d_framed = dot_nn(d_branch, out_full).astype(low_type)
            for m in range(df_ref.shape[0]):
                df_ref[m, at, :] = d_framed[:, m * local : (m + 1) * local]
            d_embed += thin_product(noisy_ref[f], d_state)
            d_bias += fold(d_state)
        small_ref[1] = d_embed
        sums_ref[1:2, :] = d_bias


def ff_backward(
    me, d_pred, state_one, mixed, branch, mod, noisy_t, gain, pw_out, parts, orders, layout,
    out_full, slope, members,
):
    tokens, width = state_one.shape
    steps = 1 << (len(orders[0]) - 1)
    chunk = 4 * sum(rows for _, _, rows in layout[0])
    frames, patch, ftok = noisy_t.shape
    local = width // members
    columns = lambda: pl.BlockSpec((tokens, chunk), lambda n, me: (0, n))
    return pl.pallas_call(
        partial(
            ff_back_kernel, width=width, frames=frames, ftok=ftok, layout=layout[:2],
            places=[(o.index("z1"), o.index("z0")) for o in orders],
        ),
        grid_spec=pltpu.PrefetchScalarGridSpec(
            num_scalar_prefetch=1,
            grid=(steps,),
            in_specs=[
                once(d_pred.shape),
                once(state_one.shape),
                once(state_one.shape),
                once(state_one.shape),
                once(mod.shape),
                once(noisy_t.shape),
                once(gain.shape),
                once(pw_out.shape),
            ]
            + part_specs(line_apart, orders, [p[0].shape for p in parts])
            + [once(out_full.shape), columns()],
            out_specs=[
                columns(),
                once((tokens, width)),
                once((tokens, width)),
                once((members, tokens, local)),
                once((2, patch, width)),
                once((2, width)),
                once((frames, 4, width)),
            ],
            scratch_shapes=[
                pltpu.VMEM((tokens, width), wide),
                pltpu.VMEM((tokens, width), wide),
                pltpu.VMEM((chunk, width), low_type),
                pltpu.VMEM((chunk, width), low_type),
            ],
        ),
        out_shape=[
            jax.ShapeDtypeStruct((tokens, chunk * steps), low_type),
            jax.ShapeDtypeStruct((tokens, width), low_type),
            jax.ShapeDtypeStruct((tokens, width), low_type),
            jax.ShapeDtypeStruct((members, tokens, local), low_type),
            jax.ShapeDtypeStruct((2, patch, width), wide),
            jax.ShapeDtypeStruct((2, width), wide),
            jax.ShapeDtypeStruct((frames, 4, width), wide),
        ],
        compiler_params=pltpu.CompilerParams(
            dimension_semantics=("arbitrary",), vmem_limit_bytes=42 * MIB
        ),
        cost_estimate=pl.CostEstimate(
            flops=4 * tokens * width * chunk * steps, bytes_accessed=40 * MIB, transcendentals=0
        ),
        name="ff_backward",
    )(
        me, d_pred, state_one, mixed, branch, mod, noisy_t, gain, pw_out, *parts[0], *parts[1],
        *parts[2], out_full, slope,
    )


def wide_grads_kernel(
    me_ref, dh_ref, act_ref, db_ref, h_ref, dm_ref, fr_ref, *outs, spans, places, narrow, half
):
    *outs, scr = outs
    adds, outs = outs[: len(outs) - len(spans)], outs[len(outs) - len(spans) :]
    up = dot_tn(dh_ref[...], h_ref[...])
    down = dot_tn(act_ref[...], dm_ref[...])
    left = db_ref[...]
    out = jnp.concatenate([dot_tn(left, fr_ref[m]) for m in range(fr_ref.shape[0])], axis=1)
    if narrow < left.shape[1]:
        scr[...] = out
        block = jnp.bitwise_xor(me_ref[0], 2 * pl.program_id(0) + half)
        at = lax.rem(block, left.shape[1] // narrow) * narrow
        out = scr[pl.ds(pl.multiple_of(at, narrow), narrow), :]
    my_z = me_ref[1]
    for zz in range(4):
        pieces = [
            arr[zz * (arr.shape[0] // 4) : (zz + 1) * (arr.shape[0] // 4)] for arr in (up, down, out)
        ]
        whole = jnp.concatenate(pieces, axis=0)
        apart = jnp.bitwise_xor(my_z, zz)
        for k, (ref, (begin, end), (dim_one, dim_zero)) in enumerate(zip(outs, spans, places)):
            index = [0] * (len(ref.shape) - 2)
            index[dim_one] = lax.shift_right_logical(apart, 1)
            index[dim_zero] = jnp.bitwise_and(apart, 1)
            part = whole[begin:end]
            if adds:
                part = part + adds[k][tuple(index)].astype(wide)
            ref[tuple(index)] = part.astype(ref.dtype)


def wide_grads(me, half, d_hidden, act, d_branch, h_two, d_mixed, framed, orders, devices, adds=()):
    tokens, width = h_two.shape
    members, _, local = framed.shape
    chunk = act.shape[1] // (devices // 4)
    out_chunk = width // (devices // 4)
    out_wide = max(out_chunk, 128)
    bits = sorted((n for n in orders[0] if n[0] == "a"), reverse=True) + ["x"]
    rows_dev = (2 * chunk + out_chunk) // 4
    part_rows = rows_dev // 3
    spans = [(k * part_rows, (k + 1) * part_rows) for k in range(3)]

    def block(q, me):
        return jnp.bitwise_xor(me[0], 2 * q + half)

    def out_spec(order):
        def place(q, me):
            index = []
            for name in order:
                if name[0] in "ax":
                    index.append(
                        jnp.bitwise_and(
                            lax.shift_right_logical(q, len(bits) - 1 - bits.index(name)), 1
                        )
                    )
                else:
                    index.append(0)
            return tuple(index) + (0, 0)

        shape = tuple(1 if n[0] in "ax" else 2 for n in order) + (part_rows, width)
        return pl.BlockSpec(shape, place)

    return pl.pallas_call(
        partial(
            wide_grads_kernel,
            spans=spans,
            places=[(o.index("z1"), o.index("z0")) for o in orders],
            narrow=out_chunk,
            half=half,
        ),
        grid_spec=pltpu.PrefetchScalarGridSpec(
            num_scalar_prefetch=1,
            grid=(devices // 8,),
            in_specs=[
                pl.BlockSpec((tokens, chunk), lambda q, me: (0, block(q, me))),
                pl.BlockSpec((tokens, chunk), lambda q, me: (0, block(q, me))),
                pl.BlockSpec(
                    (tokens, out_wide),
                    lambda q, me: (0, lax.div(block(q, me), out_wide // out_chunk)),
                ),
                once(h_two.shape),
                once(d_mixed.shape),
                once(framed.shape),
            ] + [out_spec(o) for o in orders][: len(adds)],
            out_specs=[out_spec(o) for o in orders],
            scratch_shapes=[pltpu.VMEM((out_wide, width), wide)],
        ),
        out_shape=[
            jax.ShapeDtypeStruct((2,) * len(o) + (part_rows, width), low_type) for o in orders
        ],
        compiler_params=pltpu.CompilerParams(
            dimension_semantics=("arbitrary",), vmem_limit_bytes=36 * MIB
        ),
        cost_estimate=pl.CostEstimate(
            flops=2 * tokens * width * (2 * chunk + out_chunk) * (devices // 8),
            bytes_accessed=24 * MIB, transcendentals=0,
        ),
        name="wide_grads",
    )(me, d_hidden, act, d_branch, h_two, d_mixed, framed, *adds)


def qkv_back_kernel(
    me_ref, dq_ref, dk_ref, dv_ref, noisy_ref, pw_ref, bias_ref, mod_ref, w_ref, sel_ref,
    cs_ref, sn_ref, tc_ref, ts_ref, *refs, width, local, maps, begin, last,
):
    i = pl.program_id(0)
    if begin:
        dw_in, demb_in, dbias_in, *refs = refs
    *dw_refs, dmod_ref, demb_ref, dbias_ref, acc_scr, emb_scr, bias_scr, pw_scr = refs

    @pl.when(i == 0)
    def _():
        pw_scr[...] = pack_right(pw_ref[...])
        bias_scr[...] = jnp.zeros_like(bias_scr)
        if begin:
            acc_scr[...] = dw_in[...]
            emb_scr[...] = demb_in[...]
            bias_scr[0:1, :] = dbias_in[...]
        else:
            acc_scr[...] = jnp.zeros_like(acc_scr)
            emb_scr[...] = jnp.zeros_like(emb_scr)

    ftok = cs_ref.shape[0]
    half = local // 2
    count = noisy_ref.shape[0]
    grads, hs, stats = [None] * count, [None] * count, [None] * count

    def turn(f):
        at = slice(f * ftok, (f + 1) * ftok)
        cosine = cs_ref[...] + tc_ref[f]
        sine = sn_ref[...] + ts_ref[f]
        parts = []
        for ref in (dq_ref, dk_ref):
            first = ref[at, 0:half].astype(wide)
            second = ref[at, half:local].astype(wide)
            turned = jnp.concatenate(
                [first * cosine + second * sine, second * cosine - first * sine], axis=1
            ).astype(low_type)
            parts.append(dot_nn(turned, sel_ref[...]).astype(low_type))
        parts.append(dv_ref[at, :])
        grads[f] = jnp.concatenate(parts, axis=1)

    def prepare(f):
        state = dot_tn(pack_left(noisy_ref[f]), pw_scr[...]) + bias_ref[...]
        normed, rstd = layer_stats(state)
        scl = mod_ref[f, :, width : 2 * width]
        hs[f] = (normed * (1.0 + scl) + mod_ref[f, :, 0:width]).astype(low_type)
        stats[f] = (normed, rstd, scl)

    def finish(f, d_h):
        normed, rstd, scl = stats[f]
        dmod_ref[f, :, 0:width] = jnp.sum(d_h, axis=0, keepdims=True)
        dmod_ref[f, :, width : 2 * width] = jnp.sum(d_h * normed, axis=0, keepdims=True)
        d_state = layer_back(normed, rstd, d_h * (1.0 + scl))
        emb_scr[...] += thin_product(noisy_ref[f], d_state)
        bias_scr[...] += jnp.sum(d_state.reshape(-1, 8, width), axis=0)

    turn(0)
    for f in range(count):
        d_h = dot_nn(grads[f], w_ref[...])
        prepare(f)
        acc_scr[...] += dot_tn(grads[f], hs[f])
        if f + 1 < count:
            turn(f + 1)
        finish(f, d_h)

    @pl.when(i == pl.num_programs(0) - 1)
    def _():
        demb_ref[...] = emb_scr[...]
        dbias_ref[...] = jnp.sum(bias_scr[...], axis=0, keepdims=True)
        if not last:
            dw_refs[0][...] = acc_scr[...]
            return
        rows = acc_scr.shape[0] // len(maps[0])
        at = 0
        for ref, places in zip(dw_refs, maps):
            count = ref.shape[1]
            for pos, apart in enumerate(places):
                dev = jnp.bitwise_xor(me_ref[0], apart)
                begin = pl.multiple_of(dev * rows + at, 8)
                ref[pos] = acc_scr[pl.ds(begin, count), :].astype(ref.dtype)
            at += count


def near_places(order):
    natural = sorted((n for n in order if n[0] == "a"), reverse=True) + ["z1", "z0"]
    places = []
    for pos in range(1 << len(order)):
        value = 0
        for d, name in enumerate(order):
            if (pos >> (len(order) - 1 - d)) & 1:
                value |= 1 << (len(natural) - 1 - natural.index(name))
        places.append(value)
    return places


def qkv_back(me, orders, dq, dk, dv, noisy_t, pw, bias, mod, w_local, tables, tcos, tsin, sums, begin, last):
    frames, patch, ftok = noisy_t.shape
    tokens, local = dq.shape
    width = pw.shape[1]
    cs, sn, _, _, sel = tables
    step = math.gcd(math.gcd(begin, last), 3)
    at = begin // step
    count = 1 << len(orders[0])
    rows = w_local.shape[0] // count
    first = -(-rows // 16) * 8
    blocks = [(count, first, width), (count, rows - first, width)]
    if last < frames:
        blocks = [w_local.shape]
    full = lambda shape: pl.BlockSpec(shape, lambda i, me: (0,) * len(shape))
    row = lambda cols: pl.BlockSpec((step * ftok, cols), lambda i, me: (i + at, 0))
    return pl.pallas_call(
        partial(
            qkv_back_kernel, width=width, local=local, maps=[near_places(o) for o in orders],
            begin=begin, last=last == frames,
        ),
        grid_spec=pltpu.PrefetchScalarGridSpec(num_scalar_prefetch=1, grid=((last - begin) // step,),
        in_specs=[
            row(local), row(local), row(local),
            pl.BlockSpec((step, patch, ftok), lambda i, me: (i + at, 0, 0)),
            full(pw.shape),
            full((1, width)),
            pl.BlockSpec((step, 1, 6 * width), lambda i, me: (i + at, 0, 0)),
            full(w_local.shape),
            full(sel.shape),
            full(cs.shape),
            full(sn.shape),
            pl.BlockSpec((step, 1, local // 2), lambda i, me: (i + at, 0, 0)),
            pl.BlockSpec((step, 1, local // 2), lambda i, me: (i + at, 0, 0)),
        ] + [full(a.shape) for a in sums],
        out_specs=[
            *(full(b) for b in blocks),
            pl.BlockSpec((step, 1, 2 * width), lambda i, me: (i, 0, 0)),
            full(pw.shape),
            full((1, width)),
        ],
        scratch_shapes=[
            pltpu.VMEM(w_local.shape, wide),
            pltpu.VMEM(pw.shape, wide),
            pltpu.VMEM((8, width), wide),
            pltpu.VMEM((6 * patch, width), low_type),
        ],
        ),
        out_shape=[
            *(jax.ShapeDtypeStruct(b, low_type if last == frames else wide) for b in blocks),
            jax.ShapeDtypeStruct((last - begin, 1, 2 * width), wide),
            jax.ShapeDtypeStruct(pw.shape, wide),
            jax.ShapeDtypeStruct((1, width), wide),
        ],
        compiler_params=pltpu.CompilerParams(
            dimension_semantics=("arbitrary",), vmem_limit_bytes=32 * MIB
        ),
        cost_estimate=pl.CostEstimate(
            flops=2 * 2 * tokens * width * 3 * local, bytes_accessed=16 * MIB, transcendentals=0
        ),
        name="qkv_back",
    )(me, dq, dk, dv, noisy_t, pw, bias, mod, w_local, sel, cs, sn, tcos, tsin, *sums)


def tri_blocks(count):
    return [(r, c) for r in range(count) for c in range(r, count)]


def tile_places(order):
    natural = sorted((n for n in order if n[0] == "a"), reverse=True) + ["x", "c", "z1", "z0"]
    places = []
    for pos in range(1 << len(order)):
        value = 0
        for d, name in enumerate(order):
            if (pos >> (len(order) - 1 - d)) & 1:
                value |= 1 << (len(natural) - 1 - natural.index(name))
        places.append(value)
    return places


def steer_kernel(
    tab_ref, clip_ref, *refs, blk, cuts, maps, rows
):
    mats = len(rows)
    arrived, sums = refs[:3], refs[3:6]
    olds, refs = refs[6 : 6 + mats], refs[6 + mats :]
    news, u_ref = refs[:mats], refs[mats]
    outs, scr = refs[mats + 1 : -1], refs[-1]
    clip = clip_ref[0]
    me = tab_ref[12]
    width = u_ref.shape[2]
    units = []
    for slot in range(3):
        source = tab_ref[9 + slot]
        units.append(
            jnp.where(
                source == 0, arrived[0][...], jnp.where(source == 1, arrived[1][...], arrived[2][...])
            )
        )
    whole = jnp.concatenate([ref[...] for ref in sums], axis=0)
    up, down, out = rows[2], rows[3], rows[1]
    grads = (
        jnp.concatenate(units, axis=0), whole[up + down :], whole[:up], whole[up : up + down]
    )
    low = []
    for m in range(mats):
        grad = clip * grads[m]
        moment = 0.95 * olds[m][...] + grad
        news[m][...] = moment
        steer = grad + 0.95 * moment
        u_ref[m, : rows[m], :] = steer
        if rows[m] < u_ref.shape[1]:
            u_ref[m, rows[m] :, :] = jnp.zeros((u_ref.shape[1] - rows[m], width), wide)
        low.append(steer.astype(low_type))
    pairs = tri_blocks(width // blk)
    clusters = len(maps[0]) // 32
    for n, (r, c) in enumerate(pairs):
        for m in range(mats):
            scr[m] = dot_tn(low[m][:, r * blk : (r + 1) * blk], low[m][:, c * blk : (c + 1) * blk])
        for m in range(mats // clusters):
            index = m * len(pairs) + n
            for part, ref in enumerate(outs):
                if cuts[part] <= index < cuts[part + 1]:
                    inner = index - cuts[part]
                    for pos, apart in enumerate(maps[part]):
                        which, top, left = tile_of(jnp.bitwise_xor(me, apart), mats // clusters, blk)
                        ref[pos, inner * 16 : (inner + 1) * 16, :] = scr[
                            which + m, pl.ds(pl.multiple_of(top, 16), 16),
                            pl.ds(pl.multiple_of(left, blk // 2), blk // 2),
                        ].astype(ref.dtype)


def tile_of(dev, mats_each, blk):
    return (
        lax.shift_right_logical(dev, 5) * mats_each,
        jnp.bitwise_and(lax.shift_right_logical(dev, 1), 15) * 16,
        jnp.bitwise_and(dev, 1) * (blk // 2),
    )


def steer_grams(table, clip, arrived, sums, moments, blk, cuts, orders, devices):
    width = moments[0].shape[1]
    rows = [m.shape[0] for m in moments]
    maps = [tile_places(o) for o in orders]
    shapes = [(devices, (cuts[k + 1] - cuts[k]) * 16, blk // 2) for k in range(len(orders))]
    steer_shape = (len(rows), max(rows), width)
    results = pl.pallas_call(
        partial(steer_kernel, blk=blk, cuts=cuts, maps=maps, rows=rows),
        grid_spec=pltpu.PrefetchScalarGridSpec(
            num_scalar_prefetch=2,
            grid=(1,),
            in_specs=[once(a.shape) for a in (*arrived, *sums, *moments)],
            out_specs=[once(m.shape) for m in moments]
            + [once(steer_shape)]
            + [once(s) for s in shapes],
            scratch_shapes=[pltpu.VMEM((len(rows), blk, blk), wide)],
        ),
        out_shape=[jax.ShapeDtypeStruct(m.shape, wide) for m in moments]
        + [jax.ShapeDtypeStruct(steer_shape, wide)]
        + [jax.ShapeDtypeStruct(s, low_type) for s in shapes],
        compiler_params=pltpu.CompilerParams(
            dimension_semantics=("arbitrary",), vmem_limit_bytes=24 * MIB
        ),
        name="steer_grams",
    )(table, clip, *arrived, *sums, *moments)
    return results[:4], results[4], results[5:]


def home_kernel(tab_ref, one_ref, two_ref, *refs):
    outs, sq_ref = refs[:3], refs[3]
    rows = outs[0].shape[0]
    whole = jnp.concatenate([one_ref[...], two_ref[...]], axis=0)
    pieces = [whole[n * rows : (n + 1) * rows] for n in range(3)]
    for color in range(3):
        slot = tab_ref[6 + color]
        outs[color][...] = jnp.where(
            slot == 0, pieces[0], jnp.where(slot == 1, pieces[1], pieces[2])
        )
    sq_ref[...] = jnp.sum(whole * whole, keepdims=True)


def home_units(table, one, two):
    rows = (one.shape[0] + two.shape[0]) // 3
    width = one.shape[1]
    piece = (rows, width)
    *pieces, squares = pl.pallas_call(
        home_kernel,
        grid_spec=pltpu.PrefetchScalarGridSpec(
            num_scalar_prefetch=1,
            grid=(1,),
            in_specs=[once(one.shape), once(two.shape)],
            out_specs=[once(piece)] * 3 + [once((1, 1))],
        ),
        out_shape=[jax.ShapeDtypeStruct(piece, wide)] * 3 + [jax.ShapeDtypeStruct((1, 1), wide)],
        compiler_params=pltpu.CompilerParams(
            dimension_semantics=("arbitrary",), vmem_limit_bytes=16 * MIB
        ),
        name="home_units",
    )(table, one, two)
    return pieces, squares[0, 0]


def polish_kernel(me_ref, u_ref, *refs, blk, cuts, maps, factors):
    mats, rows, width = u_ref.shape
    parts, olds, outs, g_scr = refs[: 2 * len(maps)], refs[2 * len(maps) : -mats - 1], refs[-mats - 1 : -1], refs[-1]
    pairs = tri_blocks(width // blk)
    me = me_ref[0]
    clusters = len(maps[0]) // 16
    diag = lax.broadcasted_iota(jnp.int32, (blk, blk), 0) == lax.broadcasted_iota(
        jnp.int32, (blk, blk), 1
    )
    for m in range(mats // clusters):
        for n, (r, c) in enumerate(pairs):
            index = m * len(pairs) + n
            for part, places in enumerate(maps):
                if not cuts[part] <= index < cuts[part + 1]:
                    continue
                inner = index - cuts[part]
                for ref, other in ((parts[2 * part], 0), (parts[2 * part + 1], 4)):
                    for pos, apart in enumerate(places):
                        which, top, left = tile_of(
                            jnp.bitwise_xor(me, apart + other), mats // clusters, blk
                        )
                        g_scr[
                            which + m, pl.ds(pl.multiple_of(r * blk + top, 16), 16),
                            pl.ds(pl.multiple_of(c * blk + left, blk // 2), blk // 2),
                        ] = ref[pos, inner * 16 : (inner + 1) * 16, :]
    for m in range(mats):
        trace = jnp.zeros((1, 1), wide)
        for r, c in pairs:
            piece = g_scr[m, r * blk : (r + 1) * blk, c * blk : (c + 1) * blk]
            if r == c:
                trace += jnp.sum(jnp.where(diag, piece.astype(wide), 0.0), keepdims=True)
            else:
                g_scr[m, c * blk : (c + 1) * blk, r * blk : (r + 1) * blk] = piece.T
        scale = jnp.sqrt(trace) + 1e-07
        inverse = 1.0 / scale
        inverse_sq = inverse * inverse
        own = outs[m].shape[0]

        def times(value):
            return dot_nn(value.astype(low_type), g_scr[m]) * inverse_sq

        def cubic(value):
            once_ = times(value)
            return coef_one * value + coef_two * once_ + coef_three * times(once_)

        current = cubic(u_ref[m, :own, :] * inverse)
        for _ in range(NS_ITERS - 1):
            second = cubic(cubic(times(current)))
            third = cubic(cubic(times(second)))
            current = coef_one * current + coef_two * second + coef_three * third
        outs[m][...] = olds[m][...] * (1.0 - 2.0 * 0.01) - factors[m] * current


def polish(me, u, parts, olds, blk, cuts, orders, factors):
    mats, rows, width = u.shape
    maps = [tile_places(o) for o in orders]
    return pl.pallas_call(
        partial(polish_kernel, blk=blk, cuts=cuts, maps=maps, factors=factors),
        grid_spec=pltpu.PrefetchScalarGridSpec(
            num_scalar_prefetch=1,
            grid=(1,),
            in_specs=[once(u.shape)] + [once(p.shape) for p in parts] + [once(o.shape) for o in olds],
            out_specs=[once(o.shape) for o in olds],
            scratch_shapes=[pltpu.VMEM((mats, width, width), low_type)],
        ),
        out_shape=[jax.ShapeDtypeStruct(o.shape, wide) for o in olds],
        compiler_params=pltpu.CompilerParams(
            dimension_semantics=("arbitrary",), vmem_limit_bytes=32 * MIB
        ),
        cost_estimate=pl.CostEstimate(
            flops=2 * 24 * mats * rows * width * width, bytes_accessed=12 * MIB, transcendentals=0
        ),
        name="polish",
    )(me, u, *parts, *olds)


def bit_stages(count_a):
    stages = {}
    bits_a = count_a.bit_length() - 1
    for b in range(bits_a):
        stages["a%d" % (bits_a - 1 - b)] = ("a", 1 << (bits_a - 1 - b), b)
    stages["x"] = ("x", 1, bits_a)
    stages["c"] = ("c", 1, bits_a + 1)
    stages["z1"] = ("z", 2, bits_a + 2)
    stages["z0"] = ("z", 1, bits_a + 3)
    return stages


def swap(value, axis, distance):
    size = lax.axis_size(axis)
    return lax.ppermute(value, axis, [(i, i ^ distance) for i in range(size)])


def bit_of(axis, distance):
    return (lax.axis_index(axis) // distance) % 2


def in_order(blocks, names):
    for dim, name in enumerate(names):
        axis = name[0]
        distance = {"z1": 2, "a1": 2, "a2": 4}.get(name, 1)
        mine = bit_of(axis, distance)
        flipped = jnp.flip(blocks, dim)
        blocks = jnp.where(mine == 0, blocks, flipped)
    natural = sorted(n for n in names if n[0] == "a")[::-1] + [
        n for n in ("x", "c", "z1", "z0") if n in names
    ]
    order = [names.index(n) for n in natural] + list(range(len(names), blocks.ndim))
    return blocks.transpose(order)


def three_orders(stages):
    names_a = [n for n in stages if n.startswith("a")]
    return (
        ["x"] + names_a + ["z0", "z1"],
        names_a + ["z0", "x", "z1"],
        ["z0", "x"] + names_a + ["z1"],
    )


def after(value, *others):
    return lax.optimization_barrier((value,) + others)[0]


def halve(blocks, order, stages):
    keep, send = blocks[0], blocks[1]
    for step, name in enumerate(order):
        axis, distance, _ = stages[name]
        got = swap(send.astype(low_type), axis, distance)
        if step == len(order) - 1:
            return keep.astype(wide) + got.astype(wide)
        send = (keep[1].astype(wide) + got[1].astype(wide)).astype(low_type)
        keep = keep[0].astype(wide) + got[0].astype(wide)


class Ladder:
    def __init__(self, blocks, orders, stages):
        self.orders, self.stages, self.rung = orders, stages, 0
        self.keep = [b[0] for b in blocks]
        self.send = [b[1] for b in blocks]

    def exchange(self):
        self.got = []
        for order, send in zip(self.orders, self.send):
            axis, distance, _ = self.stages[order[self.rung]]
            self.got.append(swap(send.astype(low_type), axis, distance))
        self.rung += 1

    def add(self, *first):
        got = lax.optimization_barrier(tuple(self.got) + first)[: len(self.got)]
        pairs = list(zip(self.keep, got))
        if self.rung == len(self.orders[0]):
            return [k.astype(wide) + g.astype(wide) for k, g in pairs]
        self.send = [(k[1].astype(wide) + g[1].astype(wide)).astype(low_type) for k, g in pairs]
        self.keep = [k[0].astype(wide) + g[0].astype(wide) for k, g in pairs]


def double(block, order, stages):
    for name in order:
        axis, distance, _ = stages[name]
        block = jnp.stack([block, swap(block, axis, distance)])
    return block


def spread(payload):
    count = math.prod(lax.axis_size(n) for n in ALL)
    return lax.all_to_all(
        jnp.broadcast_to(payload[None], (count,) + payload.shape),
        ALL, split_axis=0, concat_axis=0, tiled=True,
    )


def unit_plan(devices):
    quarter = devices // 4
    edges = []
    for unit in range(3 * devices):
        section, place = unit // devices, unit % devices
        member, rest = place // quarter, place % quarter
        index = section * quarter + rest
        pos, slot = index // 3, index % 3
        a, z = pos // 4, pos % 4
        dest = ((a * 2 + member // 2) * 2 + member % 2) * 4 + z
        edges.append((unit // 3, unit % 3, dest, slot))
    left = list(edges)
    colors = []
    for _ in range(3):
        match = {}

        def augment(src, seen):
            for e in left:
                if e[0] != src or e[2] in seen:
                    continue
                seen.add(e[2])
                if e[2] not in match or augment(match[e[2]][0], seen):
                    match[e[2]] = e
                    return True
            return False

        for src in range(devices):
            assert augment(src, set())
        chosen = list(match.values())
        for e in chosen:
            left.remove(e)
        colors.append(chosen)
    return colors


def unit_tables(plan):
    devices = len(plan[0])
    tables = np.zeros((devices, 2, 2, 3), np.int32)
    for color, chosen in enumerate(plan):
        for src, src_slot, dst, dst_slot in chosen:
            tables[src, 0, 0, color], tables[dst, 0, 1, dst_slot] = src_slot, color
            tables[dst, 1, 0, color], tables[src, 1, 1, src_slot] = dst_slot, color
    return tables.reshape(devices, 12)


def away_kernel(tab_ref, w_ref, *outs):
    rows = outs[0].shape[0]
    whole = w_ref[...].astype(low_type)
    pieces = [whole[n * rows : (n + 1) * rows] for n in range(3)]
    for color in range(3):
        slot = tab_ref[color]
        outs[color][...] = jnp.where(
            slot == 0, pieces[0], jnp.where(slot == 1, pieces[1], pieces[2])
        )


def away_units(table, weight):
    piece = (weight.shape[0] // 3, weight.shape[1])
    return pl.pallas_call(
        away_kernel,
        grid_spec=pltpu.PrefetchScalarGridSpec(
            num_scalar_prefetch=1,
            grid=(1,),
            in_specs=[once(weight.shape)],
            out_specs=[once(piece)] * 3,
        ),
        out_shape=[jax.ShapeDtypeStruct(piece, low_type)] * 3,
        compiler_params=pltpu.CompilerParams(
            dimension_semantics=("arbitrary",), vmem_limit_bytes=16 * MIB
        ),
        name="away_units",
    )(table, weight)


def place_kernel(tab_ref, *refs):
    pieces, out_ref = refs[:3], refs[3]
    rows = pieces[0].shape[0]
    for slot in range(3):
        source = tab_ref[3 + slot]
        out_ref[slot * rows : (slot + 1) * rows, :] = jnp.where(
            source == 0, pieces[0][...], jnp.where(source == 1, pieces[1][...], pieces[2][...])
        )


def place_units(table, pieces):
    rows, width = pieces[0].shape
    return pl.pallas_call(
        place_kernel,
        grid_spec=pltpu.PrefetchScalarGridSpec(
            num_scalar_prefetch=1,
            grid=(1,),
            in_specs=[once((rows, width))] * 3,
            out_specs=once((3 * rows, width)),
        ),
        out_shape=jax.ShapeDtypeStruct((3 * rows, width), low_type),
        compiler_params=pltpu.CompilerParams(
            dimension_semantics=("arbitrary",), vmem_limit_bytes=16 * MIB
        ),
        name="place_units",
    )(table, *pieces)


def send_units(pieces, plan, back):
    src, dst = (2, 0) if back else (0, 2)
    return [
        lax.ppermute(piece, ALL, [(e[src], e[dst]) for e in chosen])
        for piece, chosen in zip(pieces, plan)
    ]


def body(
    noisy_latents,
    target_latents,
    noise_levels,
    clip_start,
    qkv_weight,
    qkv_moment,
    out_weight,
    out_moment,
    up_weight,
    up_moment,
    down_weight,
    down_moment,
    ada_weight,
    ada_first,
    ada_second,
    patch_weight,
    patch_first,
    patch_second,
    vectors,
    vec_first,
    vec_second,
):
    count_a = lax.axis_size("a")
    members = lax.axis_size("x") * lax.axis_size("c")
    devices = count_a * members * lax.axis_size("z")
    groups = count_a * lax.axis_size("z")
    frames_dev = noise_levels.shape[0]
    tokens_dev = noisy_latents.shape[0]
    frame_tok = tokens_dev // frames_dev
    width = patch_weight.shape[2]
    patch_size = patch_weight.shape[1]
    head_dim = width // HEADS
    local_heads = HEADS // members
    local = local_heads * head_dim
    group_frames = frames_dev * members
    frames_all = frames_dev * devices
    group_tokens = group_frames * frame_tok
    score_scale = 1.0 / math.sqrt(head_dim)
    stages = bit_stages(count_a)
    my_a, my_z = lax.axis_index("a"), lax.axis_index("z")
    my_group = my_a * 4 + my_z
    my_member = lax.axis_index("x") * 2 + lax.axis_index("c")
    tables = rope_tables(head_dim, local_heads, frame_tok)
    tables = tables[:4] + (jnp.asarray(tables[4], low_type),)
    plan = unit_plan(devices)

    rows_unit = qkv_weight.shape[0] // 3
    me = lax.axis_index(ALL).astype(jnp.int32)
    table = jnp.concatenate([jnp.asarray(unit_tables(plan))[me], me[None]])
    units = place_units(table, send_units(away_units(table, qkv_weight), plan, False))
    units = units.reshape(3, rows_unit, width)
    names_a = [n for n in stages if n.startswith("a")]

    swap_axes = ("x", "c", "z")
    moves = [(g * 4 + z, z * 4 + g) for g in range(4) for z in range(4)]
    noisy_t = noisy_latents.T.reshape(patch_size, frames_dev, frame_tok).transpose(1, 0, 2)
    target_t = target_latents.T.reshape(patch_size, frames_dev, frame_tok).transpose(1, 0, 2)
    mine = lax.ppermute(jnp.stack([noisy_t, target_t]), swap_axes, moves)

    meta = jnp.concatenate([noise_levels, clip_start]).astype(wide)
    meta = jnp.pad(meta, (0, 128 - meta.shape[0]))[None]
    meta_all = spread(after(meta, units))[:, 0]
    rows_up, rows_out = up_weight.shape[0], out_weight.shape[0]
    layout = part_layout(rows_up, rows_out)
    rising = [
        ["z1", "z0"] + names_a[::-1] + ["x"],
        ["z1", "x", "z0"] + names_a[::-1],
        ["z1"] + names_a[::-1] + ["x", "z0"],
    ]
    gather_orders = [o[::-1] for o in rising]
    rows_part = (2 * rows_up + rows_out) // 3
    bulk = jnp.concatenate([up_weight, down_weight, out_weight], axis=0).astype(low_type)
    shares = [bulk[n * rows_part : (n + 1) * rows_part] for n in range(3)]
    climb = lambda shares, rung: [
        double(share, [order[rung]], stages) for share, order in zip(shares, rising)
    ]
    far = double(units, ["z1"], stages)
    meta_all, far, mine = lax.optimization_barrier((meta_all, far, mine))
    shares = climb([after(share, far) for share in shares], 0)
    levels_all = meta_all[:, :frames_dev].reshape(frames_all)
    starts_all = meta_all[:, frames_dev : 2 * frames_dev].reshape(frames_all)
    starts_group = lax.dynamic_slice_in_dim(starts_all, my_group * group_frames, group_frames)
    starts_int = starts_group.astype(jnp.int32)
    noisy_mine, target_mine = mine[0], mine[1]
    pair = double(noisy_mine, ["c"], stages)

    half_one = double(far[:, :, : rows_unit // 2], ["z0"], stages)
    half_two = double(far[:, :, rows_unit // 2 :], names_a[::-1], stages)
    cond_low = jax.nn.silu(level_features(levels_all, width)).astype(low_type)
    ada_rows = ada_weight.shape[0]
    mod_rows = dot_nt(cond_low, ada_weight.astype(low_type))
    mod_rows, pair = lax.optimization_barrier((mod_rows, pair))
    mod_out = jnp.broadcast_to(
        mod_rows.reshape(count_a, 1, 4, group_frames, ada_rows),
        (count_a, members, 4, group_frames, ada_rows),
    ).reshape(devices, group_frames, ada_rows)
    mod_in = lax.all_to_all(
        mod_out.astype(low_type), ALL, split_axis=0, concat_axis=0, tiled=True
    ).astype(wide)
    noisy_group = in_order(double(pair, ["x"], stages), ["x", "c"]).reshape(
        group_frames, patch_size, frame_tok
    )
    half_one = double(half_one, names_a[::-1], stages)
    half_two = double(half_two, ["z0"], stages)
    *shares, mod_in = lax.optimization_barrier((*shares, mod_in))
    shares = climb(shares, 1)
    mod_in, half_one, half_two, noisy_group = lax.optimization_barrier(
        (mod_in, half_one, half_two, noisy_group)
    )
    half_one = in_order(half_one, names_a + ["z0", "z1"])
    half_two = in_order(half_two, ["z0"] + names_a + ["z1"])
    qkv_local = jnp.concatenate(
        [half_one.reshape(3 * groups, -1, width), half_two.reshape(3 * groups, -1, width)], axis=1
    ).reshape(3 * local, width)
    modul = mod_in.transpose(1, 0, 2).reshape(group_frames, 6 * width) + vectors[2:8].reshape(
        1, 6 * width
    )
    mod3 = modul.reshape(group_frames, 1, 6 * width)
    *shares, mod3 = lax.optimization_barrier((*shares, mod3))
    shares = climb(shares, 2)
    mod_mine = lax.dynamic_slice_in_dim(mod3, my_member * frames_dev, frames_dev)

    frame_ids = jnp.arange(group_frames, dtype=jnp.int32)
    time_pos = (frame_ids - starts_int).astype(wide)
    t_angle = time_pos[:, None] * tables[2][None, :]
    tcos = (jnp.cos(t_angle) * tables[3][None, :])[:, None, :]
    tsin = (jnp.sin(t_angle) * tables[3][None, :])[:, None, :]

    pw_in = patch_weight[0]
    bias_in = vectors[0:1]
    q, k, v = embed_qkv(
        noisy_group, pw_in, bias_in, mod3, qkv_local, tables, tcos, tsin, score_scale
    )
    place = jnp.stack([me // 4, me % 4])
    *shares, q = lax.optimization_barrier((*shares, q))
    for rung in range(3, len(rising[0]) - 1):
        shares = climb(shares, rung)
    final = []
    for share, order in zip(shares, rising):
        axis, distance, _ = stages[order[-1]]
        final.append(swap(share, axis, distance))
    att, att_low, lse = attend(starts_int, q, k, v, group_frames, local_heads)
    final = lax.optimization_barrier((*final, lse))[:3]
    shares = [jnp.stack(pair) for pair in zip(shares, final)]
    shares = [(share, swap(share, "c", 1)) for share in shares]
    framed = lax.all_to_all(
        att_low.reshape(members, tokens_dev, local), ("x", "c"), split_axis=0, concat_axis=0,
        tiled=True,
    )

    gain = vectors[1:2]
    pw_out = patch_weight[1]
    state_one, branch, h_two, out_full = post_attend(
        me[None], framed, noisy_mine, pw_in, bias_in, mod_mine, shares[2], gather_orders[2],
        layout[2][0][1],
    )
    act, slope, mixed, pred = ff_forward(
        place, h_two, state_one, mod_mine, shares, gather_orders, layout, gain, pw_out, frame_tok,
    )
    member_axes = ("x", "c")
    ahead = [(i, i + 1) for i in range(members - 1)]
    behind = [(i + 1, i) for i in range(members - 1)]
    edge = lax.ppermute(
        jnp.stack([pred[-1], target_mine[-1]]).astype(low_type), member_axes, ahead
    ).astype(wide)
    prev_pred = jnp.concatenate([edge[0:1], pred[:-1]], axis=0)
    prev_goal = jnp.concatenate([edge[1:2], target_mine[:-1]], axis=0)
    diff = pred - prev_pred - (target_mine - prev_goal)
    my_frames = my_member * frames_dev + jnp.arange(frames_dev, dtype=jnp.int32)
    valid = my_frames > lax.dynamic_slice_in_dim(starts_int, my_member * frames_dev, frames_dev)
    loss_local = jnp.sum(jnp.where(valid[:, None, None], diff * diff, 0.0))
    entry_count = float(frames_all * frame_tok * patch_size)
    d_diff = jnp.where(valid[:, None, None], (2.0 / entry_count) * diff, 0.0)
    returned = lax.ppermute(d_diff[0], member_axes, behind)
    d_pred = d_diff - jnp.concatenate([d_diff[1:], returned[None]], axis=0)
    d_hidden, d_mixed, d_branch, d_framed, d_small, d_sums, d_mod_rest = ff_backward(
        place, d_pred, state_one, mixed, branch, mod_mine, noisy_mine, gain, pw_out, shares,
        gather_orders, layout, out_full, slope, members,
    )
    d_att = lax.all_to_all(d_framed, ("x", "c"), split_axis=0, concat_axis=0, tiled=True).reshape(
        group_tokens, local
    )

    orders = three_orders(stages)
    grads_of = lambda half, adds=(): wide_grads(
        place, half, d_hidden, act, d_branch, h_two, d_mixed, framed, orders, devices, adds
    )
    others = grads_of(1)
    core_axis, core_distance, _ = stages["c"]
    passed = [swap(o, core_axis, core_distance) for o in others]

    cuts = [group_frames * n // 12 for n in (0, 9, 12)]

    def part_back(n, q, sums):
        return attend_back(
            starts_int, q, d_att, att, lse, k, v, sums, cuts[n], cuts[n + 1], group_frames,
            local_heads, score_scale,
        )

    ladder = Ladder(grads_of(0, passed), orders, stages)
    ladder.exchange()
    dq, dk, dv = part_back(0, after(q, *ladder.send), ())
    ladder.add(dk)
    ladder.exchange()
    dq, dk, dv = part_back(1, after(q, *ladder.send), (dq, dk, dv))
    ladder.add(dk)
    ladder.exchange()
    dv = after(dv, *ladder.send)
    near_orders = [names_a + ["z0", "z1"], ["z0"] + names_a + ["z1"]]

    def tail_back(dv, sums, begin, last):
        return qkv_back(
            (my_a * 4 + my_z).astype(jnp.int32)[None], near_orders, dq, dk, dv, noisy_group, pw_in,
            bias_in, mod3, qkv_local, tables, tcos, tsin, sums, begin, last,
        )

    middle = group_frames // 2
    dw, d_mod_early, d_embed, d_bias = tail_back(dv, (), 0, middle)
    while ladder.rung < len(orders[0]):
        ladder.add(d_bias)
        ladder.exchange()
    dw_one, dw_two, d_mod_late, d_embed, d_bias = tail_back(
        after(dv, *ladder.send), (dw, d_embed, d_bias), middle, group_frames
    )
    d_mod_one = jnp.concatenate([d_mod_early, d_mod_late], axis=0)
    near_dims = (2,) * len(near_orders[0])
    near = Ladder(
        [d.reshape(near_dims + d.shape[1:]) for d in (dw_one, dw_two)], near_orders, stages
    )
    near.exchange()
    near.got = list(lax.optimization_barrier((*near.got, *ladder.got)))[: len(near.got)]
    d_rest = lax.dynamic_update_slice_in_dim(
        jnp.zeros((group_frames, 4 * width), wide),
        d_mod_rest.reshape(frames_dev, 4 * width), my_member * frames_dev, 0,
    )
    d_mod = jnp.concatenate([d_mod_one[:, 0], d_rest], axis=1)
    d_mod = d_mod.reshape(group_frames, devices, ada_rows).transpose(1, 0, 2)
    smalls = jnp.concatenate(
        [d_embed + d_small[1], d_small[0], d_bias + d_sums[1:2], d_sums[0:1]], axis=0
    )
    small_rows = smalls.shape[0]
    small_part = small_rows * width // devices
    mod_part = group_frames * ada_rows
    packed = jnp.concatenate(
        [d_mod.reshape(devices, mod_part), smalls.reshape(devices, small_part)], axis=1
    )
    pad = -packed.shape[1] % 128
    packed = jnp.pad(packed, ((0, 0), (0, pad))).reshape(devices, -1, 128)
    arrived = lax.all_to_all(packed, ALL, split_axis=0, concat_axis=0, tiled=True).reshape(
        devices, -1
    )
    small_mine = jnp.sum(arrived[:, mod_part : mod_part + small_part], axis=0)
    mod_grad = (
        arrived[:, :mod_part]
        .reshape(count_a, members, 4, group_frames, ada_rows)
        .sum(axis=1)
        .reshape(frames_all, ada_rows)
    )
    bias_mine = jnp.sum(mod_grad, axis=0)
    g_ada = dot_tn(mod_grad.astype(low_type), cond_low)

    g_wide = ladder.add()
    rest_sq = (
        sum((jnp.sum(piece * piece) for piece in g_wide))
        + jnp.sum(g_ada * g_ada)
        + jnp.sum(small_mine * small_mine)
        + jnp.sum(bias_mine * bias_mine)
    )
    while near.rung < len(near_orders[0]):
        near.add()
        near.exchange()
    *near.got, rest_sq, g_ada = lax.optimization_barrier((*near.got, rest_sq, g_ada))
    g_one, g_two = near.add()
    units_out, units_sq = home_units(table, g_one, g_two)
    units_home = send_units(units_out, plan, True)
    local_sq = rest_sq + units_sq
    totals = jnp.where(lax.broadcasted_iota(jnp.int32, (1, 128), 1) == 0, local_sq, loss_local)
    totals = jnp.sum(spread(totals)[:, 0, :2], axis=0)
    norm = jnp.sqrt(totals[0])
    loss_total = totals[1]
    report = jnp.concatenate([small_mine, bias_mine])
    report = jnp.pad(report, (0, -report.shape[0] % 128)).reshape(-1, 128)
    report = after(report, norm)
    clip = jnp.minimum(1.0, 0.01 / norm)

    olds = (qkv_weight, out_weight, up_weight, down_weight)
    moments = (qkv_moment, out_moment, up_moment, down_moment)
    ada_new, ada_one, ada_two = adamw(ada_weight, ada_first, ada_second, clip * g_ada, 0.08)
    blk = 256
    gram_orders = [["c"] + o for o in orders[:2]]
    pairs = len(tri_blocks(width // blk)) * 4 // (devices // 32)
    cuts = (0, pairs // 2, pairs)
    parts = []
    report_order = ["z1", "z0"] + names_a[::-1] + ["x", "c"]
    ladders = []
    moments_new, steers, tiles = steer_grams(
        table, clip[None], units_home, g_wide, moments, blk, cuts, gram_orders, devices
    )
    for k, part in enumerate(tiles):
        ladders.append(Ladder([part.reshape((2,) * len(stages) + part.shape[1:])], [gram_orders[k]], stages))
    for rung in range(len(stages)):
        for ladder in ladders:
            ladder.exchange()
        report = double(after(report, ladders[0].got[0]), [report_order[rung]], stages)
        ties = []
        if rung == 2:
            ties = [ada_new, ada_one, ada_two]
        results = []
        for ladder in ladders:
            got, *ties = lax.optimization_barrier((ladder.got[0], *ties))
            ladder.got = [got]
            results.append(ladder.add())
        if rung == 2:
            ada_new, ada_one, ada_two = ties
    everyone = in_order(report, report_order[::-1]).reshape(devices, -1)
    small_all = everyone[:, :small_part].reshape(small_rows, width)
    bias_all = everyone[:, small_part : small_part + ada_rows].reshape(6, width)
    g_patch = small_all[: 2 * patch_size].reshape(2, patch_size, width)
    g_vec = jnp.concatenate([small_all[2 * patch_size :], bias_all], axis=0)
    patch_new, patch_one, patch_two = adamw(
        patch_weight, patch_first, patch_second, clip * g_patch, 0.15
    )
    vec_new, vec_one, vec_two = adamw(vectors, vec_first, vec_second, clip * g_vec, 0.5)
    lines = [result[0].astype(low_type) for result in results]
    late = [patch_new, patch_one, patch_two, vec_new, vec_one, vec_two]
    for rung in range(1, len(stages)):
        lines = [
            double(line, [gram_orders[n][:0:-1][rung - 1]], stages) for n, line in enumerate(lines)
        ]
        if rung == len(stages) - 2:
            lines[0], *late = lax.optimization_barrier((lines[0], *late))
    patch_new, patch_one, patch_two, vec_new, vec_one, vec_two = late
    parts = []
    for line in lines:
        line = line.reshape((-1,) + line.shape[-2:])
        parts += [line, swap(line, "c", 1)]
    factors = [2.0 * math.sqrt(max(1.0, o.shape[0] * devices / width)) for o in olds]
    updated = polish(
        me[None], steers, parts, olds, blk, cuts, [o[1:] for o in gram_orders], factors
    )
    return (
        loss_total,
        norm,
        updated[0],
        moments_new[0],
        updated[1],
        moments_new[1],
        updated[2],
        moments_new[2],
        updated[3],
        moments_new[3],
        ada_new,
        ada_one,
        ada_two,
        patch_new,
        patch_one,
        patch_two,
        vec_new,
        vec_one,
        vec_two,
    )


def solution(mesh):
    groups, line = mesh.shape["dp"], mesh.shape["seq"]
    inner = Mesh(mesh.devices.reshape(groups // 4, 2, 2, line), ALL)
    split = P(ALL, None)
    copied = P()
    placed = (split, split, P(ALL), P(ALL)) + (split,) * 11 + (copied,) * 6
    return jax.shard_map(
        body,
        mesh=inner,
        in_specs=placed,
        out_specs=(copied, copied) + (split,) * 11 + (copied,) * 6,
        check_vma=False,
    )
```

```python
from functools import partial
import math

import jax
import jax.numpy as jnp
import numpy as np
from jax import lax
from jax.experimental import pallas as pl
from jax.experimental.pallas import tpu as pltpu
from jax.sharding import Mesh, PartitionSpec as P

HEADS = 16
NS_ITERS = 2
STEP = 10
ALL = ("a", "x", "c", "z")

highest = lax.Precision.HIGHEST
coef_one = 3.4445
coef_two = -4.775
coef_three = 2.0315
low_type = jnp.bfloat16
wide = jnp.float32
NT = (((1,), (1,)), ((), ()))
TN = (((0,), (0,)), ((), ()))
MIB = 1 << 20


def dot_nt(left, right):
    return lax.dot_general(left, right, NT, preferred_element_type=wide)


def dot_tn(left, right):
    return lax.dot_general(left, right, TN, preferred_element_type=wide)


def dot_nn(left, right):
    return jnp.dot(left, right, preferred_element_type=wide)


def layer_stats(value):
    mean = jnp.mean(value, axis=-1, keepdims=True)
    centred = value - mean
    rstd = lax.rsqrt(jnp.mean(centred * centred, axis=-1, keepdims=True) + 1e-06)
    return (centred * rstd, rstd)


def layer_back(normed, rstd, upstream):
    return rstd * (
        upstream
        - jnp.mean(upstream, axis=-1, keepdims=True)
        - normed * jnp.mean(upstream * normed, axis=-1, keepdims=True)
    )


def level_features(levels, width):
    half = width // 2
    freqs = jnp.exp(-math.log(10000.0) * jnp.arange(half, dtype=jnp.float32) / half)
    angle = levels.astype(jnp.float32)[:, None] * freqs[None, :]
    return jnp.concatenate([jnp.sin(angle), jnp.cos(angle)], axis=-1)


def adamw(weight, first, second, grad, rate):
    first = 0.9 * first + 0.1 * grad
    second = 0.95 * second + 0.05 * grad * grad
    first_hat = first / (1.0 - 0.9**STEP)
    second_hat = second / (1.0 - 0.95**STEP)
    weight = weight - rate * (first_hat / (jnp.sqrt(second_hat) + 1e-08) + 0.01 * weight)
    return (weight, first, second)


def rope_tables(head_dim, heads, frame_tok):
    sec_time = head_dim // 4
    sec_space = (head_dim - sec_time) // 2
    side = math.isqrt(frame_tok)
    spot = np.arange(frame_tok)
    firsts, seconds, time_freq, space = [], [], [], []
    offset = 0
    for kind, size in ((0, sec_time), (1, sec_space), (2, sec_space)):
        half = size // 2
        freqs = np.exp(-math.log(10000.0) * np.arange(half, dtype=np.float64) * 2.0 / size)
        firsts += list(range(offset, offset + half))
        seconds += list(range(offset + half, offset + size))
        offset += size
        where = {0: np.zeros(frame_tok), 1: spot // side, 2: spot % side}[kind]
        space.append(where[:, None] * freqs[None, :])
        time_freq.append(freqs if kind == 0 else np.zeros(half))
    is_time = np.concatenate([np.ones(sec_time // 2), np.zeros(sec_space)])
    space = np.concatenate(space, axis=1)
    space_cos = np.where(is_time[None] > 0, 0.0, np.cos(space))
    space_sin = np.where(is_time[None] > 0, 0.0, np.sin(space))
    time_freq = np.concatenate(time_freq)
    order = np.concatenate(
        [
            np.concatenate([np.asarray(part) + h * head_dim for h in range(heads)])
            for part in (firsts, seconds)
        ]
    )
    total = heads * head_dim
    select = np.zeros((total, total), np.float32)
    select[np.arange(total), order] = 1.0
    tile = lambda t: np.tile(t, (1, heads)).astype(np.float32)
    return (
        tile(space_cos),
        tile(space_sin),
        np.tile(time_freq, heads).astype(np.float32),
        np.tile(is_time, heads).astype(np.float32),
        select,
    )


def split_mask(shape, axis, heads, half_lanes, value):
    lane = lax.broadcasted_iota(jnp.int32, shape, axis)
    if half_lanes is not None:
        lane = lane % half_lanes
        return lane // (half_lanes // heads) == value
    return lane // (shape[axis] // heads) == value


def split_two(value):
    high = value.astype(low_type)
    return high, (value - high.astype(wide)).astype(low_type)


def split_three(value):
    high = value.astype(low_type)
    rest = value - high.astype(wide)
    middle = rest.astype(low_type)
    return high, middle, (rest - middle.astype(wide)).astype(low_type)


def pack_left(value):
    high, middle, least = split_three(value)
    return jnp.concatenate([high, high, middle, high, middle, least], axis=0)


def pack_right(value):
    high, middle, least = split_three(value)
    return jnp.concatenate([high, middle, high, least, middle, high], axis=0)


def thin_product(thin, tall):
    t_high, t_low = split_two(thin)
    high, low = split_two(tall)
    rows = thin.shape[0]
    both = dot_nn(jnp.concatenate([t_high, t_low], axis=0), high)
    return both[:rows] + both[rows:] + dot_nn(t_high, low)


def line_rows(scrs, refs, me_ref, layout, places):
    other = jnp.bitwise_and(jnp.bitwise_xor(pl.program_id(0), me_ref[0]), 1)

    def fill(parts):
        for zz in range(4):
            apart = jnp.bitwise_xor(me_ref[1], zz)
            for scr, pieces in zip(scrs, layout):
                at = zz * (scr.shape[0] // 4)
                for part, begin, rows in pieces:
                    ref, (dim_one, dim_zero) = parts[part], places[part]
                    index = [0] * (len(ref.shape) - 2)
                    index[dim_one] = lax.shift_right_logical(apart, 1)
                    index[dim_zero] = jnp.bitwise_and(apart, 1)
                    scr[at : at + rows, :] = ref[tuple(index) + (slice(begin, begin + rows),)]
                    at += rows

    @pl.when(other == 0)
    def _():
        fill(refs[0::2])

    @pl.when(other == 1)
    def _():
        fill(refs[1::2])


def part_layout(rows_up, rows_out):
    size = (2 * rows_up + rows_out) // 3
    layout, at = [], 0
    for rows in (rows_up, rows_up, rows_out):
        pieces = []
        while rows:
            count = min(rows, size - at % size)
            pieces.append((at // size, at % size, count))
            at, rows = at + count, rows - count
        layout.append(pieces)
    return layout


def once(shape):
    return pl.BlockSpec(shape, lambda *_: (0,) * len(shape), pipeline_mode=pl.Buffered(1))


def embed_qkv_kernel(
    noisy_ref, pw_ref, bias_ref, mod_ref, w_ref, sel_ref, cs_ref, sn_ref, tc_ref, ts_ref,
    q_ref, k_ref, v_ref, wq_scr, pw_scr, *, width, local, scale,
):
    @pl.when(pl.program_id(0) == 0)
    def _():
        pw_scr[...] = pack_right(pw_ref[...])
        for part in range(2):
            rows = pl.ds(part * local, local)
            wq_scr[rows, :] = dot_nn(sel_ref[...], w_ref[rows, :]).astype(low_type)
        rows = pl.ds(2 * local, local)
        wq_scr[rows, :] = w_ref[rows, :]

    ftok = cs_ref.shape[0]
    half = local // 2
    count = noisy_ref.shape[0]
    lows, outs = [None] * count, [None] * count

    def prepare(f):
        state = dot_tn(pack_left(noisy_ref[f]), pw_scr[...]) + bias_ref[...]
        normed, _ = layer_stats(state)
        shift = mod_ref[f, :, 0:width]
        scl = mod_ref[f, :, width : 2 * width]
        lows[f] = (normed * (1.0 + scl) + shift).astype(low_type)

    def turn(f):
        out = outs[f]
        at = slice(f * ftok, (f + 1) * ftok)
        cosine = cs_ref[...] + tc_ref[f]
        sine = sn_ref[...] + ts_ref[f]
        for part, ref, mult in ((0, q_ref, scale), (1, k_ref, 1.0)):
            first = out[:, part * local : part * local + half]
            second = out[:, part * local + half : (part + 1) * local]
            for lanes, value in (
                (slice(0, half), first * cosine - second * sine),
                (slice(half, local), second * cosine + first * sine),
            ):
                ref[at, lanes] = (value.astype(low_type).astype(wide) * mult).astype(low_type)
        v_ref[at, :] = out[:, 2 * local : 3 * local].astype(low_type)

    prepare(0)
    for f in range(count):
        outs[f] = dot_nt(lows[f], wq_scr[...])
        if f + 1 < count:
            prepare(f + 1)
        if f > 0:
            turn(f - 1)
    turn(count - 1)


def embed_qkv(noisy_t, pw, bias, mod, w_local, tables, tcos, tsin, scale):
    frames, patch, ftok = noisy_t.shape
    width = pw.shape[1]
    local = w_local.shape[0] // 3
    cs, sn, _, _, sel = tables
    tokens = frames * ftok
    step = math.gcd(frames, 3)
    full = lambda shape: pl.BlockSpec(shape, lambda i: (0,) * len(shape))
    row = lambda cols: pl.BlockSpec((step * ftok, cols), lambda i: (i, 0))
    return pl.pallas_call(
        partial(embed_qkv_kernel, width=width, local=local, scale=scale),
        grid=(frames // step,),
        in_specs=[
            pl.BlockSpec((step, patch, ftok), lambda i: (i, 0, 0)),
            full(pw.shape),
            full((1, width)),
            pl.BlockSpec((step, 1, 6 * width), lambda i: (i, 0, 0)),
            full(w_local.shape),
            full(sel.shape),
            full(cs.shape),
            full(sn.shape),
            pl.BlockSpec((step, 1, local // 2), lambda i: (i, 0, 0)),
            pl.BlockSpec((step, 1, local // 2), lambda i: (i, 0, 0)),
        ],
        out_specs=[row(local), row(local), row(local)],
        out_shape=[
            jax.ShapeDtypeStruct((tokens, local), low_type),
            jax.ShapeDtypeStruct((tokens, local), low_type),
            jax.ShapeDtypeStruct((tokens, local), low_type),
        ],
        scratch_shapes=[
            pltpu.VMEM(w_local.shape, low_type),
            pltpu.VMEM((6 * patch, width), low_type),
        ],
        compiler_params=pltpu.CompilerParams(
            dimension_semantics=("arbitrary",), vmem_limit_bytes=24 * MIB
        ),
        cost_estimate=pl.CostEstimate(
            flops=2 * tokens * width * 3 * local, bytes_accessed=12 * MIB, transcendentals=0
        ),
        name="embed_qkv",
    )(noisy_t, pw, bias, mod, w_local, sel, cs, sn, tcos, tsin)


def attend_kernel(
    st_ref, q_ref, k_ref, v_ref, o_ref, ol_ref, lse_ref, vt_scr, even, odd, *, heads, ftok
):
    i = pl.program_id(0)
    local = q_ref.shape[1]
    hd = local // heads

    @pl.when(i == 0)
    def _():
        for f in range(vt_scr.shape[0]):
            vt_scr[f] = v_ref[f * ftok : (f + 1) * ftok, :].T

    first = st_ref[i]
    query = q_ref[...]
    zero = jnp.zeros_like(query)
    masked = [
        jnp.where(split_mask(query.shape, 1, heads, local // 2, h), query, zero)
        for h in range(heads)
    ]

    def key_rows(j):
        return k_ref[pl.ds(pl.multiple_of(j * ftok, ftok), ftok), :]

    def step(j, here, following, there, carry):
        vt = vt_scr[j]
        key = None if following is None else key_rows(following)
        new, probs, stats = [], [], []

        def attended(g):
            top, total, shrink = stats[g]
            acc = carry[g][2] * shrink + dot_nn(vt[g * hd : (g + 1) * hd, :], probs[g])
            new.append((top, total, acc))

        for h in range(heads):
            if key is not None:
                there[h] = dot_nt(key, masked[h])
            top, total, _ = carry[h]
            s = here[h]
            peak = jnp.max(jnp.max(s.reshape(ftok // 8, 8, ftok), axis=0), axis=0, keepdims=True)
            higher = jnp.maximum(top, peak)
            p = jnp.exp(s - higher)
            shrink = jnp.exp(top - higher)
            total = total * shrink + jnp.sum(p.reshape(ftok // 8, 8, ftok), axis=0)
            probs.append(p.astype(low_type))
            stats.append((higher, total, shrink))
            if h > 0:
                attended(h - 1)
        attended(heads - 1)
        return tuple(new)

    count = i + 1 - first
    key = key_rows(first)
    for h in range(heads):
        even[h] = dot_nt(key, masked[h])

    def pair(t, carry):
        j = first + 2 * t
        carry = step(j, even, j + 1, odd, carry)
        return step(j + 1, odd, jnp.minimum(j + 2, i), even, carry)

    start = tuple(
        (
            jnp.full((1, ftok), -1e30, wide),
            jnp.zeros((8, ftok), wide),
            jnp.zeros((hd, ftok), wide),
        )
        for _ in range(heads)
    )
    carry = lax.fori_loop(0, lax.div(count, 2), pair, start)
    carry = lax.cond(
        lax.rem(count, 2) == 1, lambda c: step(i, even, None, None, c), lambda c: c, carry
    )
    outs, logs = [], []
    for top, total, acc in carry:
        total = jnp.sum(total, axis=0, keepdims=True)
        outs.append(acc * (1.0 / total))
        logs.append(top + jnp.log(total))
    out = jnp.concatenate(outs, axis=0)
    o_ref[0] = out
    ol_ref[...] = out.astype(low_type).T
    lse_ref[0] = jnp.concatenate(logs + [jnp.zeros((8 - heads, ftok), wide)], axis=0)


def attend(starts, q, k, v, frames, heads):
    tokens, local = q.shape
    ftok = tokens // frames
    row = lambda: pl.BlockSpec((ftok, local), lambda i, s: (i, 0))
    return pl.pallas_call(
        partial(attend_kernel, heads=heads, ftok=ftok),
        grid_spec=pltpu.PrefetchScalarGridSpec(
            num_scalar_prefetch=1,
            grid=(frames,),
            in_specs=[row(), once(k.shape), once(v.shape)],
            out_specs=[
                pl.BlockSpec((1, local, ftok), lambda i, s: (i, 0, 0)),
                row(),
                pl.BlockSpec((1, 8, ftok), lambda i, s: (i, 0, 0)),
            ],
            scratch_shapes=[
                pltpu.VMEM((frames, local, ftok), low_type),
                pltpu.VMEM((heads, ftok, ftok), wide),
                pltpu.VMEM((heads, ftok, ftok), wide),
            ],
        ),
        out_shape=[
            jax.ShapeDtypeStruct((frames, local, ftok), wide),
            jax.ShapeDtypeStruct((tokens, local), low_type),
            jax.ShapeDtypeStruct((frames, 8, ftok), wide),
        ],
        compiler_params=pltpu.CompilerParams(
            dimension_semantics=("arbitrary",), vmem_limit_bytes=16 * MIB
        ),
        cost_estimate=pl.CostEstimate(
            flops=40_000_000_000, bytes_accessed=12 * MIB, transcendentals=0
        ),
        name="attend",
    )(starts, q, k, v)


def attend_back_kernel(
    st_ref, q_ref, do_ref, o_ref, lse_ref, k_ref, v_ref, *rest, heads, ftok, scale, begin, last
):
    if begin:
        _, dk_in, dv_in, *rest = rest
    dq_ref, dk_ref, dv_ref, kt_scr, dk_scr, dv_scr, dqt_scr, *slots = rest
    step_id = pl.program_id(0)
    steps = pl.num_programs(0)
    i = step_id + begin
    local = q_ref.shape[1]
    hd = local // heads
    hh = hd // 2
    half = local // 2

    @pl.when(step_id == 0)
    def _():
        for f in range(last):
            kt_scr[f] = k_ref[f * ftok : (f + 1) * ftok, :].T
        if begin:
            dk_scr[...] = dk_in[...]
            dv_scr[...] = dv_in[...]
        else:
            dk_scr[...] = jnp.zeros_like(dk_scr)
            dv_scr[...] = jnp.zeros_like(dv_scr)

    first = st_ref[i]
    query = q_ref[...]
    grad = do_ref[...]
    zero = jnp.zeros_like(query)
    q_mask = [
        jnp.where(split_mask(query.shape, 1, heads, half, h), query, zero) for h in range(heads)
    ]
    g_mask = [
        jnp.where(split_mask(query.shape, 1, heads, None, h), grad, zero) for h in range(heads)
    ]
    prod = grad.T.astype(wide) * o_ref[0]
    delta = [
        jnp.sum(prod[h * hd : (h + 1) * hd, :], axis=0, keepdims=True) for h in range(heads)
    ]
    lse = [lse_ref[0, h : h + 1, :] for h in range(heads)]
    dqt_scr[...] = jnp.zeros_like(dqt_scr)

    def rows(j):
        return pl.ds(pl.multiple_of(j * ftok, ftok), ftok)

    def front(h, key, val, slot):
        s_ref, p_ref = slot
        s_ref[h] = dot_nt(key, q_mask[h])
        p_ref[h] = dot_nt(val, g_mask[h])

    def step(j, here, following, there):
        kt = kt_scr[j]
        if following is not None:
            key, val = k_ref[rows(following), :], v_ref[rows(following), :]
        s_ref, p_ref = here
        probs, d_scores = [], []

        def sums(g):
            kt_g = jnp.concatenate(
                [kt[g * hh : (g + 1) * hh, :], kt[half + g * hh : half + (g + 1) * hh, :]], axis=0
            )
            dqt_scr[g] += dot_nn(kt_g, d_scores[g])
            dv_scr[rows(j), :] += dot_nn(probs[g], g_mask[g])
            dk_scr[rows(j), :] += dot_nn(d_scores[g], q_mask[g])

        for h in range(heads):
            if following is not None:
                front(h, key, val, there)
            p = jnp.exp(s_ref[h] - lse[h])
            d_scores.append((p * (p_ref[h] - delta[h])).astype(low_type))
            probs.append(p.astype(low_type))
            if h > 0:
                sums(h - 1)
        sums(heads - 1)

    even, odd = slots[:2], slots[2:]
    count = i + 1 - first
    key, val = k_ref[rows(first), :], v_ref[rows(first), :]
    for h in range(heads):
        front(h, key, val, even)

    def pair(t, carry):
        j = first + 2 * t
        step(j, even, j + 1, odd)
        step(j + 1, odd, jnp.minimum(j + 2, i), even)
        return carry

    lax.fori_loop(0, lax.div(count, 2), pair, 0)

    @pl.when(lax.rem(count, 2) == 1)
    def _():
        step(i, even, None, None)

    dqt = jnp.concatenate(
        [dqt_scr[h, 0:hh, :] for h in range(heads)] + [dqt_scr[h, hh:hd, :] for h in range(heads)],
        axis=0,
    )
    dq_ref[...] = (dqt * scale).astype(low_type).T

    @pl.when(step_id == steps - 1)
    def _():
        dk_ref[...] = dk_scr[...].astype(dk_ref.dtype)
        dv_ref[...] = dv_scr[...].astype(dv_ref.dtype)


def attend_back(starts, q, grad, out, lse, k, v, sums, begin, last, frames, heads, scale):
    tokens, local = q.shape
    ftok = tokens // frames
    row = lambda cols: pl.BlockSpec((ftok, cols), lambda i, s: (i + begin, 0))
    kind = low_type if last == frames else wide
    return pl.pallas_call(
        partial(attend_back_kernel, heads=heads, ftok=ftok, scale=scale, begin=begin, last=last),
        grid_spec=pltpu.PrefetchScalarGridSpec(
            num_scalar_prefetch=1,
            grid=(last - begin,),
            in_specs=[
                row(local), row(local),
                pl.BlockSpec((1, local, ftok), lambda i, s: (i + begin, 0, 0)),
                pl.BlockSpec((1, 8, ftok), lambda i, s: (i + begin, 0, 0)),
                once(k.shape), once(v.shape),
            ] + ([pl.BlockSpec(memory_space=pl.ANY)] + [once(k.shape)] * 2)[: len(sums)],
            out_specs=[row(local), once(k.shape), once(v.shape)],
            scratch_shapes=[
                pltpu.VMEM((frames, local, ftok), low_type),
                pltpu.VMEM((tokens, local), wide),
                pltpu.VMEM((tokens, local), wide),
                pltpu.VMEM((heads, local // heads, ftok), wide),
            ] + [pltpu.VMEM((heads, ftok, ftok), wide)] * 4,
        ),
        out_shape=[
            jax.ShapeDtypeStruct((tokens, local), low_type),
            jax.ShapeDtypeStruct((tokens, local), kind),
            jax.ShapeDtypeStruct((tokens, local), kind),
        ],
        input_output_aliases={7: 0} if sums else {},
        compiler_params=pltpu.CompilerParams(
            dimension_semantics=("arbitrary",), vmem_limit_bytes=44 * MIB
        ),
        cost_estimate=pl.CostEstimate(
            flops=30_000_000_000, bytes_accessed=16 * MIB, transcendentals=0
        ),
        name="attend_back",
    )(starts, q, grad, out, lse, k, v, *sums)


def post_attend_kernel(
    me_ref, fr_ref, noisy_ref, pw_ref, bias_ref, mod_ref, two_a, two_b, st_ref, br_ref, h_ref,
    full_ref, *, width, maps, skip,
):
    local = fr_ref.shape[2]

    @pl.when(pl.program_id(0) == 0)
    def _():
        rows_out = width // (2 * len(maps))
        for two_ref, other in ((two_a, 0), (two_b, 4)):
            for pos, apart in enumerate(maps):
                dev = jnp.bitwise_xor(me_ref[0], apart + other)
                full_ref[pl.ds(pl.multiple_of(dev * rows_out, rows_out), rows_out), :] = two_ref[
                    pos, skip:, :
                ]

    out_full = full_ref[...]
    state = dot_tn(pack_left(noisy_ref[0]), pack_right(pw_ref[...])) + bias_ref[...]
    branch = dot_nt(fr_ref[0], out_full[:, 0:local])
    for m in range(1, fr_ref.shape[0]):
        branch += dot_nt(fr_ref[m], out_full[:, m * local : (m + 1) * local])
    state = state + mod_ref[0, :, 2 * width : 3 * width] * branch
    normed, _ = layer_stats(state)
    st_ref[...] = state
    br_ref[...] = branch
    h_ref[...] = (
        normed * (1.0 + mod_ref[0, :, 4 * width : 5 * width])
        + mod_ref[0, :, 3 * width : 4 * width]
    ).astype(low_type)


def post_attend(me, framed, noisy_t, pw, bias, mod, part_two, order_two, skip):
    members, tokens, local = framed.shape
    frames, patch, ftok = noisy_t.shape
    width = pw.shape[1]
    part_two = [p.reshape((-1,) + p.shape[-2:]) for p in part_two]
    row = lambda: pl.BlockSpec((ftok, width), lambda i, me: (i, 0))
    return pl.pallas_call(
        partial(post_attend_kernel, width=width, maps=tile_places(order_two), skip=skip),
        grid_spec=pltpu.PrefetchScalarGridSpec(
            num_scalar_prefetch=1,
            grid=(frames,),
            in_specs=[
                pl.BlockSpec((members, ftok, local), lambda i, me: (0, i, 0)),
                pl.BlockSpec((1, patch, ftok), lambda i, me: (i, 0, 0)),
                once(pw.shape),
                once((1, width)),
                pl.BlockSpec((1, 1, 6 * width), lambda i, me: (i, 0, 0)),
            ] + [once(p.shape) for p in part_two],
            out_specs=[row(), row(), row(), once((width, width))],
        ),
        out_shape=[
            jax.ShapeDtypeStruct((tokens, width), wide),
            jax.ShapeDtypeStruct((tokens, width), wide),
            jax.ShapeDtypeStruct((tokens, width), low_type),
            jax.ShapeDtypeStruct((width, width), low_type),
        ],
        compiler_params=pltpu.CompilerParams(
            dimension_semantics=("arbitrary",), vmem_limit_bytes=18 * MIB
        ),
        cost_estimate=pl.CostEstimate(
            flops=2 * tokens * width * width, bytes_accessed=12 * MIB, transcendentals=0
        ),
        name="post_attend",
    )(me, framed, noisy_t, pw, bias, mod, *part_two)


def part_specs(me_block, orders, shapes):
    bits = sorted((n for n in orders[0] if n[0] == "a"), reverse=True) + ["x", "c"]
    specs = []
    for order, shape in zip(orders, shapes):

        def place(n, me, order=order):
            apart = me_block(n, me)
            index = []
            for name in order:
                if name[0] == "z":
                    index.append(0)
                else:
                    index.append(
                        jnp.bitwise_and(
                            lax.shift_right_logical(apart, len(bits) - 1 - bits.index(name)), 1
                        )
                    )
            return tuple(index) + (0, 0)

        block = tuple(2 if n[0] == "z" else 1 for n in order) + shape[-2:]
        specs += [pl.BlockSpec(block, place)] * 2
    return specs


def line_apart(n, me):
    return jnp.bitwise_xor(n, me[0])


def gelu_parts(value):
    k = math.sqrt(2.0 / math.pi)
    square = value * value
    t = jnp.tanh(k * value * (1.0 + 0.044715 * square))
    half = 0.5 * (1.0 + t)
    slope = half + (0.5 * k) * value * (1.0 - t * t) * (1.0 + (3 * 0.044715) * square)
    return value * half, slope


def ff_kernel(
    me_ref, h_ref, st_ref, mod_ref, one_a, one_b, two_a, two_b, three_a, three_b, gain_ref, pw_ref,
    act_ref, slope_ref, mixed_ref, pred_ref, acc_scr, up_scr, down_scr,
    *, width, frames, ftok, layout, places,
):
    n = pl.program_id(0)
    line_rows(
        (up_scr, down_scr), (one_a, one_b, two_a, two_b, three_a, three_b), me_ref, layout, places
    )
    @pl.when(n == 0)
    def _():
        acc_scr[...] = jnp.zeros_like(acc_scr)

    spots = [slice(f * ftok, (f + 1) * ftok) for f in range(frames)]
    hidden = [None] * frames
    acts = [None] * frames

    def activate(f):
        act, slope = gelu_parts(hidden[f])
        acts[f] = act.astype(low_type)
        act_ref[spots[f], :] = acts[f]
        slope_ref[spots[f], :] = slope.astype(low_type)

    for f in range(frames + 2):
        if f < frames:
            hidden[f] = dot_nt(h_ref[spots[f], :], up_scr[...])
        if 0 < f <= frames:
            activate(f - 1)
        if f > 1:
            acc_scr[spots[f - 2], :] += dot_nn(acts[f - 2], down_scr[...])

    @pl.when(n == pl.num_programs(0) - 1)
    def _():
        patch = pw_ref.shape[0]
        head, rest = split_two(pw_ref[...])
        both = jnp.concatenate([head, rest], axis=0)
        for f in range(frames):
            at = slice(f * ftok, (f + 1) * ftok)
            mixed = acc_scr[at, :]
            mixed_ref[at, :] = mixed
            normed, _ = layer_stats(st_ref[at, :] + mod_ref[f, :, 5 * width : 6 * width] * mixed)
            f_high, f_low = split_two(normed * gain_ref[...])
            two = dot_nt(f_high, both)
            one = dot_nt(f_low, head)
            pred_ref[f] = (two[:, :patch] + two[:, patch:] + one).T


def ff_forward(me, h_two, state_one, mod, parts, orders, layout, gain, pw_out, ftok):
    tokens, width = h_two.shape
    steps = 1 << (len(orders[0]) - 1)
    chunk = 4 * sum(rows for _, _, rows in layout[0])
    frames = tokens // ftok
    patch = pw_out.shape[0]
    columns = lambda: pl.BlockSpec((tokens, chunk), lambda n, me: (0, n))
    return pl.pallas_call(
        partial(
            ff_kernel, width=width, frames=frames, ftok=ftok, layout=layout[:2],
            places=[(o.index("z1"), o.index("z0")) for o in orders],
        ),
        grid_spec=pltpu.PrefetchScalarGridSpec(
            num_scalar_prefetch=1,
            grid=(steps,),
            in_specs=[once(h_two.shape), once(state_one.shape), once(mod.shape)]
            + part_specs(line_apart, orders, [p[0].shape for p in parts])
            + [once(gain.shape), once(pw_out.shape)],
            out_specs=[columns(), columns(), once((tokens, width)), once((frames, patch, ftok))],
            scratch_shapes=[
                pltpu.VMEM((tokens, width), wide),
                pltpu.VMEM((chunk, width), low_type),
                pltpu.VMEM((chunk, width), low_type),
            ],
        ),
        out_shape=[
            jax.ShapeDtypeStruct((tokens, chunk * steps), low_type),
            jax.ShapeDtypeStruct((tokens, chunk * steps), low_type),
            jax.ShapeDtypeStruct((tokens, width), wide),
            jax.ShapeDtypeStruct((frames, patch, ftok), wide),
        ],
        compiler_params=pltpu.CompilerParams(
            dimension_semantics=("arbitrary",), vmem_limit_bytes=32 * MIB
        ),
        cost_estimate=pl.CostEstimate(
            flops=4 * tokens * width * chunk * steps, bytes_accessed=40 * MIB, transcendentals=0
        ),
        name="ff_forward",
    )(me, h_two, state_one, mod, *parts[0], *parts[1], *parts[2], gain, pw_out)


def ff_back_kernel(
    me_ref, dp_ref, st_ref, mixed_ref, br_ref, mod_ref, noisy_ref, gain_ref, pw_ref, one_a,
    one_b, two_a, two_b, three_a, three_b, out_ref, slope_ref, dh_ref, dm_ref, db_ref, df_ref,
    small_ref, sums_ref, dmod_ref, ds_scr, acc_scr, up_scr, down_scr,
    *, width, frames, ftok, layout, places,
):
    n = pl.program_id(0)
    line_rows(
        (up_scr, down_scr), (one_a, one_b, two_a, two_b, three_a, three_b), me_ref, layout, places
    )
    patch = pw_ref.shape[0]

    def fold(value):
        return jnp.sum(value.reshape(-1, 8, width), axis=0).sum(axis=0, keepdims=True)

    @pl.when(n == 0)
    def _():
        d_head = jnp.zeros((patch, width), wide)
        d_gain = jnp.zeros((1, width), wide)
        right = pack_right(pw_ref[...])
        for f in range(frames):
            at = slice(f * ftok, (f + 1) * ftok)
            gate = mod_ref[f, :, 5 * width : 6 * width]
            mixed = mixed_ref[at, :]
            normed, rstd = layer_stats(st_ref[at, :] + gate * mixed)
            d_pred = dp_ref[f]
            d_final = dot_tn(pack_left(d_pred), right)
            d_head += thin_product(d_pred, normed * gain_ref[...])
            d_gain += fold(d_final * normed)
            d_state = layer_back(normed, rstd, d_final * gain_ref[...])
            ds_scr[at, :] = d_state
            dmod_ref[f, 3:4, :] = fold(d_state * mixed)
            dm_ref[at, :] = (d_state * gate).astype(low_type)
        small_ref[0] = d_head
        sums_ref[0:1, :] = d_gain

    @pl.when(n == 0)
    def _():
        acc_scr[...] = jnp.zeros_like(acc_scr)

    spots = [slice(f * ftok, (f + 1) * ftok) for f in range(frames)]
    d_acts = [None] * frames
    for f in range(frames + 1):
        if f < frames:
            d_acts[f] = dot_nt(dm_ref[spots[f], :], down_scr[...])
        if f > 0:
            at = spots[f - 1]
            d_hidden = (d_acts[f - 1] * slope_ref[at, :].astype(wide)).astype(low_type)
            dh_ref[at, :] = d_hidden
            acc_scr[at, :] += dot_nn(d_hidden, up_scr[...])

    @pl.when(n == pl.num_programs(0) - 1)
    def _():
        out_full = out_ref[...]
        d_embed = jnp.zeros((patch, width), wide)
        d_bias = jnp.zeros((1, width), wide)
        local = df_ref.shape[2]
        for f in range(frames):
            at = slice(f * ftok, (f + 1) * ftok)
            normed, rstd = layer_stats(st_ref[at, :])
            d_h = acc_scr[at, :]
            dmod_ref[f, 1:2, :] = fold(d_h)
            dmod_ref[f, 2:3, :] = fold(d_h * normed)
            d_state = ds_scr[at, :] + layer_back(
                normed, rstd, d_h * (1.0 + mod_ref[f, :, 4 * width : 5 * width])
            )
            dmod_ref[f, 0:1, :] = fold(d_state * br_ref[at, :])
            d_branch = (d_state * mod_ref[f, :, 2 * width : 3 * width]).astype(low_type)
            db_ref[at, :] = d_branch
            d_framed = dot_nn(d_branch, out_full).astype(low_type)
            for m in range(df_ref.shape[0]):
                df_ref[m, at, :] = d_framed[:, m * local : (m + 1) * local]
            d_embed += thin_product(noisy_ref[f], d_state)
            d_bias += fold(d_state)
        small_ref[1] = d_embed
        sums_ref[1:2, :] = d_bias


def ff_backward(
    me, d_pred, state_one, mixed, branch, mod, noisy_t, gain, pw_out, parts, orders, layout,
    out_full, slope, members,
):
    tokens, width = state_one.shape
    steps = 1 << (len(orders[0]) - 1)
    chunk = 4 * sum(rows for _, _, rows in layout[0])
    frames, patch, ftok = noisy_t.shape
    local = width // members
    columns = lambda: pl.BlockSpec((tokens, chunk), lambda n, me: (0, n))
    return pl.pallas_call(
        partial(
            ff_back_kernel, width=width, frames=frames, ftok=ftok, layout=layout[:2],
            places=[(o.index("z1"), o.index("z0")) for o in orders],
        ),
        grid_spec=pltpu.PrefetchScalarGridSpec(
            num_scalar_prefetch=1,
            grid=(steps,),
            in_specs=[
                once(d_pred.shape),
                once(state_one.shape),
                once(state_one.shape),
                once(state_one.shape),
                once(mod.shape),
                once(noisy_t.shape),
                once(gain.shape),
                once(pw_out.shape),
            ]
            + part_specs(line_apart, orders, [p[0].shape for p in parts])
            + [once(out_full.shape), columns()],
            out_specs=[
                columns(),
                once((tokens, width)),
                once((tokens, width)),
                once((members, tokens, local)),
                once((2, patch, width)),
                once((2, width)),
                once((frames, 4, width)),
            ],
            scratch_shapes=[
                pltpu.VMEM((tokens, width), wide),
                pltpu.VMEM((tokens, width), wide),
                pltpu.VMEM((chunk, width), low_type),
                pltpu.VMEM((chunk, width), low_type),
            ],
        ),
        out_shape=[
            jax.ShapeDtypeStruct((tokens, chunk * steps), low_type),
            jax.ShapeDtypeStruct((tokens, width), low_type),
            jax.ShapeDtypeStruct((tokens, width), low_type),
            jax.ShapeDtypeStruct((members, tokens, local), low_type),
            jax.ShapeDtypeStruct((2, patch, width), wide),
            jax.ShapeDtypeStruct((2, width), wide),
            jax.ShapeDtypeStruct((frames, 4, width), wide),
        ],
        compiler_params=pltpu.CompilerParams(
            dimension_semantics=("arbitrary",), vmem_limit_bytes=42 * MIB
        ),
        cost_estimate=pl.CostEstimate(
            flops=4 * tokens * width * chunk * steps, bytes_accessed=40 * MIB, transcendentals=0
        ),
        name="ff_backward",
    )(
        me, d_pred, state_one, mixed, branch, mod, noisy_t, gain, pw_out, *parts[0], *parts[1],
        *parts[2], out_full, slope,
    )


def wide_grads_kernel(
    me_ref, dh_ref, act_ref, db_ref, h_ref, dm_ref, fr_ref, *outs, spans, places, narrow, half
):
    *outs, scr = outs
    adds, outs = outs[: len(outs) - len(spans)], outs[len(outs) - len(spans) :]
    up = dot_tn(dh_ref[...], h_ref[...])
    down = dot_tn(act_ref[...], dm_ref[...])
    left = db_ref[...]
    out = jnp.concatenate([dot_tn(left, fr_ref[m]) for m in range(fr_ref.shape[0])], axis=1)
    if narrow < left.shape[1]:
        scr[...] = out
        block = jnp.bitwise_xor(me_ref[0], 2 * pl.program_id(0) + half)
        at = lax.rem(block, left.shape[1] // narrow) * narrow
        out = scr[pl.ds(pl.multiple_of(at, narrow), narrow), :]
    my_z = me_ref[1]
    for zz in range(4):
        pieces = [
            arr[zz * (arr.shape[0] // 4) : (zz + 1) * (arr.shape[0] // 4)] for arr in (up, down, out)
        ]
        whole = jnp.concatenate(pieces, axis=0)
        apart = jnp.bitwise_xor(my_z, zz)
        for k, (ref, (begin, end), (dim_one, dim_zero)) in enumerate(zip(outs, spans, places)):
            index = [0] * (len(ref.shape) - 2)
            index[dim_one] = lax.shift_right_logical(apart, 1)
            index[dim_zero] = jnp.bitwise_and(apart, 1)
            part = whole[begin:end]
            if adds:
                part = part + adds[k][tuple(index)].astype(wide)
            ref[tuple(index)] = part.astype(ref.dtype)


def wide_grads(me, half, d_hidden, act, d_branch, h_two, d_mixed, framed, orders, devices, adds=()):
    tokens, width = h_two.shape
    members, _, local = framed.shape
    chunk = act.shape[1] // (devices // 4)
    out_chunk = width // (devices // 4)
    out_wide = max(out_chunk, 128)
    bits = sorted((n for n in orders[0] if n[0] == "a"), reverse=True) + ["x"]
    rows_dev = (2 * chunk + out_chunk) // 4
    part_rows = rows_dev // 3
    spans = [(k * part_rows, (k + 1) * part_rows) for k in range(3)]

    def block(q, me):
        return jnp.bitwise_xor(me[0], 2 * q + half)

    def out_spec(order):
        def place(q, me):
            index = []
            for name in order:
                if name[0] in "ax":
                    index.append(
                        jnp.bitwise_and(
                            lax.shift_right_logical(q, len(bits) - 1 - bits.index(name)), 1
                        )
                    )
                else:
                    index.append(0)
            return tuple(index) + (0, 0)

        shape = tuple(1 if n[0] in "ax" else 2 for n in order) + (part_rows, width)
        return pl.BlockSpec(shape, place)

    return pl.pallas_call(
        partial(
            wide_grads_kernel,
            spans=spans,
            places=[(o.index("z1"), o.index("z0")) for o in orders],
            narrow=out_chunk,
            half=half,
        ),
        grid_spec=pltpu.PrefetchScalarGridSpec(
            num_scalar_prefetch=1,
            grid=(devices // 8,),
            in_specs=[
                pl.BlockSpec((tokens, chunk), lambda q, me: (0, block(q, me))),
                pl.BlockSpec((tokens, chunk), lambda q, me: (0, block(q, me))),
                pl.BlockSpec(
                    (tokens, out_wide),
                    lambda q, me: (0, lax.div(block(q, me), out_wide // out_chunk)),
                ),
                once(h_two.shape),
                once(d_mixed.shape),
                once(framed.shape),
            ] + [out_spec(o) for o in orders][: len(adds)],
            out_specs=[out_spec(o) for o in orders],
            scratch_shapes=[pltpu.VMEM((out_wide, width), wide)],
        ),
        out_shape=[
            jax.ShapeDtypeStruct((2,) * len(o) + (part_rows, width), low_type) for o in orders
        ],
        compiler_params=pltpu.CompilerParams(
            dimension_semantics=("arbitrary",), vmem_limit_bytes=36 * MIB
        ),
        cost_estimate=pl.CostEstimate(
            flops=2 * tokens * width * (2 * chunk + out_chunk) * (devices // 8),
            bytes_accessed=24 * MIB, transcendentals=0,
        ),
        name="wide_grads",
    )(me, d_hidden, act, d_branch, h_two, d_mixed, framed, *adds)


def qkv_back_kernel(
    me_ref, dq_ref, dk_ref, dv_ref, noisy_ref, pw_ref, bias_ref, mod_ref, w_ref, sel_ref,
    cs_ref, sn_ref, tc_ref, ts_ref, *refs, width, local, maps, begin, last,
):
    i = pl.program_id(0)
    if begin:
        dw_in, demb_in, dbias_in, *refs = refs
    *dw_refs, dmod_ref, demb_ref, dbias_ref, acc_scr, emb_scr, bias_scr, pw_scr = refs

    @pl.when(i == 0)
    def _():
        pw_scr[...] = pack_right(pw_ref[...])
        bias_scr[...] = jnp.zeros_like(bias_scr)
        if begin:
            acc_scr[...] = dw_in[...]
            emb_scr[...] = demb_in[...]
            bias_scr[0:1, :] = dbias_in[...]
        else:
            acc_scr[...] = jnp.zeros_like(acc_scr)
            emb_scr[...] = jnp.zeros_like(emb_scr)

    ftok = cs_ref.shape[0]
    half = local // 2
    count = noisy_ref.shape[0]
    grads, hs, stats = [None] * count, [None] * count, [None] * count

    def turn(f):
        at = slice(f * ftok, (f + 1) * ftok)
        cosine = cs_ref[...] + tc_ref[f]
        sine = sn_ref[...] + ts_ref[f]
        parts = []
        for ref in (dq_ref, dk_ref):
            first = ref[at, 0:half].astype(wide)
            second = ref[at, half:local].astype(wide)
            turned = jnp.concatenate(
                [first * cosine + second * sine, second * cosine - first * sine], axis=1
            ).astype(low_type)
            parts.append(dot_nn(turned, sel_ref[...]).astype(low_type))
        parts.append(dv_ref[at, :])
        grads[f] = jnp.concatenate(parts, axis=1)

    def prepare(f):
        state = dot_tn(pack_left(noisy_ref[f]), pw_scr[...]) + bias_ref[...]
        normed, rstd = layer_stats(state)
        scl = mod_ref[f, :, width : 2 * width]
        hs[f] = (normed * (1.0 + scl) + mod_ref[f, :, 0:width]).astype(low_type)
        stats[f] = (normed, rstd, scl)

    def finish(f, d_h):
        normed, rstd, scl = stats[f]
        dmod_ref[f, :, 0:width] = jnp.sum(d_h, axis=0, keepdims=True)
        dmod_ref[f, :, width : 2 * width] = jnp.sum(d_h * normed, axis=0, keepdims=True)
        d_state = layer_back(normed, rstd, d_h * (1.0 + scl))
        emb_scr[...] += thin_product(noisy_ref[f], d_state)
        bias_scr[...] += jnp.sum(d_state.reshape(-1, 8, width), axis=0)

    turn(0)
    for f in range(count):
        d_h = dot_nn(grads[f], w_ref[...])
        prepare(f)
        acc_scr[...] += dot_tn(grads[f], hs[f])
        if f + 1 < count:
            turn(f + 1)
        finish(f, d_h)

    @pl.when(i == pl.num_programs(0) - 1)
    def _():
        demb_ref[...] = emb_scr[...]
        dbias_ref[...] = jnp.sum(bias_scr[...], axis=0, keepdims=True)
        if not last:
            dw_refs[0][...] = acc_scr[...]
            return
        rows = acc_scr.shape[0] // len(maps[0])
        at = 0
        for ref, places in zip(dw_refs, maps):
            count = ref.shape[1]
            for pos, apart in enumerate(places):
                dev = jnp.bitwise_xor(me_ref[0], apart)
                begin = pl.multiple_of(dev * rows + at, 8)
                ref[pos] = acc_scr[pl.ds(begin, count), :].astype(ref.dtype)
            at += count


def near_places(order):
    natural = sorted((n for n in order if n[0] == "a"), reverse=True) + ["z1", "z0"]
    places = []
    for pos in range(1 << len(order)):
        value = 0
        for d, name in enumerate(order):
            if (pos >> (len(order) - 1 - d)) & 1:
                value |= 1 << (len(natural) - 1 - natural.index(name))
        places.append(value)
    return places


def qkv_back(me, orders, dq, dk, dv, noisy_t, pw, bias, mod, w_local, tables, tcos, tsin, sums, begin, last):
    frames, patch, ftok = noisy_t.shape
    tokens, local = dq.shape
    width = pw.shape[1]
    cs, sn, _, _, sel = tables
    step = math.gcd(math.gcd(begin, last), 3)
    at = begin // step
    count = 1 << len(orders[0])
    rows = w_local.shape[0] // count
    first = -(-rows // 16) * 8
    blocks = [(count, first, width), (count, rows - first, width)]
    if last < frames:
        blocks = [w_local.shape]
    full = lambda shape: pl.BlockSpec(shape, lambda i, me: (0,) * len(shape))
    row = lambda cols: pl.BlockSpec((step * ftok, cols), lambda i, me: (i + at, 0))
    return pl.pallas_call(
        partial(
            qkv_back_kernel, width=width, local=local, maps=[near_places(o) for o in orders],
            begin=begin, last=last == frames,
        ),
        grid_spec=pltpu.PrefetchScalarGridSpec(num_scalar_prefetch=1, grid=((last - begin) // step,),
        in_specs=[
            row(local), row(local), row(local),
            pl.BlockSpec((step, patch, ftok), lambda i, me: (i + at, 0, 0)),
            full(pw.shape),
            full((1, width)),
            pl.BlockSpec((step, 1, 6 * width), lambda i, me: (i + at, 0, 0)),
            full(w_local.shape),
            full(sel.shape),
            full(cs.shape),
            full(sn.shape),
            pl.BlockSpec((step, 1, local // 2), lambda i, me: (i + at, 0, 0)),
            pl.BlockSpec((step, 1, local // 2), lambda i, me: (i + at, 0, 0)),
        ] + [full(a.shape) for a in sums],
        out_specs=[
            *(full(b) for b in blocks),
            pl.BlockSpec((step, 1, 2 * width), lambda i, me: (i, 0, 0)),
            full(pw.shape),
            full((1, width)),
        ],
        scratch_shapes=[
            pltpu.VMEM(w_local.shape, wide),
            pltpu.VMEM(pw.shape, wide),
            pltpu.VMEM((8, width), wide),
            pltpu.VMEM((6 * patch, width), low_type),
        ],
        ),
        out_shape=[
            *(jax.ShapeDtypeStruct(b, low_type if last == frames else wide) for b in blocks),
            jax.ShapeDtypeStruct((last - begin, 1, 2 * width), wide),
            jax.ShapeDtypeStruct(pw.shape, wide),
            jax.ShapeDtypeStruct((1, width), wide),
        ],
        compiler_params=pltpu.CompilerParams(
            dimension_semantics=("arbitrary",), vmem_limit_bytes=32 * MIB
        ),
        cost_estimate=pl.CostEstimate(
            flops=2 * 2 * tokens * width * 3 * local, bytes_accessed=16 * MIB, transcendentals=0
        ),
        name="qkv_back",
    )(me, dq, dk, dv, noisy_t, pw, bias, mod, w_local, sel, cs, sn, tcos, tsin, *sums)


def tri_blocks(count):
    return [(r, c) for r in range(count) for c in range(r, count)]


def tile_places(order):
    natural = sorted((n for n in order if n[0] == "a"), reverse=True) + ["x", "c", "z1", "z0"]
    places = []
    for pos in range(1 << len(order)):
        value = 0
        for d, name in enumerate(order):
            if (pos >> (len(order) - 1 - d)) & 1:
                value |= 1 << (len(natural) - 1 - natural.index(name))
        places.append(value)
    return places


def steer_kernel(
    tab_ref, clip_ref, *refs, blk, cuts, maps, rows
):
    mats = len(rows)
    arrived, sums = refs[:3], refs[3:6]
    olds, refs = refs[6 : 6 + mats], refs[6 + mats :]
    news, u_ref = refs[:mats], refs[mats]
    outs, scr = refs[mats + 1 : -1], refs[-1]
    clip = clip_ref[0]
    me = tab_ref[12]
    width = u_ref.shape[2]
    units = []
    for slot in range(3):
        source = tab_ref[9 + slot]
        units.append(
            jnp.where(
                source == 0, arrived[0][...], jnp.where(source == 1, arrived[1][...], arrived[2][...])
            )
        )
    whole = jnp.concatenate([ref[...] for ref in sums], axis=0)
    up, down, out = rows[2], rows[3], rows[1]
    grads = (
        jnp.concatenate(units, axis=0), whole[up + down :], whole[:up], whole[up : up + down]
    )
    low = []
    for m in range(mats):
        grad = clip * grads[m]
        moment = 0.95 * olds[m][...] + grad
        news[m][...] = moment
        steer = grad + 0.95 * moment
        u_ref[m, : rows[m], :] = steer
        if rows[m] < u_ref.shape[1]:
            u_ref[m, rows[m] :, :] = jnp.zeros((u_ref.shape[1] - rows[m], width), wide)
        low.append(steer.astype(low_type))
    pairs = tri_blocks(width // blk)
    clusters = len(maps[0]) // 32
    for n, (r, c) in enumerate(pairs):
        for m in range(mats):
            scr[m] = dot_tn(low[m][:, r * blk : (r + 1) * blk], low[m][:, c * blk : (c + 1) * blk])
        for m in range(mats // clusters):
            index = m * len(pairs) + n
            for part, ref in enumerate(outs):
                if cuts[part] <= index < cuts[part + 1]:
                    inner = index - cuts[part]
                    for pos, apart in enumerate(maps[part]):
                        which, top, left = tile_of(jnp.bitwise_xor(me, apart), mats // clusters, blk)
                        ref[pos, inner * 16 : (inner + 1) * 16, :] = scr[
                            which + m, pl.ds(pl.multiple_of(top, 16), 16),
                            pl.ds(pl.multiple_of(left, blk // 2), blk // 2),
                        ].astype(ref.dtype)


def tile_of(dev, mats_each, blk):
    return (
        lax.shift_right_logical(dev, 5) * mats_each,
        jnp.bitwise_and(lax.shift_right_logical(dev, 1), 15) * 16,
        jnp.bitwise_and(dev, 1) * (blk // 2),
    )


def steer_grams(table, clip, arrived, sums, moments, blk, cuts, orders, devices):
    width = moments[0].shape[1]
    rows = [m.shape[0] for m in moments]
    maps = [tile_places(o) for o in orders]
    shapes = [(devices, (cuts[k + 1] - cuts[k]) * 16, blk // 2) for k in range(len(orders))]
    steer_shape = (len(rows), max(rows), width)
    results = pl.pallas_call(
        partial(steer_kernel, blk=blk, cuts=cuts, maps=maps, rows=rows),
        grid_spec=pltpu.PrefetchScalarGridSpec(
            num_scalar_prefetch=2,
            grid=(1,),
            in_specs=[once(a.shape) for a in (*arrived, *sums, *moments)],
            out_specs=[once(m.shape) for m in moments]
            + [once(steer_shape)]
            + [once(s) for s in shapes],
            scratch_shapes=[pltpu.VMEM((len(rows), blk, blk), wide)],
        ),
        out_shape=[jax.ShapeDtypeStruct(m.shape, wide) for m in moments]
        + [jax.ShapeDtypeStruct(steer_shape, wide)]
        + [jax.ShapeDtypeStruct(s, low_type) for s in shapes],
        compiler_params=pltpu.CompilerParams(
            dimension_semantics=("arbitrary",), vmem_limit_bytes=24 * MIB
        ),
        name="steer_grams",
    )(table, clip, *arrived, *sums, *moments)
    return results[:4], results[4], results[5:]


def home_kernel(tab_ref, one_ref, two_ref, *refs):
    outs, sq_ref = refs[:3], refs[3]
    rows = outs[0].shape[0]
    whole = jnp.concatenate([one_ref[...], two_ref[...]], axis=0)
    pieces = [whole[n * rows : (n + 1) * rows] for n in range(3)]
    for color in range(3):
        slot = tab_ref[6 + color]
        outs[color][...] = jnp.where(
            slot == 0, pieces[0], jnp.where(slot == 1, pieces[1], pieces[2])
        )
    sq_ref[...] = jnp.sum(whole * whole, keepdims=True)


def home_units(table, one, two):
    rows = (one.shape[0] + two.shape[0]) // 3
    width = one.shape[1]
    piece = (rows, width)
    *pieces, squares = pl.pallas_call(
        home_kernel,
        grid_spec=pltpu.PrefetchScalarGridSpec(
            num_scalar_prefetch=1,
            grid=(1,),
            in_specs=[once(one.shape), once(two.shape)],
            out_specs=[once(piece)] * 3 + [once((1, 1))],
        ),
        out_shape=[jax.ShapeDtypeStruct(piece, wide)] * 3 + [jax.ShapeDtypeStruct((1, 1), wide)],
        compiler_params=pltpu.CompilerParams(
            dimension_semantics=("arbitrary",), vmem_limit_bytes=16 * MIB
        ),
        name="home_units",
    )(table, one, two)
    return pieces, squares[0, 0]


def polish_kernel(me_ref, u_ref, *refs, blk, cuts, maps, factors):
    mats, rows, width = u_ref.shape
    parts, olds, outs, g_scr = refs[: 2 * len(maps)], refs[2 * len(maps) : -mats - 1], refs[-mats - 1 : -1], refs[-1]
    pairs = tri_blocks(width // blk)
    me = me_ref[0]
    clusters = len(maps[0]) // 16
    diag = lax.broadcasted_iota(jnp.int32, (blk, blk), 0) == lax.broadcasted_iota(
        jnp.int32, (blk, blk), 1
    )
    for m in range(mats // clusters):
        for n, (r, c) in enumerate(pairs):
            index = m * len(pairs) + n
            for part, places in enumerate(maps):
                if not cuts[part] <= index < cuts[part + 1]:
                    continue
                inner = index - cuts[part]
                for ref, other in ((parts[2 * part], 0), (parts[2 * part + 1], 4)):
                    for pos, apart in enumerate(places):
                        which, top, left = tile_of(
                            jnp.bitwise_xor(me, apart + other), mats // clusters, blk
                        )
                        g_scr[
                            which + m, pl.ds(pl.multiple_of(r * blk + top, 16), 16),
                            pl.ds(pl.multiple_of(c * blk + left, blk // 2), blk // 2),
                        ] = ref[pos, inner * 16 : (inner + 1) * 16, :]
    for m in range(mats):
        trace = jnp.zeros((1, 1), wide)
        for r, c in pairs:
            piece = g_scr[m, r * blk : (r + 1) * blk, c * blk : (c + 1) * blk]
            if r == c:
                trace += jnp.sum(jnp.where(diag, piece.astype(wide), 0.0), keepdims=True)
            else:
                g_scr[m, c * blk : (c + 1) * blk, r * blk : (r + 1) * blk] = piece.T
        scale = jnp.sqrt(trace) + 1e-07
        inverse = 1.0 / scale
        inverse_sq = inverse * inverse
        own = outs[m].shape[0]

        def times(value):
            return dot_nn(value.astype(low_type), g_scr[m]) * inverse_sq

        def cubic(value):
            once_ = times(value)
            return coef_one * value + coef_two * once_ + coef_three * times(once_)

        current = cubic(u_ref[m, :own, :] * inverse)
        for _ in range(NS_ITERS - 1):
            second = cubic(cubic(times(current)))
            third = cubic(cubic(times(second)))
            current = coef_one * current + coef_two * second + coef_three * third
        outs[m][...] = olds[m][...] * (1.0 - 2.0 * 0.01) - factors[m] * current


def polish(me, u, parts, olds, blk, cuts, orders, factors):
    mats, rows, width = u.shape
    maps = [tile_places(o) for o in orders]
    return pl.pallas_call(
        partial(polish_kernel, blk=blk, cuts=cuts, maps=maps, factors=factors),
        grid_spec=pltpu.PrefetchScalarGridSpec(
            num_scalar_prefetch=1,
            grid=(1,),
            in_specs=[once(u.shape)] + [once(p.shape) for p in parts] + [once(o.shape) for o in olds],
            out_specs=[once(o.shape) for o in olds],
            scratch_shapes=[pltpu.VMEM((mats, width, width), low_type)],
        ),
        out_shape=[jax.ShapeDtypeStruct(o.shape, wide) for o in olds],
        compiler_params=pltpu.CompilerParams(
            dimension_semantics=("arbitrary",), vmem_limit_bytes=32 * MIB
        ),
        cost_estimate=pl.CostEstimate(
            flops=2 * 24 * mats * rows * width * width, bytes_accessed=12 * MIB, transcendentals=0
        ),
        name="polish",
    )(me, u, *parts, *olds)


def bit_stages(count_a):
    stages = {}
    bits_a = count_a.bit_length() - 1
    for b in range(bits_a):
        stages["a%d" % (bits_a - 1 - b)] = ("a", 1 << (bits_a - 1 - b), b)
    stages["x"] = ("x", 1, bits_a)
    stages["c"] = ("c", 1, bits_a + 1)
    stages["z1"] = ("z", 2, bits_a + 2)
    stages["z0"] = ("z", 1, bits_a + 3)
    return stages


def swap(value, axis, distance):
    size = lax.axis_size(axis)
    return lax.ppermute(value, axis, [(i, i ^ distance) for i in range(size)])


def bit_of(axis, distance):
    return (lax.axis_index(axis) // distance) % 2


def in_order(blocks, names):
    for dim, name in enumerate(names):
        axis = name[0]
        distance = {"z1": 2, "a1": 2, "a2": 4}.get(name, 1)
        mine = bit_of(axis, distance)
        flipped = jnp.flip(blocks, dim)
        blocks = jnp.where(mine == 0, blocks, flipped)
    natural = sorted(n for n in names if n[0] == "a")[::-1] + [
        n for n in ("x", "c", "z1", "z0") if n in names
    ]
    order = [names.index(n) for n in natural] + list(range(len(names), blocks.ndim))
    return blocks.transpose(order)


def three_orders(stages):
    names_a = [n for n in stages if n.startswith("a")]
    return (
        ["x"] + names_a + ["z0", "z1"],
        names_a + ["z0", "x", "z1"],
        ["z0", "x"] + names_a + ["z1"],
    )


def after(value, *others):
    return lax.optimization_barrier((value,) + others)[0]


def halve(blocks, order, stages):
    keep, send = blocks[0], blocks[1]
    for step, name in enumerate(order):
        axis, distance, _ = stages[name]
        got = swap(send.astype(low_type), axis, distance)
        if step == len(order) - 1:
            return keep.astype(wide) + got.astype(wide)
        send = (keep[1].astype(wide) + got[1].astype(wide)).astype(low_type)
        keep = keep[0].astype(wide) + got[0].astype(wide)


class Ladder:
    def __init__(self, blocks, orders, stages, held=low_type):
        self.orders, self.stages, self.rung, self.held = orders, stages, 0, held
        self.keep = [b[0] for b in blocks]
        self.send = [b[1] for b in blocks]

    def exchange(self):
        self.got = []
        for order, send in zip(self.orders, self.send):
            axis, distance, _ = self.stages[order[self.rung]]
            self.got.append(swap(send.astype(low_type), axis, distance))
        self.rung += 1

    def add(self, *first):
        got = lax.optimization_barrier(tuple(self.got) + first)[: len(self.got)]
        pairs = list(zip(self.keep, got))
        if self.rung == len(self.orders[0]):
            return [k.astype(wide) + g.astype(wide) for k, g in pairs]
        self.send = [(k[1].astype(wide) + g[1].astype(wide)).astype(low_type) for k, g in pairs]
        self.keep = [(k[0].astype(wide) + g[0].astype(wide)).astype(self.held) for k, g in pairs]


def double(block, order, stages):
    for name in order:
        axis, distance, _ = stages[name]
        block = jnp.stack([block, swap(block, axis, distance)])
    return block


def spread(payload):
    count = math.prod(lax.axis_size(n) for n in ALL)
    return lax.all_to_all(
        jnp.broadcast_to(payload[None], (count,) + payload.shape),
        ALL, split_axis=0, concat_axis=0, tiled=True,
    )


def unit_plan(devices):
    quarter = devices // 4
    edges = []
    for unit in range(3 * devices):
        section, place = unit // devices, unit % devices
        member, rest = place // quarter, place % quarter
        index = section * quarter + rest
        pos, slot = index // 3, index % 3
        a, z = pos // 4, pos % 4
        dest = ((a * 2 + member // 2) * 2 + member % 2) * 4 + z
        edges.append((unit // 3, unit % 3, dest, slot))
    left = list(edges)
    colors = []
    for _ in range(3):
        match = {}

        def augment(src, seen):
            for e in left:
                if e[0] != src or e[2] in seen:
                    continue
                seen.add(e[2])
                if e[2] not in match or augment(match[e[2]][0], seen):
                    match[e[2]] = e
                    return True
            return False

        for src in range(devices):
            assert augment(src, set())
        chosen = list(match.values())
        for e in chosen:
            left.remove(e)
        colors.append(chosen)
    return colors


def unit_tables(plan):
    devices = len(plan[0])
    tables = np.zeros((devices, 2, 2, 3), np.int32)
    for color, chosen in enumerate(plan):
        for src, src_slot, dst, dst_slot in chosen:
            tables[src, 0, 0, color], tables[dst, 0, 1, dst_slot] = src_slot, color
            tables[dst, 1, 0, color], tables[src, 1, 1, src_slot] = dst_slot, color
    return tables.reshape(devices, 12)


def away_kernel(tab_ref, w_ref, *outs):
    rows = outs[0].shape[0]
    whole = w_ref[...].astype(low_type)
    pieces = [whole[n * rows : (n + 1) * rows] for n in range(3)]
    for color in range(3):
        slot = tab_ref[color]
        outs[color][...] = jnp.where(
            slot == 0, pieces[0], jnp.where(slot == 1, pieces[1], pieces[2])
        )


def away_units(table, weight):
    piece = (weight.shape[0] // 3, weight.shape[1])
    return pl.pallas_call(
        away_kernel,
        grid_spec=pltpu.PrefetchScalarGridSpec(
            num_scalar_prefetch=1,
            grid=(1,),
            in_specs=[once(weight.shape)],
            out_specs=[once(piece)] * 3,
        ),
        out_shape=[jax.ShapeDtypeStruct(piece, low_type)] * 3,
        compiler_params=pltpu.CompilerParams(
            dimension_semantics=("arbitrary",), vmem_limit_bytes=16 * MIB
        ),
        name="away_units",
    )(table, weight)


def place_kernel(tab_ref, *refs):
    pieces, out_ref = refs[:3], refs[3]
    rows = pieces[0].shape[0]
    for slot in range(3):
        source = tab_ref[3 + slot]
        out_ref[slot * rows : (slot + 1) * rows, :] = jnp.where(
            source == 0, pieces[0][...], jnp.where(source == 1, pieces[1][...], pieces[2][...])
        )


def place_units(table, pieces):
    rows, width = pieces[0].shape
    return pl.pallas_call(
        place_kernel,
        grid_spec=pltpu.PrefetchScalarGridSpec(
            num_scalar_prefetch=1,
            grid=(1,),
            in_specs=[once((rows, width))] * 3,
            out_specs=once((3 * rows, width)),
        ),
        out_shape=jax.ShapeDtypeStruct((3 * rows, width), low_type),
        compiler_params=pltpu.CompilerParams(
            dimension_semantics=("arbitrary",), vmem_limit_bytes=16 * MIB
        ),
        name="place_units",
    )(table, *pieces)


def send_units(pieces, plan, back):
    src, dst = (2, 0) if back else (0, 2)
    return [
        lax.ppermute(piece, ALL, [(e[src], e[dst]) for e in chosen])
        for piece, chosen in zip(pieces, plan)
    ]


def body(
    noisy_latents,
    target_latents,
    noise_levels,
    clip_start,
    qkv_weight,
    qkv_moment,
    out_weight,
    out_moment,
    up_weight,
    up_moment,
    down_weight,
    down_moment,
    ada_weight,
    ada_first,
    ada_second,
    patch_weight,
    patch_first,
    patch_second,
    vectors,
    vec_first,
    vec_second,
):
    count_a = lax.axis_size("a")
    members = lax.axis_size("x") * lax.axis_size("c")
    devices = count_a * members * lax.axis_size("z")
    groups = count_a * lax.axis_size("z")
    frames_dev = noise_levels.shape[0]
    tokens_dev = noisy_latents.shape[0]
    frame_tok = tokens_dev // frames_dev
    width = patch_weight.shape[2]
    patch_size = patch_weight.shape[1]
    head_dim = width // HEADS
    local_heads = HEADS // members
    local = local_heads * head_dim
    group_frames = frames_dev * members
    frames_all = frames_dev * devices
    group_tokens = group_frames * frame_tok
    score_scale = 1.0 / math.sqrt(head_dim)
    stages = bit_stages(count_a)
    my_a, my_z = lax.axis_index("a"), lax.axis_index("z")
    my_group = my_a * 4 + my_z
    my_member = lax.axis_index("x") * 2 + lax.axis_index("c")
    tables = rope_tables(head_dim, local_heads, frame_tok)
    tables = tables[:4] + (jnp.asarray(tables[4], low_type),)
    plan = unit_plan(devices)

    rows_unit = qkv_weight.shape[0] // 3
    me = lax.axis_index(ALL).astype(jnp.int32)
    table = jnp.concatenate([jnp.asarray(unit_tables(plan))[me], me[None]])
    units = place_units(table, send_units(away_units(table, qkv_weight), plan, False))
    units = units.reshape(3, rows_unit, width)
    names_a = [n for n in stages if n.startswith("a")]

    swap_axes = ("x", "c", "z")
    moves = [(g * 4 + z, z * 4 + g) for g in range(4) for z in range(4)]
    noisy_t = noisy_latents.T.reshape(patch_size, frames_dev, frame_tok).transpose(1, 0, 2)
    target_t = target_latents.T.reshape(patch_size, frames_dev, frame_tok).transpose(1, 0, 2)
    mine = lax.ppermute(jnp.stack([noisy_t, target_t]), swap_axes, moves)

    meta = jnp.concatenate([noise_levels, clip_start]).astype(wide)
    meta = jnp.pad(meta, (0, 128 - meta.shape[0]))[None]
    meta_all = spread(after(meta, units))[:, 0]
    rows_up, rows_out = up_weight.shape[0], out_weight.shape[0]
    layout = part_layout(rows_up, rows_out)
    rising = [
        ["z1", "z0"] + names_a[::-1] + ["x"],
        ["z1", "x", "z0"] + names_a[::-1],
        ["z1"] + names_a[::-1] + ["x", "z0"],
    ]
    gather_orders = [o[::-1] for o in rising]
    rows_part = (2 * rows_up + rows_out) // 3
    bulk = jnp.concatenate([up_weight, down_weight, out_weight], axis=0).astype(low_type)
    shares = [bulk[n * rows_part : (n + 1) * rows_part] for n in range(3)]
    climb = lambda shares, rung: [
        double(share, [order[rung]], stages) for share, order in zip(shares, rising)
    ]
    far = double(units, ["z1"], stages)
    meta_all, far, mine = lax.optimization_barrier((meta_all, far, mine))
    shares = climb([after(share, far) for share in shares], 0)
    levels_all = meta_all[:, :frames_dev].reshape(frames_all)
    starts_all = meta_all[:, frames_dev : 2 * frames_dev].reshape(frames_all)
    starts_group = lax.dynamic_slice_in_dim(starts_all, my_group * group_frames, group_frames)
    starts_int = starts_group.astype(jnp.int32)
    noisy_mine, target_mine = mine[0], mine[1]
    pair = double(noisy_mine, ["c"], stages)

    half_one = double(far[:, :, : rows_unit // 2], ["z0"], stages)
    half_two = double(far[:, :, rows_unit // 2 :], names_a[::-1], stages)
    cond_low = jax.nn.silu(level_features(levels_all, width)).astype(low_type)
    ada_rows = ada_weight.shape[0]
    mod_rows = dot_nt(cond_low, ada_weight.astype(low_type))
    mod_rows, pair = lax.optimization_barrier((mod_rows, pair))
    mod_out = jnp.broadcast_to(
        mod_rows.reshape(count_a, 1, 4, group_frames, ada_rows),
        (count_a, members, 4, group_frames, ada_rows),
    ).reshape(devices, group_frames, ada_rows)
    mod_in = lax.all_to_all(
        mod_out.astype(low_type), ALL, split_axis=0, concat_axis=0, tiled=True
    ).astype(wide)
    noisy_group = in_order(double(pair, ["x"], stages), ["x", "c"]).reshape(
        group_frames, patch_size, frame_tok
    )
    half_one = double(half_one, names_a[::-1], stages)
    half_two = double(half_two, ["z0"], stages)
    *shares, mod_in = lax.optimization_barrier((*shares, mod_in))
    shares = climb(shares, 1)
    mod_in, half_one, half_two, noisy_group = lax.optimization_barrier(
        (mod_in, half_one, half_two, noisy_group)
    )
    half_one = in_order(half_one, names_a + ["z0", "z1"])
    half_two = in_order(half_two, ["z0"] + names_a + ["z1"])
    qkv_local = jnp.concatenate(
        [half_one.reshape(3 * groups, -1, width), half_two.reshape(3 * groups, -1, width)], axis=1
    ).reshape(3 * local, width)
    modul = mod_in.transpose(1, 0, 2).reshape(group_frames, 6 * width) + vectors[2:8].reshape(
        1, 6 * width
    )
    mod3 = modul.reshape(group_frames, 1, 6 * width)
    *shares, mod3 = lax.optimization_barrier((*shares, mod3))
    shares = climb(shares, 2)
    mod_mine = lax.dynamic_slice_in_dim(mod3, my_member * frames_dev, frames_dev)

    frame_ids = jnp.arange(group_frames, dtype=jnp.int32)
    time_pos = (frame_ids - starts_int).astype(wide)
    t_angle = time_pos[:, None] * tables[2][None, :]
    tcos = (jnp.cos(t_angle) * tables[3][None, :])[:, None, :]
    tsin = (jnp.sin(t_angle) * tables[3][None, :])[:, None, :]

    pw_in = patch_weight[0]
    bias_in = vectors[0:1]
    q, k, v = embed_qkv(
        noisy_group, pw_in, bias_in, mod3, qkv_local, tables, tcos, tsin, score_scale
    )
    place = jnp.stack([me // 4, me % 4])
    *shares, q = lax.optimization_barrier((*shares, q))
    for rung in range(3, len(rising[0]) - 1):
        shares = climb(shares, rung)
    final = []
    for share, order in zip(shares, rising):
        axis, distance, _ = stages[order[-1]]
        final.append(swap(share, axis, distance))
    att, att_low, lse = attend(starts_int, q, k, v, group_frames, local_heads)
    final = lax.optimization_barrier((*final, lse))[:3]
    shares = [jnp.stack(pair) for pair in zip(shares, final)]
    shares = [(share, swap(share, "c", 1)) for share in shares]
    framed = lax.all_to_all(
        att_low.reshape(members, tokens_dev, local), ("x", "c"), split_axis=0, concat_axis=0,
        tiled=True,
    )

    gain = vectors[1:2]
    pw_out = patch_weight[1]
    state_one, branch, h_two, out_full = post_attend(
        me[None], framed, noisy_mine, pw_in, bias_in, mod_mine, shares[2], gather_orders[2],
        layout[2][0][1],
    )
    act, slope, mixed, pred = ff_forward(
        place, h_two, state_one, mod_mine, shares, gather_orders, layout, gain, pw_out, frame_tok,
    )
    member_axes = ("x", "c")
    ahead = [(i, i + 1) for i in range(members - 1)]
    behind = [(i + 1, i) for i in range(members - 1)]
    edge = lax.ppermute(
        jnp.stack([pred[-1], target_mine[-1]]).astype(low_type), member_axes, ahead
    ).astype(wide)
    prev_pred = jnp.concatenate([edge[0:1], pred[:-1]], axis=0)
    prev_goal = jnp.concatenate([edge[1:2], target_mine[:-1]], axis=0)
    diff = pred - prev_pred - (target_mine - prev_goal)
    my_frames = my_member * frames_dev + jnp.arange(frames_dev, dtype=jnp.int32)
    valid = my_frames > lax.dynamic_slice_in_dim(starts_int, my_member * frames_dev, frames_dev)
    loss_local = jnp.sum(jnp.where(valid[:, None, None], diff * diff, 0.0))
    entry_count = float(frames_all * frame_tok * patch_size)
    d_diff = jnp.where(valid[:, None, None], (2.0 / entry_count) * diff, 0.0)
    returned = lax.ppermute(d_diff[0], member_axes, behind)
    d_pred = d_diff - jnp.concatenate([d_diff[1:], returned[None]], axis=0)
    d_hidden, d_mixed, d_branch, d_framed, d_small, d_sums, d_mod_rest = ff_backward(
        place, d_pred, state_one, mixed, branch, mod_mine, noisy_mine, gain, pw_out, shares,
        gather_orders, layout, out_full, slope, members,
    )
    d_att = lax.all_to_all(d_framed, ("x", "c"), split_axis=0, concat_axis=0, tiled=True).reshape(
        group_tokens, local
    )

    orders = three_orders(stages)
    grads_of = lambda half, adds=(): wide_grads(
        place, half, d_hidden, act, d_branch, h_two, d_mixed, framed, orders, devices, adds
    )
    others = grads_of(1)
    core_axis, core_distance, _ = stages["c"]
    passed = [swap(o, core_axis, core_distance) for o in others]

    cuts = [group_frames * n // 12 for n in (0, 9, 12)]

    def part_back(n, q, sums):
        return attend_back(
            starts_int, q, d_att, att, lse, k, v, sums, cuts[n], cuts[n + 1], group_frames,
            local_heads, score_scale,
        )

    ladder = Ladder(grads_of(0, passed), orders, stages)
    ladder.exchange()
    dq, dk, dv = part_back(0, after(q, *ladder.send), ())
    ladder.add(dk)
    ladder.exchange()
    dq, dk, dv = part_back(1, after(q, *ladder.send), (dq, dk, dv))
    ladder.add(dk)
    ladder.exchange()
    dv = after(dv, *ladder.send)
    near_orders = [names_a + ["z0", "z1"], ["z0"] + names_a + ["z1"]]

    def tail_back(dv, sums, begin, last):
        return qkv_back(
            (my_a * 4 + my_z).astype(jnp.int32)[None], near_orders, dq, dk, dv, noisy_group, pw_in,
            bias_in, mod3, qkv_local, tables, tcos, tsin, sums, begin, last,
        )

    middle = group_frames // 2
    dw, d_mod_early, d_embed, d_bias = tail_back(dv, (), 0, middle)
    while ladder.rung < len(orders[0]):
        ladder.add(d_bias)
        ladder.exchange()
    dw_one, dw_two, d_mod_late, d_embed, d_bias = tail_back(
        after(dv, *ladder.send), (dw, d_embed, d_bias), middle, group_frames
    )
    d_mod_one = jnp.concatenate([d_mod_early, d_mod_late], axis=0)
    near_dims = (2,) * len(near_orders[0])
    near = Ladder(
        [d.reshape(near_dims + d.shape[1:]) for d in (dw_one, dw_two)], near_orders, stages, wide
    )
    near.exchange()
    near.got = list(lax.optimization_barrier((*near.got, *ladder.got)))[: len(near.got)]
    d_rest = lax.dynamic_update_slice_in_dim(
        jnp.zeros((group_frames, 4 * width), wide),
        d_mod_rest.reshape(frames_dev, 4 * width), my_member * frames_dev, 0,
    )
    d_mod = jnp.concatenate([d_mod_one[:, 0], d_rest], axis=1)
    d_mod = d_mod.reshape(group_frames, devices, ada_rows).transpose(1, 0, 2)
    smalls = jnp.concatenate(
        [d_embed + d_small[1], d_small[0], d_bias + d_sums[1:2], d_sums[0:1]], axis=0
    )
    small_rows = smalls.shape[0]
    small_part = small_rows * width // devices
    mod_part = group_frames * ada_rows
    packed = jnp.concatenate(
        [d_mod.reshape(devices, mod_part), smalls.reshape(devices, small_part)], axis=1
    )
    pad = -packed.shape[1] % 128
    packed = jnp.pad(packed, ((0, 0), (0, pad))).reshape(devices, -1, 128)
    arrived = lax.all_to_all(packed, ALL, split_axis=0, concat_axis=0, tiled=True).reshape(
        devices, -1
    )
    small_mine = jnp.sum(arrived[:, mod_part : mod_part + small_part], axis=0)
    mod_grad = (
        arrived[:, :mod_part]
        .reshape(count_a, members, 4, group_frames, ada_rows)
        .sum(axis=1)
        .reshape(frames_all, ada_rows)
    )
    bias_mine = jnp.sum(mod_grad, axis=0)
    g_ada = dot_tn(mod_grad.astype(low_type), cond_low)

    g_wide = ladder.add()
    rest_sq = (
        sum((jnp.sum(piece * piece) for piece in g_wide))
        + jnp.sum(g_ada * g_ada)
        + jnp.sum(small_mine * small_mine)
        + jnp.sum(bias_mine * bias_mine)
    )
    while near.rung < len(near_orders[0]):
        near.add()
        near.exchange()
    *near.got, rest_sq, g_ada = lax.optimization_barrier((*near.got, rest_sq, g_ada))
    g_one, g_two = near.add()
    units_out, units_sq = home_units(table, g_one, g_two)
    units_home = send_units(units_out, plan, True)
    local_sq = rest_sq + units_sq
    totals = jnp.where(lax.broadcasted_iota(jnp.int32, (1, 128), 1) == 0, local_sq, loss_local)
    totals = jnp.sum(spread(totals)[:, 0, :2], axis=0)
    norm = jnp.sqrt(totals[0])
    loss_total = totals[1]
    report = jnp.concatenate([small_mine, bias_mine])
    report = jnp.pad(report, (0, -report.shape[0] % 128)).reshape(-1, 128)
    report = after(report, norm)
    clip = jnp.minimum(1.0, 0.01 / norm)

    olds = (qkv_weight, out_weight, up_weight, down_weight)
    moments = (qkv_moment, out_moment, up_moment, down_moment)
    ada_new, ada_one, ada_two = adamw(ada_weight, ada_first, ada_second, clip * g_ada, 0.08)
    blk = 256
    gram_orders = [["c"] + o for o in orders[:2]]
    pairs = len(tri_blocks(width // blk)) * 4 // (devices // 32)
    cuts = (0, pairs // 2, pairs)
    parts = []
    report_order = ["z1", "z0"] + names_a[::-1] + ["x", "c"]
    ladders = []
    moments_new, steers, tiles = steer_grams(
        table, clip[None], units_home, g_wide, moments, blk, cuts, gram_orders, devices
    )
    for k, part in enumerate(tiles):
        ladders.append(Ladder([part.reshape((2,) * len(stages) + part.shape[1:])], [gram_orders[k]], stages))
    for rung in range(len(stages)):
        for ladder in ladders:
            ladder.exchange()
        report = double(after(report, ladders[0].got[0]), [report_order[rung]], stages)
        ties = []
        if rung == 2:
            ties = [ada_new, ada_one, ada_two]
        results = []
        for ladder in ladders:
            got, *ties = lax.optimization_barrier((ladder.got[0], *ties))
            ladder.got = [got]
            results.append(ladder.add())
        if rung == 2:
            ada_new, ada_one, ada_two = ties
    everyone = in_order(report, report_order[::-1]).reshape(devices, -1)
    small_all = everyone[:, :small_part].reshape(small_rows, width)
    bias_all = everyone[:, small_part : small_part + ada_rows].reshape(6, width)
    g_patch = small_all[: 2 * patch_size].reshape(2, patch_size, width)
    g_vec = jnp.concatenate([small_all[2 * patch_size :], bias_all], axis=0)
    patch_new, patch_one, patch_two = adamw(
        patch_weight, patch_first, patch_second, clip * g_patch, 0.15
    )
    vec_new, vec_one, vec_two = adamw(vectors, vec_first, vec_second, clip * g_vec, 0.5)
    lines = [result[0].astype(low_type) for result in results]
    late = [patch_new, patch_one, patch_two, vec_new, vec_one, vec_two]
    for rung in range(1, len(stages)):
        lines = [
            double(line, [gram_orders[n][:0:-1][rung - 1]], stages) for n, line in enumerate(lines)
        ]
        if rung == len(stages) - 2:
            lines[0], *late = lax.optimization_barrier((lines[0], *late))
    patch_new, patch_one, patch_two, vec_new, vec_one, vec_two = late
    parts = []
    for line in lines:
        line = line.reshape((-1,) + line.shape[-2:])
        parts += [line, swap(line, "c", 1)]
    factors = [2.0 * math.sqrt(max(1.0, o.shape[0] * devices / width)) for o in olds]
    updated = polish(
        me[None], steers, parts, olds, blk, cuts, [o[1:] for o in gram_orders], factors
    )
    return (
        loss_total,
        norm,
        updated[0],
        moments_new[0],
        updated[1],
        moments_new[1],
        updated[2],
        moments_new[2],
        updated[3],
        moments_new[3],
        ada_new,
        ada_one,
        ada_two,
        patch_new,
        patch_one,
        patch_two,
        vec_new,
        vec_one,
        vec_two,
    )


def solution(mesh):
    groups, line = mesh.shape["dp"], mesh.shape["seq"]
    inner = Mesh(mesh.devices.reshape(groups // 4, 2, 2, line), ALL)
    split = P(ALL, None)
    copied = P()
    placed = (split, split, P(ALL), P(ALL)) + (split,) * 11 + (copied,) * 6
    return jax.shard_map(
        body,
        mesh=inner,
        in_specs=placed,
        out_specs=(copied, copied) + (split,) * 11 + (copied,) * 6,
        check_vma=False,
    )
```
